32 devices in a mesh: grp: 2 (over y), shot: 16 (over z, x, core), depth: 1.
Axes of the slice: x: 2, y: 2, z: 4, core: 2. Of those that a mesh axis runs over, the one named last changes fastest.
Arguments:
- velocity_p: bfloat16 [128, 8, 8, 128], P(('grp', 'shot'), None, None, 'depth'), parts along dimension 0, may hold values from 0.5 to 0.8984375
- velocity_s: bfloat16 [128, 8, 8, 128], P(('grp', 'shot'), None, None, 'depth'), parts along dimension 0, may hold values from 0.19921875 to 0.5
- density: bfloat16 [128, 8, 8, 128], P(('grp', 'shot'), None, None, 'depth'), parts along dimension 0, may hold values from 1 to 2
- perturbation: bfloat16 [128, 8, 8, 128], P(('grp', 'shot'), None, None, 'depth'), parts along dimension 0, may hold values from -4 to 4
- seafloor: int32 [128, 8, 8], P(('grp', 'shot')), parts along dimension 0, may hold values from 16 to 63
- owner_ids: int32 [128], P(('grp', 'shot')), parts along dimension 0, may hold values from 0 to 63, each once
- corner_x: int32 [32], P(('grp', 'shot')), parts along dimension 0, may hold values from 0 to 4
- corner_y: int32 [32], P(('grp', 'shot')), parts along dimension 0, may hold values from 0 to 4
- wave_prev: bfloat16 [32, 32, 32, 128], P(('grp', 'shot'), None, None, 'depth'), parts along dimension 0, may hold values from -6 to 6
- wave_now: bfloat16 [32, 32, 32, 128], P(('grp', 'shot'), None, None, 'depth'), parts along dimension 0, may hold values from -6 to 6
Outputs:
- hessian_vec: float32 [128, 8, 8, 128], P(('grp', 'shot'), None, None, 'depth'), parts along dimension 0
The draws below stay inside these ranges and needn't reach their ends.
There are 2 independent parts, one for each index of `grp`. The reference program is written for one: setup_inputs(seed, part) draws one part's arguments, and reference() takes and returns one part's arrays. A program takes and returns all parts, laid end to end along the dimension named above; each array names one. Nothing has to cross between parts.
Inputs may be any that keep to these rules, and one draw needn't show every extreme that they name: `owner_ids`: each lateral block is held by exactly one slot. Shot s images the block rows corner_x[s] to corner_x[s] + 3. Shot s images the block columns corner_y[s] to corner_y[s] + 3.
All inputs are finite; a program needn't handle non-finite values.
Results may differ from the reference program's by a relative error of at most 0.0048.
Values may be sent and summed in bfloat16 or wider, within the bound.
No kernel may reach another device: no remote copies, remote signals or barrier semaphores. Data moves between devices by JAX's collectives and lax.ppermute only.
A program may use at most 64 MiB of HBM per device.

```python
import jax
import jax.numpy as jnp
from jax import lax

BX = 8
BY = 8
APX = 4
APY = 4
STEPS = 4
SHOTS = 16
BLOCKS = 64
GRID_Y = 8
GRID_X = 8
NZ = 128
AX = 32
AY = 32


def with_ends(drawn, stream_key, least, top_value):
    longest = drawn.shape.index(max(drawn.shape))
    spots = []
    for shift in (0, 1):
        where = [jax.random.randint(jax.random.fold_in(stream_key, axis), (), 0, length) for axis, length in enumerate(drawn.shape)]
        where[longest] = (where[longest] + shift) % drawn.shape[longest]
        spots.append(tuple(where))
    return drawn.at[spots[0]].set(least).at[spots[1]].set(top_value)


def level_of(rng, dims, split, least, largest):
    def one(position, parts):
        draws = jax.random.uniform(jax.random.fold_in(jax.random.fold_in(rng, 6), position), (parts,), jnp.float32, least / len(split), largest / len(split))
        return jnp.repeat(jnp.exp(draws), dims[position] // parts).reshape((-1,) + (1,) * (len(dims) - position - 1))

    factor_of = one(*split[0])
    for cut in split[1:]:
        factor_of = factor_of * one(*cut)
    return factor_of


def noise(rng, extent, width, most, cuts=(), kind=jnp.bfloat16):
    result = jax.random.normal(rng, extent, jnp.float32) * width
    if len(cuts) > 0:
        result = level_of(rng, extent, cuts, -0.22, 0.18) * result
    return jnp.clip(result, min=-most, max=most).astype(kind)


def setup_inputs(seed: int = 0, part: int = 0) -> dict:
    key_of = jax.random.split(jax.random.key(seed), 11)
    own_keys = jax.random.split(jax.random.fold_in(key_of[10], part), 11)
    return {
        "velocity_p": jnp.clip(0.5 + 0.3984375 * jax.random.uniform(own_keys[0], (BLOCKS, BX, BY, NZ), jnp.float32) ** level_of(own_keys[0], (BLOCKS, BX, BY, NZ), ((0, 16),), -0.2, 0.2), 0.5, 0.8984375).astype(jnp.bfloat16),
        "velocity_s": jnp.clip(0.19921875 + 0.30078125 * jax.random.uniform(own_keys[1], (BLOCKS, BX, BY, NZ), jnp.float32) ** level_of(own_keys[1], (BLOCKS, BX, BY, NZ), ((0, 16),), -0.2, 0.2), 0.19921875, 0.5).astype(jnp.bfloat16),
        "density": jnp.clip(1.0 + 1.0 * jax.random.uniform(own_keys[2], (BLOCKS, BX, BY, NZ), jnp.float32) ** level_of(own_keys[2], (BLOCKS, BX, BY, NZ), ((0, 16),), -0.2, 0.2), 1.0, 2.0).astype(jnp.bfloat16),
        "perturbation": noise(own_keys[3], (BLOCKS, BX, BY, NZ), 1.0, 4.0, ((0, 16),)),
        "seafloor": with_ends(jax.random.randint(own_keys[4], (BLOCKS, BX, BY), NZ // 8, NZ // 2), jax.random.fold_in(own_keys[4], 1), NZ // 8, (NZ // 2) - 1).astype(jnp.int32),
        "owner_ids": jax.random.permutation(own_keys[5], BLOCKS).astype(jnp.int32),
        "corner_x": with_ends(jax.random.randint(own_keys[6], (SHOTS,), 0, GRID_X - APX + 1), jax.random.fold_in(own_keys[6], 1), 0, GRID_X - APX).astype(jnp.int32),
        "corner_y": with_ends(jax.random.randint(own_keys[7], (SHOTS,), 0, GRID_Y - APY + 1), jax.random.fold_in(own_keys[7], 1), 0, GRID_Y - APY).astype(jnp.int32),
        "wave_prev": noise(own_keys[8], (SHOTS, AX, AY, NZ), 1.0, 6.0, ((0, 16),)),
        "wave_now": noise(own_keys[9], (SHOTS, AX, AY, NZ), 1.0, 6.0, ((0, 16),)),
    }


speed_factor = 0.28
image_scale = 0.01


def laplace(field):
    padded = jnp.pad(field, 1)
    beside = padded[2:, 1:-1, 1:-1] + padded[:-2, 1:-1, 1:-1]
    beside = beside + padded[1:-1, 2:, 1:-1] + padded[1:-1, :-2, 1:-1]
    beside = beside + padded[1:-1, 1:-1, 2:] + padded[1:-1, 1:-1, :-2]
    return beside - 6.0 * field


def laplace_many(fields):
    return [laplace(field) for field in fields]


def coefficient(velocity_p, velocity_s, density, seafloor, depth_base):
    depth_index = depth_base + lax.broadcasted_iota(jnp.int32, velocity_p.shape, 3)
    solid = depth_index >= seafloor[..., None]
    primary = velocity_p.astype(jnp.float32)
    shear = velocity_s.astype(jnp.float32)
    stiffness = jnp.where(solid, primary * primary + shear * shear, primary * primary)
    return (speed_factor * stiffness / density.astype(jnp.float32)).astype(jnp.bfloat16)


def propagate(kappa, contrast, before, current, apply):
    grads = []
    datas = []
    first = apply([current])
    grad_now = first[0]
    delta_prev = jnp.zeros_like(current)
    delta_now = contrast * grad_now
    grads.append(grad_now)
    datas.append(delta_now)
    following = 2.0 * current - before + kappa * grad_now
    before, current = current, following
    for step in range(1, STEPS):
        both = apply([current, delta_now])
        grad_now = both[0]
        delta_next = 2.0 * delta_now - delta_prev + kappa * both[1] + contrast * grad_now
        grads.append(grad_now)
        datas.append(delta_next)
        delta_prev, delta_now = delta_now, delta_next
        if step + 1 < STEPS:
            following = 2.0 * current - before + kappa * grad_now
            before, current = current, following
    back = datas[STEPS - 1]
    back_after = jnp.zeros_like(back)
    image = grads[STEPS - 1] * back
    for step in range(STEPS - 2, -1, -1):
        spread = apply([kappa * back])
        back_new = 2.0 * back - back_after + spread[0] + datas[step]
        image = image + grads[step] * back_new
        back_after, back = back, back_new
    return image


def take_patch(grid, start_x, start_y):
    zero = jnp.zeros((), jnp.int32)
    patch = lax.dynamic_slice(grid, (start_x.astype(jnp.int32), start_y.astype(jnp.int32), zero, zero, zero), (APX, APY, BX, BY, NZ))
    return patch.transpose(0, 2, 1, 3, 4).reshape(APX * BX, APY * BY, NZ)


def reference(velocity_p, velocity_s, density, perturbation, seafloor, owner_ids, corner_x, corner_y, wave_prev, wave_now):
    coef = coefficient(velocity_p, velocity_s, density, seafloor, 0)
    coef_block = jnp.zeros_like(coef).at[owner_ids].set(coef).reshape(GRID_X, GRID_Y, BX, BY, NZ)
    pert_block = jnp.zeros_like(perturbation).at[owner_ids].set(perturbation).reshape(GRID_X, GRID_Y, BX, BY, NZ)

    def one_shot(total, index):
        start_x = corner_x[index].astype(jnp.int32)
        start_y = corner_y[index].astype(jnp.int32)
        kappa = take_patch(coef_block, start_x, start_y).astype(jnp.float32)
        contrast = speed_factor * take_patch(pert_block, start_x, start_y).astype(jnp.float32)
        image = propagate(kappa, contrast, wave_prev[index].astype(jnp.float32), wave_now[index].astype(jnp.float32), laplace_many)
        image = (image_scale * image).reshape(APX, BX, APY, BY, NZ).transpose(0, 2, 1, 3, 4)
        zero = jnp.zeros((), jnp.int32)
        anchor = (start_x, start_y, zero, zero, zero)
        present = lax.dynamic_slice(total, anchor, (APX, APY, BX, BY, NZ))
        return lax.dynamic_update_slice(total, present + image, anchor), None

    total, _ = lax.scan(one_shot, jnp.zeros((GRID_X, GRID_Y, BX, BY, NZ), jnp.float32), jnp.arange(SHOTS, dtype=jnp.int32))
    return total.reshape(BLOCKS, BX, BY, NZ)[owner_ids]
```

```python
import jax
import jax.numpy as jnp
from jax import lax
from jax.experimental import pallas as pl
from jax.experimental.pallas import tpu as pltpu
from jax.sharding import PartitionSpec as P

APX = 4
APY = 4
STEPS = 4
GRID_COLS = 8
EDGE = 8

speed_factor = 0.28
image_scale = 0.01


def with_halo(block, sides, width):
    for axis, dim in sides:
        count = lax.axis_size(axis)
        forward = [(i, i + 1) for i in range(count - 1)]
        backward = [(target, source) for source, target in forward]
        low = lax.ppermute(
            lax.slice_in_dim(block, block.shape[dim] - width, None, axis=dim), axis, forward
        )
        high = lax.ppermute(lax.slice_in_dim(block, 0, width, axis=dim), axis, backward)
        block = jnp.concatenate([low, block, high], axis=dim)
    return block


def laplace_many(fields):
    stacked = jnp.stack(fields)
    padded = with_halo(stacked.astype(jnp.bfloat16), (("depth", 3),), 1).astype(stacked.dtype)
    padded = jnp.pad(padded, ((0, 0), (1, 1), (1, 1), (0, 0)))
    beside = padded[:, 2:, 1:-1, 1:-1] + padded[:, :-2, 1:-1, 1:-1]
    beside = beside + padded[:, 1:-1, 2:, 1:-1] + padded[:, 1:-1, :-2, 1:-1]
    beside = beside + padded[:, 1:-1, 1:-1, 2:] + padded[:, 1:-1, 1:-1, :-2]
    result = beside - 6.0 * stacked
    return [result[index] for index in range(len(fields))]


def coefficient(velocity_p, velocity_s, density, seafloor, depth_base):
    depth_index = depth_base + lax.broadcasted_iota(jnp.int32, velocity_p.shape, 3)
    solid = depth_index >= seafloor[..., None]
    primary = velocity_p.astype(jnp.float32)
    shear = velocity_s.astype(jnp.float32)
    stiffness = jnp.where(solid, primary * primary + shear * shear, primary * primary)
    return (speed_factor * stiffness / density.astype(jnp.float32)).astype(jnp.bfloat16)


def propagate(kappa, contrast, before, current, apply):
    grads = []
    datas = []
    grad_now = apply([current])[0]
    delta_prev = jnp.zeros_like(current)
    delta_now = contrast * grad_now
    grads.append(grad_now)
    datas.append(delta_now)
    before, current = (current, 2.0 * current - before + kappa * grad_now)
    for step in range(1, STEPS):
        grad_now, spread = apply([current, delta_now])
        delta_next = 2.0 * delta_now - delta_prev + kappa * spread + contrast * grad_now
        grads.append(grad_now)
        datas.append(delta_next)
        delta_prev, delta_now = (delta_now, delta_next)
        if step + 1 < STEPS:
            before, current = (current, 2.0 * current - before + kappa * grad_now)
    back = datas[STEPS - 1]
    back_after = jnp.zeros_like(back)
    image = grads[STEPS - 1] * back
    for step in range(STEPS - 2, -1, -1):
        spread = apply([kappa * back])
        back_new = 2.0 * back - back_after + spread[0] + datas[step]
        image = image + grads[step] * back_new
        back_after, back = (back, back_new)
    return image


def vmem():
    return pl.BlockSpec(memory_space=pltpu.VMEM)


def smem():
    return pl.BlockSpec(memory_space=pltpu.SMEM)


def pick_kernel(table_ref, pieces_ref, out_ref):
    count = out_ref.shape[0]

    def one(index, carry):
        for inner in range(16):
            spot = index * 16 + inner
            out_ref[spot] = pieces_ref[table_ref[spot]]
        return carry

    lax.fori_loop(0, count // 16, one, 0)


def wave_kernel(
    corner_ref, model_ref, prev_ref, now_ref, out_ref,
    kap, con, fields, flats, image,
):
    span_x, span_y, depth = prev_ref.shape
    block_x = span_x // APX
    block_y = span_y // APY
    lo, hi = EDGE, EDGE + span_y
    lane = lax.broadcasted_iota(jnp.int32, (span_y, depth), 1)
    first_lane = lane == 0
    last_lane = lane == depth - 1
    u_a, u_b, d_0, d_1, d_2, kb_a, kb_b = [fields.at[i] for i in range(7)]
    g_0, g_1, g_2, d_3, b_2, b_1 = [flats.at[i] for i in range(6)]

    flat_edge = jnp.zeros((8, depth), jnp.float32)
    for index in range(fields.shape[0]):
        fields[index, 0] = jnp.zeros((span_y + 2 * EDGE, depth), jnp.float32)
        fields[index, span_x + 1] = jnp.zeros((span_y + 2 * EDGE, depth), jnp.float32)

    def clear(row, carry):
        for index in range(fields.shape[0]):
            fields[index, row, 0:lo] = flat_edge
            fields[index, row, hi:hi + EDGE] = flat_edge
        return carry

    lax.fori_loop(1, span_x + 1, clear, 0)

    def at(ref, x):
        return ref[x + 1, lo:hi]

    def laplace(ref, x):
        here = ref[x + 1, lo:hi]
        total = ref[x, lo:hi] + ref[x + 2, lo:hi]
        total = total + (ref[x + 1, lo - 1:hi - 1] + ref[x + 1, lo + 1:hi + 1])
        up = jnp.where(first_lane, 0.0, pltpu.roll(here, 1, 1))
        down = jnp.where(last_lane, 0.0, pltpu.roll(here, depth - 1, 1))
        return total + (up + down) - 6.0 * here, here

    def sweep(body):
        def step(x, carry):
            body(x)
            return carry

        lax.fori_loop(0, span_x, step, 0, unroll=2)

    def load(x):
        at_x = x // block_x
        piece = 2 * (x % block_x)
        for y in range(APY):
            rows = pl.ds(y * block_y, block_y)
            kap[x, rows] = model_ref[piece, at_x * APY + y].astype(jnp.float32)
            con[x, rows] = speed_factor * model_ref[piece + 1, at_x * APY + y].astype(jnp.float32)
        u_a[x + 1, lo:hi] = now_ref[x].astype(jnp.float32)

    sweep(load)

    def forward_0(x):
        grad, here = laplace(u_a, x)
        g_0[x] = grad
        d_0[x + 1, lo:hi] = con[x] * grad
        u_b[x + 1, lo:hi] = 2.0 * here - prev_ref[x].astype(jnp.float32) + kap[x] * grad

    sweep(forward_0)

    def forward_1(x):
        grad, here = laplace(u_b, x)
        spread, delta = laplace(d_0, x)
        g_1[x] = grad
        d_1[x + 1, lo:hi] = 2.0 * delta + kap[x] * spread + con[x] * grad
        u_a[x + 1, lo:hi] = 2.0 * here - at(u_a, x) + kap[x] * grad

    sweep(forward_1)

    def forward_2(x):
        grad, here = laplace(u_a, x)
        spread, delta = laplace(d_1, x)
        g_2[x] = grad
        d_2[x + 1, lo:hi] = 2.0 * delta - at(d_0, x) + kap[x] * spread + con[x] * grad
        u_b[x + 1, lo:hi] = 2.0 * here - at(u_b, x) + kap[x] * grad

    sweep(forward_2)

    def forward_3(x):
        grad, _ = laplace(u_b, x)
        spread, delta = laplace(d_2, x)
        last = 2.0 * delta - at(d_1, x) + kap[x] * spread + con[x] * grad
        d_3[x] = last
        image[x] = grad * last
        kb_a[x + 1, lo:hi] = kap[x] * last

    sweep(forward_3)

    def adjoint_2(x):
        spread, _ = laplace(kb_a, x)
        back = 2.0 * d_3[x] + spread + at(d_2, x)
        b_2[x] = back
        image[x] = image[x] + g_2[x] * back
        kb_b[x + 1, lo:hi] = kap[x] * back

    sweep(adjoint_2)

    def adjoint_1(x):
        spread, _ = laplace(kb_b, x)
        back = 2.0 * b_2[x] - d_3[x] + spread + at(d_1, x)
        b_1[x] = back
        image[x] = image[x] + g_1[x] * back
        kb_a[x + 1, lo:hi] = kap[x] * back

    sweep(adjoint_1)

    shift = corner_ref[0]

    def adjoint_0(x):
        spread, _ = laplace(kb_a, x)
        back = 2.0 * b_1[x] - b_2[x] + spread + at(d_0, x)
        result = (image_scale * (image[x] + g_0[x] * back)).astype(out_ref.dtype)
        at_x = x // block_x
        piece = 2 * (x % block_x)
        for y in range(APY):
            out_ref[piece + (shift + y) % 2, at_x * (APY // 2) + y // 2] = (
                result[y * block_y:(y + 1) * block_y]
            )

    sweep(adjoint_0)


def wave(corner_y, model, before, current):
    span_x, span_y, depth = before.shape
    pieces, blocks, block_y, _ = model.shape
    padded = (span_x + 2, span_y + 2 * EDGE, depth)
    return pl.pallas_call(
        wave_kernel,
        out_shape=jax.ShapeDtypeStruct((pieces, blocks // 2, block_y, depth), jnp.bfloat16),
        in_specs=[smem(), vmem(), vmem(), vmem()],
        out_specs=vmem(),
        scratch_shapes=[
            pltpu.VMEM((span_x, span_y, depth), jnp.float32),
            pltpu.VMEM((span_x, span_y, depth), jnp.float32),
            pltpu.VMEM((7,) + padded, jnp.float32),
            pltpu.VMEM((6, span_x, span_y, depth), jnp.float32),
            pltpu.VMEM((span_x, span_y, depth), jnp.float32),
        ],
        compiler_params=pltpu.CompilerParams(vmem_limit_bytes=40 * 2**20),
        name="wave",
    )(corner_y, model, before, current)


def wave_split_depth(corner_y, model, before, current):
    span_x, span_y, depth = before.shape
    pieces, blocks, block_y, _ = model.shape
    block_x = pieces // 2
    grids = model.reshape(block_x, 2, APX, APY, block_y, depth).transpose(1, 2, 0, 3, 4, 5)
    grids = grids.reshape(2, span_x, span_y, depth).astype(jnp.float32)
    image = image_scale * propagate(
        grids[0],
        speed_factor * grids[1],
        before.astype(jnp.float32),
        current.astype(jnp.float32),
        laplace_many,
    )
    image = image.reshape(APX, block_x, APY // 2, 2, block_y, depth).transpose(1, 3, 0, 2, 4, 5)
    image = jnp.where(corner_y[0] % 2 == 1, image[:, ::-1], image)
    return image.reshape(pieces, blocks // 2, block_y, depth).astype(jnp.bfloat16)


def stack_kernel(where_ref, take_ref, terms_ref, out_ref, total):
    shots, blocks = terms_ref.shape[:2]

    def clear(index, carry):
        total[index] = jnp.zeros(total.shape[1:], total.dtype)
        return carry

    lax.fori_loop(0, total.shape[0], clear, 0, unroll=8)

    def add(shot, carry):
        for block in range(blocks):
            spot = where_ref[shot * blocks + block]
            total[spot] = total[spot] + terms_ref[shot, block].astype(jnp.float32)
        return carry

    lax.fori_loop(0, shots, add, 0)

    def give(index, carry):
        for inner in range(16):
            spot = index * 16 + inner
            out_ref[spot] = total[take_ref[spot]].astype(out_ref.dtype)
        return carry

    lax.fori_loop(0, out_ref.shape[0] // 16, give, 0)


def per_device(
    velocity_p,
    velocity_s,
    density,
    perturbation,
    seafloor,
    owner_ids,
    corner_x,
    corner_y,
    wave_prev,
    wave_now,
):
    slots, block_x, block_y, depth = velocity_p.shape
    count = lax.axis_size("shot")
    assert count == 2 * block_x
    total_slots = count * slots
    patch = APX * APY
    depth_base = lax.axis_index("depth") * depth

    coef = coefficient(velocity_p, velocity_s, density, seafloor, depth_base)
    both = jnp.stack([coef, perturbation], axis=1)
    both = both.transpose(2, 1, 0, 3, 4).reshape(count, slots, block_y, depth)
    facts = jnp.concatenate([owner_ids, corner_x, corner_y]).astype(jnp.bfloat16)
    facts = jnp.pad(facts, (0, depth - slots - 2))
    facts = jnp.broadcast_to(facts, (count, 1, block_y, depth))
    sent = jnp.concatenate([both, facts], axis=1)
    pieces = lax.all_to_all(sent, "shot", 0, 0, tiled=True)

    facts = pieces[:, slots, 0, : slots + 2].astype(jnp.int32)
    ids = facts[:, :slots].reshape(total_slots)
    rows = facts[:, slots]
    cols = facts[:, slots + 1]
    steps_x = jnp.arange(APX, dtype=jnp.int32)
    steps_y = jnp.arange(APY, dtype=jnp.int32)
    wanted = (rows[:, None, None] + steps_x[None, :, None]) * GRID_COLS
    wanted = (wanted + cols[:, None, None] + steps_y[None, None, :]).reshape(count * patch)
    place = jnp.arange(total_slots, dtype=jnp.int32)
    place = place // slots * (slots + 1) + place % slots
    table = jnp.sum(jnp.where(wanted[:, None] == ids[None, :], place[None, :], 0), axis=1)

    picked = pl.pallas_call(
        pick_kernel,
        out_shape=jax.ShapeDtypeStruct((count * patch, block_y, depth), jnp.bfloat16),
        in_specs=[smem(), vmem()],
        out_specs=vmem(),
        name="pick",
    )(table, pieces.reshape(count * (slots + 1), block_y, depth))
    model = lax.all_to_all(
        picked.reshape(count, patch, block_y, depth), "shot", 0, 0, tiled=True
    )

    run = wave if lax.axis_size("depth") == 1 else wave_split_depth
    terms = run(corner_y, model, wave_prev[0], wave_now[0])
    terms = lax.all_to_all(terms, "shot", 0, 0, tiled=True)

    parity = lax.axis_index("shot") % 2
    half = jnp.arange(APY // 2, dtype=jnp.int32)
    line = rows[:, None, None] + steps_x[None, :, None]
    column = (cols + (cols + parity) % 2)[:, None, None] + 2 * half[None, None, :]
    where = (line * (GRID_COLS // 2) + column // 2).reshape(count * patch // 2)
    take = ids // 2
    sums = pl.pallas_call(
        stack_kernel,
        out_shape=jax.ShapeDtypeStruct((total_slots, block_y, depth), jnp.bfloat16),
        in_specs=[smem(), smem(), vmem()],
        out_specs=vmem(),
        scratch_shapes=[pltpu.VMEM((total_slots // 2, block_y, depth), jnp.float32)],
        name="stack",
    )(where, take, terms)
    sums = lax.all_to_all(
        sums.reshape(count, slots, block_y, depth), "shot", 0, 0, tiled=True
    )
    sums = sums.reshape(block_x, 2, slots, block_y, depth).astype(jnp.float32)
    odd = (owner_ids % 2 == 1)[None, :, None, None]
    mine = jnp.where(odd, sums[:, 1], sums[:, 0])
    return mine.transpose(1, 0, 2, 3)


def solution(mesh):
    in_specs = (
        P(("grp", "shot"), None, None, "depth"),
        P(("grp", "shot"), None, None, "depth"),
        P(("grp", "shot"), None, None, "depth"),
        P(("grp", "shot"), None, None, "depth"),
        P(("grp", "shot"), None, None),
        P(("grp", "shot")),
        P(("grp", "shot")),
        P(("grp", "shot")),
        P(("grp", "shot"), None, None, "depth"),
        P(("grp", "shot"), None, None, "depth"),
    )
    out_specs = P(("grp", "shot"), None, None, "depth")
    return jax.shard_map(
        per_device, mesh=mesh, in_specs=in_specs, out_specs=out_specs, check_vma=False
    )
```

```python
import functools

import jax
import jax.numpy as jnp
from jax import lax
from jax.experimental import pallas as pl
from jax.experimental.pallas import tpu as pltpu
from jax.sharding import PartitionSpec as P

APX = 4
APY = 4
STEPS = 4
GRID_COLS = 8
LANES = 8

speed_factor = 0.28
image_scale = 0.01


def with_halo(block, sides, width):
    for axis, dim in sides:
        count = lax.axis_size(axis)
        forward = [(i, i + 1) for i in range(count - 1)]
        backward = [(target, source) for source, target in forward]
        low = lax.ppermute(
            lax.slice_in_dim(block, block.shape[dim] - width, None, axis=dim), axis, forward
        )
        high = lax.ppermute(lax.slice_in_dim(block, 0, width, axis=dim), axis, backward)
        block = jnp.concatenate([low, block, high], axis=dim)
    return block


def laplace_many(fields):
    stacked = jnp.stack(fields)
    padded = with_halo(stacked.astype(jnp.bfloat16), (("depth", 3),), 1).astype(stacked.dtype)
    padded = jnp.pad(padded, ((0, 0), (1, 1), (1, 1), (0, 0)))
    beside = padded[:, 2:, 1:-1, 1:-1] + padded[:, :-2, 1:-1, 1:-1]
    beside = beside + padded[:, 1:-1, 2:, 1:-1] + padded[:, 1:-1, :-2, 1:-1]
    beside = beside + padded[:, 1:-1, 1:-1, 2:] + padded[:, 1:-1, 1:-1, :-2]
    result = beside - 6.0 * stacked
    return [result[index] for index in range(len(fields))]


def propagate(kappa, contrast, before, current, apply):
    grads = []
    datas = []
    grad_now = apply([current])[0]
    delta_prev = jnp.zeros_like(current)
    delta_now = contrast * grad_now
    grads.append(grad_now)
    datas.append(delta_now)
    before, current = (current, 2.0 * current - before + kappa * grad_now)
    for step in range(1, STEPS):
        grad_now, spread = apply([current, delta_now])
        delta_next = 2.0 * delta_now - delta_prev + kappa * spread + contrast * grad_now
        grads.append(grad_now)
        datas.append(delta_next)
        delta_prev, delta_now = (delta_now, delta_next)
        if step + 1 < STEPS:
            before, current = (current, 2.0 * current - before + kappa * grad_now)
    back = datas[STEPS - 1]
    back_after = jnp.zeros_like(back)
    image = grads[STEPS - 1] * back
    for step in range(STEPS - 2, -1, -1):
        spread = apply([kappa * back])
        back_new = 2.0 * back - back_after + spread[0] + datas[step]
        image = image + grads[step] * back_new
        back_after, back = (back, back_new)
    return image


def vmem():
    return pl.BlockSpec(memory_space=pltpu.VMEM)


def smem():
    return pl.BlockSpec(memory_space=pltpu.SMEM)


def prepare_kernel(
    ids_ref, row_ref, col_ref, floor_ref, p_ref, s_ref, rho_ref, pert_ref, out_ref
):
    slots, block_x, block_y, depth = p_ref.shape
    shape = (block_y, depth)
    deep = lax.broadcasted_iota(jnp.int32, shape, 1).astype(jnp.float32)
    near = lax.broadcasted_iota(jnp.int32, (block_y, block_y), 0) == (
        lax.broadcasted_iota(jnp.int32, (block_y, block_y), 1)
    )
    for slot in range(slots):
        floors = floor_ref[slot].astype(jnp.float32)
        for x in range(block_x):
            line = jnp.broadcast_to(floors[x:x + 1], (block_y, block_y))
            floor = jnp.sum(jnp.where(near, line, 0.0), axis=1, keepdims=True)
            primary = p_ref[slot, x].astype(jnp.float32)
            shear = s_ref[slot, x].astype(jnp.float32)
            square = primary * primary
            stiffness = jnp.where(deep >= floor, square + shear * shear, square)
            coef = speed_factor * stiffness / rho_ref[slot, x].astype(jnp.float32)
            out_ref[2 * x, slot] = coef.astype(out_ref.dtype)
            out_ref[2 * x + 1, slot] = pert_ref[slot, x]
    lane = lax.broadcasted_iota(jnp.int32, shape, 1)
    facts = jnp.where(lane == slots, row_ref[0], 0)
    facts = jnp.where(lane == slots + 1, col_ref[0], facts)
    for slot in range(slots):
        facts = jnp.where(lane == slot, ids_ref[slot], facts)
    facts = facts.astype(jnp.float32).astype(out_ref.dtype)
    for piece in range(out_ref.shape[0]):
        out_ref[piece, slots] = facts


def pick_kernel(slots, pieces_ref, out_ref, facts_ref, facts, spots, sem):
    count = facts_ref.shape[0]
    for piece in range(count):
        tile = pieces_ref[piece * (slots + 1) + slots].astype(jnp.float32)
        facts_ref[piece:piece + 1] = tile.astype(jnp.int32)[0:1]
    copy = pltpu.make_async_copy(facts_ref, facts, sem)
    copy.start()
    copy.wait()
    for piece in range(count):
        for slot in range(slots):
            spots[facts[piece, slot]] = piece * (slots + 1) + slot

    def one(shot, carry):
        first = facts[shot, slots] * GRID_COLS + facts[shot, slots + 1]
        tiles = []
        for x in range(APX):
            for y in range(APY):
                tiles.append(pieces_ref[spots[first + x * GRID_COLS + y]])
        for index, tile in enumerate(tiles):
            out_ref[shot * APX * APY + index] = tile
        return carry

    lax.fori_loop(0, count, one, 0)


def ends(shape):
    lane = lax.broadcasted_iota(jnp.int32, shape, 1)
    row = lax.broadcasted_iota(jnp.int32, shape, 0)
    return lane == 0, lane == shape[1] - 1, row == 0, row == shape[0] - 1


def laplace(before, here, after, masks):
    lane_0, lane_n, row_0, row_n = masks
    many = len(here)
    depth = here[0].shape[1]
    low = [jnp.where(row_0, 0.0, pltpu.roll(here[-1], 1, 0))] + here[:-1]
    high = here[1:] + [jnp.where(row_n, 0.0, pltpu.roll(here[0], LANES - 1, 0))]
    result = []
    for v in range(many):
        up = jnp.where(lane_0, 0.0, pltpu.roll(here[v], 1, 1))
        down = jnp.where(lane_n, 0.0, pltpu.roll(here[v], depth - 1, 1))
        total = (before[v] + after[v]) + (low[v] + high[v]) + (up + down)
        result.append(total - 6.0 * here[v])
    return result


def registers(ref, x):
    return [ref[x, v] for v in range(ref.shape[1])]


def strided(ref, x):
    many = ref.shape[1] // LANES
    return [ref[x, pl.ds(v, LANES, stride=many)] for v in range(many)]


def sweep(count, fields, body, unroll):
    many = fields[0].shape[1]
    zero = [jnp.zeros(fields[0].shape[2:], jnp.float32)] * many
    first = [(zero, registers(field, 0)) for field in fields]

    def step(x, carry):
        rows = [
            (before, here, registers(field, x + 1))
            for (before, here), field in zip(carry, fields)
        ]
        body(x, rows)
        return [(here, after) for _, here, after in rows]

    lax.fori_loop(0, count, step, first, unroll=unroll)


def start_kernel(prev_ref, now_ref, wave_ref, grad_ref, next_ref, flat, flat_prev, field):
    span_x, span_y, depth = now_ref.shape
    many = span_y // LANES
    masks = ends((LANES, depth))

    def load(x, carry):
        flat[x] = now_ref[x].astype(jnp.float32)
        flat_prev[x] = prev_ref[x].astype(jnp.float32)
        return carry

    lax.fori_loop(0, span_x, load, 0, unroll=2)

    def order(x, carry):
        rows = strided(flat, x)
        older = strided(flat_prev, x)
        for v in range(many):
            field[x, v] = rows[v]
            wave_ref[x, v] = rows[v]
            next_ref[x, v] = 2.0 * rows[v] - older[v]
        return carry

    lax.fori_loop(0, span_x, order, 0, unroll=2)
    for v in range(many):
        field[span_x, v] = jnp.zeros((LANES, depth), jnp.float32)

    def body(x, rows):
        grads = laplace(*rows[0], masks)
        for v in range(many):
            grad_ref[x, v] = grads[v]

    sweep(span_x, [field], body, 2)


def start(before, current):
    span_x, span_y, depth = before.shape
    many = span_y // LANES
    out = jax.ShapeDtypeStruct((span_x, many, LANES, depth), jnp.float32)
    flat = pltpu.VMEM((span_x, span_y, depth), jnp.float32)
    return pl.pallas_call(
        start_kernel,
        out_shape=(out, out, out),
        in_specs=[vmem()] * 2,
        out_specs=(vmem(),) * 3,
        scratch_shapes=[flat, flat, pltpu.VMEM((span_x + 1, many, LANES, depth), jnp.float32)],
        compiler_params=pltpu.CompilerParams(vmem_limit_bytes=24 * 2**20),
        cost_estimate=pl.CostEstimate(
            flops=20 * before.size, bytes_accessed=16 * before.size, transcendentals=0
        ),
        name="start",
    )(before, current)


def wave_kernel(
    model_ref, u_0, g_0, next_ref, out_ref,
    kap, con, u_1, u_2, u_3, d_0, d_1, d_2, kb_3, kb_2, kb_1, g_1, g_2, d_3, b_2, b_1, image,
):
    span_x, many = u_0.shape[:2]
    depth = u_0.shape[3]
    block_y = model_ref.shape[2]
    block_x = span_x // APX
    masks = ends((LANES, depth))
    each = range(many)
    for field in (u_1, u_2, u_3, d_0, d_1, d_2, kb_3, kb_2, kb_1):
        for v in each:
            field[span_x, v] = jnp.zeros((LANES, depth), jnp.float32)

    def load(piece, carry):
        for x in range(APX):
            for y in range(APY):
                rows = pl.ds(y * block_y, block_y)
                at = x * block_x + piece
                kap[at, rows] = model_ref[2 * piece, x * APY + y].astype(jnp.float32)
                con[at, rows] = speed_factor * (
                    model_ref[2 * piece + 1, x * APY + y].astype(jnp.float32)
                )
        return carry

    lax.fori_loop(0, block_x, load, 0)

    def forward_0(x, carry):
        kaps, cons, grads = strided(kap, x), strided(con, x), registers(g_0, x)
        older = registers(next_ref, x)
        for v in each:
            d_0[x, v] = cons[v] * grads[v]
            u_1[x, v] = older[v] + kaps[v] * grads[v]
        return carry

    lax.fori_loop(0, span_x, forward_0, 0, unroll=2)

    def forward(u_now, u_prev, d_now, d_prev, u_next, d_next, g_now):
        def body(x, rows):
            waves, deltas = rows
            grads = laplace(*waves, masks)
            spread = laplace(*deltas, masks)
            kaps, cons = strided(kap, x), strided(con, x)
            for v in each:
                value = 2.0 * deltas[1][v] + kaps[v] * spread[v] + cons[v] * grads[v]
                if d_prev is not None:
                    value = value - d_prev[x, v]
                d_next[x, v] = value
                if u_next is None:
                    image[x, v] = grads[v] * value
                    kb_3[x, v] = kaps[v] * value
                else:
                    g_now[x, v] = grads[v]
                    u_next[x, v] = 2.0 * waves[1][v] - u_prev[x, v] + kaps[v] * grads[v]

        sweep(span_x, [u_now, d_now], body, 2)

    forward(u_1, u_0, d_0, None, u_2, d_1, g_1)
    forward(u_2, u_1, d_1, d_0, u_3, d_2, g_2)
    forward(u_3, u_2, d_2, d_1, None, d_3, None)

    def adjoint(kb, b_now, b_after, data, grad, kb_next, b_next):
        def body(x, rows):
            spread = laplace(*rows[0], masks)
            kaps = None if kb_next is None else strided(kap, x)
            for v in each:
                back = 2.0 * b_now[x, v] + spread[v] + data[x, v]
                if b_after is not None:
                    back = back - b_after[x, v]
                total = image[x, v] + grad[x, v] * back
                if kb_next is None:
                    total = (image_scale * total).astype(out_ref.dtype)
                    piece = 2 * (x % block_x) + v // 2
                    out_ref[piece, 2 * (x // block_x) + v % 2] = total
                else:
                    image[x, v] = total
                    b_next[x, v] = back
                    kb_next[x, v] = kaps[v] * back

        sweep(span_x, [kb], body, 2)

    adjoint(kb_3, d_3, None, d_2, g_2, kb_2, b_2)
    adjoint(kb_2, b_2, d_3, d_1, g_1, kb_1, b_1)
    adjoint(kb_1, b_1, b_2, d_0, g_0, None, None)


def wave(model, before, current):
    span_x, span_y, depth = before.shape
    pieces, blocks, block_y, _ = model.shape
    many = span_y // LANES
    flat = pltpu.VMEM((span_x, span_y, depth), jnp.float32)
    field = pltpu.VMEM((span_x + 1, many, LANES, depth), jnp.float32)
    plain = pltpu.VMEM((span_x, many, LANES, depth), jnp.float32)
    return pl.pallas_call(
        wave_kernel,
        out_shape=jax.ShapeDtypeStruct((pieces, blocks // 2, block_y, depth), jnp.bfloat16),
        in_specs=[vmem()] * 4,
        out_specs=vmem(),
        scratch_shapes=[flat] * 2 + [field] * 9 + [plain] * 6,
        compiler_params=pltpu.CompilerParams(vmem_limit_bytes=40 * 2**20),
        name="wave",
    )(model, *start(before, current))


def wave_split_depth(model, before, current):
    span_x, span_y, depth = before.shape
    pieces, blocks, block_y, _ = model.shape
    block_x = pieces // 2
    grids = model.reshape(block_x, 2, APX, APY, block_y, depth).transpose(1, 2, 0, 3, 4, 5)
    grids = grids.reshape(2, span_x, span_y, depth).astype(jnp.float32)
    image = image_scale * propagate(
        grids[0],
        speed_factor * grids[1],
        before.astype(jnp.float32),
        current.astype(jnp.float32),
        laplace_many,
    )
    many = span_y // LANES
    image = image.reshape(APX, block_x, LANES, 2, many // 2, depth).transpose(1, 3, 0, 4, 2, 5)
    return image.reshape(pieces, blocks // 2, block_y, depth).astype(jnp.bfloat16)


def stack_kernel(slots, facts_ref, terms_ref, out_ref, total, chunks):
    shots, tiles = terms_ref.shape[:2]
    wide = tiles // APX
    width = LANES // APY

    def clear(index, carry):
        total[index] = jnp.zeros(total.shape[1:], total.dtype)
        return carry

    lax.fori_loop(0, total.shape[0], clear, 0, unroll=8)

    def add(shot, carry):
        first = facts_ref[shot, slots] * wide
        rows = pl.ds(facts_ref[shot, slots + 1] * width, LANES)
        sums = [
            total[first + tile, rows] + terms_ref[shot, tile].astype(jnp.float32)
            for tile in range(tiles)
        ]
        for tile in range(tiles):
            total[first + tile, rows] = sums[tile]
        return carry

    lax.fori_loop(0, shots, add, 0)

    def give(owner, carry):
        parts = []
        for slot in range(slots):
            block = facts_ref[owner, slot]
            for part in range(wide):
                rows = pl.ds(block % GRID_COLS * width, width)
                parts.append(total[block // GRID_COLS * wide + part, rows])
        for index, part in enumerate(parts):
            chunks[owner, pl.ds(index * width, width)] = part
        return carry

    lax.fori_loop(0, shots, give, 0)

    def close(owner, carry):
        out_ref[owner] = chunks[owner].astype(out_ref.dtype)
        return carry

    lax.fori_loop(0, shots, close, 0, unroll=4)


def finish_kernel(sums_ref, out_ref, rows):
    slots, block_x = out_ref.shape[:2]
    width = LANES // APY
    wide = sums_ref.shape[1] // slots // width
    for piece in range(sums_ref.shape[0]):
        rows[piece] = sums_ref[piece].astype(jnp.float32)
    for x in range(block_x):
        for half in range(2):
            for slot in range(slots):
                for part in range(wide):
                    index = (slot * wide + part) * width
                    at = pl.ds(half * wide + part, width, stride=2 * wide)
                    out_ref[slot, x, at] = rows[2 * x + half, index:index + width]


def per_device(
    velocity_p,
    velocity_s,
    density,
    perturbation,
    seafloor,
    owner_ids,
    corner_x,
    corner_y,
    wave_prev,
    wave_now,
):
    slots, block_x, block_y, depth = velocity_p.shape
    count = lax.axis_size("shot")
    assert count == 2 * block_x and block_y == LANES
    patch = APX * APY
    split = lax.axis_size("depth") > 1
    if split:
        seafloor = seafloor - lax.axis_index("depth") * depth

    sent = pl.pallas_call(
        prepare_kernel,
        out_shape=jax.ShapeDtypeStruct((count, slots + 1, block_y, depth), jnp.bfloat16),
        in_specs=[smem()] * 3 + [vmem()] * 5,
        out_specs=vmem(),
        name="prepare",
    )(owner_ids, corner_x, corner_y, seafloor, velocity_p, velocity_s, density, perturbation)
    pieces = lax.all_to_all(sent, "shot", 0, 0, tiled=True)

    picked, facts = pl.pallas_call(
        functools.partial(pick_kernel, slots),
        out_shape=(
            jax.ShapeDtypeStruct((count * patch, block_y, depth), jnp.bfloat16),
            jax.ShapeDtypeStruct((count, depth), jnp.int32),
        ),
        in_specs=[vmem()],
        out_specs=(vmem(), vmem()),
        scratch_shapes=[
            pltpu.SMEM((count, depth), jnp.int32),
            pltpu.SMEM((count * slots,), jnp.int32),
            pltpu.SemaphoreType.DMA,
        ],
        name="pick",
    )(pieces.reshape(count * (slots + 1), block_y, depth))
    model = lax.all_to_all(
        picked.reshape(count, patch, block_y, depth), "shot", 0, 0, tiled=True
    )

    run = wave_split_depth if split else wave
    terms = run(model, wave_prev[0], wave_now[0])
    terms = lax.all_to_all(terms, "shot", 0, 0, tiled=True)

    rows = block_x * block_y // count
    grid_rows = count * slots // GRID_COLS
    wide = terms.shape[1] // APX
    sums = pl.pallas_call(
        functools.partial(stack_kernel, slots),
        out_shape=jax.ShapeDtypeStruct((count, slots * rows, depth), jnp.bfloat16),
        in_specs=[smem(), vmem()],
        out_specs=vmem(),
        scratch_shapes=[
            pltpu.VMEM((grid_rows * wide, GRID_COLS * LANES // APY, depth), jnp.float32),
            pltpu.VMEM((count, slots * rows, depth), jnp.float32),
        ],
        name="stack",
    )(facts, terms)
    sums = lax.all_to_all(sums, "shot", 0, 0, tiled=True)
    return pl.pallas_call(
        finish_kernel,
        out_shape=jax.ShapeDtypeStruct(velocity_p.shape, jnp.float32),
        in_specs=[vmem()],
        out_specs=vmem(),
        scratch_shapes=[pltpu.VMEM(sums.shape, jnp.float32)],
        name="finish",
    )(sums)


def solution(mesh):
    in_specs = (
        P(("grp", "shot"), None, None, "depth"),
        P(("grp", "shot"), None, None, "depth"),
        P(("grp", "shot"), None, None, "depth"),
        P(("grp", "shot"), None, None, "depth"),
        P(("grp", "shot"), None, None),
        P(("grp", "shot")),
        P(("grp", "shot")),
        P(("grp", "shot")),
        P(("grp", "shot"), None, None, "depth"),
        P(("grp", "shot"), None, None, "depth"),
    )
    out_specs = P(("grp", "shot"), None, None, "depth")
    return jax.shard_map(
        per_device, mesh=mesh, in_specs=in_specs, out_specs=out_specs, check_vma=False
    )
```

```python
import functools

import jax
import jax.numpy as jnp
from jax import lax
from jax.experimental import pallas as pl
from jax.experimental.pallas import tpu as pltpu
from jax.sharding import PartitionSpec as P

APX = 4
APY = 4
STEPS = 4
GRID_COLS = 8
NEAR = 4
LANES = 8

speed_factor = 0.28
image_scale = 0.01


def with_halo(block, sides, width):
    for axis, dim in sides:
        count = lax.axis_size(axis)
        forward = [(i, i + 1) for i in range(count - 1)]
        backward = [(target, source) for source, target in forward]
        low = lax.ppermute(
            lax.slice_in_dim(block, block.shape[dim] - width, None, axis=dim), axis, forward
        )
        high = lax.ppermute(lax.slice_in_dim(block, 0, width, axis=dim), axis, backward)
        block = jnp.concatenate([low, block, high], axis=dim)
    return block


def laplace_many(fields):
    stacked = jnp.stack(fields)
    padded = with_halo(stacked.astype(jnp.bfloat16), (("depth", 3),), 1).astype(stacked.dtype)
    padded = jnp.pad(padded, ((0, 0), (1, 1), (1, 1), (0, 0)))
    beside = padded[:, 2:, 1:-1, 1:-1] + padded[:, :-2, 1:-1, 1:-1]
    beside = beside + padded[:, 1:-1, 2:, 1:-1] + padded[:, 1:-1, :-2, 1:-1]
    beside = beside + padded[:, 1:-1, 1:-1, 2:] + padded[:, 1:-1, 1:-1, :-2]
    result = beside - 6.0 * stacked
    return [result[index] for index in range(len(fields))]


def propagate(kappa, contrast, before, current, apply):
    grads = []
    datas = []
    grad_now = apply([current])[0]
    delta_prev = jnp.zeros_like(current)
    delta_now = contrast * grad_now
    grads.append(grad_now)
    datas.append(delta_now)
    before, current = (current, 2.0 * current - before + kappa * grad_now)
    for step in range(1, STEPS):
        grad_now, spread = apply([current, delta_now])
        delta_next = 2.0 * delta_now - delta_prev + kappa * spread + contrast * grad_now
        grads.append(grad_now)
        datas.append(delta_next)
        delta_prev, delta_now = (delta_now, delta_next)
        if step + 1 < STEPS:
            before, current = (current, 2.0 * current - before + kappa * grad_now)
    back = datas[STEPS - 1]
    back_after = jnp.zeros_like(back)
    image = grads[STEPS - 1] * back
    for step in range(STEPS - 2, -1, -1):
        spread = apply([kappa * back])
        back_new = 2.0 * back - back_after + spread[0] + datas[step]
        image = image + grads[step] * back_new
        back_after, back = (back, back_new)
    return image


def vmem():
    return pl.BlockSpec(memory_space=pltpu.VMEM)


def smem():
    return pl.BlockSpec(memory_space=pltpu.SMEM)


def prepare_kernel(
    ids_ref, row_ref, col_ref, floor_ref, p_ref, s_ref, rho_ref, pert_ref, out_ref
):
    slots, block_x, block_y, depth = p_ref.shape
    shape = (block_y, depth)
    deep = lax.broadcasted_iota(jnp.int32, shape, 1).astype(jnp.float32)
    near = lax.broadcasted_iota(jnp.int32, (block_y, block_y), 0) == (
        lax.broadcasted_iota(jnp.int32, (block_y, block_y), 1)
    )
    for slot in range(slots):
        floors = floor_ref[slot].astype(jnp.float32)
        for x in range(block_x):
            line = jnp.broadcast_to(floors[x:x + 1], (block_y, block_y))
            floor = jnp.sum(jnp.where(near, line, 0.0), axis=1, keepdims=True)
            primary = p_ref[slot, x].astype(jnp.float32)
            shear = s_ref[slot, x].astype(jnp.float32)
            square = primary * primary
            stiffness = jnp.where(deep >= floor, square + shear * shear, square)
            coef = speed_factor * stiffness / rho_ref[slot, x].astype(jnp.float32)
            out_ref[2 * x, slot] = coef.astype(out_ref.dtype)
            out_ref[2 * x + 1, slot] = pert_ref[slot, x]
    lane = lax.broadcasted_iota(jnp.int32, shape, 1)
    facts = jnp.where(lane == slots, row_ref[0], 0)
    facts = jnp.where(lane == slots + 1, col_ref[0], facts)
    for slot in range(slots):
        facts = jnp.where(lane == slot, ids_ref[slot], facts)
    facts = facts.astype(jnp.float32).astype(out_ref.dtype)
    for piece in range(out_ref.shape[0]):
        out_ref[piece, slots] = facts


def pick_kernel(slots, pieces_ref, out_ref, facts_ref, facts, spots, sem):
    count = facts_ref.shape[0]
    for piece in range(count):
        tile = pieces_ref[piece * (slots + 1) + slots].astype(jnp.float32)
        facts_ref[piece:piece + 1] = tile.astype(jnp.int32)[0:1]
    copy = pltpu.make_async_copy(facts_ref, facts, sem)
    copy.start()
    copy.wait()
    for piece in range(count):
        for slot in range(slots):
            spots[facts[piece, slot]] = piece * (slots + 1) + slot

    def one(shot, carry):
        first = facts[shot, slots] * GRID_COLS + facts[shot, slots + 1]
        tiles = []
        for x in range(APX):
            for y in range(APY):
                tiles.append(pieces_ref[spots[first + x * GRID_COLS + y]])
        for index, tile in enumerate(tiles):
            out_ref[shot * APX * APY + index] = tile
        return carry

    lax.fori_loop(0, count, one, 0, unroll=4)


def ends(shape):
    lane = lax.broadcasted_iota(jnp.int32, shape, 1)
    row = lax.broadcasted_iota(jnp.int32, shape, 0)
    return lane == 0, lane == shape[1] - 1, row == 0, row == shape[0] - 1


def laplace(before, here, after, masks):
    lane_0, lane_n, row_0, row_n = masks
    many = len(here)
    depth = here[0].shape[1]
    low = [jnp.where(row_0, 0.0, pltpu.roll(here[-1], 1, 0))] + here[:-1]
    high = here[1:] + [jnp.where(row_n, 0.0, pltpu.roll(here[0], LANES - 1, 0))]
    result = []
    for v in range(many):
        up = jnp.where(lane_0, 0.0, pltpu.roll(here[v], 1, 1))
        down = jnp.where(lane_n, 0.0, pltpu.roll(here[v], depth - 1, 1))
        total = (before[v] + after[v]) + (low[v] + high[v]) + (up + down)
        result.append(total - 6.0 * here[v])
    return result


def registers(ref, x):
    return [ref[x, v] for v in range(ref.shape[1])]


def strided(ref, x):
    many = ref.shape[1] // LANES
    return [ref[x, pl.ds(v, LANES, stride=many)] for v in range(many)]


def sweep(count, fields, body, unroll):
    many = fields[0].shape[1]
    zero = [jnp.zeros(fields[0].shape[2:], jnp.float32)] * many
    first = [(zero, registers(field, 0)) for field in fields]

    def step(x, carry):
        rows = [
            (before, here, registers(field, x + 1))
            for (before, here), field in zip(carry, fields)
        ]
        body(x, rows)
        return [(here, after) for _, here, after in rows]

    lax.fori_loop(0, count, step, first, unroll=unroll)


def start_kernel(prev_ref, now_ref, wave_ref, grad_ref, next_ref, flat, flat_prev, field):
    span_x, span_y, depth = now_ref.shape
    many = span_y // LANES
    masks = ends((LANES, depth))

    def load(x, carry):
        flat[x] = now_ref[x].astype(jnp.float32)
        flat_prev[x] = prev_ref[x].astype(jnp.float32)
        return carry

    lax.fori_loop(0, span_x, load, 0, unroll=2)

    def order(x, carry):
        rows = strided(flat, x)
        older = strided(flat_prev, x)
        for v in range(many):
            field[x, v] = rows[v]
            wave_ref[x, v] = rows[v]
            next_ref[x, v] = 2.0 * rows[v] - older[v]
        return carry

    lax.fori_loop(0, span_x, order, 0, unroll=2)
    for v in range(many):
        field[span_x, v] = jnp.zeros((LANES, depth), jnp.float32)

    def body(x, rows):
        grads = laplace(*rows[0], masks)
        for v in range(many):
            grad_ref[x, v] = grads[v]

    sweep(span_x, [field], body, 8)


def start(before, current):
    span_x, span_y, depth = before.shape
    many = span_y // LANES
    out = jax.ShapeDtypeStruct((span_x, many, LANES, depth), jnp.float32)
    flat = pltpu.VMEM((span_x, span_y, depth), jnp.float32)
    return pl.pallas_call(
        start_kernel,
        out_shape=(out, out, out),
        in_specs=[vmem()] * 2,
        out_specs=(vmem(),) * 3,
        scratch_shapes=[flat, flat, pltpu.VMEM((span_x + 1, many, LANES, depth), jnp.float32)],
        compiler_params=pltpu.CompilerParams(vmem_limit_bytes=24 * 2**20),
        cost_estimate=pl.CostEstimate(
            flops=20 * before.size, bytes_accessed=16 * before.size, transcendentals=0
        ),
        name="start",
    )(before, current)


def wave_kernel(
    model_ref, u_0, g_0, next_ref, out_ref,
    kap, con, u_1, u_2, u_3, d_0, d_1, d_2, kb_3, kb_2, kb_1, g_1, g_2, d_3, b_2, b_1, image,
):
    span_x, many = u_0.shape[:2]
    depth = u_0.shape[3]
    block_y = model_ref.shape[2]
    block_x = span_x // APX
    masks = ends((LANES, depth))
    each = range(many)
    for field in (u_1, u_2, u_3, d_0, d_1, d_2, kb_3, kb_2, kb_1):
        for v in each:
            field[span_x, v] = jnp.zeros((LANES, depth), jnp.float32)

    def load(piece, carry):
        for x in range(APX):
            for y in range(APY):
                rows = pl.ds(y * block_y, block_y)
                at = x * block_x + piece
                kap[at, rows] = model_ref[2 * piece, x * APY + y].astype(jnp.float32)
                con[at, rows] = speed_factor * (
                    model_ref[2 * piece + 1, x * APY + y].astype(jnp.float32)
                )
        return carry

    lax.fori_loop(0, block_x, load, 0, unroll=4)

    def forward_0(x, carry):
        kaps, cons, grads = strided(kap, x), strided(con, x), registers(g_0, x)
        older = registers(next_ref, x)
        for v in each:
            d_0[x, v] = cons[v] * grads[v]
            u_1[x, v] = older[v] + kaps[v] * grads[v]
        return carry

    lax.fori_loop(0, span_x, forward_0, 0, unroll=8)

    def forward(u_now, u_prev, d_now, d_prev, u_next, d_next, g_now):
        def body(x, rows):
            waves, deltas = rows
            grads = laplace(*waves, masks)
            spread = laplace(*deltas, masks)
            kaps, cons = strided(kap, x), strided(con, x)
            for v in each:
                value = 2.0 * deltas[1][v] + kaps[v] * spread[v] + cons[v] * grads[v]
                if d_prev is not None:
                    value = value - d_prev[x, v]
                d_next[x, v] = value
                if u_next is None:
                    image[x, v] = grads[v] * value
                    kb_3[x, v] = kaps[v] * value
                else:
                    g_now[x, v] = grads[v]
                    u_next[x, v] = 2.0 * waves[1][v] - u_prev[x, v] + kaps[v] * grads[v]

        sweep(span_x, [u_now, d_now], body, 8)

    forward(u_1, u_0, d_0, None, u_2, d_1, g_1)
    forward(u_2, u_1, d_1, d_0, u_3, d_2, g_2)
    forward(u_3, u_2, d_2, d_1, None, d_3, None)

    def adjoint(kb, b_now, b_after, data, grad, kb_next, b_next):
        def body(x, rows):
            spread = laplace(*rows[0], masks)
            kaps = None if kb_next is None else strided(kap, x)
            for v in each:
                back = 2.0 * b_now[x, v] + spread[v] + data[x, v]
                if b_after is not None:
                    back = back - b_after[x, v]
                total = image[x, v] + grad[x, v] * back
                if kb_next is None:
                    total = (image_scale * total).astype(out_ref.dtype)
                    piece = 2 * (x % block_x) + v // 2
                    out_ref[piece, 2 * (x // block_x) + v % 2] = total
                else:
                    image[x, v] = total
                    b_next[x, v] = back
                    kb_next[x, v] = kaps[v] * back

        sweep(span_x, [kb], body, 8)

    adjoint(kb_3, d_3, None, d_2, g_2, kb_2, b_2)
    adjoint(kb_2, b_2, d_3, d_1, g_1, kb_1, b_1)
    adjoint(kb_1, b_1, b_2, d_0, g_0, None, None)


def wave(model, before, current):
    span_x, span_y, depth = before.shape
    pieces, blocks, block_y, _ = model.shape
    many = span_y // LANES
    flat = pltpu.VMEM((span_x, span_y, depth), jnp.float32)
    field = pltpu.VMEM((span_x + 1, many, LANES, depth), jnp.float32)
    plain = pltpu.VMEM((span_x, many, LANES, depth), jnp.float32)
    return pl.pallas_call(
        wave_kernel,
        out_shape=jax.ShapeDtypeStruct((pieces, blocks // 2, block_y, depth), jnp.bfloat16),
        in_specs=[vmem()] * 4,
        out_specs=vmem(),
        scratch_shapes=[flat] * 2 + [field] * 9 + [plain] * 6,
        compiler_params=pltpu.CompilerParams(vmem_limit_bytes=40 * 2**20),
        name="wave",
    )(model, *start(before, current))


def wave_split_depth(model, before, current):
    span_x, span_y, depth = before.shape
    pieces, blocks, block_y, _ = model.shape
    block_x = pieces // 2
    grids = model.reshape(block_x, 2, APX, APY, block_y, depth).transpose(1, 2, 0, 3, 4, 5)
    grids = grids.reshape(2, span_x, span_y, depth).astype(jnp.float32)
    image = image_scale * propagate(
        grids[0],
        speed_factor * grids[1],
        before.astype(jnp.float32),
        current.astype(jnp.float32),
        laplace_many,
    )
    many = span_y // LANES
    image = image.reshape(APX, block_x, LANES, 2, many // 2, depth).transpose(1, 3, 0, 4, 2, 5)
    return image.reshape(pieces, blocks // 2, block_y, depth).astype(jnp.bfloat16)


def stack_kernel(slots, facts_ref, terms_ref, out_ref, total, lined):
    shots, tiles = terms_ref.shape[:2]
    wide = tiles // APX
    width = LANES // APY
    long = width * wide
    grid_rows = total.shape[0] // wide
    depth = total.shape[2]

    def clear(index, carry):
        total[index] = jnp.zeros(total.shape[1:], total.dtype)
        return carry

    lax.fori_loop(0, total.shape[0], clear, 0, unroll=8)

    def add(shot, carry):
        first = facts_ref[shot, slots] * wide
        rows = pl.ds(facts_ref[shot, slots + 1] * width, LANES)
        sums = [
            total[first + tile, rows] + terms_ref[shot, tile].astype(jnp.float32)
            for tile in range(tiles)
        ]
        for tile in range(tiles):
            total[first + tile, rows] = sums[tile]
        return carry

    lax.fori_loop(0, shots, add, 0, unroll=2)

    for row in range(grid_rows):
        for part in range(wide):
            for tile in range(total.shape[1] // LANES):
                at = pl.ds(LANES + tile * LANES * wide + part, LANES, stride=wide)
                lined[row, at] = total[row * wide + part, tile * LANES:(tile + 1) * LANES]

    low = lax.broadcasted_iota(jnp.int32, (LANES, depth), 0) < long

    def window(owner, slot, shift):
        block = facts_ref[owner, slot]
        return lined[block // GRID_COLS, pl.ds(LANES - shift + block % GRID_COLS * long, LANES)]

    def give(owner, carry):
        pairs = [
            jnp.where(low, window(owner, slot, 0), window(owner, slot + 1, long))
            for slot in range(0, slots, 2)
        ]
        to = owner % NEAR * (shots // NEAR) + owner // NEAR
        out_ref[to] = jnp.concatenate(pairs, axis=0).astype(out_ref.dtype)
        return carry

    lax.fori_loop(0, shots, give, 0, unroll=4)


def finish_kernel(sums_ref, out_ref):
    slots, block_x = out_ref.shape[:2]
    depth = out_ref.shape[3]
    row = lax.broadcasted_iota(jnp.int32, (LANES, depth), 0)
    pair = row // 2
    for x in range(block_x):
        first = sums_ref[2 * x].astype(jnp.float32)
        second = sums_ref[2 * x + 1].astype(jnp.float32)
        for slot in range(slots):
            at = slot // 2 * LANES
            back = slot % 2 * (LANES // 2)
            one = first[at:at + LANES]
            two = second[at:at + LANES]

            def turned(value, shift):
                shift = (shift - back) % LANES
                return pltpu.roll(value, shift, 0) if shift else value

            result = jnp.where(pair == 0, turned(one, 0), turned(two, 2))
            result = jnp.where(pair == 2, turned(one, 2), result)
            out_ref[slot, x] = jnp.where(pair == 3, turned(two, 4), result)


def exchange(values):
    count = values.shape[0]
    far = count // NEAR
    inner = [[o * NEAR + i for i in range(NEAR)] for o in range(far)]
    outer = [[o * NEAR + i for o in range(far)] for i in range(NEAR)]
    values = lax.all_to_all(values, "shot", 0, 0, axis_index_groups=inner, tiled=True)
    values = values.reshape(NEAR, far, *values.shape[1:]).swapaxes(0, 1)
    values = values.reshape(count, *values.shape[2:])
    return lax.all_to_all(values, "shot", 0, 0, axis_index_groups=outer, tiled=True)


def per_device(
    velocity_p,
    velocity_s,
    density,
    perturbation,
    seafloor,
    owner_ids,
    corner_x,
    corner_y,
    wave_prev,
    wave_now,
):
    slots, block_x, block_y, depth = velocity_p.shape
    count = lax.axis_size("shot")
    assert count == 2 * block_x and block_y == LANES
    patch = APX * APY
    split = lax.axis_size("depth") > 1
    if split:
        seafloor = seafloor - lax.axis_index("depth") * depth

    sent = pl.pallas_call(
        prepare_kernel,
        out_shape=jax.ShapeDtypeStruct((count, slots + 1, block_y, depth), jnp.bfloat16),
        in_specs=[smem()] * 3 + [vmem()] * 5,
        out_specs=vmem(),
        name="prepare",
    )(owner_ids, corner_x, corner_y, seafloor, velocity_p, velocity_s, density, perturbation)
    pieces = lax.all_to_all(sent, "shot", 0, 0, tiled=True)

    picked, facts = pl.pallas_call(
        functools.partial(pick_kernel, slots),
        out_shape=(
            jax.ShapeDtypeStruct((count * patch, block_y, depth), jnp.bfloat16),
            jax.ShapeDtypeStruct((count, depth), jnp.int32),
        ),
        in_specs=[vmem()],
        out_specs=(vmem(), vmem()),
        scratch_shapes=[
            pltpu.SMEM((count, depth), jnp.int32),
            pltpu.SMEM((count * slots,), jnp.int32),
            pltpu.SemaphoreType.DMA,
        ],
        name="pick",
    )(pieces.reshape(count * (slots + 1), block_y, depth))
    model = lax.all_to_all(
        picked.reshape(count, patch, block_y, depth), "shot", 0, 0, tiled=True
    )

    run = wave_split_depth if split else wave
    terms = run(model, wave_prev[0], wave_now[0])
    terms = lax.all_to_all(terms, "shot", 0, 0, tiled=True)

    rows = block_x * block_y // count
    grid_rows = count * slots // GRID_COLS
    wide = terms.shape[1] // APX
    sums = pl.pallas_call(
        functools.partial(stack_kernel, slots),
        out_shape=jax.ShapeDtypeStruct((count, slots * rows, depth), jnp.bfloat16),
        in_specs=[smem(), vmem()],
        out_specs=vmem(),
        scratch_shapes=[
            pltpu.VMEM((grid_rows * wide, GRID_COLS * LANES // APY, depth), jnp.float32),
            pltpu.VMEM((grid_rows, 2 * LANES + GRID_COLS * rows, depth), jnp.float32),
        ],
        name="stack",
    )(facts, terms)
    sums = exchange(sums)
    return pl.pallas_call(
        finish_kernel,
        out_shape=jax.ShapeDtypeStruct(velocity_p.shape, jnp.float32),
        in_specs=[vmem()],
        out_specs=vmem(),
        name="finish",
    )(sums)


def solution(mesh):
    in_specs = (
        P(("grp", "shot"), None, None, "depth"),
        P(("grp", "shot"), None, None, "depth"),
        P(("grp", "shot"), None, None, "depth"),
        P(("grp", "shot"), None, None, "depth"),
        P(("grp", "shot"), None, None),
        P(("grp", "shot")),
        P(("grp", "shot")),
        P(("grp", "shot")),
        P(("grp", "shot"), None, None, "depth"),
        P(("grp", "shot"), None, None, "depth"),
    )
    out_specs = P(("grp", "shot"), None, None, "depth")
    return jax.shard_map(
        per_device, mesh=mesh, in_specs=in_specs, out_specs=out_specs, check_vma=False
    )
```

```python
import functools

import jax
import jax.numpy as jnp
from jax import lax
from jax.experimental import pallas as pl
from jax.experimental.pallas import tpu as pltpu
from jax.sharding import PartitionSpec as P

APX = 4
APY = 4
STEPS = 4
GRID_COLS = 8
LANES = 8

speed_factor = 0.28
image_scale = 0.01


def with_halo(block, sides, width):
    for axis, dim in sides:
        count = lax.axis_size(axis)
        forward = [(i, i + 1) for i in range(count - 1)]
        backward = [(target, source) for source, target in forward]
        low = lax.ppermute(
            lax.slice_in_dim(block, block.shape[dim] - width, None, axis=dim), axis, forward
        )
        high = lax.ppermute(lax.slice_in_dim(block, 0, width, axis=dim), axis, backward)
        block = jnp.concatenate([low, block, high], axis=dim)
    return block


def laplace_many(fields):
    stacked = jnp.stack(fields)
    padded = with_halo(stacked.astype(jnp.bfloat16), (("depth", 3),), 1).astype(stacked.dtype)
    padded = jnp.pad(padded, ((0, 0), (1, 1), (1, 1), (0, 0)))
    beside = padded[:, 2:, 1:-1, 1:-1] + padded[:, :-2, 1:-1, 1:-1]
    beside = beside + padded[:, 1:-1, 2:, 1:-1] + padded[:, 1:-1, :-2, 1:-1]
    beside = beside + padded[:, 1:-1, 1:-1, 2:] + padded[:, 1:-1, 1:-1, :-2]
    result = beside - 6.0 * stacked
    return [result[index] for index in range(len(fields))]


def propagate(kappa, contrast, before, current, apply):
    grads = []
    datas = []
    grad_now = apply([current])[0]
    delta_prev = jnp.zeros_like(current)
    delta_now = contrast * grad_now
    grads.append(grad_now)
    datas.append(delta_now)
    before, current = (current, 2.0 * current - before + kappa * grad_now)
    for step in range(1, STEPS):
        grad_now, spread = apply([current, delta_now])
        delta_next = 2.0 * delta_now - delta_prev + kappa * spread + contrast * grad_now
        grads.append(grad_now)
        datas.append(delta_next)
        delta_prev, delta_now = (delta_now, delta_next)
        if step + 1 < STEPS:
            before, current = (current, 2.0 * current - before + kappa * grad_now)
    back = datas[STEPS - 1]
    back_after = jnp.zeros_like(back)
    image = grads[STEPS - 1] * back
    for step in range(STEPS - 2, -1, -1):
        spread = apply([kappa * back])
        back_new = 2.0 * back - back_after + spread[0] + datas[step]
        image = image + grads[step] * back_new
        back_after, back = (back, back_new)
    return image


def limit(mebibytes):
    return pltpu.CompilerParams(vmem_limit_bytes=mebibytes * 2**20)


def vmem():
    return pl.BlockSpec(memory_space=pltpu.VMEM)


def smem():
    return pl.BlockSpec(memory_space=pltpu.SMEM)


def prepare_kernel(
    ids_ref, row_ref, col_ref, floor_ref, p_ref, s_ref, rho_ref, pert_ref, out_ref, lined
):
    slots, block_x, block_y, depth = p_ref.shape
    shape = (block_y, depth)
    deep = lax.broadcasted_iota(jnp.int32, shape, 1).astype(jnp.float32)
    near = lax.broadcasted_iota(jnp.int32, (block_y, block_y), 0) == (
        lax.broadcasted_iota(jnp.int32, (block_y, block_y), 1)
    )
    for slot in range(slots):
        floors = floor_ref[slot].astype(jnp.float32)
        for x in range(block_x):
            line = jnp.broadcast_to(floors[x:x + 1], (block_y, block_y))
            floor = jnp.sum(jnp.where(near, line, 0.0), axis=1, keepdims=True)
            primary = p_ref[slot, x].astype(jnp.float32)
            shear = s_ref[slot, x].astype(jnp.float32)
            square = primary * primary
            stiffness = jnp.where(deep >= floor, square + shear * shear, square)
            coef = speed_factor * stiffness / rho_ref[slot, x].astype(jnp.float32)
            out_ref[2 * x, slot] = coef.astype(out_ref.dtype)
            out_ref[2 * x + 1, slot] = pert_ref[slot, x]
    lined[...] = jnp.zeros(shape, jnp.int32)
    lined[0:1, 0:slots] = ids_ref[...]
    lane = lax.broadcasted_iota(jnp.int32, shape, 1)
    facts = jnp.where(lane == slots, row_ref[0], lined[...])
    facts = jnp.where(lane == slots + 1, col_ref[0], facts)
    facts = facts.astype(jnp.float32).astype(out_ref.dtype)
    for piece in range(out_ref.shape[0]):
        out_ref[piece, slots] = facts


def pick_kernel(slots, pieces_ref, out_ref, facts_ref, facts, spots, sem):
    count = facts_ref.shape[0]
    for piece in range(count):
        tile = pieces_ref[piece * (slots + 1) + slots].astype(jnp.float32)
        facts_ref[piece:piece + 1] = tile.astype(jnp.int32)[0:1]
    copy = pltpu.make_async_copy(facts_ref, facts, sem)
    copy.start()
    copy.wait()
    for piece in range(count):
        for slot in range(slots):
            spots[facts[piece, slot]] = piece * (slots + 1) + slot

    def one(shot, carry):
        first = facts[shot, slots] * GRID_COLS + facts[shot, slots + 1]
        tiles = []
        for x in range(APX):
            for y in range(APY):
                tiles.append(pieces_ref[spots[first + x * GRID_COLS + y]])
        for index, tile in enumerate(tiles):
            out_ref[shot * APX * APY + index] = tile
        return carry

    lax.fori_loop(0, count, one, 0, unroll=4)


def ends(shape):
    lane = lax.broadcasted_iota(jnp.int32, shape, 1)
    row = lax.broadcasted_iota(jnp.int32, shape, 0)
    return lane == 0, lane == shape[1] - 1, row == 0, row == shape[0] - 1


def laplace(before, here, after, masks):
    lane_0, lane_n, row_0, row_n = masks
    many = len(here)
    depth = here[0].shape[1]
    low = [jnp.where(row_0, 0.0, pltpu.roll(here[-1], 1, 0))] + here[:-1]
    high = here[1:] + [jnp.where(row_n, 0.0, pltpu.roll(here[0], LANES - 1, 0))]
    result = []
    for v in range(many):
        up = jnp.where(lane_0, 0.0, pltpu.roll(here[v], 1, 1))
        down = jnp.where(lane_n, 0.0, pltpu.roll(here[v], depth - 1, 1))
        total = (before[v] + after[v]) + (low[v] + high[v]) + (up + down)
        result.append(total - 6.0 * here[v])
    return result


def registers(ref, x):
    return [ref[x, v] for v in range(ref.shape[1])]


def strided(ref, x):
    many = ref.shape[1] // LANES
    return [ref[x, pl.ds(v, LANES, stride=many)] for v in range(many)]


def sweep(count, fields, body, unroll):
    many = fields[0].shape[1]
    zero = [jnp.zeros(fields[0].shape[2:], jnp.float32)] * many
    first = [(zero, registers(field, 0)) for field in fields]

    def step(x, carry):
        rows = [
            (before, here, registers(field, x + 1))
            for (before, here), field in zip(carry, fields)
        ]
        body(x, rows)
        return [(here, after) for _, here, after in rows]

    lax.fori_loop(0, count, step, first, unroll=unroll)


def start_kernel(prev_ref, now_ref, wave_ref, grad_ref, next_ref, flat, flat_prev, field):
    span_x, span_y, depth = now_ref.shape
    many = span_y // LANES
    masks = ends((LANES, depth))

    def load(x, carry):
        flat[x] = now_ref[x].astype(jnp.float32)
        flat_prev[x] = prev_ref[x].astype(jnp.float32)
        return carry

    lax.fori_loop(0, span_x, load, 0, unroll=2)

    def order(x, carry):
        rows = strided(flat, x)
        older = strided(flat_prev, x)
        for v in range(many):
            field[x, v] = rows[v]
            wave_ref[x, v] = rows[v]
            next_ref[x, v] = 2.0 * rows[v] - older[v]
        return carry

    lax.fori_loop(0, span_x, order, 0, unroll=2)
    for v in range(many):
        field[span_x, v] = jnp.zeros((LANES, depth), jnp.float32)

    def body(x, rows):
        grads = laplace(*rows[0], masks)
        for v in range(many):
            grad_ref[x, v] = grads[v]

    sweep(span_x, [field], body, 8)


def start(before, current):
    span_x, span_y, depth = before.shape
    many = span_y // LANES
    out = jax.ShapeDtypeStruct((span_x, many, LANES, depth), jnp.float32)
    flat = pltpu.VMEM((span_x, span_y, depth), jnp.float32)
    return pl.pallas_call(
        start_kernel,
        out_shape=(out, out, out),
        in_specs=[vmem()] * 2,
        out_specs=(vmem(),) * 3,
        scratch_shapes=[flat, flat, pltpu.VMEM((span_x + 1, many, LANES, depth), jnp.float32)],
        compiler_params=limit(8),
        cost_estimate=pl.CostEstimate(
            flops=20 * before.size, bytes_accessed=16 * before.size, transcendentals=0
        ),
        name="start",
    )(before, current)


def wave_kernel(
    model_ref, u_0, g_0, next_ref, out_ref,
    kap, con, u_1, u_2, u_3, d_0, d_1, d_2, kb_3, kb_2, kb_1, g_1, g_2, d_3, b_2, b_1, image,
):
    span_x, many = u_0.shape[:2]
    depth = u_0.shape[3]
    block_y = model_ref.shape[2]
    block_x = span_x // APX
    masks = ends((LANES, depth))
    each = range(many)
    for field in (u_1, u_2, u_3, d_0, d_1, d_2, kb_3, kb_2, kb_1):
        for v in each:
            field[span_x, v] = jnp.zeros((LANES, depth), jnp.float32)

    def load(piece, carry):
        for x in range(APX):
            for y in range(APY):
                rows = pl.ds(y * block_y, block_y)
                at = x * block_x + piece
                kap[at, rows] = model_ref[2 * piece, x * APY + y].astype(jnp.float32)
                con[at, rows] = speed_factor * (
                    model_ref[2 * piece + 1, x * APY + y].astype(jnp.float32)
                )
        return carry

    lax.fori_loop(0, block_x, load, 0, unroll=4)

    def forward_0(x, carry):
        kaps, cons, grads = strided(kap, x), strided(con, x), registers(g_0, x)
        older = registers(next_ref, x)
        for v in each:
            d_0[x, v] = cons[v] * grads[v]
            u_1[x, v] = older[v] + kaps[v] * grads[v]
        return carry

    lax.fori_loop(0, span_x, forward_0, 0, unroll=8)

    def forward(u_now, u_prev, d_now, d_prev, u_next, d_next, g_now):
        def body(x, rows):
            waves, deltas = rows
            grads = laplace(*waves, masks)
            spread = laplace(*deltas, masks)
            kaps, cons = strided(kap, x), strided(con, x)
            for v in each:
                value = 2.0 * deltas[1][v] + kaps[v] * spread[v] + cons[v] * grads[v]
                if d_prev is not None:
                    value = value - d_prev[x, v]
                d_next[x, v] = value
                if u_next is None:
                    image[x, v] = grads[v] * value
                    kb_3[x, v] = kaps[v] * value
                else:
                    g_now[x, v] = grads[v]
                    u_next[x, v] = 2.0 * waves[1][v] - u_prev[x, v] + kaps[v] * grads[v]

        sweep(span_x, [u_now, d_now], body, 8)

    forward(u_1, u_0, d_0, None, u_2, d_1, g_1)
    forward(u_2, u_1, d_1, d_0, u_3, d_2, g_2)
    forward(u_3, u_2, d_2, d_1, None, d_3, None)

    def adjoint(kb, b_now, b_after, data, grad, kb_next, b_next):
        def body(x, rows):
            spread = laplace(*rows[0], masks)
            kaps = None if kb_next is None else strided(kap, x)
            for v in each:
                back = 2.0 * b_now[x, v] + spread[v] + data[x, v]
                if b_after is not None:
                    back = back - b_after[x, v]
                total = image[x, v] + grad[x, v] * back
                if kb_next is None:
                    total = (image_scale * total).astype(out_ref.dtype)
                    piece = 2 * (x % block_x) + v // 2
                    out_ref[piece, 2 * (x // block_x) + v % 2] = total
                else:
                    image[x, v] = total
                    b_next[x, v] = back
                    kb_next[x, v] = kaps[v] * back

        sweep(span_x, [kb], body, 8)

    adjoint(kb_3, d_3, None, d_2, g_2, kb_2, b_2)
    adjoint(kb_2, b_2, d_3, d_1, g_1, kb_1, b_1)
    adjoint(kb_1, b_1, b_2, d_0, g_0, None, None)


def wave(model, before, current):
    span_x, span_y, depth = before.shape
    pieces, blocks, block_y, _ = model.shape
    many = span_y // LANES
    flat = pltpu.VMEM((span_x, span_y, depth), jnp.float32)
    field = pltpu.VMEM((span_x + 1, many, LANES, depth), jnp.float32)
    plain = pltpu.VMEM((span_x, many, LANES, depth), jnp.float32)
    return pl.pallas_call(
        wave_kernel,
        out_shape=jax.ShapeDtypeStruct((pieces, blocks // 2, block_y, depth), jnp.bfloat16),
        in_specs=[vmem()] * 4,
        out_specs=vmem(),
        scratch_shapes=[flat] * 2 + [field] * 9 + [plain] * 6,
        compiler_params=limit(20),
        name="wave",
    )(model, *start(before, current))


def wave_split_depth(model, before, current):
    span_x, span_y, depth = before.shape
    pieces, blocks, block_y, _ = model.shape
    block_x = pieces // 2
    grids = model.reshape(block_x, 2, APX, APY, block_y, depth).transpose(1, 2, 0, 3, 4, 5)
    grids = grids.reshape(2, span_x, span_y, depth).astype(jnp.float32)
    image = image_scale * propagate(
        grids[0],
        speed_factor * grids[1],
        before.astype(jnp.float32),
        current.astype(jnp.float32),
        laplace_many,
    )
    many = span_y // LANES
    image = image.reshape(APX, block_x, LANES, 2, many // 2, depth).transpose(1, 3, 0, 4, 2, 5)
    return image.reshape(pieces, blocks // 2, block_y, depth).astype(jnp.bfloat16)


def stack_kernel(slots, facts_ref, terms_ref, out_ref, facts, total, lined, sem):
    shots, tiles = terms_ref.shape[:2]
    wide = tiles // APX
    width = LANES // APY
    long = width * wide
    grid_rows = total.shape[0] // wide
    depth = total.shape[2]
    copy = pltpu.make_async_copy(facts_ref, facts, sem)
    copy.start()

    def clear(index, carry):
        total[index] = jnp.zeros(total.shape[1:], total.dtype)
        return carry

    lax.fori_loop(0, total.shape[0], clear, 0, unroll=8)
    copy.wait()

    def add(shot, carry):
        first = facts[shot, slots] * wide
        rows = pl.ds(facts[shot, slots + 1] * width, LANES)
        sums = [
            total[first + tile, rows] + terms_ref[shot, tile].astype(jnp.float32)
            for tile in range(tiles)
        ]
        for tile in range(tiles):
            total[first + tile, rows] = sums[tile]
        return carry

    lax.fori_loop(0, shots, add, 0, unroll=2)

    for row in range(grid_rows):
        for part in range(wide):
            for tile in range(total.shape[1] // LANES):
                at = pl.ds(LANES + tile * LANES * wide + part, LANES, stride=wide)
                lined[row, at] = total[row * wide + part, tile * LANES:(tile + 1) * LANES]

    low = lax.broadcasted_iota(jnp.int32, (LANES, depth), 0) < long

    def window(owner, slot, shift):
        block = facts[owner, slot]
        return lined[block // GRID_COLS, pl.ds(LANES - shift + block % GRID_COLS * long, LANES)]

    def give(owner, carry):
        pairs = [
            jnp.where(low, window(owner, slot, 0), window(owner, slot + 1, long))
            for slot in range(0, slots, 2)
        ]
        out_ref[owner] = jnp.concatenate(pairs, axis=0).astype(out_ref.dtype)
        return carry

    lax.fori_loop(0, shots, give, 0, unroll=4)


def finish_kernel(sums_ref, out_ref):
    slots, block_x = out_ref.shape[:2]
    depth = out_ref.shape[3]
    row = lax.broadcasted_iota(jnp.int32, (LANES, depth), 0)
    pair = row // 2
    for x in range(block_x):
        first = sums_ref[2 * x].astype(jnp.float32)
        second = sums_ref[2 * x + 1].astype(jnp.float32)
        for slot in range(slots):
            at = slot // 2 * LANES
            back = slot % 2 * (LANES // 2)
            one = first[at:at + LANES]
            two = second[at:at + LANES]

            def turned(value, shift):
                shift = (shift - back) % LANES
                return pltpu.roll(value, shift, 0) if shift else value

            result = jnp.where(pair == 0, turned(one, 0), turned(two, 2))
            result = jnp.where(pair == 2, turned(one, 2), result)
            out_ref[slot, x] = jnp.where(pair == 3, turned(two, 4), result)


def per_device(
    velocity_p,
    velocity_s,
    density,
    perturbation,
    seafloor,
    owner_ids,
    corner_x,
    corner_y,
    wave_prev,
    wave_now,
):
    slots, block_x, block_y, depth = velocity_p.shape
    count = lax.axis_size("shot")
    assert count == 2 * block_x and block_y == LANES
    patch = APX * APY
    split = lax.axis_size("depth") > 1
    if split:
        seafloor = seafloor - lax.axis_index("depth") * depth

    sent = pl.pallas_call(
        prepare_kernel,
        out_shape=jax.ShapeDtypeStruct((count, slots + 1, block_y, depth), jnp.bfloat16),
        in_specs=[vmem()] + [smem()] * 2 + [vmem()] * 5,
        out_specs=vmem(),
        scratch_shapes=[pltpu.VMEM((block_y, depth), jnp.int32)],
        compiler_params=limit(2),
        name="prepare",
    )(
        owner_ids[None], corner_x, corner_y, seafloor,
        velocity_p, velocity_s, density, perturbation,
    )
    pieces = lax.all_to_all(sent, "shot", 0, 0, tiled=True)

    picked, facts = pl.pallas_call(
        functools.partial(pick_kernel, slots),
        out_shape=(
            jax.ShapeDtypeStruct((count * patch, block_y, depth), jnp.bfloat16),
            jax.ShapeDtypeStruct((count, depth), jnp.int32),
        ),
        in_specs=[vmem()],
        out_specs=(vmem(), vmem()),
        scratch_shapes=[
            pltpu.SMEM((count, depth), jnp.int32),
            pltpu.SMEM((count * slots,), jnp.int32),
            pltpu.SemaphoreType.DMA,
        ],
        compiler_params=limit(3),
        name="pick",
    )(pieces.reshape(count * (slots + 1), block_y, depth))
    model = lax.all_to_all(
        picked.reshape(count, patch, block_y, depth), "shot", 0, 0, tiled=True
    )

    run = wave_split_depth if split else wave
    terms = run(model, wave_prev[0], wave_now[0])
    terms = lax.all_to_all(terms, "shot", 0, 0, tiled=True)

    rows = block_x * block_y // count
    grid_rows = count * slots // GRID_COLS
    wide = terms.shape[1] // APX
    sums = pl.pallas_call(
        functools.partial(stack_kernel, slots),
        out_shape=jax.ShapeDtypeStruct((count, slots * rows, depth), jnp.bfloat16),
        in_specs=[vmem(), vmem()],
        out_specs=vmem(),
        scratch_shapes=[
            pltpu.SMEM(facts.shape, jnp.int32),
            pltpu.VMEM((grid_rows * wide, GRID_COLS * LANES // APY, depth), jnp.float32),
            pltpu.VMEM((grid_rows, 2 * LANES + GRID_COLS * rows, depth), jnp.float32),
            pltpu.SemaphoreType.DMA,
        ],
        compiler_params=limit(3),
        name="stack",
    )(facts, terms)
    sums = lax.all_to_all(sums, "shot", 0, 0, tiled=True)
    return pl.pallas_call(
        finish_kernel,
        out_shape=jax.ShapeDtypeStruct(velocity_p.shape, jnp.float32),
        in_specs=[vmem()],
        out_specs=vmem(),
        compiler_params=limit(2),
        name="finish",
    )(sums)


def solution(mesh):
    in_specs = (
        P(("grp", "shot"), None, None, "depth"),
        P(("grp", "shot"), None, None, "depth"),
        P(("grp", "shot"), None, None, "depth"),
        P(("grp", "shot"), None, None, "depth"),
        P(("grp", "shot"), None, None),
        P(("grp", "shot")),
        P(("grp", "shot")),
        P(("grp", "shot")),
        P(("grp", "shot"), None, None, "depth"),
        P(("grp", "shot"), None, None, "depth"),
    )
    out_specs = P(("grp", "shot"), None, None, "depth")
    return jax.shard_map(
        per_device, mesh=mesh, in_specs=in_specs, out_specs=out_specs, check_vma=False
    )
```

```python
import functools

import jax
import jax.numpy as jnp
from jax import lax
from jax.experimental import pallas as pl
from jax.experimental.pallas import tpu as pltpu
from jax.sharding import PartitionSpec as P

APX = 4
APY = 4
STEPS = 4
GRID_COLS = 8
LANES = 8

speed_factor = 0.28
image_scale = 0.01


def with_halo(block, sides, width):
    for axis, dim in sides:
        count = lax.axis_size(axis)
        forward = [(i, i + 1) for i in range(count - 1)]
        backward = [(target, source) for source, target in forward]
        low = lax.ppermute(
            lax.slice_in_dim(block, block.shape[dim] - width, None, axis=dim), axis, forward
        )
        high = lax.ppermute(lax.slice_in_dim(block, 0, width, axis=dim), axis, backward)
        block = jnp.concatenate([low, block, high], axis=dim)
    return block


def laplace_many(fields):
    stacked = jnp.stack(fields)
    padded = with_halo(stacked.astype(jnp.bfloat16), (("depth", 3),), 1).astype(stacked.dtype)
    padded = jnp.pad(padded, ((0, 0), (1, 1), (1, 1), (0, 0)))
    beside = padded[:, 2:, 1:-1, 1:-1] + padded[:, :-2, 1:-1, 1:-1]
    beside = beside + padded[:, 1:-1, 2:, 1:-1] + padded[:, 1:-1, :-2, 1:-1]
    beside = beside + padded[:, 1:-1, 1:-1, 2:] + padded[:, 1:-1, 1:-1, :-2]
    result = beside - 6.0 * stacked
    return [result[index] for index in range(len(fields))]


def propagate(kappa, contrast, before, current, apply):
    grads = []
    datas = []
    grad_now = apply([current])[0]
    delta_prev = jnp.zeros_like(current)
    delta_now = contrast * grad_now
    grads.append(grad_now)
    datas.append(delta_now)
    before, current = (current, 2.0 * current - before + kappa * grad_now)
    for step in range(1, STEPS):
        grad_now, spread = apply([current, delta_now])
        delta_next = 2.0 * delta_now - delta_prev + kappa * spread + contrast * grad_now
        grads.append(grad_now)
        datas.append(delta_next)
        delta_prev, delta_now = (delta_now, delta_next)
        if step + 1 < STEPS:
            before, current = (current, 2.0 * current - before + kappa * grad_now)
    back = datas[STEPS - 1]
    back_after = jnp.zeros_like(back)
    image = grads[STEPS - 1] * back
    for step in range(STEPS - 2, -1, -1):
        spread = apply([kappa * back])
        back_new = 2.0 * back - back_after + spread[0] + datas[step]
        image = image + grads[step] * back_new
        back_after, back = (back, back_new)
    return image


def limit(mebibytes):
    return pltpu.CompilerParams(vmem_limit_bytes=mebibytes * 2**20)


def vmem():
    return pl.BlockSpec(memory_space=pltpu.VMEM)


def smem():
    return pl.BlockSpec(memory_space=pltpu.SMEM)


def prepare_kernel(
    row_ref, col_ref, ids_hbm, floor_hbm, p_hbm, s_hbm, rho_hbm, pert_hbm, out_ref,
    ids, floors, p, s, rho, pert, sems,
):
    slots, block_x, block_y, depth = p.shape
    near = block_x
    copies = [
        pltpu.make_async_copy(source, target, sems.at[index])
        for index, (source, target) in enumerate(
            [(p_hbm, p), (s_hbm, s), (rho_hbm, rho), (floor_hbm, floors), (pert_hbm, pert),
             (ids_hbm, ids)]
        )
    ]
    for copy in copies:
        copy.start()
    shape = (block_y, depth)
    deep = lax.broadcasted_iota(jnp.int32, shape, 1).astype(jnp.float32)
    lane = lax.broadcasted_iota(jnp.int32, shape, 1)
    same = lax.broadcasted_iota(jnp.int32, (block_y, block_y), 0) == (
        lax.broadcasted_iota(jnp.int32, (block_y, block_y), 1)
    )
    for copy in copies:
        copy.wait()
    for slot in range(slots):
        lines = floors[slot].astype(jnp.float32)
        for x in range(block_x):
            line = jnp.broadcast_to(lines[x:x + 1], (block_y, block_y))
            floor = jnp.sum(jnp.where(same, line, 0.0), axis=1, keepdims=True)
            primary = p[slot, x].astype(jnp.float32)
            shear = s[slot, x].astype(jnp.float32)
            square = primary * primary
            stiffness = jnp.where(deep >= floor, square + shear * shear, square)
            coef = speed_factor * stiffness / rho[slot, x].astype(jnp.float32)
            coef = coef.astype(out_ref.dtype)
            for piece in range(x, out_ref.shape[0], near):
                out_ref[piece, 2 * slot] = coef
                out_ref[piece, 2 * slot + 1] = pert[slot, x]
    facts = jnp.where(lane == slots, row_ref[0], 0)
    facts = jnp.where(lane == slots + 1, col_ref[0], facts)
    for slot in range(slots):
        facts = jnp.where(lane == slot, ids[slot], facts)
    facts = facts.astype(jnp.float32).astype(out_ref.dtype)
    for piece in range(out_ref.shape[0]):
        out_ref[piece, 2 * slots] = facts


def pick_kernel(slots, pieces_ref, out_ref, facts_ref, facts, spots, sem):
    count = facts_ref.shape[0]
    tiles = 2 * slots + 1
    near = out_ref.shape[0] // (2 * APX * APY)
    for piece in range(count):
        tile = pieces_ref[piece * tiles + 2 * slots].astype(jnp.float32)
        facts_ref[piece:piece + 1] = tile.astype(jnp.int32)[0:1]
    copy = pltpu.make_async_copy(facts_ref, facts, sem)
    copy.start()
    base = lax.axis_index("shot") // near * near
    copy.wait()
    for piece in range(count):
        for slot in range(slots):
            spots[facts[piece, slot]] = piece * tiles + 2 * slot

    def one(shot, carry):
        first = facts[base + shot, slots] * GRID_COLS + facts[base + shot, slots + 1]
        for x in range(APX):
            found = []
            for y in range(APY):
                spot = spots[first + x * GRID_COLS + y]
                found += [pieces_ref[spot], pieces_ref[spot + 1]]
            for index, tile in enumerate(found):
                out_ref[(shot * APX + x) * APY * 2 + index] = tile
        return carry

    lax.fori_loop(0, near, one, 0, unroll=2)


def ends(shape):
    lane = lax.broadcasted_iota(jnp.int32, shape, 1)
    row = lax.broadcasted_iota(jnp.int32, shape, 0)
    return lane == 0, lane == shape[1] - 1, row == 0, row == shape[0] - 1


def laplace(before, here, after, masks):
    lane_0, lane_n, row_0, row_n = masks
    many = len(here)
    depth = here[0].shape[1]
    low = [jnp.where(row_0, 0.0, pltpu.roll(here[-1], 1, 0))] + here[:-1]
    high = here[1:] + [jnp.where(row_n, 0.0, pltpu.roll(here[0], LANES - 1, 0))]
    result = []
    for v in range(many):
        up = jnp.where(lane_0, 0.0, pltpu.roll(here[v], 1, 1))
        down = jnp.where(lane_n, 0.0, pltpu.roll(here[v], depth - 1, 1))
        total = (before[v] + after[v]) + (low[v] + high[v]) + (up + down)
        result.append(total - 6.0 * here[v])
    return result


def registers(ref, x):
    return [ref[x, v] for v in range(ref.shape[1])]


def strided(ref, x):
    many = ref.shape[1] // LANES
    return [ref[x, pl.ds(v, LANES, stride=many)] for v in range(many)]


def sweep(count, fields, body, unroll):
    many = fields[0].shape[1]
    zero = [jnp.zeros(fields[0].shape[2:], jnp.float32)] * many
    first = [(zero, registers(field, 0)) for field in fields]

    def step(x, carry):
        rows = [
            (before, here, registers(field, x + 1))
            for (before, here), field in zip(carry, fields)
        ]
        body(x, rows)
        return [(here, after) for _, here, after in rows]

    lax.fori_loop(0, count, step, first, unroll=unroll)


def start_kernel(prev_ref, now_ref, wave_ref, grad_ref, next_ref, flat, flat_prev, field):
    span_x, span_y, depth = now_ref.shape
    many = span_y // LANES
    masks = ends((LANES, depth))

    def load(x, carry):
        flat[x] = now_ref[x].astype(jnp.float32)
        flat_prev[x] = prev_ref[x].astype(jnp.float32)
        return carry

    lax.fori_loop(0, span_x, load, 0, unroll=2)

    def order(x, carry):
        rows = strided(flat, x)
        older = strided(flat_prev, x)
        for v in range(many):
            field[x, v] = rows[v]
            wave_ref[x, v] = rows[v]
            next_ref[x, v] = 2.0 * rows[v] - older[v]
        return carry

    lax.fori_loop(0, span_x, order, 0, unroll=2)
    for v in range(many):
        field[span_x, v] = jnp.zeros((LANES, depth), jnp.float32)

    def body(x, rows):
        grads = laplace(*rows[0], masks)
        for v in range(many):
            grad_ref[x, v] = grads[v]

    sweep(span_x, [field], body, 8)


def start(before, current):
    span_x, span_y, depth = before.shape
    many = span_y // LANES
    out = jax.ShapeDtypeStruct((span_x, many, LANES, depth), jnp.float32)
    flat = pltpu.VMEM((span_x, span_y, depth), jnp.float32)
    return pl.pallas_call(
        start_kernel,
        out_shape=(out, out, out),
        in_specs=[vmem()] * 2,
        out_specs=(vmem(),) * 3,
        scratch_shapes=[flat, flat, pltpu.VMEM((span_x + 1, many, LANES, depth), jnp.float32)],
        compiler_params=limit(8),
        cost_estimate=pl.CostEstimate(
            flops=20 * before.size, bytes_accessed=16 * before.size, transcendentals=0
        ),
        name="start",
    )(before, current)


def wave_kernel(
    model_ref, u_0, g_0, next_ref, out_ref,
    kap, con, u_1, u_2, u_3, d_0, d_1, d_2, kb_3, kb_2, kb_1, g_1, g_2, d_3, b_2, b_1, image,
):
    span_x, many = u_0.shape[:2]
    depth = u_0.shape[3]
    block_y = model_ref.shape[2]
    block_x = span_x // APX
    masks = ends((LANES, depth))
    each = range(many)
    for field in (u_1, u_2, u_3, d_0, d_1, d_2, kb_3, kb_2, kb_1):
        for v in each:
            field[span_x, v] = jnp.zeros((LANES, depth), jnp.float32)

    def load(piece, carry):
        for x in range(APX):
            for y in range(APY):
                rows = pl.ds(y * block_y, block_y)
                at = x * block_x + piece
                tile = 2 * (x * APY + y)
                kap[at, rows] = model_ref[piece, tile].astype(jnp.float32)
                con[at, rows] = speed_factor * model_ref[piece, tile + 1].astype(jnp.float32)
        return carry

    lax.fori_loop(0, block_x, load, 0, unroll=4)

    def forward_0(x, carry):
        kaps, cons, grads = strided(kap, x), strided(con, x), registers(g_0, x)
        older = registers(next_ref, x)
        for v in each:
            d_0[x, v] = cons[v] * grads[v]
            u_1[x, v] = older[v] + kaps[v] * grads[v]
        return carry

    lax.fori_loop(0, span_x, forward_0, 0, unroll=8)

    def forward(u_now, u_prev, d_now, d_prev, u_next, d_next, g_now):
        def body(x, rows):
            waves, deltas = rows
            grads = laplace(*waves, masks)
            spread = laplace(*deltas, masks)
            kaps, cons = strided(kap, x), strided(con, x)
            for v in each:
                value = 2.0 * deltas[1][v] + kaps[v] * spread[v] + cons[v] * grads[v]
                if d_prev is not None:
                    value = value - d_prev[x, v]
                d_next[x, v] = value
                if u_next is None:
                    image[x, v] = grads[v] * value
                    kb_3[x, v] = kaps[v] * value
                else:
                    g_now[x, v] = grads[v]
                    u_next[x, v] = 2.0 * waves[1][v] - u_prev[x, v] + kaps[v] * grads[v]

        sweep(span_x, [u_now, d_now], body, 8)

    forward(u_1, u_0, d_0, None, u_2, d_1, g_1)
    forward(u_2, u_1, d_1, d_0, u_3, d_2, g_2)
    forward(u_3, u_2, d_2, d_1, None, d_3, None)

    def adjoint(kb, b_now, b_after, data, grad, kb_next, b_next):
        def body(x, rows):
            spread = laplace(*rows[0], masks)
            kaps = None if kb_next is None else strided(kap, x)
            for v in each:
                back = 2.0 * b_now[x, v] + spread[v] + data[x, v]
                if b_after is not None:
                    back = back - b_after[x, v]
                total = image[x, v] + grad[x, v] * back
                if kb_next is None:
                    total = (image_scale * total).astype(out_ref.dtype)
                    piece = 2 * (x % block_x) + v // 2
                    out_ref[piece, 2 * (x // block_x) + v % 2] = total
                else:
                    image[x, v] = total
                    b_next[x, v] = back
                    kb_next[x, v] = kaps[v] * back

        sweep(span_x, [kb], body, 8)

    adjoint(kb_3, d_3, None, d_2, g_2, kb_2, b_2)
    adjoint(kb_2, b_2, d_3, d_1, g_1, kb_1, b_1)
    adjoint(kb_1, b_1, b_2, d_0, g_0, None, None)


def wave(model, before, current):
    span_x, span_y, depth = before.shape
    near, tiles, block_y, _ = model.shape
    pieces, blocks = 2 * near, tiles // 2
    many = span_y // LANES
    flat = pltpu.VMEM((span_x, span_y, depth), jnp.float32)
    field = pltpu.VMEM((span_x + 1, many, LANES, depth), jnp.float32)
    plain = pltpu.VMEM((span_x, many, LANES, depth), jnp.float32)
    return pl.pallas_call(
        wave_kernel,
        out_shape=jax.ShapeDtypeStruct((pieces, blocks // 2, block_y, depth), jnp.bfloat16),
        in_specs=[vmem()] * 4,
        out_specs=vmem(),
        scratch_shapes=[flat] * 2 + [field] * 9 + [plain] * 6,
        compiler_params=limit(20),
        name="wave",
    )(model, *start(before, current))


def wave_split_depth(model, before, current):
    span_x, span_y, depth = before.shape
    block_x, tiles, block_y, _ = model.shape
    pieces, blocks = 2 * block_x, tiles // 2
    grids = model.reshape(block_x, APX, APY, 2, block_y, depth).transpose(3, 1, 0, 2, 4, 5)
    grids = grids.reshape(2, span_x, span_y, depth).astype(jnp.float32)
    image = image_scale * propagate(
        grids[0],
        speed_factor * grids[1],
        before.astype(jnp.float32),
        current.astype(jnp.float32),
        laplace_many,
    )
    many = span_y // LANES
    image = image.reshape(APX, block_x, LANES, 2, many // 2, depth).transpose(1, 3, 0, 4, 2, 5)
    return image.reshape(pieces, blocks // 2, block_y, depth).astype(jnp.bfloat16)


def stack_kernel(slots, facts_ref, terms_ref, out_ref, facts, total, lined, sem):
    shots, tiles = terms_ref.shape[:2]
    wide = tiles // APX
    width = LANES // APY
    long = width * wide
    grid_rows = total.shape[0] // wide
    depth = total.shape[2]
    copy = pltpu.make_async_copy(facts_ref, facts, sem)
    copy.start()

    def clear(index, carry):
        total[index] = jnp.zeros(total.shape[1:], total.dtype)
        return carry

    lax.fori_loop(0, total.shape[0], clear, 0, unroll=8)
    copy.wait()

    def add(shot, carry):
        first = facts[shot, slots] * wide
        rows = pl.ds(facts[shot, slots + 1] * width, LANES)
        sums = [
            total[first + tile, rows] + terms_ref[shot, tile].astype(jnp.float32)
            for tile in range(tiles)
        ]
        for tile in range(tiles):
            total[first + tile, rows] = sums[tile]
        return carry

    lax.fori_loop(0, shots, add, 0, unroll=2)

    for row in range(grid_rows):
        for part in range(wide):
            for tile in range(total.shape[1] // LANES):
                at = pl.ds(LANES + tile * LANES * wide + part, LANES, stride=wide)
                lined[row, at] = total[row * wide + part, tile * LANES:(tile + 1) * LANES]

    low = lax.broadcasted_iota(jnp.int32, (LANES, depth), 0) < long

    def window(owner, slot, shift):
        block = facts[owner, slot]
        return lined[block // GRID_COLS, pl.ds(LANES - shift + block % GRID_COLS * long, LANES)]

    def give(owner, carry):
        pairs = [
            jnp.where(low, window(owner, slot, 0), window(owner, slot + 1, long))
            for slot in range(0, slots, 2)
        ]
        out_ref[owner] = jnp.concatenate(pairs, axis=0).astype(out_ref.dtype)
        return carry

    lax.fori_loop(0, shots, give, 0, unroll=4)


def finish_kernel(sums_ref, out_ref):
    slots, block_x = out_ref.shape[:2]
    depth = out_ref.shape[3]
    row = lax.broadcasted_iota(jnp.int32, (LANES, depth), 0)
    pair = row // 2
    for x in range(block_x):
        first = sums_ref[2 * x].astype(jnp.float32)
        second = sums_ref[2 * x + 1].astype(jnp.float32)
        for slot in range(slots):
            at = slot // 2 * LANES
            back = slot % 2 * (LANES // 2)
            one = first[at:at + LANES]
            two = second[at:at + LANES]

            def turned(value, shift):
                shift = (shift - back) % LANES
                return pltpu.roll(value, shift, 0) if shift else value

            result = jnp.where(pair == 0, turned(one, 0), turned(two, 2))
            result = jnp.where(pair == 2, turned(one, 2), result)
            out_ref[slot, x] = jnp.where(pair == 3, turned(two, 4), result)


def per_device(
    velocity_p,
    velocity_s,
    density,
    perturbation,
    seafloor,
    owner_ids,
    corner_x,
    corner_y,
    wave_prev,
    wave_now,
):
    slots, block_x, block_y, depth = velocity_p.shape
    count = lax.axis_size("shot")
    assert count == 2 * block_x and block_y == LANES
    patch = APX * APY
    split = lax.axis_size("depth") > 1
    if split:
        seafloor = seafloor - lax.axis_index("depth") * depth

    near = block_x
    groups = [list(range(first, first + near)) for first in range(0, count, near)]
    sent = pl.pallas_call(
        prepare_kernel,
        out_shape=jax.ShapeDtypeStruct((count, 2 * slots + 1, block_y, depth), jnp.bfloat16),
        in_specs=[smem()] * 2 + [pl.BlockSpec(memory_space=pltpu.HBM)] * 6,
        out_specs=vmem(),
        scratch_shapes=[
            pltpu.SMEM(owner_ids.shape, jnp.int32),
            pltpu.VMEM(seafloor.shape, jnp.int32),
            *[pltpu.VMEM(velocity_p.shape, jnp.bfloat16) for _ in range(4)],
            pltpu.SemaphoreType.DMA((6,)),
        ],
        name="prepare",
    )(
        corner_x, corner_y, owner_ids, seafloor,
        velocity_p, velocity_s, density, perturbation,
    )
    pieces = lax.all_to_all(sent, "shot", 0, 0, tiled=True)

    picked, facts = pl.pallas_call(
        functools.partial(pick_kernel, slots),
        out_shape=(
            jax.ShapeDtypeStruct((near * patch * 2, block_y, depth), jnp.bfloat16),
            jax.ShapeDtypeStruct((count, depth), jnp.int32),
        ),
        in_specs=[vmem()],
        out_specs=(vmem(), vmem()),
        scratch_shapes=[
            pltpu.SMEM((count, depth), jnp.int32),
            pltpu.SMEM((count * slots,), jnp.int32),
            pltpu.SemaphoreType.DMA,
        ],
        compiler_params=limit(3),
        name="pick",
    )(pieces.reshape(count * (2 * slots + 1), block_y, depth))
    model = lax.all_to_all(
        picked.reshape(near, patch * 2, block_y, depth), "shot", 0, 0,
        axis_index_groups=groups, tiled=True,
    )

    run = wave_split_depth if split else wave
    terms = run(model, wave_prev[0], wave_now[0])
    terms = lax.all_to_all(terms, "shot", 0, 0, tiled=True)

    rows = block_x * block_y // count
    grid_rows = count * slots // GRID_COLS
    wide = terms.shape[1] // APX
    sums = pl.pallas_call(
        functools.partial(stack_kernel, slots),
        out_shape=jax.ShapeDtypeStruct((count, slots * rows, depth), jnp.bfloat16),
        in_specs=[vmem(), vmem()],
        out_specs=vmem(),
        scratch_shapes=[
            pltpu.SMEM(facts.shape, jnp.int32),
            pltpu.VMEM((grid_rows * wide, GRID_COLS * LANES // APY, depth), jnp.float32),
            pltpu.VMEM((grid_rows, 2 * LANES + GRID_COLS * rows, depth), jnp.float32),
            pltpu.SemaphoreType.DMA,
        ],
        compiler_params=limit(3),
        name="stack",
    )(facts, terms)
    sums = lax.all_to_all(sums, "shot", 0, 0, tiled=True)
    return pl.pallas_call(
        finish_kernel,
        out_shape=jax.ShapeDtypeStruct(velocity_p.shape, jnp.float32),
        in_specs=[vmem()],
        out_specs=vmem(),
        compiler_params=limit(2),
        name="finish",
    )(sums)


def solution(mesh):
    in_specs = (
        P(("grp", "shot"), None, None, "depth"),
        P(("grp", "shot"), None, None, "depth"),
        P(("grp", "shot"), None, None, "depth"),
        P(("grp", "shot"), None, None, "depth"),
        P(("grp", "shot"), None, None),
        P(("grp", "shot")),
        P(("grp", "shot")),
        P(("grp", "shot")),
        P(("grp", "shot"), None, None, "depth"),
        P(("grp", "shot"), None, None, "depth"),
    )
    out_specs = P(("grp", "shot"), None, None, "depth")
    return jax.shard_map(
        per_device, mesh=mesh, in_specs=in_specs, out_specs=out_specs, check_vma=False
    )
```

```python
import functools

import jax
import jax.numpy as jnp
from jax import lax
from jax.experimental import pallas as pl
from jax.experimental.pallas import tpu as pltpu
from jax.sharding import PartitionSpec as P

APX = 4
APY = 4
STEPS = 4
GRID_COLS = 8
LANES = 8

speed_factor = 0.28
image_scale = 0.01


def with_halo(block, sides, width):
    for axis, dim in sides:
        count = lax.axis_size(axis)
        forward = [(i, i + 1) for i in range(count - 1)]
        backward = [(target, source) for source, target in forward]
        low = lax.ppermute(
            lax.slice_in_dim(block, block.shape[dim] - width, None, axis=dim), axis, forward
        )
        high = lax.ppermute(lax.slice_in_dim(block, 0, width, axis=dim), axis, backward)
        block = jnp.concatenate([low, block, high], axis=dim)
    return block


def laplace_many(fields):
    stacked = jnp.stack(fields)
    padded = with_halo(stacked.astype(jnp.bfloat16), (("depth", 3),), 1).astype(stacked.dtype)
    padded = jnp.pad(padded, ((0, 0), (1, 1), (1, 1), (0, 0)))
    beside = padded[:, 2:, 1:-1, 1:-1] + padded[:, :-2, 1:-1, 1:-1]
    beside = beside + padded[:, 1:-1, 2:, 1:-1] + padded[:, 1:-1, :-2, 1:-1]
    beside = beside + padded[:, 1:-1, 1:-1, 2:] + padded[:, 1:-1, 1:-1, :-2]
    result = beside - 6.0 * stacked
    return [result[index] for index in range(len(fields))]


def propagate(kappa, contrast, before, current, apply):
    grads = []
    datas = []
    grad_now = apply([current])[0]
    delta_prev = jnp.zeros_like(current)
    delta_now = contrast * grad_now
    grads.append(grad_now)
    datas.append(delta_now)
    before, current = (current, 2.0 * current - before + kappa * grad_now)
    for step in range(1, STEPS):
        grad_now, spread = apply([current, delta_now])
        delta_next = 2.0 * delta_now - delta_prev + kappa * spread + contrast * grad_now
        grads.append(grad_now)
        datas.append(delta_next)
        delta_prev, delta_now = (delta_now, delta_next)
        if step + 1 < STEPS:
            before, current = (current, 2.0 * current - before + kappa * grad_now)
    back = datas[STEPS - 1]
    back_after = jnp.zeros_like(back)
    image = grads[STEPS - 1] * back
    for step in range(STEPS - 2, -1, -1):
        spread = apply([kappa * back])
        back_new = 2.0 * back - back_after + spread[0] + datas[step]
        image = image + grads[step] * back_new
        back_after, back = (back, back_new)
    return image


def limit(mebibytes):
    return pltpu.CompilerParams(vmem_limit_bytes=mebibytes * 2**20)


def vmem():
    return pl.BlockSpec(memory_space=pltpu.VMEM)


def smem():
    return pl.BlockSpec(memory_space=pltpu.SMEM)


def prepare_kernel(
    row_ref, col_ref, ids_hbm, floor_hbm, p_hbm, s_hbm, rho_hbm, pert_hbm, out_ref,
    ids, floors, p, s, rho, pert, sems,
):
    slots, block_x, block_y, depth = p.shape
    near = block_x
    copies = [
        pltpu.make_async_copy(source, target, sems.at[index])
        for index, (source, target) in enumerate(
            [(p_hbm, p), (s_hbm, s), (rho_hbm, rho), (floor_hbm, floors), (pert_hbm, pert),
             (ids_hbm, ids)]
        )
    ]
    for copy in copies:
        copy.start()
    shape = (block_y, depth)
    deep = lax.broadcasted_iota(jnp.int32, shape, 1).astype(jnp.float32)
    lane = lax.broadcasted_iota(jnp.int32, shape, 1)
    same = lax.broadcasted_iota(jnp.int32, (block_y, block_y), 0) == (
        lax.broadcasted_iota(jnp.int32, (block_y, block_y), 1)
    )
    for copy in copies:
        copy.wait()
    for slot in range(slots):
        lines = floors[slot].astype(jnp.float32)
        for x in range(block_x):
            line = jnp.broadcast_to(lines[x:x + 1], (block_y, block_y))
            floor = jnp.sum(jnp.where(same, line, 0.0), axis=1, keepdims=True)
            primary = p[slot, x].astype(jnp.float32)
            shear = s[slot, x].astype(jnp.float32)
            square = primary * primary
            stiffness = jnp.where(deep >= floor, square + shear * shear, square)
            coef = speed_factor * stiffness / rho[slot, x].astype(jnp.float32)
            coef = coef.astype(out_ref.dtype)
            for piece in range(x, out_ref.shape[0], near):
                out_ref[piece, 2 * slot] = coef
                out_ref[piece, 2 * slot + 1] = pert[slot, x]
    facts = jnp.where(lane == slots, row_ref[0], 0)
    facts = jnp.where(lane == slots + 1, col_ref[0], facts)
    for slot in range(slots):
        facts = jnp.where(lane == slot, ids[slot], facts)
    facts = facts.astype(jnp.float32).astype(out_ref.dtype)
    for piece in range(out_ref.shape[0]):
        out_ref[piece, 2 * slots] = facts


def pick_kernel(slots, pieces_ref, out_ref, facts_ref, facts, spots, sem):
    count = facts_ref.shape[0]
    tiles = 2 * slots + 1
    near = out_ref.shape[0] // (2 * APX * APY)
    for piece in range(count):
        tile = pieces_ref[piece * tiles + 2 * slots].astype(jnp.float32)
        facts_ref[piece:piece + 1] = tile.astype(jnp.int32)[0:1]
    copy = pltpu.make_async_copy(facts_ref, facts, sem)
    copy.start()
    base = lax.axis_index("shot") // near * near
    copy.wait()
    for piece in range(count):
        for slot in range(slots):
            spots[facts[piece, slot]] = piece * tiles + 2 * slot

    def one(shot, carry):
        first = facts[base + shot, slots] * GRID_COLS + facts[base + shot, slots + 1]
        for x in range(APX):
            found = []
            for y in range(APY):
                spot = spots[first + x * GRID_COLS + y]
                found += [pieces_ref[spot], pieces_ref[spot + 1]]
            for index, tile in enumerate(found):
                out_ref[(shot * APX + x) * APY * 2 + index] = tile
        return carry

    lax.fori_loop(0, near, one, 0, unroll=2)


def ends(shape):
    lane = lax.broadcasted_iota(jnp.int32, shape, 1)
    row = lax.broadcasted_iota(jnp.int32, shape, 0)
    return lane == 0, lane == shape[1] - 1, row == 0, row == shape[0] - 1


def laplace(before, here, after, masks):
    lane_0, lane_n, row_0, row_n = masks
    many = len(here)
    depth = here[0].shape[1]
    low = [jnp.where(row_0, 0.0, pltpu.roll(here[-1], 1, 0))] + here[:-1]
    high = here[1:] + [jnp.where(row_n, 0.0, pltpu.roll(here[0], LANES - 1, 0))]
    result = []
    for v in range(many):
        up = jnp.where(lane_0, 0.0, pltpu.roll(here[v], 1, 1))
        down = jnp.where(lane_n, 0.0, pltpu.roll(here[v], depth - 1, 1))
        total = (before[v] + after[v]) + (low[v] + high[v]) + (up + down)
        result.append(total - 6.0 * here[v])
    return result


def registers(ref, x):
    return [ref[x, v] for v in range(ref.shape[1])]


def strided(ref, x):
    many = ref.shape[1] // LANES
    return [ref[x, pl.ds(v, LANES, stride=many)] for v in range(many)]


def sweep(count, fields, body, unroll):
    many = fields[0].shape[1]
    zero = [jnp.zeros(fields[0].shape[2:], jnp.float32)] * many
    first = [(zero, registers(field, 0)) for field in fields]

    def step(x, carry):
        rows = [
            (before, here, registers(field, x + 1))
            for (before, here), field in zip(carry, fields)
        ]
        body(x, rows)
        return [(here, after) for _, here, after in rows]

    lax.fori_loop(0, count, step, first, unroll=unroll)


def start_kernel(prev_ref, now_ref, wave_ref, grad_ref, next_ref, flat, flat_prev, field):
    span_x, span_y, depth = now_ref.shape
    many = span_y // LANES
    masks = ends((LANES, depth))

    def load(x, carry):
        flat[x] = now_ref[x].astype(jnp.float32)
        flat_prev[x] = prev_ref[x].astype(jnp.float32)
        return carry

    lax.fori_loop(0, span_x, load, 0, unroll=2)

    def order(x, carry):
        rows = strided(flat, x)
        older = strided(flat_prev, x)
        for v in range(many):
            field[x, v] = rows[v]
            wave_ref[x, v] = rows[v]
            next_ref[x, v] = 2.0 * rows[v] - older[v]
        return carry

    lax.fori_loop(0, span_x, order, 0, unroll=2)
    for v in range(many):
        field[span_x, v] = jnp.zeros((LANES, depth), jnp.float32)

    def body(x, rows):
        grads = laplace(*rows[0], masks)
        for v in range(many):
            grad_ref[x, v] = grads[v]

    sweep(span_x, [field], body, 16)


def start(before, current):
    span_x, span_y, depth = before.shape
    many = span_y // LANES
    out = jax.ShapeDtypeStruct((span_x, many, LANES, depth), jnp.float32)
    flat = pltpu.VMEM((span_x, span_y, depth), jnp.float32)
    return pl.pallas_call(
        start_kernel,
        out_shape=(out, out, out),
        in_specs=[vmem()] * 2,
        out_specs=(vmem(),) * 3,
        scratch_shapes=[flat, flat, pltpu.VMEM((span_x + 1, many, LANES, depth), jnp.float32)],
        compiler_params=limit(8),
        cost_estimate=pl.CostEstimate(
            flops=20 * before.size, bytes_accessed=16 * before.size, transcendentals=0
        ),
        name="start",
    )(before, current)


def wave_kernel(
    model_ref, u_0, g_0, next_ref, out_ref,
    kap, con, u_1, u_2, u_3, d_0, d_1, d_2, kb_3, kb_2, kb_1, g_1, g_2, d_3, b_2, b_1, image,
):
    span_x, many = u_0.shape[:2]
    depth = u_0.shape[3]
    block_y = model_ref.shape[2]
    block_x = span_x // APX
    masks = ends((LANES, depth))
    each = range(many)
    for field in (u_1, u_2, u_3, d_0, d_1, d_2, kb_3, kb_2, kb_1):
        for v in each:
            field[span_x, v] = jnp.zeros((LANES, depth), jnp.float32)

    def load(piece, carry):
        for x in range(APX):
            for y in range(APY):
                rows = pl.ds(y * block_y, block_y)
                at = x * block_x + piece
                tile = 2 * (x * APY + y)
                kap[at, rows] = model_ref[piece, tile].astype(jnp.float32)
                con[at, rows] = speed_factor * model_ref[piece, tile + 1].astype(jnp.float32)
        return carry

    lax.fori_loop(0, block_x, load, 0, unroll=4)

    def forward_0(x, carry):
        kaps, cons, grads = strided(kap, x), strided(con, x), registers(g_0, x)
        older = registers(next_ref, x)
        for v in each:
            d_0[x, v] = cons[v] * grads[v]
            u_1[x, v] = older[v] + kaps[v] * grads[v]
        return carry

    lax.fori_loop(0, span_x, forward_0, 0, unroll=16)

    def forward(u_now, u_prev, d_now, d_prev, u_next, d_next, g_now):
        def body(x, rows):
            waves, deltas = rows
            grads = laplace(*waves, masks)
            spread = laplace(*deltas, masks)
            kaps, cons = strided(kap, x), strided(con, x)
            for v in each:
                value = 2.0 * deltas[1][v] + kaps[v] * spread[v] + cons[v] * grads[v]
                if d_prev is not None:
                    value = value - d_prev[x, v]
                d_next[x, v] = value
                if u_next is None:
                    image[x, v] = grads[v] * value
                    kb_3[x, v] = kaps[v] * value
                else:
                    g_now[x, v] = grads[v]
                    u_next[x, v] = 2.0 * waves[1][v] - u_prev[x, v] + kaps[v] * grads[v]

        sweep(span_x, [u_now, d_now], body, 16)

    forward(u_1, u_0, d_0, None, u_2, d_1, g_1)
    forward(u_2, u_1, d_1, d_0, u_3, d_2, g_2)
    forward(u_3, u_2, d_2, d_1, None, d_3, None)

    def adjoint(kb, b_now, b_after, data, grad, kb_next, b_next):
        def body(x, rows):
            spread = laplace(*rows[0], masks)
            kaps = None if kb_next is None else strided(kap, x)
            for v in each:
                back = 2.0 * b_now[x, v] + spread[v] + data[x, v]
                if b_after is not None:
                    back = back - b_after[x, v]
                total = image[x, v] + grad[x, v] * back
                if kb_next is None:
                    total = (image_scale * total).astype(out_ref.dtype)
                    out_ref[x % block_x, x // block_x * many + v] = total
                else:
                    image[x, v] = total
                    b_next[x, v] = back
                    kb_next[x, v] = kaps[v] * back

        sweep(span_x, [kb], body, 16)

    adjoint(kb_3, d_3, None, d_2, g_2, kb_2, b_2)
    adjoint(kb_2, b_2, d_3, d_1, g_1, kb_1, b_1)
    adjoint(kb_1, b_1, b_2, d_0, g_0, None, None)


def wave(model, started):
    span_x, many, _, depth = started[0].shape
    near, tiles, _, _ = model.shape
    flat = pltpu.VMEM((span_x, many * LANES, depth), jnp.float32)
    field = pltpu.VMEM((span_x + 1, many, LANES, depth), jnp.float32)
    plain = pltpu.VMEM((span_x, many, LANES, depth), jnp.float32)
    return pl.pallas_call(
        wave_kernel,
        out_shape=jax.ShapeDtypeStruct((near, APX * many, LANES, depth), jnp.bfloat16),
        in_specs=[vmem()] * 4,
        out_specs=vmem(),
        scratch_shapes=[flat] * 2 + [field] * 9 + [plain] * 6,
        compiler_params=limit(20),
        name="wave",
    )(model, *started)


def wave_split_depth(model, before, current):
    span_x, span_y, depth = before.shape
    block_x, tiles, block_y, _ = model.shape
    grids = model.reshape(block_x, APX, APY, 2, block_y, depth).transpose(3, 1, 0, 2, 4, 5)
    grids = grids.reshape(2, span_x, span_y, depth).astype(jnp.float32)
    image = image_scale * propagate(
        grids[0],
        speed_factor * grids[1],
        before.astype(jnp.float32),
        current.astype(jnp.float32),
        laplace_many,
    )
    many = span_y // LANES
    image = image.reshape(APX, block_x, LANES, many, depth).transpose(1, 0, 3, 2, 4)
    return image.reshape(block_x, APX * many, LANES, depth).astype(jnp.bfloat16)


def stack_kernel(slots, facts_ref, terms_ref, out_ref, facts, total, lined, sem):
    shots, tiles = terms_ref.shape[:2]
    wide = tiles // APX
    width = LANES // APY
    grid_rows = total.shape[0] // wide
    copy = pltpu.make_async_copy(facts_ref, facts, sem)
    copy.start()
    base = lax.axis_index("shot") // shots * shots

    def clear(index, carry):
        total[index] = jnp.zeros(total.shape[1:], total.dtype)
        return carry

    lax.fori_loop(0, total.shape[0], clear, 0, unroll=8)
    copy.wait()

    def add(shot, carry):
        first = facts[base + shot, slots] * wide
        rows = pl.ds(facts[base + shot, slots + 1] * width, LANES)
        sums = [
            total[first + tile, rows] + terms_ref[shot, tile].astype(jnp.float32)
            for tile in range(tiles)
        ]
        for tile in range(tiles):
            total[first + tile, rows] = sums[tile]
        return carry

    lax.fori_loop(0, shots, add, 0, unroll=2)

    for row in range(grid_rows):
        for part in range(wide):
            for tile in range(total.shape[1] // LANES):
                at = pl.ds(tile * LANES * wide + part, LANES, stride=wide)
                lined[row, at] = total[row * wide + part, tile * LANES:(tile + 1) * LANES]

    def give(owner, carry):
        found = []
        for slot in range(slots):
            block = facts[owner, slot]
            rows = pl.ds(pl.multiple_of(block % GRID_COLS * LANES, LANES), LANES)
            found.append(lined[block // GRID_COLS, rows])
        for slot in range(slots):
            out_ref[owner, slot] = found[slot].astype(out_ref.dtype)
        return carry

    lax.fori_loop(0, out_ref.shape[0], give, 0, unroll=4)


def finish_kernel(sums_ref, out_ref):
    slots, block_x = out_ref.shape[:2]
    for x in range(block_x):
        for slot in range(slots):
            result = sums_ref[x, slot].astype(jnp.float32)
            for piece in range(x + block_x, sums_ref.shape[0], block_x):
                result = result + sums_ref[piece, slot].astype(jnp.float32)
            out_ref[slot, x] = result


def per_device(
    velocity_p,
    velocity_s,
    density,
    perturbation,
    seafloor,
    owner_ids,
    corner_x,
    corner_y,
    wave_prev,
    wave_now,
):
    slots, block_x, block_y, depth = velocity_p.shape
    count = lax.axis_size("shot")
    assert count == 2 * block_x and block_y == LANES
    patch = APX * APY
    split = lax.axis_size("depth") > 1
    if split:
        seafloor = seafloor - lax.axis_index("depth") * depth

    near = block_x
    groups = [list(range(first, first + near)) for first in range(0, count, near)]
    sent = pl.pallas_call(
        prepare_kernel,
        out_shape=jax.ShapeDtypeStruct((count, 2 * slots + 1, block_y, depth), jnp.bfloat16),
        in_specs=[smem()] * 2 + [pl.BlockSpec(memory_space=pltpu.HBM)] * 6,
        out_specs=vmem(),
        scratch_shapes=[
            pltpu.SMEM(owner_ids.shape, jnp.int32),
            pltpu.VMEM(seafloor.shape, jnp.int32),
            *[pltpu.VMEM(velocity_p.shape, jnp.bfloat16) for _ in range(4)],
            pltpu.SemaphoreType.DMA((6,)),
        ],
        name="prepare",
    )(
        corner_x, corner_y, owner_ids, seafloor,
        velocity_p, velocity_s, density, perturbation,
    )
    pieces = lax.all_to_all(sent, "shot", 0, 0, tiled=True)

    if not split:
        started = start(wave_prev[0], wave_now[0])
        pieces, started = lax.optimization_barrier((pieces, started))
    picked, facts = pl.pallas_call(
        functools.partial(pick_kernel, slots),
        out_shape=(
            jax.ShapeDtypeStruct((near * patch * 2, block_y, depth), jnp.bfloat16),
            jax.ShapeDtypeStruct((count, depth), jnp.int32),
        ),
        in_specs=[vmem()],
        out_specs=(vmem(), vmem()),
        scratch_shapes=[
            pltpu.SMEM((count, depth), jnp.int32),
            pltpu.SMEM((count * slots,), jnp.int32),
            pltpu.SemaphoreType.DMA,
        ],
        compiler_params=limit(3),
        name="pick",
    )(pieces.reshape(count * (2 * slots + 1), block_y, depth))
    model = lax.all_to_all(
        picked.reshape(near, patch * 2, block_y, depth), "shot", 0, 0,
        axis_index_groups=groups, tiled=True,
    )

    if split:
        terms = wave_split_depth(model, wave_prev[0], wave_now[0])
    else:
        terms = wave(model, started)
    terms = lax.all_to_all(terms, "shot", 0, 0, axis_index_groups=groups, tiled=True)

    grid_rows = count * slots // GRID_COLS
    wide = terms.shape[1] // APX
    sums = pl.pallas_call(
        functools.partial(stack_kernel, slots),
        out_shape=jax.ShapeDtypeStruct((count, slots, block_y, depth), jnp.bfloat16),
        in_specs=[vmem(), vmem()],
        out_specs=vmem(),
        scratch_shapes=[
            pltpu.SMEM(facts.shape, jnp.int32),
            pltpu.VMEM((grid_rows * wide, GRID_COLS * LANES // APY, depth), jnp.float32),
            pltpu.VMEM((grid_rows, GRID_COLS * block_y, depth), jnp.float32),
            pltpu.SemaphoreType.DMA,
        ],
        compiler_params=limit(3),
        name="stack",
    )(facts, terms)
    sums = lax.all_to_all(sums, "shot", 0, 0, tiled=True)
    return pl.pallas_call(
        finish_kernel,
        out_shape=jax.ShapeDtypeStruct(velocity_p.shape, jnp.float32),
        in_specs=[vmem()],
        out_specs=vmem(),
        compiler_params=limit(2),
        name="finish",
    )(sums)


def solution(mesh):
    in_specs = (
        P(("grp", "shot"), None, None, "depth"),
        P(("grp", "shot"), None, None, "depth"),
        P(("grp", "shot"), None, None, "depth"),
        P(("grp", "shot"), None, None, "depth"),
        P(("grp", "shot"), None, None),
        P(("grp", "shot")),
        P(("grp", "shot")),
        P(("grp", "shot")),
        P(("grp", "shot"), None, None, "depth"),
        P(("grp", "shot"), None, None, "depth"),
    )
    out_specs = P(("grp", "shot"), None, None, "depth")
    return jax.shard_map(
        per_device, mesh=mesh, in_specs=in_specs, out_specs=out_specs, check_vma=False
    )
```

```python
import functools

import jax
import jax.numpy as jnp
from jax import lax
from jax.experimental import pallas as pl
from jax.experimental.pallas import tpu as pltpu
from jax.sharding import PartitionSpec as P

APX = 4
APY = 4
STEPS = 4
GRID_COLS = 8
LANES = 8

speed_factor = 0.28
image_scale = 0.01


def with_halo(block, sides, width):
    for axis, dim in sides:
        count = lax.axis_size(axis)
        forward = [(i, i + 1) for i in range(count - 1)]
        backward = [(target, source) for source, target in forward]
        low = lax.ppermute(
            lax.slice_in_dim(block, block.shape[dim] - width, None, axis=dim), axis, forward
        )
        high = lax.ppermute(lax.slice_in_dim(block, 0, width, axis=dim), axis, backward)
        block = jnp.concatenate([low, block, high], axis=dim)
    return block


def laplace_many(fields):
    stacked = jnp.stack(fields)
    padded = with_halo(stacked.astype(jnp.bfloat16), (("depth", 3),), 1).astype(stacked.dtype)
    padded = jnp.pad(padded, ((0, 0), (1, 1), (1, 1), (0, 0)))
    beside = padded[:, 2:, 1:-1, 1:-1] + padded[:, :-2, 1:-1, 1:-1]
    beside = beside + padded[:, 1:-1, 2:, 1:-1] + padded[:, 1:-1, :-2, 1:-1]
    beside = beside + padded[:, 1:-1, 1:-1, 2:] + padded[:, 1:-1, 1:-1, :-2]
    result = beside - 6.0 * stacked
    return [result[index] for index in range(len(fields))]


def propagate(kappa, contrast, before, current, apply):
    grads = []
    datas = []
    grad_now = apply([current])[0]
    delta_prev = jnp.zeros_like(current)
    delta_now = contrast * grad_now
    grads.append(grad_now)
    datas.append(delta_now)
    before, current = (current, 2.0 * current - before + kappa * grad_now)
    for step in range(1, STEPS):
        grad_now, spread = apply([current, delta_now])
        delta_next = 2.0 * delta_now - delta_prev + kappa * spread + contrast * grad_now
        grads.append(grad_now)
        datas.append(delta_next)
        delta_prev, delta_now = (delta_now, delta_next)
        if step + 1 < STEPS:
            before, current = (current, 2.0 * current - before + kappa * grad_now)
    back = datas[STEPS - 1]
    back_after = jnp.zeros_like(back)
    image = grads[STEPS - 1] * back
    for step in range(STEPS - 2, -1, -1):
        spread = apply([kappa * back])
        back_new = 2.0 * back - back_after + spread[0] + datas[step]
        image = image + grads[step] * back_new
        back_after, back = (back, back_new)
    return image


def limit(mebibytes):
    return pltpu.CompilerParams(vmem_limit_bytes=mebibytes * 2**20)


def vmem():
    return pl.BlockSpec(memory_space=pltpu.VMEM)


def smem():
    return pl.BlockSpec(memory_space=pltpu.SMEM)


def prepare_kernel(
    row_ref, col_ref, ids_hbm, floor_hbm, p_hbm, s_hbm, rho_hbm, pert_hbm, out_ref, pert_ref,
    ids, floors, p, s, rho, pert, sems,
):
    slots, block_x, block_y, depth = p.shape
    near = block_x
    copies = [
        pltpu.make_async_copy(source, target, sems.at[index])
        for index, (source, target) in enumerate(
            [(p_hbm, p), (s_hbm, s), (rho_hbm, rho), (floor_hbm, floors), (pert_hbm, pert),
             (ids_hbm, ids)]
        )
    ]
    for copy in copies:
        copy.start()
    shape = (block_y, depth)
    deep = lax.broadcasted_iota(jnp.int32, shape, 1).astype(jnp.float32)
    lane = lax.broadcasted_iota(jnp.int32, shape, 1)
    same = lax.broadcasted_iota(jnp.int32, (block_y, block_y), 0) == (
        lax.broadcasted_iota(jnp.int32, (block_y, block_y), 1)
    )
    for copy in copies:
        copy.wait()
    for slot in range(slots):
        lines = floors[slot].astype(jnp.float32)
        for x in range(block_x):
            line = jnp.broadcast_to(lines[x:x + 1], (block_y, block_y))
            floor = jnp.sum(jnp.where(same, line, 0.0), axis=1, keepdims=True)
            primary = p[slot, x].astype(jnp.float32)
            shear = s[slot, x].astype(jnp.float32)
            square = primary * primary
            stiffness = jnp.where(deep >= floor, square + shear * shear, square)
            coef = speed_factor * stiffness / rho[slot, x].astype(jnp.float32)
            coef = coef.astype(out_ref.dtype)
            for piece in range(x, out_ref.shape[0], near):
                out_ref[piece, slot] = coef
                pert_ref[piece, slot] = pert[slot, x]
    facts = jnp.where(lane == slots, row_ref[0], 0)
    facts = jnp.where(lane == slots + 1, col_ref[0], facts)
    for slot in range(slots):
        facts = jnp.where(lane == slot, ids[slot], facts)
    facts = facts.astype(jnp.float32).astype(out_ref.dtype)
    for piece in range(out_ref.shape[0]):
        out_ref[piece, slots] = facts


def pick_tiles(slots, stride, pieces_ref, facts_ref, out_ref, facts, spots, sem):
    count = facts_ref.shape[0]
    near = out_ref.shape[0] // (APX * APY)
    copy = pltpu.make_async_copy(facts_ref, facts, sem)
    copy.start()
    base = lax.axis_index("shot") // near * near
    copy.wait()
    for piece in range(count):
        for slot in range(slots):
            spots[facts[piece, slot]] = piece * stride + slot

    def one(shot, carry):
        first = facts[base + shot, slots] * GRID_COLS + facts[base + shot, slots + 1]
        found = [
            pieces_ref[spots[first + x * GRID_COLS + y]] for x in range(APX) for y in range(APY)
        ]
        for index, tile in enumerate(found):
            out_ref[shot * APX * APY + index] = tile
        return carry

    lax.fori_loop(0, near, one, 0, unroll=2)


def pick_kernel(slots, pieces_ref, out_ref, facts_ref, facts, spots, sem):
    for piece in range(facts_ref.shape[0]):
        tile = pieces_ref[piece * (slots + 1) + slots].astype(jnp.float32)
        facts_ref[piece:piece + 1] = tile.astype(jnp.int32)[0:1]
    pick_tiles(slots, slots + 1, pieces_ref, facts_ref, out_ref, facts, spots, sem)


def pick_more_kernel(slots, facts_ref, pieces_ref, out_ref, facts, spots, sem):
    pick_tiles(slots, slots, pieces_ref, facts_ref, out_ref, facts, spots, sem)


def ends(shape):
    lane = lax.broadcasted_iota(jnp.int32, shape, 1)
    row = lax.broadcasted_iota(jnp.int32, shape, 0)
    return lane == 0, lane == shape[1] - 1, row == 0, row == shape[0] - 1


def laplace(before, here, after, masks):
    lane_0, lane_n, row_0, row_n = masks
    many = len(here)
    depth = here[0].shape[1]
    low = [jnp.where(row_0, 0.0, pltpu.roll(here[-1], 1, 0))] + here[:-1]
    high = here[1:] + [jnp.where(row_n, 0.0, pltpu.roll(here[0], LANES - 1, 0))]
    result = []
    for v in range(many):
        up = jnp.where(lane_0, 0.0, pltpu.roll(here[v], 1, 1))
        down = jnp.where(lane_n, 0.0, pltpu.roll(here[v], depth - 1, 1))
        total = (before[v] + after[v]) + (low[v] + high[v]) + (up + down)
        result.append(total - 6.0 * here[v])
    return result


def registers(ref, x):
    return [ref[x, v] for v in range(ref.shape[1])]


def strided(ref, x):
    many = ref.shape[1] // LANES
    return [ref[x, pl.ds(v, LANES, stride=many)] for v in range(many)]


def sweep(count, fields, body, unroll):
    many = fields[0].shape[1]
    zero = [jnp.zeros(fields[0].shape[2:], jnp.float32)] * many
    first = [(zero, registers(field, 0)) for field in fields]

    def step(x, carry):
        rows = [
            (before, here, registers(field, x + 1))
            for (before, here), field in zip(carry, fields)
        ]
        body(x, rows)
        return [(here, after) for _, here, after in rows]

    lax.fori_loop(0, count, step, first, unroll=unroll)


def start_kernel(prev_ref, now_ref, wave_ref, grad_ref, next_ref, flat, flat_prev, field):
    span_x, span_y, depth = now_ref.shape
    many = span_y // LANES
    masks = ends((LANES, depth))

    def load(x, carry):
        flat[x] = now_ref[x].astype(jnp.float32)
        flat_prev[x] = prev_ref[x].astype(jnp.float32)
        return carry

    lax.fori_loop(0, span_x, load, 0, unroll=2)

    def order(x, carry):
        rows = strided(flat, x)
        older = strided(flat_prev, x)
        for v in range(many):
            field[x, v] = rows[v]
            wave_ref[x, v] = rows[v]
            next_ref[x, v] = 2.0 * rows[v] - older[v]
        return carry

    lax.fori_loop(0, span_x, order, 0, unroll=2)
    for v in range(many):
        field[span_x, v] = jnp.zeros((LANES, depth), jnp.float32)

    def body(x, rows):
        grads = laplace(*rows[0], masks)
        for v in range(many):
            grad_ref[x, v] = grads[v]

    sweep(span_x, [field], body, 16)


def start(before, current):
    span_x, span_y, depth = before.shape
    many = span_y // LANES
    out = jax.ShapeDtypeStruct((span_x, many, LANES, depth), jnp.float32)
    flat = pltpu.VMEM((span_x, span_y, depth), jnp.float32)
    return pl.pallas_call(
        start_kernel,
        out_shape=(out, out, out),
        in_specs=[vmem()] * 2,
        out_specs=(vmem(),) * 3,
        scratch_shapes=[flat, flat, pltpu.VMEM((span_x + 1, many, LANES, depth), jnp.float32)],
        compiler_params=limit(8),
        cost_estimate=pl.CostEstimate(
            flops=20 * before.size, bytes_accessed=16 * before.size, transcendentals=0
        ),
        name="start",
    )(before, current)


def flatten(model_ref, flat, factor):
    block_x, _, block_y, _ = model_ref.shape

    def load(piece, carry):
        for x in range(APX):
            for y in range(APY):
                tile = model_ref[piece, x * APY + y].astype(jnp.float32)
                tile = tile if factor is None else factor * tile
                flat[x * block_x + piece, pl.ds(y * block_y, block_y)] = tile
        return carry

    lax.fori_loop(0, block_x, load, 0, unroll=4)


def close(*fields):
    for field in fields:
        for v in range(field.shape[1]):
            field[field.shape[0] - 1, v] = jnp.zeros(field.shape[2:], jnp.float32)


def background_kernel(model_ref, u_0, g_0, next_ref, kap, g_1, g_2, g_3, u_1, u_2, u_3):
    span_x, many, _, depth = u_0.shape
    masks = ends((LANES, depth))
    each = range(many)
    close(u_1, u_2, u_3)
    flatten(model_ref, kap, None)

    def forward_0(x, carry):
        kaps, grads, older = strided(kap, x), registers(g_0, x), registers(next_ref, x)
        for v in each:
            u_1[x, v] = older[v] + kaps[v] * grads[v]
        return carry

    lax.fori_loop(0, span_x, forward_0, 0, unroll=16)

    def forward(u_now, u_prev, u_next, g_now):
        def body(x, rows):
            grads = laplace(*rows[0], masks)
            kaps = None if u_next is None else strided(kap, x)
            for v in each:
                g_now[x, v] = grads[v]
                if u_next is not None:
                    u_next[x, v] = 2.0 * rows[0][1][v] - u_prev[x, v] + kaps[v] * grads[v]

        sweep(span_x, [u_now], body, 16)

    forward(u_1, u_0, u_2, g_1)
    forward(u_2, u_1, u_3, g_2)
    forward(u_3, u_2, None, g_3)


def background(model, started):
    span_x, many, _, depth = started[0].shape
    flat = (span_x, many * LANES, depth)
    plain = jax.ShapeDtypeStruct(started[0].shape, jnp.float32)
    field = pltpu.VMEM((span_x + 1, many, LANES, depth), jnp.float32)
    return pl.pallas_call(
        background_kernel,
        out_shape=(jax.ShapeDtypeStruct(flat, jnp.float32), plain, plain, plain),
        in_specs=[vmem()] * 4,
        out_specs=(vmem(),) * 4,
        scratch_shapes=[field] * 3,
        compiler_params=limit(8),
        cost_estimate=pl.CostEstimate(
            flops=50 * plain.size, bytes_accessed=32 * plain.size, transcendentals=0
        ),
        name="background",
    )(model, *started)


def wave_kernel(
    model_ref, kap, g_0, g_1, g_2, g_3, out_ref,
    con, d_0, d_1, d_2, kb_3, kb_2, kb_1, d_3, b_2, b_1, image,
):
    span_x, many, _, depth = g_0.shape
    block_x = model_ref.shape[0]
    masks = ends((LANES, depth))
    each = range(many)
    close(d_0, d_1, d_2, kb_3, kb_2, kb_1)
    flatten(model_ref, con, speed_factor)

    def forward_0(x, carry):
        cons, grads = strided(con, x), registers(g_0, x)
        for v in each:
            d_0[x, v] = cons[v] * grads[v]
        return carry

    lax.fori_loop(0, span_x, forward_0, 0, unroll=16)

    def forward(d_now, d_prev, d_next, grad, last):
        def body(x, rows):
            spread = laplace(*rows[0], masks)
            kaps, cons, grads = strided(kap, x), strided(con, x), registers(grad, x)
            for v in each:
                value = 2.0 * rows[0][1][v] + kaps[v] * spread[v] + cons[v] * grads[v]
                if d_prev is not None:
                    value = value - d_prev[x, v]
                d_next[x, v] = value
                if last:
                    image[x, v] = grads[v] * value
                    kb_3[x, v] = kaps[v] * value

        sweep(span_x, [d_now], body, 16)

    forward(d_0, None, d_1, g_1, False)
    forward(d_1, d_0, d_2, g_2, False)
    forward(d_2, d_1, d_3, g_3, True)

    def adjoint(kb, b_now, b_after, data, grad, kb_next, b_next):
        def body(x, rows):
            spread = laplace(*rows[0], masks)
            kaps = None if kb_next is None else strided(kap, x)
            for v in each:
                back = 2.0 * b_now[x, v] + spread[v] + data[x, v]
                if b_after is not None:
                    back = back - b_after[x, v]
                total = image[x, v] + grad[x, v] * back
                if kb_next is None:
                    total = (image_scale * total).astype(out_ref.dtype)
                    out_ref[x % block_x, x // block_x * many + v] = total
                else:
                    image[x, v] = total
                    b_next[x, v] = back
                    kb_next[x, v] = kaps[v] * back

        sweep(span_x, [kb], body, 16)

    adjoint(kb_3, d_3, None, d_2, g_2, kb_2, b_2)
    adjoint(kb_2, b_2, d_3, d_1, g_1, kb_1, b_1)
    adjoint(kb_1, b_1, b_2, d_0, g_0, None, None)


def wave(model, g_0, kap, *grads):
    span_x, many, _, depth = g_0.shape
    near = model.shape[0]
    flat = pltpu.VMEM((span_x, many * LANES, depth), jnp.float32)
    field = pltpu.VMEM((span_x + 1, many, LANES, depth), jnp.float32)
    plain = pltpu.VMEM((span_x, many, LANES, depth), jnp.float32)
    return pl.pallas_call(
        wave_kernel,
        out_shape=jax.ShapeDtypeStruct((near, APX * many, LANES, depth), jnp.bfloat16),
        in_specs=[vmem()] * 6,
        out_specs=vmem(),
        scratch_shapes=[flat] + [field] * 6 + [plain] * 4,
        compiler_params=limit(16),
        name="wave",
    )(model, kap, g_0, *grads)


def wave_split_depth(coef, pert, before, current):
    span_x, span_y, depth = before.shape
    block_x, _, block_y, _ = coef.shape

    def grid(model):
        model = model.reshape(block_x, APX, APY, block_y, depth).transpose(1, 0, 2, 3, 4)
        return model.reshape(span_x, span_y, depth).astype(jnp.float32)

    image = image_scale * propagate(
        grid(coef),
        speed_factor * grid(pert),
        before.astype(jnp.float32),
        current.astype(jnp.float32),
        laplace_many,
    )
    many = span_y // LANES
    image = image.reshape(APX, block_x, LANES, many, depth).transpose(1, 0, 3, 2, 4)
    return image.reshape(block_x, APX * many, LANES, depth).astype(jnp.bfloat16)


def stack_kernel(slots, facts_ref, terms_ref, out_ref, facts, total, lined, sem):
    shots, tiles = terms_ref.shape[:2]
    wide = tiles // APX
    width = LANES // APY
    grid_rows = total.shape[0] // wide
    copy = pltpu.make_async_copy(facts_ref, facts, sem)
    copy.start()
    base = lax.axis_index("shot") // shots * shots

    def clear(index, carry):
        total[index] = jnp.zeros(total.shape[1:], total.dtype)
        return carry

    lax.fori_loop(0, total.shape[0], clear, 0, unroll=8)
    copy.wait()

    def add(shot, carry):
        first = facts[base + shot, slots] * wide
        rows = pl.ds(facts[base + shot, slots + 1] * width, LANES)
        sums = [
            total[first + tile, rows] + terms_ref[shot, tile].astype(jnp.float32)
            for tile in range(tiles)
        ]
        for tile in range(tiles):
            total[first + tile, rows] = sums[tile]
        return carry

    lax.fori_loop(0, shots, add, 0, unroll=2)

    for row in range(grid_rows):
        for part in range(wide):
            for tile in range(total.shape[1] // LANES):
                at = pl.ds(tile * LANES * wide + part, LANES, stride=wide)
                lined[row, at] = total[row * wide + part, tile * LANES:(tile + 1) * LANES]

    def give(owner, carry):
        found = []
        for slot in range(slots):
            block = facts[owner, slot]
            rows = pl.ds(pl.multiple_of(block % GRID_COLS * LANES, LANES), LANES)
            found.append(lined[block // GRID_COLS, rows])
        for slot in range(slots):
            out_ref[owner, slot] = found[slot].astype(out_ref.dtype)
        return carry

    lax.fori_loop(0, out_ref.shape[0], give, 0, unroll=4)


def finish_kernel(sums_ref, out_ref):
    slots, block_x = out_ref.shape[:2]
    for x in range(block_x):
        for slot in range(slots):
            result = sums_ref[x, slot].astype(jnp.float32)
            for piece in range(x + block_x, sums_ref.shape[0], block_x):
                result = result + sums_ref[piece, slot].astype(jnp.float32)
            out_ref[slot, x] = result


def per_device(
    velocity_p,
    velocity_s,
    density,
    perturbation,
    seafloor,
    owner_ids,
    corner_x,
    corner_y,
    wave_prev,
    wave_now,
):
    slots, block_x, block_y, depth = velocity_p.shape
    count = lax.axis_size("shot")
    assert count == 2 * block_x and block_y == LANES
    patch = APX * APY
    split = lax.axis_size("depth") > 1
    if split:
        seafloor = seafloor - lax.axis_index("depth") * depth

    near = block_x
    groups = [list(range(first, first + near)) for first in range(0, count, near)]
    sent, sent_pert = pl.pallas_call(
        prepare_kernel,
        out_shape=(
            jax.ShapeDtypeStruct((count, slots + 1, block_y, depth), jnp.bfloat16),
            jax.ShapeDtypeStruct((count, slots, block_y, depth), jnp.bfloat16),
        ),
        in_specs=[smem()] * 2 + [pl.BlockSpec(memory_space=pltpu.HBM)] * 6,
        out_specs=(vmem(), vmem()),
        scratch_shapes=[
            pltpu.SMEM(owner_ids.shape, jnp.int32),
            pltpu.VMEM(seafloor.shape, jnp.int32),
            *[pltpu.VMEM(velocity_p.shape, jnp.bfloat16) for _ in range(4)],
            pltpu.SemaphoreType.DMA((6,)),
        ],
        name="prepare",
    )(
        corner_x, corner_y, owner_ids, seafloor,
        velocity_p, velocity_s, density, perturbation,
    )
    pieces = lax.all_to_all(sent, "shot", 0, 0, tiled=True)
    pieces_pert = lax.all_to_all(sent_pert, "shot", 0, 0, tiled=True)
    if not split:
        started = start(wave_prev[0], wave_now[0])
        pieces, started = lax.optimization_barrier((pieces, started))
    picked_shape = jax.ShapeDtypeStruct((near * patch, block_y, depth), jnp.bfloat16)
    pick_scratch = [
        pltpu.SMEM((count, depth), jnp.int32),
        pltpu.SMEM((count * slots,), jnp.int32),
        pltpu.SemaphoreType.DMA,
    ]
    picked, facts = pl.pallas_call(
        functools.partial(pick_kernel, slots),
        out_shape=(picked_shape, jax.ShapeDtypeStruct((count, depth), jnp.int32)),
        in_specs=[vmem()],
        out_specs=(vmem(), vmem()),
        scratch_shapes=pick_scratch,
        compiler_params=limit(3),
        name="pick",
    )(pieces.reshape(count * (slots + 1), block_y, depth))
    picked_pert = pl.pallas_call(
        functools.partial(pick_more_kernel, slots),
        out_shape=picked_shape,
        in_specs=[vmem()] * 2,
        out_specs=vmem(),
        scratch_shapes=pick_scratch,
        compiler_params=limit(3),
        name="pick_more",
    )(facts, pieces_pert.reshape(count * slots, block_y, depth))
    coef, pert = [
        lax.all_to_all(
            tiles.reshape(near, patch, block_y, depth), "shot", 0, 0,
            axis_index_groups=groups, tiled=True,
        )
        for tiles in (picked, picked_pert)
    ]

    if split:
        terms = wave_split_depth(coef, pert, wave_prev[0], wave_now[0])
    else:
        terms = wave(pert, started[1], *background(coef, started))
    terms = lax.all_to_all(terms, "shot", 0, 0, axis_index_groups=groups, tiled=True)

    grid_rows = count * slots // GRID_COLS
    wide = terms.shape[1] // APX
    sums = pl.pallas_call(
        functools.partial(stack_kernel, slots),
        out_shape=jax.ShapeDtypeStruct((count, slots, block_y, depth), jnp.bfloat16),
        in_specs=[vmem(), vmem()],
        out_specs=vmem(),
        scratch_shapes=[
            pltpu.SMEM(facts.shape, jnp.int32),
            pltpu.VMEM((grid_rows * wide, GRID_COLS * LANES // APY, depth), jnp.float32),
            pltpu.VMEM((grid_rows, GRID_COLS * block_y, depth), jnp.float32),
            pltpu.SemaphoreType.DMA,
        ],
        compiler_params=limit(3),
        name="stack",
    )(facts, terms)
    sums = lax.all_to_all(sums, "shot", 0, 0, tiled=True)
    return pl.pallas_call(
        finish_kernel,
        out_shape=jax.ShapeDtypeStruct(velocity_p.shape, jnp.float32),
        in_specs=[vmem()],
        out_specs=vmem(),
        compiler_params=limit(2),
        name="finish",
    )(sums)


def solution(mesh):
    in_specs = (
        P(("grp", "shot"), None, None, "depth"),
        P(("grp", "shot"), None, None, "depth"),
        P(("grp", "shot"), None, None, "depth"),
        P(("grp", "shot"), None, None, "depth"),
        P(("grp", "shot"), None, None),
        P(("grp", "shot")),
        P(("grp", "shot")),
        P(("grp", "shot")),
        P(("grp", "shot"), None, None, "depth"),
        P(("grp", "shot"), None, None, "depth"),
    )
    out_specs = P(("grp", "shot"), None, None, "depth")
    return jax.shard_map(
        per_device, mesh=mesh, in_specs=in_specs, out_specs=out_specs, check_vma=False
    )
```

```python
import functools

import jax
import jax.numpy as jnp
from jax import lax
from jax.experimental import pallas as pl
from jax.experimental.pallas import tpu as pltpu
from jax.sharding import PartitionSpec as P

APX = 4
APY = 4
STEPS = 4
GRID_COLS = 8
LANES = 8

speed_factor = 0.28
image_scale = 0.01


def with_halo(block, sides, width):
    for axis, dim in sides:
        count = lax.axis_size(axis)
        forward = [(i, i + 1) for i in range(count - 1)]
        backward = [(target, source) for source, target in forward]
        low = lax.ppermute(
            lax.slice_in_dim(block, block.shape[dim] - width, None, axis=dim), axis, forward
        )
        high = lax.ppermute(lax.slice_in_dim(block, 0, width, axis=dim), axis, backward)
        block = jnp.concatenate([low, block, high], axis=dim)
    return block


def laplace_many(fields):
    stacked = jnp.stack(fields)
    padded = with_halo(stacked.astype(jnp.bfloat16), (("depth", 3),), 1).astype(stacked.dtype)
    padded = jnp.pad(padded, ((0, 0), (1, 1), (1, 1), (0, 0)))
    beside = padded[:, 2:, 1:-1, 1:-1] + padded[:, :-2, 1:-1, 1:-1]
    beside = beside + padded[:, 1:-1, 2:, 1:-1] + padded[:, 1:-1, :-2, 1:-1]
    beside = beside + padded[:, 1:-1, 1:-1, 2:] + padded[:, 1:-1, 1:-1, :-2]
    result = beside - 6.0 * stacked
    return [result[index] for index in range(len(fields))]


def propagate(kappa, contrast, before, current, apply):
    grads = []
    datas = []
    grad_now = apply([current])[0]
    delta_prev = jnp.zeros_like(current)
    delta_now = contrast * grad_now
    grads.append(grad_now)
    datas.append(delta_now)
    before, current = (current, 2.0 * current - before + kappa * grad_now)
    for step in range(1, STEPS):
        grad_now, spread = apply([current, delta_now])
        delta_next = 2.0 * delta_now - delta_prev + kappa * spread + contrast * grad_now
        grads.append(grad_now)
        datas.append(delta_next)
        delta_prev, delta_now = (delta_now, delta_next)
        if step + 1 < STEPS:
            before, current = (current, 2.0 * current - before + kappa * grad_now)
    back = datas[STEPS - 1]
    back_after = jnp.zeros_like(back)
    image = grads[STEPS - 1] * back
    for step in range(STEPS - 2, -1, -1):
        spread = apply([kappa * back])
        back_new = 2.0 * back - back_after + spread[0] + datas[step]
        image = image + grads[step] * back_new
        back_after, back = (back, back_new)
    return image


def limit(mebibytes):
    return pltpu.CompilerParams(vmem_limit_bytes=mebibytes * 2**20)


def vmem():
    return pl.BlockSpec(memory_space=pltpu.VMEM)


def smem():
    return pl.BlockSpec(memory_space=pltpu.SMEM)


def prepare_kernel(
    row_ref, col_ref, ids_hbm, floor_hbm, p_hbm, s_hbm, rho_hbm, pert_hbm, out_ref,
    ids, floors, p, s, rho, pert, sems,
):
    slots, block_x, block_y, depth = p.shape
    near = block_x
    copies = [
        pltpu.make_async_copy(source, target, sems.at[index])
        for index, (source, target) in enumerate(
            [(p_hbm, p), (s_hbm, s), (rho_hbm, rho), (floor_hbm, floors), (pert_hbm, pert),
             (ids_hbm, ids)]
        )
    ]
    for copy in copies:
        copy.start()
    shape = (block_y, depth)
    deep = lax.broadcasted_iota(jnp.int32, shape, 1).astype(jnp.float32)
    lane = lax.broadcasted_iota(jnp.int32, shape, 1)
    same = lax.broadcasted_iota(jnp.int32, (block_y, block_y), 0) == (
        lax.broadcasted_iota(jnp.int32, (block_y, block_y), 1)
    )
    for copy in copies:
        copy.wait()
    for slot in range(slots):
        lines = floors[slot].astype(jnp.float32)
        for x in range(block_x):
            line = jnp.broadcast_to(lines[x:x + 1], (block_y, block_y))
            floor = jnp.sum(jnp.where(same, line, 0.0), axis=1, keepdims=True)
            primary = p[slot, x].astype(jnp.float32)
            shear = s[slot, x].astype(jnp.float32)
            square = primary * primary
            stiffness = jnp.where(deep >= floor, square + shear * shear, square)
            coef = speed_factor * stiffness / rho[slot, x].astype(jnp.float32)
            coef = coef.astype(out_ref.dtype)
            for piece in range(x, out_ref.shape[0], near):
                out_ref[piece, 2 * slot] = coef
                out_ref[piece, 2 * slot + 1] = pert[slot, x]
    facts = jnp.where(lane == slots, row_ref[0], 0)
    facts = jnp.where(lane == slots + 1, col_ref[0], facts)
    for slot in range(slots):
        facts = jnp.where(lane == slot, ids[slot], facts)
    facts = facts.astype(jnp.float32).astype(out_ref.dtype)
    for piece in range(out_ref.shape[0]):
        out_ref[piece, 2 * slots] = facts


def pick_kernel(slots, near, pieces_ref, *refs):
    out_refs = refs[:near]
    facts_ref, facts, spots, sem = refs[near:]
    count = facts_ref.shape[0]
    tiles = 2 * slots + 1
    for piece in range(count):
        tile = pieces_ref[piece * tiles + 2 * slots].astype(jnp.float32)
        facts_ref[piece:piece + 1] = tile.astype(jnp.int32)[0:1]
    copy = pltpu.make_async_copy(facts_ref, facts, sem)
    copy.start()
    me = lax.axis_index("shot")
    copy.wait()
    for piece in range(count):
        for slot in range(slots):
            spots[facts[piece, slot]] = piece * tiles + 2 * slot
    for k, out_ref in enumerate(out_refs):
        shot = me ^ k
        first = facts[shot, slots] * GRID_COLS + facts[shot, slots + 1]
        for x in range(APX):
            found = []
            for y in range(APY):
                spot = spots[first + x * GRID_COLS + y]
                found += [pieces_ref[spot], pieces_ref[spot + 1]]
            for index, tile in enumerate(found):
                out_ref[x * APY * 2 + index] = tile


def ends(shape):
    lane = lax.broadcasted_iota(jnp.int32, shape, 1)
    row = lax.broadcasted_iota(jnp.int32, shape, 0)
    return lane == 0, lane == shape[1] - 1, row == 0, row == shape[0] - 1


def laplace(before, here, after, masks):
    lane_0, lane_n, row_0, row_n = masks
    many = len(here)
    depth = here[0].shape[1]
    low = [jnp.where(row_0, 0.0, pltpu.roll(here[-1], 1, 0))] + here[:-1]
    high = here[1:] + [jnp.where(row_n, 0.0, pltpu.roll(here[0], LANES - 1, 0))]
    result = []
    for v in range(many):
        up = jnp.where(lane_0, 0.0, pltpu.roll(here[v], 1, 1))
        down = jnp.where(lane_n, 0.0, pltpu.roll(here[v], depth - 1, 1))
        total = (before[v] + after[v]) + (low[v] + high[v]) + (up + down)
        result.append(total - 6.0 * here[v])
    return result


def registers(ref, x):
    return [ref[x, v] for v in range(ref.shape[1])]


def strided(ref, x):
    many = ref.shape[1] // LANES
    return [ref[x, pl.ds(v, LANES, stride=many)] for v in range(many)]


def sweep(count, fields, body, unroll):
    many = fields[0].shape[1]
    zero = [jnp.zeros(fields[0].shape[2:], jnp.float32)] * many
    first = [(zero, registers(field, 0)) for field in fields]

    def step(x, carry):
        rows = [
            (before, here, registers(field, x + 1))
            for (before, here), field in zip(carry, fields)
        ]
        body(x, rows)
        return [(here, after) for _, here, after in rows]

    lax.fori_loop(0, count, step, first, unroll=unroll)


def start_kernel(prev_ref, now_ref, wave_ref, grad_ref, next_ref, flat, flat_prev, field):
    span_x, span_y, depth = now_ref.shape
    many = span_y // LANES
    masks = ends((LANES, depth))

    def load(x, carry):
        flat[x] = now_ref[x].astype(jnp.float32)
        flat_prev[x] = prev_ref[x].astype(jnp.float32)
        return carry

    lax.fori_loop(0, span_x, load, 0, unroll=2)

    def order(x, carry):
        rows = strided(flat, x)
        older = strided(flat_prev, x)
        for v in range(many):
            field[x, v] = rows[v]
            wave_ref[x, v] = rows[v]
            next_ref[x, v] = 2.0 * rows[v] - older[v]
        return carry

    lax.fori_loop(0, span_x, order, 0, unroll=2)
    for v in range(many):
        field[span_x, v] = jnp.zeros((LANES, depth), jnp.float32)

    def body(x, rows):
        grads = laplace(*rows[0], masks)
        for v in range(many):
            grad_ref[x, v] = grads[v]

    sweep(span_x, [field], body, 16)


def start(before, current):
    span_x, span_y, depth = before.shape
    many = span_y // LANES
    out = jax.ShapeDtypeStruct((span_x, many, LANES, depth), jnp.float32)
    flat = pltpu.VMEM((span_x, span_y, depth), jnp.float32)
    return pl.pallas_call(
        start_kernel,
        out_shape=(out, out, out),
        in_specs=[vmem()] * 2,
        out_specs=(vmem(),) * 3,
        scratch_shapes=[flat, flat, pltpu.VMEM((span_x + 1, many, LANES, depth), jnp.float32)],
        compiler_params=limit(8),
        cost_estimate=pl.CostEstimate(
            flops=20 * before.size, bytes_accessed=16 * before.size, transcendentals=0
        ),
        name="start",
    )(before, current)


def wave_kernel(near, *refs):
    model_refs = refs[:near]
    u_0, g_0, next_ref = refs[near:near + 3]
    out_refs = refs[near + 3:2 * near + 3]
    kap, con, u_1, u_2, u_3, d_0, d_1, d_2, kb_3, kb_2, kb_1 = refs[2 * near + 3:2 * near + 14]
    g_1, g_2, d_3, b_2, b_1, image, result = refs[2 * near + 14:]
    span_x, many = u_0.shape[:2]
    depth = u_0.shape[3]
    block_y = model_refs[0].shape[1]
    block_x = span_x // APX
    place = lax.axis_index("shot") % near
    masks = ends((LANES, depth))
    each = range(many)
    for field in (u_1, u_2, u_3, d_0, d_1, d_2, kb_3, kb_2, kb_1):
        for v in each:
            field[span_x, v] = jnp.zeros((LANES, depth), jnp.float32)

    for k, model_ref in enumerate(model_refs):
        for x in range(APX):
            at = x * block_x + (place ^ k)
            for y in range(APY):
                rows = pl.ds(y * block_y, block_y)
                tile = 2 * (x * APY + y)
                kap[at, rows] = model_ref[tile].astype(jnp.float32)
                con[at, rows] = speed_factor * model_ref[tile + 1].astype(jnp.float32)

    def forward_0(x, carry):
        kaps, cons, grads = strided(kap, x), strided(con, x), registers(g_0, x)
        older = registers(next_ref, x)
        for v in each:
            d_0[x, v] = cons[v] * grads[v]
            u_1[x, v] = older[v] + kaps[v] * grads[v]
        return carry

    lax.fori_loop(0, span_x, forward_0, 0, unroll=16)

    def forward(u_now, u_prev, d_now, d_prev, u_next, d_next, g_now):
        def body(x, rows):
            waves, deltas = rows
            grads = laplace(*waves, masks)
            spread = laplace(*deltas, masks)
            kaps, cons = strided(kap, x), strided(con, x)
            for v in each:
                value = 2.0 * deltas[1][v] + kaps[v] * spread[v] + cons[v] * grads[v]
                if d_prev is not None:
                    value = value - d_prev[x, v]
                d_next[x, v] = value
                if u_next is None:
                    image[x, v] = grads[v] * value
                    kb_3[x, v] = kaps[v] * value
                else:
                    g_now[x, v] = grads[v]
                    u_next[x, v] = 2.0 * waves[1][v] - u_prev[x, v] + kaps[v] * grads[v]

        sweep(span_x, [u_now, d_now], body, 16)

    forward(u_1, u_0, d_0, None, u_2, d_1, g_1)
    forward(u_2, u_1, d_1, d_0, u_3, d_2, g_2)
    forward(u_3, u_2, d_2, d_1, None, d_3, None)

    def adjoint(kb, b_now, b_after, data, grad, kb_next, b_next):
        def body(x, rows):
            spread = laplace(*rows[0], masks)
            kaps = None if kb_next is None else strided(kap, x)
            for v in each:
                back = 2.0 * b_now[x, v] + spread[v] + data[x, v]
                if b_after is not None:
                    back = back - b_after[x, v]
                total = image[x, v] + grad[x, v] * back
                if kb_next is None:
                    total = (image_scale * total).astype(result.dtype)
                    result[x % block_x, x // block_x * many + v] = total
                else:
                    image[x, v] = total
                    b_next[x, v] = back
                    kb_next[x, v] = kaps[v] * back

        sweep(span_x, [kb], body, 16)

    adjoint(kb_3, d_3, None, d_2, g_2, kb_2, b_2)
    adjoint(kb_2, b_2, d_3, d_1, g_1, kb_1, b_1)
    adjoint(kb_1, b_1, b_2, d_0, g_0, None, None)
    for k, out_ref in enumerate(out_refs):
        out_ref[...] = result[place ^ k]


def wave(models, started):
    span_x, many, _, depth = started[0].shape
    near = len(models)
    flat = pltpu.VMEM((span_x, many * LANES, depth), jnp.float32)
    field = pltpu.VMEM((span_x + 1, many, LANES, depth), jnp.float32)
    plain = pltpu.VMEM((span_x, many, LANES, depth), jnp.float32)
    out = (APX * many, LANES, depth)
    return pl.pallas_call(
        functools.partial(wave_kernel, near),
        out_shape=(jax.ShapeDtypeStruct(out, jnp.bfloat16),) * near,
        in_specs=[vmem()] * (near + 3),
        out_specs=(vmem(),) * near,
        scratch_shapes=[flat] * 2 + [field] * 9 + [plain] * 6
        + [pltpu.VMEM((near,) + out, jnp.bfloat16)],
        compiler_params=limit(20),
        name="wave",
    )(*models, *started)


def wave_split_depth(models, before, current):
    near = len(models)
    order = (lax.axis_index("shot") % near) ^ jnp.arange(near)
    model = jnp.stack(models)[order]
    span_x, span_y, depth = before.shape
    block_x, tiles, block_y, _ = model.shape
    grids = model.reshape(block_x, APX, APY, 2, block_y, depth).transpose(3, 1, 0, 2, 4, 5)
    grids = grids.reshape(2, span_x, span_y, depth).astype(jnp.float32)
    image = image_scale * propagate(
        grids[0],
        speed_factor * grids[1],
        before.astype(jnp.float32),
        current.astype(jnp.float32),
        laplace_many,
    )
    many = span_y // LANES
    image = image.reshape(APX, block_x, LANES, many, depth).transpose(1, 0, 3, 2, 4)
    image = image.reshape(near, APX * many, LANES, depth).astype(jnp.bfloat16)[order]
    return [image[k] for k in range(near)]


def stack_kernel(slots, near, facts_ref, *refs):
    terms_refs = refs[:near]
    out_ref, facts, total, lined, sem = refs[near:]
    tiles = terms_refs[0].shape[0]
    wide = tiles // APX
    width = LANES // APY
    grid_rows = total.shape[0] // wide
    copy = pltpu.make_async_copy(facts_ref, facts, sem)
    copy.start()
    me = lax.axis_index("shot")

    def clear(index, carry):
        total[index] = jnp.zeros(total.shape[1:], total.dtype)
        return carry

    lax.fori_loop(0, total.shape[0], clear, 0, unroll=8)
    copy.wait()

    for k, terms_ref in enumerate(terms_refs):
        first = facts[me ^ k, slots] * wide
        rows = pl.ds(facts[me ^ k, slots + 1] * width, LANES)
        sums = [
            total[first + tile, rows] + terms_ref[tile].astype(jnp.float32)
            for tile in range(tiles)
        ]
        for tile in range(tiles):
            total[first + tile, rows] = sums[tile]

    for row in range(grid_rows):
        for part in range(wide):
            for tile in range(total.shape[1] // LANES):
                at = pl.ds(tile * LANES * wide + part, LANES, stride=wide)
                lined[row, at] = total[row * wide + part, tile * LANES:(tile + 1) * LANES]

    def give(owner, carry):
        found = []
        for slot in range(slots):
            block = facts[owner, slot]
            rows = pl.ds(pl.multiple_of(block % GRID_COLS * LANES, LANES), LANES)
            found.append(lined[block // GRID_COLS, rows])
        for slot in range(slots):
            out_ref[owner, slot] = found[slot].astype(out_ref.dtype)
        return carry

    lax.fori_loop(0, out_ref.shape[0], give, 0, unroll=4)


def finish_kernel(sums_ref, out_ref):
    slots, block_x = out_ref.shape[:2]
    for x in range(block_x):
        for slot in range(slots):
            result = sums_ref[x, slot].astype(jnp.float32)
            for piece in range(x + block_x, sums_ref.shape[0], block_x):
                result = result + sums_ref[piece, slot].astype(jnp.float32)
            out_ref[slot, x] = result


def per_device(
    velocity_p,
    velocity_s,
    density,
    perturbation,
    seafloor,
    owner_ids,
    corner_x,
    corner_y,
    wave_prev,
    wave_now,
):
    slots, block_x, block_y, depth = velocity_p.shape
    count = lax.axis_size("shot")
    assert count == 2 * block_x and block_y == LANES
    patch = APX * APY
    split = lax.axis_size("depth") > 1
    if split:
        seafloor = seafloor - lax.axis_index("depth") * depth

    near = block_x
    assert count % near == 0 and near & (near - 1) == 0

    def swap(values):
        return [
            lax.ppermute(value, "shot", [(i, i ^ k) for i in range(count)]) if k else value
            for k, value in enumerate(values)
        ]

    sent = pl.pallas_call(
        prepare_kernel,
        out_shape=jax.ShapeDtypeStruct((count, 2 * slots + 1, block_y, depth), jnp.bfloat16),
        in_specs=[smem()] * 2 + [pl.BlockSpec(memory_space=pltpu.HBM)] * 6,
        out_specs=vmem(),
        scratch_shapes=[
            pltpu.SMEM(owner_ids.shape, jnp.int32),
            pltpu.VMEM(seafloor.shape, jnp.int32),
            *[pltpu.VMEM(velocity_p.shape, jnp.bfloat16) for _ in range(4)],
            pltpu.SemaphoreType.DMA((6,)),
        ],
        name="prepare",
    )(
        corner_x, corner_y, owner_ids, seafloor,
        velocity_p, velocity_s, density, perturbation,
    )
    pieces = lax.all_to_all(sent, "shot", 0, 0, tiled=True)

    if not split:
        started = start(wave_prev[0], wave_now[0])
        pieces, started = lax.optimization_barrier((pieces, started))
    *picked, facts = pl.pallas_call(
        functools.partial(pick_kernel, slots, near),
        out_shape=(
            *[jax.ShapeDtypeStruct((patch * 2, block_y, depth), jnp.bfloat16)] * near,
            jax.ShapeDtypeStruct((count, depth), jnp.int32),
        ),
        in_specs=[vmem()],
        out_specs=(vmem(),) * (near + 1),
        scratch_shapes=[
            pltpu.SMEM((count, depth), jnp.int32),
            pltpu.SMEM((count * slots,), jnp.int32),
            pltpu.SemaphoreType.DMA,
        ],
        compiler_params=limit(3),
        name="pick",
    )(pieces.reshape(count * (2 * slots + 1), block_y, depth))
    models = swap(picked)

    if split:
        terms = wave_split_depth(models, wave_prev[0], wave_now[0])
    else:
        terms = wave(models, started)
    terms = swap(terms)

    grid_rows = count * slots // GRID_COLS
    wide = terms[0].shape[0] // APX
    sums = pl.pallas_call(
        functools.partial(stack_kernel, slots, near),
        out_shape=jax.ShapeDtypeStruct((count, slots, block_y, depth), jnp.bfloat16),
        in_specs=[vmem()] * (near + 1),
        out_specs=vmem(),
        scratch_shapes=[
            pltpu.SMEM(facts.shape, jnp.int32),
            pltpu.VMEM((grid_rows * wide, GRID_COLS * LANES // APY, depth), jnp.float32),
            pltpu.VMEM((grid_rows, GRID_COLS * block_y, depth), jnp.float32),
            pltpu.SemaphoreType.DMA,
        ],
        compiler_params=limit(3),
        name="stack",
    )(facts, *terms)
    sums = lax.all_to_all(sums, "shot", 0, 0, tiled=True)
    return pl.pallas_call(
        finish_kernel,
        out_shape=jax.ShapeDtypeStruct(velocity_p.shape, jnp.float32),
        in_specs=[vmem()],
        out_specs=vmem(),
        compiler_params=limit(2),
        name="finish",
    )(sums)


def solution(mesh):
    in_specs = (
        P(("grp", "shot"), None, None, "depth"),
        P(("grp", "shot"), None, None, "depth"),
        P(("grp", "shot"), None, None, "depth"),
        P(("grp", "shot"), None, None, "depth"),
        P(("grp", "shot"), None, None),
        P(("grp", "shot")),
        P(("grp", "shot")),
        P(("grp", "shot")),
        P(("grp", "shot"), None, None, "depth"),
        P(("grp", "shot"), None, None, "depth"),
    )
    out_specs = P(("grp", "shot"), None, None, "depth")
    return jax.shard_map(
        per_device, mesh=mesh, in_specs=in_specs, out_specs=out_specs, check_vma=False
    )
```

```python
import functools

import jax
import jax.numpy as jnp
from jax import lax
from jax.experimental import pallas as pl
from jax.experimental.pallas import tpu as pltpu
from jax.sharding import PartitionSpec as P

APX = 4
APY = 4
STEPS = 4
GRID_COLS = 8
LANES = 8

speed_factor = 0.28
image_scale = 0.01


def with_halo(block, sides, width):
    for axis, dim in sides:
        count = lax.axis_size(axis)
        forward = [(i, i + 1) for i in range(count - 1)]
        backward = [(target, source) for source, target in forward]
        low = lax.ppermute(
            lax.slice_in_dim(block, block.shape[dim] - width, None, axis=dim), axis, forward
        )
        high = lax.ppermute(lax.slice_in_dim(block, 0, width, axis=dim), axis, backward)
        block = jnp.concatenate([low, block, high], axis=dim)
    return block


def laplace_many(fields):
    stacked = jnp.stack(fields)
    padded = with_halo(stacked.astype(jnp.bfloat16), (("depth", 3),), 1).astype(stacked.dtype)
    padded = jnp.pad(padded, ((0, 0), (1, 1), (1, 1), (0, 0)))
    beside = padded[:, 2:, 1:-1, 1:-1] + padded[:, :-2, 1:-1, 1:-1]
    beside = beside + padded[:, 1:-1, 2:, 1:-1] + padded[:, 1:-1, :-2, 1:-1]
    beside = beside + padded[:, 1:-1, 1:-1, 2:] + padded[:, 1:-1, 1:-1, :-2]
    result = beside - 6.0 * stacked
    return [result[index] for index in range(len(fields))]


def propagate(kappa, contrast, before, current, apply):
    grads = []
    datas = []
    grad_now = apply([current])[0]
    delta_prev = jnp.zeros_like(current)
    delta_now = contrast * grad_now
    grads.append(grad_now)
    datas.append(delta_now)
    before, current = (current, 2.0 * current - before + kappa * grad_now)
    for step in range(1, STEPS):
        grad_now, spread = apply([current, delta_now])
        delta_next = 2.0 * delta_now - delta_prev + kappa * spread + contrast * grad_now
        grads.append(grad_now)
        datas.append(delta_next)
        delta_prev, delta_now = (delta_now, delta_next)
        if step + 1 < STEPS:
            before, current = (current, 2.0 * current - before + kappa * grad_now)
    back = datas[STEPS - 1]
    back_after = jnp.zeros_like(back)
    image = grads[STEPS - 1] * back
    for step in range(STEPS - 2, -1, -1):
        spread = apply([kappa * back])
        back_new = 2.0 * back - back_after + spread[0] + datas[step]
        image = image + grads[step] * back_new
        back_after, back = (back, back_new)
    return image


def limit(mebibytes):
    return pltpu.CompilerParams(vmem_limit_bytes=mebibytes * 2**20)


def chip_place(near):
    return lax.axis_index("shot") // 2 % near


def vmem():
    return pl.BlockSpec(memory_space=pltpu.VMEM)


def smem():
    return pl.BlockSpec(memory_space=pltpu.SMEM)


def prepare_kernel(near, row_ref, col_ref, *refs):
    ids_hbm, floor_hbm, p_hbm, s_hbm, rho_hbm, pert_hbm = refs[:6]
    out_refs = refs[6:6 + near]
    ids, floors, p, s, rho, pert, coef, sems = refs[6 + near:]
    slots, block_x, block_y, depth = p.shape
    copies = [
        pltpu.make_async_copy(source, target, sems.at[index])
        for index, (source, target) in enumerate(
            [(p_hbm, p), (s_hbm, s), (rho_hbm, rho), (floor_hbm, floors), (pert_hbm, pert),
             (ids_hbm, ids)]
        )
    ]
    for copy in copies:
        copy.start()
    shape = (block_y, depth)
    deep = lax.broadcasted_iota(jnp.int32, shape, 1).astype(jnp.float32)
    lane = lax.broadcasted_iota(jnp.int32, shape, 1)
    same = lax.broadcasted_iota(jnp.int32, (block_y, block_y), 0) == (
        lax.broadcasted_iota(jnp.int32, (block_y, block_y), 1)
    )
    place = chip_place(near)
    for copy in copies:
        copy.wait()
    for slot in range(slots):
        lines = floors[slot].astype(jnp.float32)
        for x in range(block_x):
            line = jnp.broadcast_to(lines[x:x + 1], (block_y, block_y))
            floor = jnp.sum(jnp.where(same, line, 0.0), axis=1, keepdims=True)
            primary = p[slot, x].astype(jnp.float32)
            shear = s[slot, x].astype(jnp.float32)
            square = primary * primary
            stiffness = jnp.where(deep >= floor, square + shear * shear, square)
            value = speed_factor * stiffness / rho[slot, x].astype(jnp.float32)
            coef[slot, x] = value.astype(coef.dtype)
    facts = jnp.where(lane == slots, row_ref[0], 0)
    facts = jnp.where(lane == slots + 1, col_ref[0], facts)
    for slot in range(slots):
        facts = jnp.where(lane == slot, ids[slot], facts)
    facts = facts.astype(jnp.float32).astype(coef.dtype)
    for j, out_ref in enumerate(out_refs):
        for slot in range(slots):
            for r in range(2):
                x = 2 * (place ^ j) + r
                out_ref[4 * slot + 2 * r] = coef[slot, x]
                out_ref[4 * slot + 2 * r + 1] = pert[slot, x]
        out_ref[4 * slots] = facts


def pick_kernel(slots, near, count, *refs):
    piece_refs = refs[:count]
    out_refs = refs[count:count + near]
    facts_ref, facts, spots, pieces, sem = refs[count + near:]
    tiles = 4 * slots + 1
    for t, piece_ref in enumerate(piece_refs):
        tile = piece_ref[tiles - 1].astype(jnp.float32)
        facts_ref[t:t + 1] = tile.astype(jnp.int32)[0:1]
    copy = pltpu.make_async_copy(facts_ref, facts, sem)
    copy.start()
    for t, piece_ref in enumerate(piece_refs):
        pieces[t * tiles:(t + 1) * tiles] = piece_ref[...]
    copy.wait()
    for t in range(count):
        for slot in range(slots):
            spots[facts[t, slot]] = t * tiles + 4 * slot
    for k, out_ref in enumerate(out_refs):
        first = facts[2 * k, slots] * GRID_COLS + facts[2 * k, slots + 1]
        for x in range(APX):
            found = []
            for y in range(APY):
                spot = spots[first + x * GRID_COLS + y]
                found += [pieces[spot + tile] for tile in range(4)]
            for index, tile in enumerate(found):
                out_ref[x * APY * 4 + index] = tile


def ends(shape):
    lane = lax.broadcasted_iota(jnp.int32, shape, 1)
    row = lax.broadcasted_iota(jnp.int32, shape, 0)
    return lane == 0, lane == shape[1] - 1, row == 0, row == shape[0] - 1


def laplace(before, here, after, masks):
    lane_0, lane_n, row_0, row_n = masks
    many = len(here)
    depth = here[0].shape[1]
    low = [jnp.where(row_0, 0.0, pltpu.roll(here[-1], 1, 0))] + here[:-1]
    high = here[1:] + [jnp.where(row_n, 0.0, pltpu.roll(here[0], LANES - 1, 0))]
    result = []
    for v in range(many):
        up = jnp.where(lane_0, 0.0, pltpu.roll(here[v], 1, 1))
        down = jnp.where(lane_n, 0.0, pltpu.roll(here[v], depth - 1, 1))
        total = (before[v] + after[v]) + (low[v] + high[v]) + (up + down)
        result.append(total - 6.0 * here[v])
    return result


def registers(ref, x):
    return [ref[x, v] for v in range(ref.shape[1])]


def strided(ref, x):
    many = ref.shape[1] // LANES
    return [ref[x, pl.ds(v, LANES, stride=many)] for v in range(many)]


def sweep(count, fields, body, unroll):
    many = fields[0].shape[1]
    zero = [jnp.zeros(fields[0].shape[2:], jnp.float32)] * many
    first = [(zero, registers(field, 0)) for field in fields]

    def step(x, carry):
        rows = [
            (before, here, registers(field, x + 1))
            for (before, here), field in zip(carry, fields)
        ]
        body(x, rows)
        return [(here, after) for _, here, after in rows]

    lax.fori_loop(0, count, step, first, unroll=unroll)


def start_kernel(prev_ref, now_ref, wave_ref, grad_ref, next_ref, flat, flat_prev, field):
    span_x, span_y, depth = now_ref.shape
    many = span_y // LANES
    masks = ends((LANES, depth))

    def load(x, carry):
        flat[x] = now_ref[x].astype(jnp.float32)
        flat_prev[x] = prev_ref[x].astype(jnp.float32)
        return carry

    lax.fori_loop(0, span_x, load, 0, unroll=2)

    def order(x, carry):
        rows = strided(flat, x)
        older = strided(flat_prev, x)
        for v in range(many):
            field[x, v] = rows[v]
            wave_ref[x, v] = rows[v]
            next_ref[x, v] = 2.0 * rows[v] - older[v]
        return carry

    lax.fori_loop(0, span_x, order, 0, unroll=2)
    for v in range(many):
        field[span_x, v] = jnp.zeros((LANES, depth), jnp.float32)

    def body(x, rows):
        grads = laplace(*rows[0], masks)
        for v in range(many):
            grad_ref[x, v] = grads[v]

    sweep(span_x, [field], body, 16)


def start(before, current):
    span_x, span_y, depth = before.shape
    many = span_y // LANES
    out = jax.ShapeDtypeStruct((span_x, many, LANES, depth), jnp.float32)
    flat = pltpu.VMEM((span_x, span_y, depth), jnp.float32)
    return pl.pallas_call(
        start_kernel,
        out_shape=(out, out, out),
        in_specs=[vmem()] * 2,
        out_specs=(vmem(),) * 3,
        scratch_shapes=[flat, flat, pltpu.VMEM((span_x + 1, many, LANES, depth), jnp.float32)],
        compiler_params=limit(8),
        cost_estimate=pl.CostEstimate(
            flops=20 * before.size, bytes_accessed=16 * before.size, transcendentals=0
        ),
        name="start",
    )(before, current)


def wave_kernel(near, *refs):
    model_refs = refs[:near]
    u_0, g_0, next_ref = refs[near:near + 3]
    out_refs = refs[near + 3:2 * near + 3]
    kap, con, u_1, u_2, u_3, d_0, d_1, d_2, kb_3, kb_2, kb_1 = refs[2 * near + 3:2 * near + 14]
    g_1, g_2, d_3, b_2, b_1, image, result = refs[2 * near + 14:]
    span_x, many = u_0.shape[:2]
    depth = u_0.shape[3]
    block_y = model_refs[0].shape[1]
    block_x = span_x // APX
    place = chip_place(near)
    masks = ends((LANES, depth))
    each = range(many)
    for field in (u_1, u_2, u_3, d_0, d_1, d_2, kb_3, kb_2, kb_1):
        for v in each:
            field[span_x, v] = jnp.zeros((LANES, depth), jnp.float32)

    for k, model_ref in enumerate(model_refs):
        for x in range(APX):
            for y in range(APY):
                rows = pl.ds(y * block_y, block_y)
                for r in range(2):
                    at = x * block_x + 2 * (place ^ k) + r
                    tile = 4 * (x * APY + y) + 2 * r
                    kap[at, rows] = model_ref[tile].astype(jnp.float32)
                    con[at, rows] = speed_factor * model_ref[tile + 1].astype(jnp.float32)

    def forward_0(x, carry):
        kaps, cons, grads = strided(kap, x), strided(con, x), registers(g_0, x)
        older = registers(next_ref, x)
        for v in each:
            d_0[x, v] = cons[v] * grads[v]
            u_1[x, v] = older[v] + kaps[v] * grads[v]
        return carry

    lax.fori_loop(0, span_x, forward_0, 0, unroll=16)

    def forward(u_now, u_prev, d_now, d_prev, u_next, d_next, g_now):
        def body(x, rows):
            waves, deltas = rows
            grads = laplace(*waves, masks)
            spread = laplace(*deltas, masks)
            kaps, cons = strided(kap, x), strided(con, x)
            for v in each:
                value = 2.0 * deltas[1][v] + kaps[v] * spread[v] + cons[v] * grads[v]
                if d_prev is not None:
                    value = value - d_prev[x, v]
                d_next[x, v] = value
                if u_next is None:
                    image[x, v] = grads[v] * value
                    kb_3[x, v] = kaps[v] * value
                else:
                    g_now[x, v] = grads[v]
                    u_next[x, v] = 2.0 * waves[1][v] - u_prev[x, v] + kaps[v] * grads[v]

        sweep(span_x, [u_now, d_now], body, 16)

    forward(u_1, u_0, d_0, None, u_2, d_1, g_1)
    forward(u_2, u_1, d_1, d_0, u_3, d_2, g_2)
    forward(u_3, u_2, d_2, d_1, None, d_3, None)

    def adjoint(kb, b_now, b_after, data, grad, kb_next, b_next):
        def body(x, rows):
            spread = laplace(*rows[0], masks)
            kaps = None if kb_next is None else strided(kap, x)
            for v in each:
                back = 2.0 * b_now[x, v] + spread[v] + data[x, v]
                if b_after is not None:
                    back = back - b_after[x, v]
                total = image[x, v] + grad[x, v] * back
                if kb_next is None:
                    total = (image_scale * total).astype(result.dtype)
                    result[x % block_x // 2, (x % 2 * APX + x // block_x) * many + v] = total
                else:
                    image[x, v] = total
                    b_next[x, v] = back
                    kb_next[x, v] = kaps[v] * back

        sweep(span_x, [kb], body, 16)

    adjoint(kb_3, d_3, None, d_2, g_2, kb_2, b_2)
    adjoint(kb_2, b_2, d_3, d_1, g_1, kb_1, b_1)
    adjoint(kb_1, b_1, b_2, d_0, g_0, None, None)
    for k, out_ref in enumerate(out_refs):
        out_ref[...] = result[place ^ k]


def wave(models, started):
    span_x, many, _, depth = started[0].shape
    near = len(models)
    flat = pltpu.VMEM((span_x, many * LANES, depth), jnp.float32)
    field = pltpu.VMEM((span_x + 1, many, LANES, depth), jnp.float32)
    plain = pltpu.VMEM((span_x, many, LANES, depth), jnp.float32)
    out = (2 * APX * many, LANES, depth)
    return pl.pallas_call(
        functools.partial(wave_kernel, near),
        out_shape=(jax.ShapeDtypeStruct(out, jnp.bfloat16),) * near,
        in_specs=[vmem()] * (near + 3),
        out_specs=(vmem(),) * near,
        scratch_shapes=[flat] * 2 + [field] * 9 + [plain] * 6
        + [pltpu.VMEM((near,) + out, jnp.bfloat16)],
        compiler_params=limit(20),
        name="wave",
    )(*models, *started)


def wave_split_depth(models, before, current):
    near = len(models)
    order = chip_place(near) ^ jnp.arange(near)
    model = jnp.stack(models)[order]
    span_x, span_y, depth = before.shape
    block_x, block_y = 2 * near, model.shape[2]
    grids = model.reshape(near, APX, APY, 2, 2, block_y, depth).transpose(4, 1, 0, 3, 2, 5, 6)
    grids = grids.reshape(2, span_x, span_y, depth).astype(jnp.float32)
    image = image_scale * propagate(
        grids[0],
        speed_factor * grids[1],
        before.astype(jnp.float32),
        current.astype(jnp.float32),
        laplace_many,
    )
    many = span_y // LANES
    image = image.reshape(APX, near, 2, LANES, many, depth).transpose(1, 2, 0, 4, 3, 5)
    image = image.reshape(near, 2 * APX * many, LANES, depth).astype(jnp.bfloat16)[order]
    return [image[k] for k in range(near)]


def stack_kernel(slots, near, facts_ref, *refs):
    terms_refs = refs[:near]
    mine_ref, other_ref, facts, total, lined, sem = refs[near:]
    count = facts_ref.shape[0]
    half = terms_refs[0].shape[0] // 2
    wide = half // APX
    width = LANES // APY
    grid_rows = total.shape[1] // wide
    copy = pltpu.make_async_copy(facts_ref, facts, sem)
    copy.start()

    def clear(index, carry):
        for r in range(2):
            total[r, index] = jnp.zeros(total.shape[2:], total.dtype)
        return carry

    lax.fori_loop(0, total.shape[1], clear, 0, unroll=8)
    copy.wait()
    for k, terms_ref in enumerate(terms_refs):
        first = facts[2 * k, slots] * wide
        rows = pl.ds(facts[2 * k, slots + 1] * width, LANES)
        for r in range(2):
            sums = [
                total[r, first + tile, rows] + terms_ref[r * half + tile].astype(jnp.float32)
                for tile in range(half)
            ]
            for tile in range(half):
                total[r, first + tile, rows] = sums[tile]

    def line(row, carry):
        for r in range(2):
            for part in range(wide):
                for tile in range(total.shape[2] // LANES):
                    at = pl.ds(tile * LANES * wide + part, LANES, stride=wide)
                    lined[r, row, at] = total[
                        r, row * wide + part, tile * LANES:(tile + 1) * LANES
                    ]
        return carry

    lax.fori_loop(0, grid_rows, line, 0, unroll=4)

    def give(k, carry):
        for own, out_ref in enumerate((mine_ref, other_ref)):
            found = []
            for slot in range(slots):
                block = facts[2 * k + own, slot]
                rows = pl.ds(pl.multiple_of(block % GRID_COLS * LANES, LANES), LANES)
                found += [lined[r, block // GRID_COLS, rows] for r in range(2)]
            for index, tile in enumerate(found):
                out_ref[k, index] = tile.astype(out_ref.dtype)
        return carry

    lax.fori_loop(0, count // 2, give, 0, unroll=2)


def join_kernel(mine_ref, other_ref, *out_refs):
    for k, out_ref in enumerate(out_refs):
        total = mine_ref[k] + other_ref[k].astype(jnp.float32)
        out_ref[...] = total.astype(out_ref.dtype)


def finish_kernel(near, *refs):
    sums_refs, out_ref = refs[:-1], refs[-1]
    slots = out_ref.shape[0]
    place = chip_place(near)
    for j in range(near):
        for slot in range(slots):
            for r in range(2):
                result = sums_refs[j][2 * slot + r].astype(jnp.float32)
                for k in range(j + near, len(sums_refs), near):
                    result = result + sums_refs[k][2 * slot + r].astype(jnp.float32)
                out_ref[slot, 2 * (place ^ j) + r] = result


def per_device(
    velocity_p,
    velocity_s,
    density,
    perturbation,
    seafloor,
    owner_ids,
    corner_x,
    corner_y,
    wave_prev,
    wave_now,
):
    slots, block_x, block_y, depth = velocity_p.shape
    count = lax.axis_size("shot")
    assert count == 2 * block_x and block_y == LANES
    patch = APX * APY
    split = lax.axis_size("depth") > 1
    if split:
        seafloor = seafloor - lax.axis_index("depth") * depth

    chips = count // 2
    near = block_x // 2
    assert chips % near == 0 and chips & (chips - 1) == 0

    def swap(values):
        swapped = {0: values[0]}
        for k in range(len(values) - 1, 0, -1):
            swapped[k] = lax.ppermute(values[k], "shot", [(i, i ^ 2 * k) for i in range(count)])
        return [swapped[k] for k in range(len(values))]

    def across(value):
        return lax.ppermute(value, "shot", [(i, i ^ 1) for i in range(count)])

    out = jax.ShapeDtypeStruct((4 * slots + 1, block_y, depth), jnp.bfloat16)
    sent = pl.pallas_call(
        functools.partial(prepare_kernel, near),
        out_shape=(out,) * near,
        in_specs=[smem()] * 2 + [pl.BlockSpec(memory_space=pltpu.HBM)] * 6,
        out_specs=(vmem(),) * near,
        scratch_shapes=[
            pltpu.SMEM(owner_ids.shape, jnp.int32),
            pltpu.VMEM(seafloor.shape, jnp.int32),
            *[pltpu.VMEM(velocity_p.shape, jnp.bfloat16) for _ in range(5)],
            pltpu.SemaphoreType.DMA((6,)),
        ],
        name="prepare",
    )(
        corner_x, corner_y, owner_ids, seafloor,
        velocity_p, velocity_s, density, perturbation,
    )
    pieces = swap([sent[k % near] for k in range(chips)])
    pieces = [piece for own in pieces for piece in (own, across(own))]
    if not split:
        started = start(wave_prev[0], wave_now[0])
        pieces, started = lax.optimization_barrier((pieces, started))
    *picked, facts = pl.pallas_call(
        functools.partial(pick_kernel, slots, near, count),
        out_shape=(
            *[jax.ShapeDtypeStruct((patch * 4, block_y, depth), jnp.bfloat16)] * near,
            jax.ShapeDtypeStruct((count, depth), jnp.int32),
        ),
        in_specs=[vmem()] * count,
        out_specs=(vmem(),) * (near + 1),
        scratch_shapes=[
            pltpu.SMEM((count, depth), jnp.int32),
            pltpu.SMEM((count * slots,), jnp.int32),
            pltpu.VMEM((count * (4 * slots + 1), block_y, depth), jnp.bfloat16),
            pltpu.SemaphoreType.DMA,
        ],
        compiler_params=limit(3),
        name="pick",
    )(*pieces)
    models = swap(picked)
    if split:
        terms = wave_split_depth(models, wave_prev[0], wave_now[0])
    else:
        terms = wave(models, started)
    terms = swap(terms)

    grid_rows = count * slots // GRID_COLS
    wide = terms[0].shape[0] // 2 // APX
    sums = (chips, 2 * slots, block_y, depth)
    mine, other = pl.pallas_call(
        functools.partial(stack_kernel, slots, near),
        out_shape=(
            jax.ShapeDtypeStruct(sums, jnp.float32), jax.ShapeDtypeStruct(sums, jnp.bfloat16)
        ),
        in_specs=[vmem()] * (near + 1),
        out_specs=(vmem(), vmem()),
        scratch_shapes=[
            pltpu.SMEM(facts.shape, jnp.int32),
            pltpu.VMEM((2, grid_rows * wide, GRID_COLS * LANES // APY, depth), jnp.float32),
            pltpu.VMEM((2, grid_rows, GRID_COLS * block_y, depth), jnp.float32),
            pltpu.SemaphoreType.DMA,
        ],
        compiler_params=limit(4),
        name="stack",
    )(facts, *terms)
    joined = pl.pallas_call(
        join_kernel,
        out_shape=(jax.ShapeDtypeStruct(sums[1:], jnp.bfloat16),) * chips,
        in_specs=[vmem()] * 2,
        out_specs=(vmem(),) * chips,
        compiler_params=limit(2),
        name="join",
    )(mine, across(other))
    return pl.pallas_call(
        functools.partial(finish_kernel, near),
        out_shape=jax.ShapeDtypeStruct(velocity_p.shape, jnp.float32),
        in_specs=[vmem()] * chips,
        out_specs=vmem(),
        compiler_params=limit(2),
        name="finish",
    )(*swap(joined))


def solution(mesh):
    in_specs = (
        P(("grp", "shot"), None, None, "depth"),
        P(("grp", "shot"), None, None, "depth"),
        P(("grp", "shot"), None, None, "depth"),
        P(("grp", "shot"), None, None, "depth"),
        P(("grp", "shot"), None, None),
        P(("grp", "shot")),
        P(("grp", "shot")),
        P(("grp", "shot")),
        P(("grp", "shot"), None, None, "depth"),
        P(("grp", "shot"), None, None, "depth"),
    )
    out_specs = P(("grp", "shot"), None, None, "depth")
    return jax.shard_map(
        per_device, mesh=mesh, in_specs=in_specs, out_specs=out_specs, check_vma=False
    )
```

```python
import functools

import jax
import jax.numpy as jnp
from jax import lax
from jax.experimental import pallas as pl
from jax.experimental.pallas import tpu as pltpu
from jax.sharding import PartitionSpec as P

APX = 4
APY = 4
STEPS = 4
GRID_COLS = 8
LANES = 8

speed_factor = 0.28
image_scale = 0.01


def with_halo(block, sides, width):
    for axis, dim in sides:
        count = lax.axis_size(axis)
        forward = [(i, i + 1) for i in range(count - 1)]
        backward = [(target, source) for source, target in forward]
        low = lax.ppermute(
            lax.slice_in_dim(block, block.shape[dim] - width, None, axis=dim), axis, forward
        )
        high = lax.ppermute(lax.slice_in_dim(block, 0, width, axis=dim), axis, backward)
        block = jnp.concatenate([low, block, high], axis=dim)
    return block


def laplace_many(fields):
    stacked = jnp.stack(fields)
    padded = with_halo(stacked.astype(jnp.bfloat16), (("depth", 3),), 1).astype(stacked.dtype)
    padded = jnp.pad(padded, ((0, 0), (1, 1), (1, 1), (0, 0)))
    beside = padded[:, 2:, 1:-1, 1:-1] + padded[:, :-2, 1:-1, 1:-1]
    beside = beside + padded[:, 1:-1, 2:, 1:-1] + padded[:, 1:-1, :-2, 1:-1]
    beside = beside + padded[:, 1:-1, 1:-1, 2:] + padded[:, 1:-1, 1:-1, :-2]
    result = beside - 6.0 * stacked
    return [result[index] for index in range(len(fields))]


def propagate(kappa, contrast, before, current, apply):
    grads = []
    datas = []
    grad_now = apply([current])[0]
    delta_prev = jnp.zeros_like(current)
    delta_now = contrast * grad_now
    grads.append(grad_now)
    datas.append(delta_now)
    before, current = (current, 2.0 * current - before + kappa * grad_now)
    for step in range(1, STEPS):
        grad_now, spread = apply([current, delta_now])
        delta_next = 2.0 * delta_now - delta_prev + kappa * spread + contrast * grad_now
        grads.append(grad_now)
        datas.append(delta_next)
        delta_prev, delta_now = (delta_now, delta_next)
        if step + 1 < STEPS:
            before, current = (current, 2.0 * current - before + kappa * grad_now)
    back = datas[STEPS - 1]
    back_after = jnp.zeros_like(back)
    image = grads[STEPS - 1] * back
    for step in range(STEPS - 2, -1, -1):
        spread = apply([kappa * back])
        back_new = 2.0 * back - back_after + spread[0] + datas[step]
        image = image + grads[step] * back_new
        back_after, back = (back, back_new)
    return image


def limit(mebibytes):
    return pltpu.CompilerParams(vmem_limit_bytes=mebibytes * 2**20)


def vmem():
    return pl.BlockSpec(memory_space=pltpu.VMEM)


def smem():
    return pl.BlockSpec(memory_space=pltpu.SMEM)


def prepare_kernel(
    row_ref, col_ref, ids_hbm, floor_hbm, p_hbm, s_hbm, rho_hbm, pert_hbm, out_ref,
    ids, floors, p, s, rho, pert, sems,
):
    slots, block_x, block_y, depth = p.shape
    near = block_x
    copies = [
        pltpu.make_async_copy(source, target, sems.at[index])
        for index, (source, target) in enumerate(
            [(p_hbm, p), (s_hbm, s), (rho_hbm, rho), (floor_hbm, floors), (pert_hbm, pert),
             (ids_hbm, ids)]
        )
    ]
    for copy in copies:
        copy.start()
    shape = (block_y, depth)
    deep = lax.broadcasted_iota(jnp.int32, shape, 1).astype(jnp.float32)
    lane = lax.broadcasted_iota(jnp.int32, shape, 1)
    same = lax.broadcasted_iota(jnp.int32, (block_y, block_y), 0) == (
        lax.broadcasted_iota(jnp.int32, (block_y, block_y), 1)
    )
    for copy in copies:
        copy.wait()
    for slot in range(slots):
        lines = floors[slot].astype(jnp.float32)
        for x in range(block_x):
            line = jnp.broadcast_to(lines[x:x + 1], (block_y, block_y))
            floor = jnp.sum(jnp.where(same, line, 0.0), axis=1, keepdims=True)
            primary = p[slot, x].astype(jnp.float32)
            shear = s[slot, x].astype(jnp.float32)
            square = primary * primary
            stiffness = jnp.where(deep >= floor, square + shear * shear, square)
            coef = speed_factor * stiffness / rho[slot, x].astype(jnp.float32)
            coef = coef.astype(out_ref.dtype)
            for piece in range(x, out_ref.shape[0], near):
                out_ref[piece, 2 * slot] = coef
                out_ref[piece, 2 * slot + 1] = pert[slot, x]
    facts = jnp.where(lane == slots, row_ref[0], 0)
    facts = jnp.where(lane == slots + 1, col_ref[0], facts)
    for slot in range(slots):
        facts = jnp.where(lane == slot, ids[slot], facts)
    facts = facts.astype(jnp.float32).astype(out_ref.dtype)
    for piece in range(out_ref.shape[0]):
        out_ref[piece, 2 * slots] = facts


def pick_kernel(slots, near, pieces_ref, *refs):
    out_refs = refs[:near][::-1]
    facts_ref, facts, spots, sem = refs[near:]
    count = facts_ref.shape[0]
    tiles = 2 * slots + 1
    for piece in range(count):
        tile = pieces_ref[piece * tiles + 2 * slots].astype(jnp.float32)
        facts_ref[piece:piece + 1] = tile.astype(jnp.int32)[0:1]
    copy = pltpu.make_async_copy(facts_ref, facts, sem)
    copy.start()
    me = lax.axis_index("shot")
    copy.wait()
    for piece in range(count):
        for slot in range(slots):
            spots[facts[piece, slot]] = piece * tiles + 2 * slot
    for k, out_ref in enumerate(out_refs):
        shot = me ^ k
        first = facts[shot, slots] * GRID_COLS + facts[shot, slots + 1]
        for x in range(APX):
            found = []
            for y in range(APY):
                spot = spots[first + x * GRID_COLS + y]
                found += [pieces_ref[spot], pieces_ref[spot + 1]]
            for index, tile in enumerate(found):
                out_ref[x * APY * 2 + index] = tile


def ends(shape):
    lane = lax.broadcasted_iota(jnp.int32, shape, 1)
    row = lax.broadcasted_iota(jnp.int32, shape, 0)
    return lane == 0, lane == shape[1] - 1, row == 0, row == shape[0] - 1


def laplace(before, here, after, masks):
    lane_0, lane_n, row_0, row_n = masks
    many = len(here)
    depth = here[0].shape[1]
    low = [jnp.where(row_0, 0.0, pltpu.roll(here[-1], 1, 0))] + here[:-1]
    high = here[1:] + [jnp.where(row_n, 0.0, pltpu.roll(here[0], LANES - 1, 0))]
    result = []
    for v in range(many):
        up = jnp.where(lane_0, 0.0, pltpu.roll(here[v], 1, 1))
        down = jnp.where(lane_n, 0.0, pltpu.roll(here[v], depth - 1, 1))
        total = (before[v] + after[v]) + (low[v] + high[v]) + (up + down)
        result.append(total - 6.0 * here[v])
    return result


def registers(ref, x):
    return [ref[x, v] for v in range(ref.shape[1])]


def strided(ref, x):
    many = ref.shape[1] // LANES
    return [ref[x, pl.ds(v, LANES, stride=many)] for v in range(many)]


def sweep(count, fields, body, unroll):
    many = fields[0].shape[1]
    zero = [jnp.zeros(fields[0].shape[2:], jnp.float32)] * many
    first = [(zero, registers(field, 0)) for field in fields]

    def step(x, carry):
        rows = [
            (before, here, registers(field, x + 1))
            for (before, here), field in zip(carry, fields)
        ]
        body(x, rows)
        return [(here, after) for _, here, after in rows]

    lax.fori_loop(0, count, step, first, unroll=unroll)


def start_kernel(prev_ref, now_ref, wave_ref, grad_ref, next_ref, flat, flat_prev, field):
    span_x, span_y, depth = now_ref.shape
    many = span_y // LANES
    masks = ends((LANES, depth))

    def load(x, carry):
        flat[x] = now_ref[x].astype(jnp.float32)
        flat_prev[x] = prev_ref[x].astype(jnp.float32)
        return carry

    lax.fori_loop(0, span_x, load, 0, unroll=2)

    def order(x, carry):
        rows = strided(flat, x)
        older = strided(flat_prev, x)
        for v in range(many):
            field[x, v] = rows[v]
            wave_ref[x, v] = rows[v]
            next_ref[x, v] = 2.0 * rows[v] - older[v]
        return carry

    lax.fori_loop(0, span_x, order, 0, unroll=2)
    for v in range(many):
        field[span_x, v] = jnp.zeros((LANES, depth), jnp.float32)

    def body(x, rows):
        grads = laplace(*rows[0], masks)
        for v in range(many):
            grad_ref[x, v] = grads[v]

    sweep(span_x, [field], body, 16)


def start(before, current):
    span_x, span_y, depth = before.shape
    many = span_y // LANES
    out = jax.ShapeDtypeStruct((span_x, many, LANES, depth), jnp.float32)
    flat = pltpu.VMEM((span_x, span_y, depth), jnp.float32)
    return pl.pallas_call(
        start_kernel,
        out_shape=(out, out, out),
        in_specs=[vmem()] * 2,
        out_specs=(vmem(),) * 3,
        scratch_shapes=[flat, flat, pltpu.VMEM((span_x + 1, many, LANES, depth), jnp.float32)],
        compiler_params=limit(8),
        cost_estimate=pl.CostEstimate(
            flops=20 * before.size, bytes_accessed=16 * before.size, transcendentals=0
        ),
        name="start",
    )(before, current)


def wave_kernel(near, *refs):
    model_refs = refs[:near]
    u_0, g_0, next_ref = refs[near:near + 3]
    out_refs = refs[near + 3:2 * near + 3][::-1]
    kap, con, u_1, u_2, u_3, d_0, d_1, d_2, kb_3, kb_2, kb_1 = refs[2 * near + 3:2 * near + 14]
    g_1, g_2, d_3, b_2, b_1, image, result = refs[2 * near + 14:]
    span_x, many = u_0.shape[:2]
    depth = u_0.shape[3]
    block_y = model_refs[0].shape[1]
    block_x = span_x // APX
    place = lax.axis_index("shot") % near
    masks = ends((LANES, depth))
    each = range(many)
    for field in (u_1, u_2, u_3, d_0, d_1, d_2, kb_3, kb_2, kb_1):
        for v in each:
            field[span_x, v] = jnp.zeros((LANES, depth), jnp.float32)

    for k, model_ref in enumerate(model_refs):
        for x in range(APX):
            at = x * block_x + (place ^ k)
            for y in range(APY):
                rows = pl.ds(y * block_y, block_y)
                tile = 2 * (x * APY + y)
                kap[at, rows] = model_ref[tile].astype(jnp.float32)
                con[at, rows] = speed_factor * model_ref[tile + 1].astype(jnp.float32)

    def forward_0(x, carry):
        kaps, cons, grads = strided(kap, x), strided(con, x), registers(g_0, x)
        older = registers(next_ref, x)
        for v in each:
            d_0[x, v] = cons[v] * grads[v]
            u_1[x, v] = older[v] + kaps[v] * grads[v]
        return carry

    lax.fori_loop(0, span_x, forward_0, 0, unroll=16)

    def forward(u_now, u_prev, d_now, d_prev, u_next, d_next, g_now):
        def body(x, rows):
            waves, deltas = rows
            grads = laplace(*waves, masks)
            spread = laplace(*deltas, masks)
            kaps, cons = strided(kap, x), strided(con, x)
            for v in each:
                value = 2.0 * deltas[1][v] + kaps[v] * spread[v] + cons[v] * grads[v]
                if d_prev is not None:
                    value = value - d_prev[x, v]
                d_next[x, v] = value
                if u_next is None:
                    image[x, v] = grads[v] * value
                    kb_3[x, v] = kaps[v] * value
                else:
                    g_now[x, v] = grads[v]
                    u_next[x, v] = 2.0 * waves[1][v] - u_prev[x, v] + kaps[v] * grads[v]

        sweep(span_x, [u_now, d_now], body, 16)

    forward(u_1, u_0, d_0, None, u_2, d_1, g_1)
    forward(u_2, u_1, d_1, d_0, u_3, d_2, g_2)
    forward(u_3, u_2, d_2, d_1, None, d_3, None)

    def adjoint(kb, b_now, b_after, data, grad, kb_next, b_next):
        def body(x, rows):
            spread = laplace(*rows[0], masks)
            kaps = None if kb_next is None else strided(kap, x)
            for v in each:
                back = 2.0 * b_now[x, v] + spread[v] + data[x, v]
                if b_after is not None:
                    back = back - b_after[x, v]
                total = image[x, v] + grad[x, v] * back
                if kb_next is None:
                    total = (image_scale * total).astype(result.dtype)
                    result[x % block_x, x // block_x * many + v] = total
                else:
                    image[x, v] = total
                    b_next[x, v] = back
                    kb_next[x, v] = kaps[v] * back

        sweep(span_x, [kb], body, 16)

    adjoint(kb_3, d_3, None, d_2, g_2, kb_2, b_2)
    adjoint(kb_2, b_2, d_3, d_1, g_1, kb_1, b_1)
    adjoint(kb_1, b_1, b_2, d_0, g_0, None, None)
    for k, out_ref in enumerate(out_refs):
        out_ref[...] = result[place ^ k]


def wave(models, started):
    span_x, many, _, depth = started[0].shape
    near = len(models)
    flat = pltpu.VMEM((span_x, many * LANES, depth), jnp.float32)
    field = pltpu.VMEM((span_x + 1, many, LANES, depth), jnp.float32)
    plain = pltpu.VMEM((span_x, many, LANES, depth), jnp.float32)
    out = (APX * many, LANES, depth)
    terms = pl.pallas_call(
        functools.partial(wave_kernel, near),
        out_shape=(jax.ShapeDtypeStruct(out, jnp.bfloat16),) * near,
        in_specs=[vmem()] * (near + 3),
        out_specs=(vmem(),) * near,
        scratch_shapes=[flat] * 2 + [field] * 9 + [plain] * 6
        + [pltpu.VMEM((near,) + out, jnp.bfloat16)],
        compiler_params=limit(20),
        name="wave",
    )(*models, *started)
    return terms[::-1]


def wave_split_depth(models, before, current):
    near = len(models)
    order = (lax.axis_index("shot") % near) ^ jnp.arange(near)
    model = jnp.stack(models)[order]
    span_x, span_y, depth = before.shape
    block_x, tiles, block_y, _ = model.shape
    grids = model.reshape(block_x, APX, APY, 2, block_y, depth).transpose(3, 1, 0, 2, 4, 5)
    grids = grids.reshape(2, span_x, span_y, depth).astype(jnp.float32)
    image = image_scale * propagate(
        grids[0],
        speed_factor * grids[1],
        before.astype(jnp.float32),
        current.astype(jnp.float32),
        laplace_many,
    )
    many = span_y // LANES
    image = image.reshape(APX, block_x, LANES, many, depth).transpose(1, 0, 3, 2, 4)
    image = image.reshape(near, APX * many, LANES, depth).astype(jnp.bfloat16)[order]
    return [image[k] for k in range(near)]


def stack_kernel(slots, near, facts_ref, *refs):
    terms_refs = refs[:near]
    out_ref, facts, total, lined, sem = refs[near:]
    tiles = terms_refs[0].shape[0]
    wide = tiles // APX
    width = LANES // APY
    grid_rows = total.shape[0] // wide
    copy = pltpu.make_async_copy(facts_ref, facts, sem)
    copy.start()
    me = lax.axis_index("shot")

    def clear(index, carry):
        total[index] = jnp.zeros(total.shape[1:], total.dtype)
        return carry

    lax.fori_loop(0, total.shape[0], clear, 0, unroll=8)
    copy.wait()

    for k, terms_ref in enumerate(terms_refs):
        first = facts[me ^ k, slots] * wide
        rows = pl.ds(facts[me ^ k, slots + 1] * width, LANES)
        sums = [
            total[first + tile, rows] + terms_ref[tile].astype(jnp.float32)
            for tile in range(tiles)
        ]
        for tile in range(tiles):
            total[first + tile, rows] = sums[tile]

    for row in range(grid_rows):
        for part in range(wide):
            for tile in range(total.shape[1] // LANES):
                at = pl.ds(tile * LANES * wide + part, LANES, stride=wide)
                lined[row, at] = total[row * wide + part, tile * LANES:(tile + 1) * LANES]

    def give(owner, carry):
        found = []
        for slot in range(slots):
            block = facts[owner, slot]
            rows = pl.ds(pl.multiple_of(block % GRID_COLS * LANES, LANES), LANES)
            found.append(lined[block // GRID_COLS, rows])
        for slot in range(slots):
            out_ref[owner, slot] = found[slot].astype(out_ref.dtype)
        return carry

    lax.fori_loop(0, out_ref.shape[0], give, 0, unroll=4)


def finish_kernel(sums_ref, out_ref):
    slots, block_x = out_ref.shape[:2]
    for x in range(block_x):
        for slot in range(slots):
            result = sums_ref[x, slot].astype(jnp.float32)
            for piece in range(x + block_x, sums_ref.shape[0], block_x):
                result = result + sums_ref[piece, slot].astype(jnp.float32)
            out_ref[slot, x] = result


def per_device(
    velocity_p,
    velocity_s,
    density,
    perturbation,
    seafloor,
    owner_ids,
    corner_x,
    corner_y,
    wave_prev,
    wave_now,
):
    slots, block_x, block_y, depth = velocity_p.shape
    count = lax.axis_size("shot")
    assert count == 2 * block_x and block_y == LANES
    patch = APX * APY
    split = lax.axis_size("depth") > 1
    if split:
        seafloor = seafloor - lax.axis_index("depth") * depth

    near = block_x
    assert count % near == 0 and near & (near - 1) == 0

    def swap(values):
        swapped = {0: values[0]}
        for k in range(near - 1, 0, -1):
            swapped[k] = lax.ppermute(values[k], "shot", [(i, i ^ k) for i in range(count)])
        return [swapped[k] for k in range(near)]

    sent = pl.pallas_call(
        prepare_kernel,
        out_shape=jax.ShapeDtypeStruct((count, 2 * slots + 1, block_y, depth), jnp.bfloat16),
        in_specs=[smem()] * 2 + [pl.BlockSpec(memory_space=pltpu.HBM)] * 6,
        out_specs=vmem(),
        scratch_shapes=[
            pltpu.SMEM(owner_ids.shape, jnp.int32),
            pltpu.VMEM(seafloor.shape, jnp.int32),
            *[pltpu.VMEM(velocity_p.shape, jnp.bfloat16) for _ in range(4)],
            pltpu.SemaphoreType.DMA((6,)),
        ],
        name="prepare",
    )(
        corner_x, corner_y, owner_ids, seafloor,
        velocity_p, velocity_s, density, perturbation,
    )
    pieces = lax.all_to_all(sent, "shot", 0, 0, tiled=True)

    if not split:
        started = start(wave_prev[0], wave_now[0])
        pieces, started = lax.optimization_barrier((pieces, started))
    *picked, facts = pl.pallas_call(
        functools.partial(pick_kernel, slots, near),
        out_shape=(
            *[jax.ShapeDtypeStruct((patch * 2, block_y, depth), jnp.bfloat16)] * near,
            jax.ShapeDtypeStruct((count, depth), jnp.int32),
        ),
        in_specs=[vmem()],
        out_specs=(vmem(),) * (near + 1),
        scratch_shapes=[
            pltpu.SMEM((count, depth), jnp.int32),
            pltpu.SMEM((count * slots,), jnp.int32),
            pltpu.SemaphoreType.DMA,
        ],
        compiler_params=limit(3),
        name="pick",
    )(pieces.reshape(count * (2 * slots + 1), block_y, depth))
    models = swap(picked[::-1])

    if split:
        terms = wave_split_depth(models, wave_prev[0], wave_now[0])
    else:
        terms = wave(models, started)
    terms = swap(terms)

    grid_rows = count * slots // GRID_COLS
    wide = terms[0].shape[0] // APX
    sums = pl.pallas_call(
        functools.partial(stack_kernel, slots, near),
        out_shape=jax.ShapeDtypeStruct((count, slots, block_y, depth), jnp.bfloat16),
        in_specs=[vmem()] * (near + 1),
        out_specs=vmem(),
        scratch_shapes=[
            pltpu.SMEM(facts.shape, jnp.int32),
            pltpu.VMEM((grid_rows * wide, GRID_COLS * LANES // APY, depth), jnp.float32),
            pltpu.VMEM((grid_rows, GRID_COLS * block_y, depth), jnp.float32),
            pltpu.SemaphoreType.DMA,
        ],
        compiler_params=limit(3),
        name="stack",
    )(facts, *terms)
    sums = lax.all_to_all(sums, "shot", 0, 0, tiled=True)
    return pl.pallas_call(
        finish_kernel,
        out_shape=jax.ShapeDtypeStruct(velocity_p.shape, jnp.float32),
        in_specs=[vmem()],
        out_specs=vmem(),
        compiler_params=limit(2),
        name="finish",
    )(sums)


def solution(mesh):
    in_specs = (
        P(("grp", "shot"), None, None, "depth"),
        P(("grp", "shot"), None, None, "depth"),
        P(("grp", "shot"), None, None, "depth"),
        P(("grp", "shot"), None, None, "depth"),
        P(("grp", "shot"), None, None),
        P(("grp", "shot")),
        P(("grp", "shot")),
        P(("grp", "shot")),
        P(("grp", "shot"), None, None, "depth"),
        P(("grp", "shot"), None, None, "depth"),
    )
    out_specs = P(("grp", "shot"), None, None, "depth")
    return jax.shard_map(
        per_device, mesh=mesh, in_specs=in_specs, out_specs=out_specs, check_vma=False
    )
```

```python
import functools

import jax
import jax.numpy as jnp
from jax import lax
from jax.experimental import pallas as pl
from jax.experimental.pallas import tpu as pltpu
from jax.sharding import PartitionSpec as P

APX = 4
APY = 4
STEPS = 4
GRID_COLS = 8
LANES = 8

speed_factor = 0.28
image_scale = 0.01


def with_halo(block, sides, width):
    for axis, dim in sides:
        count = lax.axis_size(axis)
        forward = [(i, i + 1) for i in range(count - 1)]
        backward = [(target, source) for source, target in forward]
        low = lax.ppermute(
            lax.slice_in_dim(block, block.shape[dim] - width, None, axis=dim), axis, forward
        )
        high = lax.ppermute(lax.slice_in_dim(block, 0, width, axis=dim), axis, backward)
        block = jnp.concatenate([low, block, high], axis=dim)
    return block


def laplace_many(fields):
    stacked = jnp.stack(fields)
    padded = with_halo(stacked.astype(jnp.bfloat16), (("depth", 3),), 1).astype(stacked.dtype)
    padded = jnp.pad(padded, ((0, 0), (1, 1), (1, 1), (0, 0)))
    beside = padded[:, 2:, 1:-1, 1:-1] + padded[:, :-2, 1:-1, 1:-1]
    beside = beside + padded[:, 1:-1, 2:, 1:-1] + padded[:, 1:-1, :-2, 1:-1]
    beside = beside + padded[:, 1:-1, 1:-1, 2:] + padded[:, 1:-1, 1:-1, :-2]
    result = beside - 6.0 * stacked
    return [result[index] for index in range(len(fields))]


def propagate(kappa, contrast, before, current, apply):
    grads = []
    datas = []
    grad_now = apply([current])[0]
    delta_prev = jnp.zeros_like(current)
    delta_now = contrast * grad_now
    grads.append(grad_now)
    datas.append(delta_now)
    before, current = (current, 2.0 * current - before + kappa * grad_now)
    for step in range(1, STEPS):
        grad_now, spread = apply([current, delta_now])
        delta_next = 2.0 * delta_now - delta_prev + kappa * spread + contrast * grad_now
        grads.append(grad_now)
        datas.append(delta_next)
        delta_prev, delta_now = (delta_now, delta_next)
        if step + 1 < STEPS:
            before, current = (current, 2.0 * current - before + kappa * grad_now)
    back = datas[STEPS - 1]
    back_after = jnp.zeros_like(back)
    image = grads[STEPS - 1] * back
    for step in range(STEPS - 2, -1, -1):
        spread = apply([kappa * back])
        back_new = 2.0 * back - back_after + spread[0] + datas[step]
        image = image + grads[step] * back_new
        back_after, back = (back, back_new)
    return image


def limit(mebibytes):
    return pltpu.CompilerParams(vmem_limit_bytes=mebibytes * 2**20)


def vmem():
    return pl.BlockSpec(memory_space=pltpu.VMEM)


def smem():
    return pl.BlockSpec(memory_space=pltpu.SMEM)


def prepare_kernel(
    row_ref, col_ref, ids_hbm, floor_hbm, p_hbm, s_hbm, rho_hbm, pert_hbm, out_ref,
    ids, floors, p, s, rho, pert, sems,
):
    slots, block_x, block_y, depth = p.shape
    near = block_x
    copies = [
        pltpu.make_async_copy(source, target, sems.at[index])
        for index, (source, target) in enumerate(
            [(p_hbm, p), (s_hbm, s), (rho_hbm, rho), (floor_hbm, floors), (pert_hbm, pert),
             (ids_hbm, ids)]
        )
    ]
    for copy in copies:
        copy.start()
    shape = (block_y, depth)
    deep = lax.broadcasted_iota(jnp.int32, shape, 1).astype(jnp.float32)
    lane = lax.broadcasted_iota(jnp.int32, shape, 1)
    same = lax.broadcasted_iota(jnp.int32, (block_y, block_y), 0) == (
        lax.broadcasted_iota(jnp.int32, (block_y, block_y), 1)
    )
    for copy in copies:
        copy.wait()
    for slot in range(slots):
        lines = floors[slot].astype(jnp.float32)
        for x in range(block_x):
            line = jnp.broadcast_to(lines[x:x + 1], (block_y, block_y))
            floor = jnp.sum(jnp.where(same, line, 0.0), axis=1, keepdims=True)
            primary = p[slot, x].astype(jnp.float32)
            shear = s[slot, x].astype(jnp.float32)
            square = primary * primary
            stiffness = jnp.where(deep >= floor, square + shear * shear, square)
            coef = speed_factor * stiffness / rho[slot, x].astype(jnp.float32)
            coef = coef.astype(out_ref.dtype)
            for piece in range(x, out_ref.shape[0], near):
                out_ref[piece, 2 * slot] = coef
                out_ref[piece, 2 * slot + 1] = pert[slot, x]
    facts = jnp.where(lane == slots, row_ref[0], 0)
    facts = jnp.where(lane == slots + 1, col_ref[0], facts)
    for slot in range(slots):
        facts = jnp.where(lane == slot, ids[slot], facts)
    facts = facts.astype(jnp.float32).astype(out_ref.dtype)
    for piece in range(out_ref.shape[0]):
        out_ref[piece, 2 * slots] = facts


def pick_kernel(slots, near, pieces_ref, *refs):
    out_refs = refs[:near][::-1]
    facts_ref, facts, spots, sem = refs[near:]
    count = facts_ref.shape[0]
    tiles = 2 * slots + 1
    for piece in range(count):
        tile = pieces_ref[piece * tiles + 2 * slots].astype(jnp.float32)
        facts_ref[piece:piece + 1] = tile.astype(jnp.int32)[0:1]
    copy = pltpu.make_async_copy(facts_ref, facts, sem)
    copy.start()
    me = lax.axis_index("shot")
    copy.wait()
    for piece in range(count):
        for slot in range(slots):
            spots[facts[piece, slot]] = piece * tiles + 2 * slot
    for k, out_ref in enumerate(out_refs):
        shot = me ^ k
        first = facts[shot, slots] * GRID_COLS + facts[shot, slots + 1]
        for x in range(APX):
            found = []
            for y in range(APY):
                spot = spots[first + x * GRID_COLS + y]
                found += [pieces_ref[spot], pieces_ref[spot + 1]]
            for index, tile in enumerate(found):
                out_ref[x * APY * 2 + index] = tile


def ends(shape):
    lane = lax.broadcasted_iota(jnp.int32, shape, 1)
    row = lax.broadcasted_iota(jnp.int32, shape, 0)
    return lane == 0, lane == shape[1] - 1, row == 0, row == shape[0] - 1


def laplace(before, here, after, masks):
    lane_0, lane_n, row_0, row_n = masks
    many = len(here)
    depth = here[0].shape[1]
    low = [jnp.where(row_0, 0.0, pltpu.roll(here[-1], 1, 0))] + here[:-1]
    high = here[1:] + [jnp.where(row_n, 0.0, pltpu.roll(here[0], LANES - 1, 0))]
    result = []
    for v in range(many):
        up = jnp.where(lane_0, 0.0, pltpu.roll(here[v], 1, 1))
        down = jnp.where(lane_n, 0.0, pltpu.roll(here[v], depth - 1, 1))
        total = (before[v] + after[v]) + (low[v] + high[v]) + (up + down)
        result.append(total - 6.0 * here[v])
    return result


def registers(ref, x):
    return [ref[x, v] for v in range(ref.shape[1])]


def strided(ref, x):
    many = ref.shape[1] // LANES
    return [ref[x, pl.ds(v, LANES, stride=many)] for v in range(many)]


def sweep(count, fields, body, unroll):
    many = fields[0].shape[1]
    zero = [jnp.zeros(fields[0].shape[2:], jnp.float32)] * many
    first = [(zero, registers(field, 0)) for field in fields]

    def step(x, carry):
        rows = [
            (before, here, registers(field, x + 1))
            for (before, here), field in zip(carry, fields)
        ]
        body(x, rows)
        return [(here, after) for _, here, after in rows]

    lax.fori_loop(0, count, step, first, unroll=unroll)


def start_kernel(prev_ref, now_ref, wave_ref, grad_ref, next_ref, flat, flat_prev, field):
    span_x, span_y, depth = now_ref.shape
    many = span_y // LANES
    masks = ends((LANES, depth))

    def load(x, carry):
        flat[x] = now_ref[x].astype(jnp.float32)
        flat_prev[x] = prev_ref[x].astype(jnp.float32)
        return carry

    lax.fori_loop(0, span_x, load, 0, unroll=2)

    def order(x, carry):
        rows = strided(flat, x)
        older = strided(flat_prev, x)
        for v in range(many):
            field[x, v] = rows[v]
            wave_ref[x, v] = rows[v]
            next_ref[x, v] = 2.0 * rows[v] - older[v]
        return carry

    lax.fori_loop(0, span_x, order, 0, unroll=2)
    for v in range(many):
        field[span_x, v] = jnp.zeros((LANES, depth), jnp.float32)

    def body(x, rows):
        grads = laplace(*rows[0], masks)
        for v in range(many):
            grad_ref[x, v] = grads[v]

    sweep(span_x, [field], body, 16)


def start(before, current):
    span_x, span_y, depth = before.shape
    many = span_y // LANES
    out = jax.ShapeDtypeStruct((span_x, many, LANES, depth), jnp.float32)
    flat = pltpu.VMEM((span_x, span_y, depth), jnp.float32)
    return pl.pallas_call(
        start_kernel,
        out_shape=(out, out, out),
        in_specs=[vmem()] * 2,
        out_specs=(vmem(),) * 3,
        scratch_shapes=[flat, flat, pltpu.VMEM((span_x + 1, many, LANES, depth), jnp.float32)],
        compiler_params=limit(8),
        cost_estimate=pl.CostEstimate(
            flops=20 * before.size, bytes_accessed=16 * before.size, transcendentals=0
        ),
        name="start",
    )(before, current)


def wave_kernel(near, *refs):
    model_refs = refs[:near][::-1]
    u_0, g_0, next_ref = refs[near:near + 3]
    out_refs = refs[near + 3:2 * near + 3][::-1]
    kap, con, u_1, u_2, u_3, d_0, d_1, d_2, kb_3, kb_2, kb_1 = refs[2 * near + 3:2 * near + 14]
    g_1, g_2, d_3, b_2, b_1, image, result = refs[2 * near + 14:]
    span_x, many = u_0.shape[:2]
    depth = u_0.shape[3]
    block_y = model_refs[0].shape[1]
    block_x = span_x // APX
    place = lax.axis_index("shot") % near
    masks = ends((LANES, depth))
    each = range(many)
    for field in (u_1, u_2, u_3, d_0, d_1, d_2, kb_3, kb_2, kb_1):
        for v in each:
            field[span_x, v] = jnp.zeros((LANES, depth), jnp.float32)

    for k, model_ref in enumerate(model_refs):
        for x in range(APX):
            at = x * block_x + (place ^ k)
            for y in range(APY):
                rows = pl.ds(y * block_y, block_y)
                tile = 2 * (x * APY + y)
                kap[at, rows] = model_ref[tile].astype(jnp.float32)
                con[at, rows] = speed_factor * model_ref[tile + 1].astype(jnp.float32)

    def forward_0(x, carry):
        kaps, cons, grads = strided(kap, x), strided(con, x), registers(g_0, x)
        older = registers(next_ref, x)
        for v in each:
            d_0[x, v] = cons[v] * grads[v]
            u_1[x, v] = older[v] + kaps[v] * grads[v]
        return carry

    lax.fori_loop(0, span_x, forward_0, 0, unroll=16)

    def forward(u_now, u_prev, d_now, d_prev, u_next, d_next, g_now):
        def body(x, rows):
            waves, deltas = rows
            grads = laplace(*waves, masks)
            spread = laplace(*deltas, masks)
            kaps, cons = strided(kap, x), strided(con, x)
            for v in each:
                value = 2.0 * deltas[1][v] + kaps[v] * spread[v] + cons[v] * grads[v]
                if d_prev is not None:
                    value = value - d_prev[x, v]
                d_next[x, v] = value
                if u_next is None:
                    image[x, v] = grads[v] * value
                    kb_3[x, v] = kaps[v] * value
                else:
                    g_now[x, v] = grads[v]
                    u_next[x, v] = 2.0 * waves[1][v] - u_prev[x, v] + kaps[v] * grads[v]

        sweep(span_x, [u_now, d_now], body, 16)

    forward(u_1, u_0, d_0, None, u_2, d_1, g_1)
    forward(u_2, u_1, d_1, d_0, u_3, d_2, g_2)
    forward(u_3, u_2, d_2, d_1, None, d_3, None)

    def adjoint(kb, b_now, b_after, data, grad, kb_next, b_next):
        def body(x, rows):
            spread = laplace(*rows[0], masks)
            kaps = None if kb_next is None else strided(kap, x)
            for v in each:
                back = 2.0 * b_now[x, v] + spread[v] + data[x, v]
                if b_after is not None:
                    back = back - b_after[x, v]
                total = image[x, v] + grad[x, v] * back
                if kb_next is None:
                    total = (image_scale * total).astype(result.dtype)
                    result[x % block_x, x // block_x * many + v] = total
                else:
                    image[x, v] = total
                    b_next[x, v] = back
                    kb_next[x, v] = kaps[v] * back

        sweep(span_x, [kb], body, 16)

    adjoint(kb_3, d_3, None, d_2, g_2, kb_2, b_2)
    adjoint(kb_2, b_2, d_3, d_1, g_1, kb_1, b_1)
    adjoint(kb_1, b_1, b_2, d_0, g_0, None, None)
    for k, out_ref in enumerate(out_refs):
        out_ref[...] = result[place ^ k]


def wave(models, started):
    span_x, many, _, depth = started[0].shape
    near = len(models)
    flat = pltpu.VMEM((span_x, many * LANES, depth), jnp.float32)
    field = pltpu.VMEM((span_x + 1, many, LANES, depth), jnp.float32)
    plain = pltpu.VMEM((span_x, many, LANES, depth), jnp.float32)
    out = (APX * many, LANES, depth)
    terms = pl.pallas_call(
        functools.partial(wave_kernel, near),
        out_shape=(jax.ShapeDtypeStruct(out, jnp.bfloat16),) * near,
        in_specs=[vmem()] * (near + 3),
        out_specs=(vmem(),) * near,
        scratch_shapes=[flat] * 2 + [field] * 9 + [plain] * 6
        + [pltpu.VMEM((near,) + out, jnp.bfloat16)],
        compiler_params=limit(20),
        name="wave",
    )(*models[::-1], *started)
    return terms[::-1]


def wave_split_depth(models, before, current):
    near = len(models)
    order = (lax.axis_index("shot") % near) ^ jnp.arange(near)
    model = jnp.stack(models)[order]
    span_x, span_y, depth = before.shape
    block_x, tiles, block_y, _ = model.shape
    grids = model.reshape(block_x, APX, APY, 2, block_y, depth).transpose(3, 1, 0, 2, 4, 5)
    grids = grids.reshape(2, span_x, span_y, depth).astype(jnp.float32)
    image = image_scale * propagate(
        grids[0],
        speed_factor * grids[1],
        before.astype(jnp.float32),
        current.astype(jnp.float32),
        laplace_many,
    )
    many = span_y // LANES
    image = image.reshape(APX, block_x, LANES, many, depth).transpose(1, 0, 3, 2, 4)
    image = image.reshape(near, APX * many, LANES, depth).astype(jnp.bfloat16)[order]
    return [image[k] for k in range(near)]


def stack_kernel(slots, near, facts_ref, *refs):
    terms_refs = refs[:near][::-1]
    out_ref, facts, total, lined, sem = refs[near:]
    tiles = terms_refs[0].shape[0]
    wide = tiles // APX
    width = LANES // APY
    grid_rows = total.shape[0] // wide
    copy = pltpu.make_async_copy(facts_ref, facts, sem)
    copy.start()
    me = lax.axis_index("shot")

    def clear(index, carry):
        total[index] = jnp.zeros(total.shape[1:], total.dtype)
        return carry

    lax.fori_loop(0, total.shape[0], clear, 0, unroll=8)
    copy.wait()

    for k, terms_ref in enumerate(terms_refs):
        first = facts[me ^ k, slots] * wide
        rows = pl.ds(facts[me ^ k, slots + 1] * width, LANES)
        sums = [
            total[first + tile, rows] + terms_ref[tile].astype(jnp.float32)
            for tile in range(tiles)
        ]
        for tile in range(tiles):
            total[first + tile, rows] = sums[tile]

    for row in range(grid_rows):
        for part in range(wide):
            for tile in range(total.shape[1] // LANES):
                at = pl.ds(tile * LANES * wide + part, LANES, stride=wide)
                lined[row, at] = total[row * wide + part, tile * LANES:(tile + 1) * LANES]

    def give(owner, carry):
        found = []
        for slot in range(slots):
            block = facts[owner, slot]
            rows = pl.ds(pl.multiple_of(block % GRID_COLS * LANES, LANES), LANES)
            found.append(lined[block // GRID_COLS, rows])
        for slot in range(slots):
            out_ref[owner, slot] = found[slot].astype(out_ref.dtype)
        return carry

    lax.fori_loop(0, out_ref.shape[0], give, 0, unroll=4)


def finish_kernel(sums_ref, out_ref):
    slots, block_x = out_ref.shape[:2]
    for x in range(block_x):
        for slot in range(slots):
            result = sums_ref[x, slot].astype(jnp.float32)
            for piece in range(x + block_x, sums_ref.shape[0], block_x):
                result = result + sums_ref[piece, slot].astype(jnp.float32)
            out_ref[slot, x] = result


def per_device(
    velocity_p,
    velocity_s,
    density,
    perturbation,
    seafloor,
    owner_ids,
    corner_x,
    corner_y,
    wave_prev,
    wave_now,
):
    slots, block_x, block_y, depth = velocity_p.shape
    count = lax.axis_size("shot")
    assert count == 2 * block_x and block_y == LANES
    patch = APX * APY
    split = lax.axis_size("depth") > 1
    if split:
        seafloor = seafloor - lax.axis_index("depth") * depth

    near = block_x
    assert count % near == 0 and near & (near - 1) == 0

    def swap(values):
        swapped = {0: values[0]}
        for k in range(near - 1, 0, -1):
            swapped[k] = lax.ppermute(values[k], "shot", [(i, i ^ k) for i in range(count)])
        return [swapped[k] for k in range(near)]

    sent = pl.pallas_call(
        prepare_kernel,
        out_shape=jax.ShapeDtypeStruct((count, 2 * slots + 1, block_y, depth), jnp.bfloat16),
        in_specs=[smem()] * 2 + [pl.BlockSpec(memory_space=pltpu.HBM)] * 6,
        out_specs=vmem(),
        scratch_shapes=[
            pltpu.SMEM(owner_ids.shape, jnp.int32),
            pltpu.VMEM(seafloor.shape, jnp.int32),
            *[pltpu.VMEM(velocity_p.shape, jnp.bfloat16) for _ in range(4)],
            pltpu.SemaphoreType.DMA((6,)),
        ],
        name="prepare",
    )(
        corner_x, corner_y, owner_ids, seafloor,
        velocity_p, velocity_s, density, perturbation,
    )
    pieces = lax.all_to_all(sent, "shot", 0, 0, tiled=True)

    if not split:
        started = start(wave_prev[0], wave_now[0])
        pieces, started = lax.optimization_barrier((pieces, started))
    *picked, facts = pl.pallas_call(
        functools.partial(pick_kernel, slots, near),
        out_shape=(
            *[jax.ShapeDtypeStruct((patch * 2, block_y, depth), jnp.bfloat16)] * near,
            jax.ShapeDtypeStruct((count, depth), jnp.int32),
        ),
        in_specs=[vmem()],
        out_specs=(vmem(),) * (near + 1),
        scratch_shapes=[
            pltpu.SMEM((count, depth), jnp.int32),
            pltpu.SMEM((count * slots,), jnp.int32),
            pltpu.SemaphoreType.DMA,
        ],
        compiler_params=limit(3),
        name="pick",
    )(pieces.reshape(count * (2 * slots + 1), block_y, depth))
    models = swap(picked[::-1])

    if split:
        terms = wave_split_depth(models, wave_prev[0], wave_now[0])
    else:
        terms = wave(models, started)
    terms = swap(terms)

    grid_rows = count * slots // GRID_COLS
    wide = terms[0].shape[0] // APX
    sums = pl.pallas_call(
        functools.partial(stack_kernel, slots, near),
        out_shape=jax.ShapeDtypeStruct((count, slots, block_y, depth), jnp.bfloat16),
        in_specs=[vmem()] * (near + 1),
        out_specs=vmem(),
        scratch_shapes=[
            pltpu.SMEM(facts.shape, jnp.int32),
            pltpu.VMEM((grid_rows * wide, GRID_COLS * LANES // APY, depth), jnp.float32),
            pltpu.VMEM((grid_rows, GRID_COLS * block_y, depth), jnp.float32),
            pltpu.SemaphoreType.DMA,
        ],
        compiler_params=limit(3),
        name="stack",
    )(facts, *terms[::-1])
    sums = lax.all_to_all(sums, "shot", 0, 0, tiled=True)
    return pl.pallas_call(
        finish_kernel,
        out_shape=jax.ShapeDtypeStruct(velocity_p.shape, jnp.float32),
        in_specs=[vmem()],
        out_specs=vmem(),
        compiler_params=limit(2),
        name="finish",
    )(sums)


def solution(mesh):
    in_specs = (
        P(("grp", "shot"), None, None, "depth"),
        P(("grp", "shot"), None, None, "depth"),
        P(("grp", "shot"), None, None, "depth"),
        P(("grp", "shot"), None, None, "depth"),
        P(("grp", "shot"), None, None),
        P(("grp", "shot")),
        P(("grp", "shot")),
        P(("grp", "shot")),
        P(("grp", "shot"), None, None, "depth"),
        P(("grp", "shot"), None, None, "depth"),
    )
    out_specs = P(("grp", "shot"), None, None, "depth")
    return jax.shard_map(
        per_device, mesh=mesh, in_specs=in_specs, out_specs=out_specs, check_vma=False
    )
```

```python
import functools

import jax
import jax.numpy as jnp
from jax import lax
from jax.experimental import pallas as pl
from jax.experimental.pallas import tpu as pltpu
from jax.sharding import PartitionSpec as P

APX = 4
APY = 4
STEPS = 4
GRID_COLS = 8
LANES = 8

speed_factor = 0.28
image_scale = 0.01


def with_halo(block, sides, width):
    for axis, dim in sides:
        count = lax.axis_size(axis)
        forward = [(i, i + 1) for i in range(count - 1)]
        backward = [(target, source) for source, target in forward]
        low = lax.ppermute(
            lax.slice_in_dim(block, block.shape[dim] - width, None, axis=dim), axis, forward
        )
        high = lax.ppermute(lax.slice_in_dim(block, 0, width, axis=dim), axis, backward)
        block = jnp.concatenate([low, block, high], axis=dim)
    return block


def laplace_many(fields):
    stacked = jnp.stack(fields)
    padded = with_halo(stacked.astype(jnp.bfloat16), (("depth", 3),), 1).astype(stacked.dtype)
    padded = jnp.pad(padded, ((0, 0), (1, 1), (1, 1), (0, 0)))
    beside = padded[:, 2:, 1:-1, 1:-1] + padded[:, :-2, 1:-1, 1:-1]
    beside = beside + padded[:, 1:-1, 2:, 1:-1] + padded[:, 1:-1, :-2, 1:-1]
    beside = beside + padded[:, 1:-1, 1:-1, 2:] + padded[:, 1:-1, 1:-1, :-2]
    result = beside - 6.0 * stacked
    return [result[index] for index in range(len(fields))]


def propagate(kappa, contrast, before, current, apply):
    grads = []
    datas = []
    grad_now = apply([current])[0]
    delta_prev = jnp.zeros_like(current)
    delta_now = contrast * grad_now
    grads.append(grad_now)
    datas.append(delta_now)
    before, current = (current, 2.0 * current - before + kappa * grad_now)
    for step in range(1, STEPS):
        grad_now, spread = apply([current, delta_now])
        delta_next = 2.0 * delta_now - delta_prev + kappa * spread + contrast * grad_now
        grads.append(grad_now)
        datas.append(delta_next)
        delta_prev, delta_now = (delta_now, delta_next)
        if step + 1 < STEPS:
            before, current = (current, 2.0 * current - before + kappa * grad_now)
    back = datas[STEPS - 1]
    back_after = jnp.zeros_like(back)
    image = grads[STEPS - 1] * back
    for step in range(STEPS - 2, -1, -1):
        spread = apply([kappa * back])
        back_new = 2.0 * back - back_after + spread[0] + datas[step]
        image = image + grads[step] * back_new
        back_after, back = (back, back_new)
    return image


def limit(mebibytes):
    return pltpu.CompilerParams(vmem_limit_bytes=mebibytes * 2**20)


def parts(refs):
    chips = len(refs) // 2
    own, other = refs[:chips][::-1], refs[chips:][::-1]
    length = refs[0].shape[0] // 2
    return [
        ref.at[pl.ds(side * length, length)]
        for pair in zip(own, other)
        for side, ref in enumerate(pair)
    ]


def vmem():
    return pl.BlockSpec(memory_space=pltpu.VMEM)


def smem():
    return pl.BlockSpec(memory_space=pltpu.SMEM)


def prepare_kernel(
    row_ref, col_ref, ids_hbm, floor_hbm, p_hbm, s_hbm, rho_hbm, pert_hbm, out_ref,
    ids, floors, p, s, rho, pert, sems,
):
    slots, block_x, block_y, depth = p.shape
    near = block_x
    copies = [
        pltpu.make_async_copy(source, target, sems.at[index])
        for index, (source, target) in enumerate(
            [(p_hbm, p), (s_hbm, s), (rho_hbm, rho), (floor_hbm, floors), (pert_hbm, pert),
             (ids_hbm, ids)]
        )
    ]
    for copy in copies:
        copy.start()
    shape = (block_y, depth)
    deep = lax.broadcasted_iota(jnp.int32, shape, 1).astype(jnp.float32)
    lane = lax.broadcasted_iota(jnp.int32, shape, 1)
    same = lax.broadcasted_iota(jnp.int32, (block_y, block_y), 0) == (
        lax.broadcasted_iota(jnp.int32, (block_y, block_y), 1)
    )
    for copy in copies:
        copy.wait()
    for slot in range(slots):
        lines = floors[slot].astype(jnp.float32)
        for x in range(block_x):
            line = jnp.broadcast_to(lines[x:x + 1], (block_y, block_y))
            floor = jnp.sum(jnp.where(same, line, 0.0), axis=1, keepdims=True)
            primary = p[slot, x].astype(jnp.float32)
            shear = s[slot, x].astype(jnp.float32)
            square = primary * primary
            stiffness = jnp.where(deep >= floor, square + shear * shear, square)
            coef = speed_factor * stiffness / rho[slot, x].astype(jnp.float32)
            coef = coef.astype(out_ref.dtype)
            for piece in range(x, out_ref.shape[0], near):
                out_ref[piece, 2 * slot] = coef
                out_ref[piece, 2 * slot + 1] = pert[slot, x]
    facts = jnp.where(lane == slots, row_ref[0], 0)
    facts = jnp.where(lane == slots + 1, col_ref[0], facts)
    for slot in range(slots):
        facts = jnp.where(lane == slot, ids[slot], facts)
    facts = facts.astype(jnp.float32).astype(out_ref.dtype)
    for piece in range(out_ref.shape[0]):
        out_ref[piece, 2 * slots] = facts


def pick_kernel(slots, near, pieces_ref, *refs):
    chips = near // 2
    out_refs = refs[:chips][::-1]
    facts_ref, facts, spots, sem = refs[chips:]
    count = facts_ref.shape[0]
    tiles = 2 * slots + 1
    for piece in range(count):
        tile = pieces_ref[piece * tiles + 2 * slots].astype(jnp.float32)
        facts_ref[piece:piece + 1] = tile.astype(jnp.int32)[0:1]
    copy = pltpu.make_async_copy(facts_ref, facts, sem)
    copy.start()
    me = lax.axis_index("shot")
    copy.wait()
    for piece in range(count):
        for slot in range(slots):
            spots[facts[piece, slot]] = piece * tiles + 2 * slot
    for t in range(near):
        shot = me ^ t
        out_ref, start_tile = out_refs[t // 2], t % 2 * APX * APY * 2
        first = facts[shot, slots] * GRID_COLS + facts[shot, slots + 1]
        for x in range(APX):
            found = []
            for y in range(APY):
                spot = spots[first + x * GRID_COLS + y]
                found += [pieces_ref[spot], pieces_ref[spot + 1]]
            for index, tile in enumerate(found):
                out_ref[start_tile + x * APY * 2 + index] = tile


def ends(shape):
    lane = lax.broadcasted_iota(jnp.int32, shape, 1)
    row = lax.broadcasted_iota(jnp.int32, shape, 0)
    return lane == 0, lane == shape[1] - 1, row == 0, row == shape[0] - 1


def laplace(before, here, after, masks):
    lane_0, lane_n, row_0, row_n = masks
    many = len(here)
    depth = here[0].shape[1]
    low = [jnp.where(row_0, 0.0, pltpu.roll(here[-1], 1, 0))] + here[:-1]
    high = here[1:] + [jnp.where(row_n, 0.0, pltpu.roll(here[0], LANES - 1, 0))]
    result = []
    for v in range(many):
        up = jnp.where(lane_0, 0.0, pltpu.roll(here[v], 1, 1))
        down = jnp.where(lane_n, 0.0, pltpu.roll(here[v], depth - 1, 1))
        total = (before[v] + after[v]) + (low[v] + high[v]) + (up + down)
        result.append(total - 6.0 * here[v])
    return result


def registers(ref, x):
    return [ref[x, v] for v in range(ref.shape[1])]


def strided(ref, x):
    many = ref.shape[1] // LANES
    return [ref[x, pl.ds(v, LANES, stride=many)] for v in range(many)]


def sweep(count, fields, body, unroll):
    many = fields[0].shape[1]
    zero = [jnp.zeros(fields[0].shape[2:], jnp.float32)] * many
    first = [(zero, registers(field, 0)) for field in fields]

    def step(x, carry):
        rows = [
            (before, here, registers(field, x + 1))
            for (before, here), field in zip(carry, fields)
        ]
        body(x, rows)
        return [(here, after) for _, here, after in rows]

    lax.fori_loop(0, count, step, first, unroll=unroll)


def start_kernel(prev_ref, now_ref, wave_ref, grad_ref, next_ref, flat, flat_prev, field):
    span_x, span_y, depth = now_ref.shape
    many = span_y // LANES
    masks = ends((LANES, depth))

    def load(x, carry):
        flat[x] = now_ref[x].astype(jnp.float32)
        flat_prev[x] = prev_ref[x].astype(jnp.float32)
        return carry

    lax.fori_loop(0, span_x, load, 0, unroll=2)

    def order(x, carry):
        rows = strided(flat, x)
        older = strided(flat_prev, x)
        for v in range(many):
            field[x, v] = rows[v]
            wave_ref[x, v] = rows[v]
            next_ref[x, v] = 2.0 * rows[v] - older[v]
        return carry

    lax.fori_loop(0, span_x, order, 0, unroll=2)
    for v in range(many):
        field[span_x, v] = jnp.zeros((LANES, depth), jnp.float32)

    def body(x, rows):
        grads = laplace(*rows[0], masks)
        for v in range(many):
            grad_ref[x, v] = grads[v]

    sweep(span_x, [field], body, 16)


def start(before, current):
    span_x, span_y, depth = before.shape
    many = span_y // LANES
    out = jax.ShapeDtypeStruct((span_x, many, LANES, depth), jnp.float32)
    flat = pltpu.VMEM((span_x, span_y, depth), jnp.float32)
    return pl.pallas_call(
        start_kernel,
        out_shape=(out, out, out),
        in_specs=[vmem()] * 2,
        out_specs=(vmem(),) * 3,
        scratch_shapes=[flat, flat, pltpu.VMEM((span_x + 1, many, LANES, depth), jnp.float32)],
        compiler_params=limit(8),
        cost_estimate=pl.CostEstimate(
            flops=20 * before.size, bytes_accessed=16 * before.size, transcendentals=0
        ),
        name="start",
    )(before, current)


def wave_kernel(near, *refs):
    chips = near // 2
    model_refs = parts(refs[:near])
    u_0, g_0, next_ref = refs[near:near + 3]
    refs = refs[near + 3:]
    out_refs = refs[:chips][::-1]
    kap, con, u_1, u_2, u_3, d_0, d_1, d_2, kb_3, kb_2, kb_1 = refs[chips:chips + 11]
    g_1, g_2, d_3, b_2, b_1, image, result = refs[chips + 11:]
    span_x, many = u_0.shape[:2]
    depth = u_0.shape[3]
    block_y = model_refs[0].shape[1]
    block_x = span_x // APX
    place = lax.axis_index("shot") % near
    masks = ends((LANES, depth))
    each = range(many)
    for field in (u_1, u_2, u_3, d_0, d_1, d_2, kb_3, kb_2, kb_1):
        for v in each:
            field[span_x, v] = jnp.zeros((LANES, depth), jnp.float32)

    for k, model_ref in enumerate(model_refs):
        for x in range(APX):
            at = x * block_x + (place ^ k)
            for y in range(APY):
                rows = pl.ds(y * block_y, block_y)
                tile = 2 * (x * APY + y)
                kap[at, rows] = model_ref[tile].astype(jnp.float32)
                con[at, rows] = speed_factor * model_ref[tile + 1].astype(jnp.float32)

    def forward_0(x, carry):
        kaps, cons, grads = strided(kap, x), strided(con, x), registers(g_0, x)
        older = registers(next_ref, x)
        for v in each:
            d_0[x, v] = cons[v] * grads[v]
            u_1[x, v] = older[v] + kaps[v] * grads[v]
        return carry

    lax.fori_loop(0, span_x, forward_0, 0, unroll=16)

    def forward(u_now, u_prev, d_now, d_prev, u_next, d_next, g_now):
        def body(x, rows):
            waves, deltas = rows
            grads = laplace(*waves, masks)
            spread = laplace(*deltas, masks)
            kaps, cons = strided(kap, x), strided(con, x)
            for v in each:
                value = 2.0 * deltas[1][v] + kaps[v] * spread[v] + cons[v] * grads[v]
                if d_prev is not None:
                    value = value - d_prev[x, v]
                d_next[x, v] = value
                if u_next is None:
                    image[x, v] = grads[v] * value
                    kb_3[x, v] = kaps[v] * value
                else:
                    g_now[x, v] = grads[v]
                    u_next[x, v] = 2.0 * waves[1][v] - u_prev[x, v] + kaps[v] * grads[v]

        sweep(span_x, [u_now, d_now], body, 16)

    forward(u_1, u_0, d_0, None, u_2, d_1, g_1)
    forward(u_2, u_1, d_1, d_0, u_3, d_2, g_2)
    forward(u_3, u_2, d_2, d_1, None, d_3, None)

    def adjoint(kb, b_now, b_after, data, grad, kb_next, b_next):
        def body(x, rows):
            spread = laplace(*rows[0], masks)
            kaps = None if kb_next is None else strided(kap, x)
            for v in each:
                back = 2.0 * b_now[x, v] + spread[v] + data[x, v]
                if b_after is not None:
                    back = back - b_after[x, v]
                total = image[x, v] + grad[x, v] * back
                if kb_next is None:
                    total = (image_scale * total).astype(result.dtype)
                    result[x % block_x, x // block_x * many + v] = total
                else:
                    image[x, v] = total
                    b_next[x, v] = back
                    kb_next[x, v] = kaps[v] * back

        sweep(span_x, [kb], body, 16)

    adjoint(kb_3, d_3, None, d_2, g_2, kb_2, b_2)
    adjoint(kb_2, b_2, d_3, d_1, g_1, kb_1, b_1)
    adjoint(kb_1, b_1, b_2, d_0, g_0, None, None)
    length = result.shape[1]
    for t in range(near):
        out_refs[t // 2][pl.ds(t % 2 * length, length)] = result[place ^ t]


def wave(models, started):
    span_x, many, _, depth = started[0].shape
    near = len(models)
    flat = pltpu.VMEM((span_x, many * LANES, depth), jnp.float32)
    field = pltpu.VMEM((span_x + 1, many, LANES, depth), jnp.float32)
    plain = pltpu.VMEM((span_x, many, LANES, depth), jnp.float32)
    tiles = APX * many
    out = jax.ShapeDtypeStruct((2 * tiles, LANES, depth), jnp.bfloat16)
    terms = pl.pallas_call(
        functools.partial(wave_kernel, near),
        out_shape=(out,) * (near // 2),
        in_specs=[vmem()] * (near + 3),
        out_specs=(vmem(),) * (near // 2),
        scratch_shapes=[flat] * 2 + [field] * 9 + [plain] * 6
        + [pltpu.VMEM((near, tiles, LANES, depth), jnp.bfloat16)],
        compiler_params=limit(20),
        name="wave",
    )(*models, *started)
    return terms[::-1]


def wave_split_depth(models, before, current):
    near = len(models)
    order = (lax.axis_index("shot") % near) ^ jnp.arange(near)
    chips = near // 2
    length = models[0].shape[0] // 2
    pairs = zip(models[:chips][::-1], models[chips:][::-1])
    model = jnp.stack([part for own, other in pairs for part in (own[:length], other[length:])])
    model = model[order]
    span_x, span_y, depth = before.shape
    block_x, tiles, block_y, _ = model.shape
    grids = model.reshape(block_x, APX, APY, 2, block_y, depth).transpose(3, 1, 0, 2, 4, 5)
    grids = grids.reshape(2, span_x, span_y, depth).astype(jnp.float32)
    image = image_scale * propagate(
        grids[0],
        speed_factor * grids[1],
        before.astype(jnp.float32),
        current.astype(jnp.float32),
        laplace_many,
    )
    many = span_y // LANES
    image = image.reshape(APX, block_x, LANES, many, depth).transpose(1, 0, 3, 2, 4)
    image = image.reshape(near, APX * many, LANES, depth).astype(jnp.bfloat16)[order]
    return [jnp.concatenate([image[2 * k], image[2 * k + 1]]) for k in range(chips)]


def stack_kernel(slots, near, facts_ref, *refs):
    terms_refs = parts(refs[:near])
    out_ref, facts, total, lined, sem = refs[near:]
    tiles = terms_refs[0].shape[0]
    wide = tiles // APX
    width = LANES // APY
    grid_rows = total.shape[0] // wide
    copy = pltpu.make_async_copy(facts_ref, facts, sem)
    copy.start()
    me = lax.axis_index("shot")

    def clear(index, carry):
        total[index] = jnp.zeros(total.shape[1:], total.dtype)
        return carry

    lax.fori_loop(0, total.shape[0], clear, 0, unroll=8)
    copy.wait()

    for k, terms_ref in enumerate(terms_refs):
        first = facts[me ^ k, slots] * wide
        rows = pl.ds(facts[me ^ k, slots + 1] * width, LANES)
        sums = [
            total[first + tile, rows] + terms_ref[tile].astype(jnp.float32)
            for tile in range(tiles)
        ]
        for tile in range(tiles):
            total[first + tile, rows] = sums[tile]

    for row in range(grid_rows):
        for part in range(wide):
            for tile in range(total.shape[1] // LANES):
                at = pl.ds(tile * LANES * wide + part, LANES, stride=wide)
                lined[row, at] = total[row * wide + part, tile * LANES:(tile + 1) * LANES]

    def give(owner, carry):
        found = []
        for slot in range(slots):
            block = facts[owner, slot]
            rows = pl.ds(pl.multiple_of(block % GRID_COLS * LANES, LANES), LANES)
            found.append(lined[block // GRID_COLS, rows])
        for slot in range(slots):
            out_ref[owner, slot] = found[slot].astype(out_ref.dtype)
        return carry

    lax.fori_loop(0, out_ref.shape[0], give, 0, unroll=4)


def finish_kernel(sums_ref, out_ref):
    slots, block_x = out_ref.shape[:2]
    for x in range(block_x):
        for slot in range(slots):
            result = sums_ref[x, slot].astype(jnp.float32)
            for piece in range(x + block_x, sums_ref.shape[0], block_x):
                result = result + sums_ref[piece, slot].astype(jnp.float32)
            out_ref[slot, x] = result


def per_device(
    velocity_p,
    velocity_s,
    density,
    perturbation,
    seafloor,
    owner_ids,
    corner_x,
    corner_y,
    wave_prev,
    wave_now,
):
    slots, block_x, block_y, depth = velocity_p.shape
    count = lax.axis_size("shot")
    assert count == 2 * block_x and block_y == LANES
    patch = APX * APY
    split = lax.axis_size("depth") > 1
    if split:
        seafloor = seafloor - lax.axis_index("depth") * depth

    near = block_x
    assert count % near == 0 and near & (near - 1) == 0

    def swap(values):
        own = [
            lax.ppermute(values[k], "shot", [(i, i ^ 2 * k) for i in range(count)])
            if k else values[0]
            for k in range(len(values) - 1, -1, -1)
        ]
        return own + [lax.ppermute(v, "shot", [(i, i ^ 1) for i in range(count)]) for v in own]

    sent = pl.pallas_call(
        prepare_kernel,
        out_shape=jax.ShapeDtypeStruct((count, 2 * slots + 1, block_y, depth), jnp.bfloat16),
        in_specs=[smem()] * 2 + [pl.BlockSpec(memory_space=pltpu.HBM)] * 6,
        out_specs=vmem(),
        scratch_shapes=[
            pltpu.SMEM(owner_ids.shape, jnp.int32),
            pltpu.VMEM(seafloor.shape, jnp.int32),
            *[pltpu.VMEM(velocity_p.shape, jnp.bfloat16) for _ in range(4)],
            pltpu.SemaphoreType.DMA((6,)),
        ],
        name="prepare",
    )(
        corner_x, corner_y, owner_ids, seafloor,
        velocity_p, velocity_s, density, perturbation,
    )
    pieces = lax.all_to_all(sent, "shot", 0, 0, tiled=True)

    if not split:
        started = start(wave_prev[0], wave_now[0])
        pieces, started = lax.optimization_barrier((pieces, started))
    *picked, facts = pl.pallas_call(
        functools.partial(pick_kernel, slots, near),
        out_shape=(
            *[jax.ShapeDtypeStruct((patch * 4, block_y, depth), jnp.bfloat16)] * (near // 2),
            jax.ShapeDtypeStruct((count, depth), jnp.int32),
        ),
        in_specs=[vmem()],
        out_specs=(vmem(),) * (near // 2 + 1),
        scratch_shapes=[
            pltpu.SMEM((count, depth), jnp.int32),
            pltpu.SMEM((count * slots,), jnp.int32),
            pltpu.SemaphoreType.DMA,
        ],
        compiler_params=limit(3),
        name="pick",
    )(pieces.reshape(count * (2 * slots + 1), block_y, depth))
    models = swap(picked[::-1])

    if split:
        terms = wave_split_depth(models, wave_prev[0], wave_now[0])
    else:
        terms = wave(models, started)
    terms = swap(terms)

    grid_rows = count * slots // GRID_COLS
    wide = terms[0].shape[0] // 2 // APX
    sums = pl.pallas_call(
        functools.partial(stack_kernel, slots, near),
        out_shape=jax.ShapeDtypeStruct((count, slots, block_y, depth), jnp.bfloat16),
        in_specs=[vmem()] * (near + 1),
        out_specs=vmem(),
        scratch_shapes=[
            pltpu.SMEM(facts.shape, jnp.int32),
            pltpu.VMEM((grid_rows * wide, GRID_COLS * LANES // APY, depth), jnp.float32),
            pltpu.VMEM((grid_rows, GRID_COLS * block_y, depth), jnp.float32),
            pltpu.SemaphoreType.DMA,
        ],
        compiler_params=limit(3),
        name="stack",
    )(facts, *terms)
    sums = lax.all_to_all(sums, "shot", 0, 0, tiled=True)
    return pl.pallas_call(
        finish_kernel,
        out_shape=jax.ShapeDtypeStruct(velocity_p.shape, jnp.float32),
        in_specs=[vmem()],
        out_specs=vmem(),
        compiler_params=limit(2),
        name="finish",
    )(sums)


def solution(mesh):
    in_specs = (
        P(("grp", "shot"), None, None, "depth"),
        P(("grp", "shot"), None, None, "depth"),
        P(("grp", "shot"), None, None, "depth"),
        P(("grp", "shot"), None, None, "depth"),
        P(("grp", "shot"), None, None),
        P(("grp", "shot")),
        P(("grp", "shot")),
        P(("grp", "shot")),
        P(("grp", "shot"), None, None, "depth"),
        P(("grp", "shot"), None, None, "depth"),
    )
    out_specs = P(("grp", "shot"), None, None, "depth")
    return jax.shard_map(
        per_device, mesh=mesh, in_specs=in_specs, out_specs=out_specs, check_vma=False
    )
```

```python
import functools

import jax
import jax.numpy as jnp
from jax import lax
from jax.experimental import pallas as pl
from jax.experimental.pallas import tpu as pltpu
from jax.sharding import PartitionSpec as P

APX = 4
APY = 4
STEPS = 4
GRID_COLS = 8
LANES = 8

speed_factor = 0.28
image_scale = 0.01


def with_halo(block, sides, width):
    for axis, dim in sides:
        count = lax.axis_size(axis)
        forward = [(i, i + 1) for i in range(count - 1)]
        backward = [(target, source) for source, target in forward]
        low = lax.ppermute(
            lax.slice_in_dim(block, block.shape[dim] - width, None, axis=dim), axis, forward
        )
        high = lax.ppermute(lax.slice_in_dim(block, 0, width, axis=dim), axis, backward)
        block = jnp.concatenate([low, block, high], axis=dim)
    return block


def laplace_many(fields):
    stacked = jnp.stack(fields)
    padded = with_halo(stacked.astype(jnp.bfloat16), (("depth", 3),), 1).astype(stacked.dtype)
    padded = jnp.pad(padded, ((0, 0), (1, 1), (1, 1), (0, 0)))
    beside = padded[:, 2:, 1:-1, 1:-1] + padded[:, :-2, 1:-1, 1:-1]
    beside = beside + padded[:, 1:-1, 2:, 1:-1] + padded[:, 1:-1, :-2, 1:-1]
    beside = beside + padded[:, 1:-1, 1:-1, 2:] + padded[:, 1:-1, 1:-1, :-2]
    result = beside - 6.0 * stacked
    return [result[index] for index in range(len(fields))]


def propagate(kappa, contrast, before, current, apply):
    grads = []
    datas = []
    grad_now = apply([current])[0]
    delta_prev = jnp.zeros_like(current)
    delta_now = contrast * grad_now
    grads.append(grad_now)
    datas.append(delta_now)
    before, current = (current, 2.0 * current - before + kappa * grad_now)
    for step in range(1, STEPS):
        grad_now, spread = apply([current, delta_now])
        delta_next = 2.0 * delta_now - delta_prev + kappa * spread + contrast * grad_now
        grads.append(grad_now)
        datas.append(delta_next)
        delta_prev, delta_now = (delta_now, delta_next)
        if step + 1 < STEPS:
            before, current = (current, 2.0 * current - before + kappa * grad_now)
    back = datas[STEPS - 1]
    back_after = jnp.zeros_like(back)
    image = grads[STEPS - 1] * back
    for step in range(STEPS - 2, -1, -1):
        spread = apply([kappa * back])
        back_new = 2.0 * back - back_after + spread[0] + datas[step]
        image = image + grads[step] * back_new
        back_after, back = (back, back_new)
    return image


def limit(mebibytes):
    return pltpu.CompilerParams(vmem_limit_bytes=mebibytes * 2**20)


def chip_place(near):
    return lax.axis_index("shot") // 2 % near


def parts(refs):
    chips = len(refs) // 2
    own, other = refs[:chips][::-1], refs[chips:][::-1]
    length = refs[0].shape[0] // 2
    return [
        ref.at[pl.ds(side * length, length)]
        for pair in zip(own, other)
        for side, ref in enumerate(pair)
    ]


def vmem():
    return pl.BlockSpec(memory_space=pltpu.VMEM)


def smem():
    return pl.BlockSpec(memory_space=pltpu.SMEM)


def prepare_kernel(near, row_ref, col_ref, *refs):
    ids_hbm, floor_hbm, p_hbm, s_hbm, rho_hbm, pert_hbm = refs[:6]
    out_refs = refs[6:6 + near]
    ids, floors, p, s, rho, pert, coef, sems = refs[6 + near:]
    slots, block_x, block_y, depth = p.shape
    copies = [
        pltpu.make_async_copy(source, target, sems.at[index])
        for index, (source, target) in enumerate(
            [(p_hbm, p), (s_hbm, s), (rho_hbm, rho), (floor_hbm, floors), (pert_hbm, pert),
             (ids_hbm, ids)]
        )
    ]
    for copy in copies:
        copy.start()
    shape = (block_y, depth)
    deep = lax.broadcasted_iota(jnp.int32, shape, 1).astype(jnp.float32)
    lane = lax.broadcasted_iota(jnp.int32, shape, 1)
    same = lax.broadcasted_iota(jnp.int32, (block_y, block_y), 0) == (
        lax.broadcasted_iota(jnp.int32, (block_y, block_y), 1)
    )
    place = chip_place(near)
    for copy in copies:
        copy.wait()
    for slot in range(slots):
        lines = floors[slot].astype(jnp.float32)
        for x in range(block_x):
            line = jnp.broadcast_to(lines[x:x + 1], (block_y, block_y))
            floor = jnp.sum(jnp.where(same, line, 0.0), axis=1, keepdims=True)
            primary = p[slot, x].astype(jnp.float32)
            shear = s[slot, x].astype(jnp.float32)
            square = primary * primary
            stiffness = jnp.where(deep >= floor, square + shear * shear, square)
            value = speed_factor * stiffness / rho[slot, x].astype(jnp.float32)
            coef[slot, x] = value.astype(coef.dtype)
    facts = jnp.where(lane == slots, row_ref[0], 0)
    facts = jnp.where(lane == slots + 1, col_ref[0], facts)
    for slot in range(slots):
        facts = jnp.where(lane == slot, ids[slot], facts)
    facts = facts.astype(jnp.float32).astype(coef.dtype)
    for j, out_ref in enumerate(out_refs):
        for slot in range(slots):
            for r in range(2):
                x = 2 * (place ^ j) + r
                out_ref[4 * slot + 2 * r] = coef[slot, x]
                out_ref[4 * slot + 2 * r + 1] = pert[slot, x]
        out_ref[4 * slots] = facts


def pick_kernel(slots, near, count, *refs):
    own, other = refs[:count // 2][::-1], refs[count // 2:count][::-1]
    piece_refs = [ref for pair in zip(own, other) for ref in pair]
    out_refs = refs[count:count + near][::-1]
    facts_ref, facts, spots, pieces, sem = refs[count + near:]
    tiles = 4 * slots + 1
    for t, piece_ref in enumerate(piece_refs):
        tile = piece_ref[tiles - 1].astype(jnp.float32)
        facts_ref[t:t + 1] = tile.astype(jnp.int32)[0:1]
    copy = pltpu.make_async_copy(facts_ref, facts, sem)
    copy.start()
    for t, piece_ref in enumerate(piece_refs):
        pieces[t * tiles:(t + 1) * tiles] = piece_ref[...]
    copy.wait()
    for t in range(count):
        for slot in range(slots):
            spots[facts[t, slot]] = t * tiles + 4 * slot
    for k, out_ref in enumerate(out_refs):
        first = facts[2 * k, slots] * GRID_COLS + facts[2 * k, slots + 1]
        for x in range(APX):
            found = []
            for y in range(APY):
                spot = spots[first + x * GRID_COLS + y]
                found += [pieces[spot + tile] for tile in range(4)]
            for index, tile in enumerate(found):
                out_ref[x * APY * 4 + index] = tile


def ends(shape):
    lane = lax.broadcasted_iota(jnp.int32, shape, 1)
    row = lax.broadcasted_iota(jnp.int32, shape, 0)
    return lane == 0, lane == shape[1] - 1, row == 0, row == shape[0] - 1


def laplace(before, here, after, masks):
    lane_0, lane_n, row_0, row_n = masks
    many = len(here)
    depth = here[0].shape[1]
    low = [jnp.where(row_0, 0.0, pltpu.roll(here[-1], 1, 0))] + here[:-1]
    high = here[1:] + [jnp.where(row_n, 0.0, pltpu.roll(here[0], LANES - 1, 0))]
    result = []
    for v in range(many):
        up = jnp.where(lane_0, 0.0, pltpu.roll(here[v], 1, 1))
        down = jnp.where(lane_n, 0.0, pltpu.roll(here[v], depth - 1, 1))
        total = (before[v] + after[v]) + (low[v] + high[v]) + (up + down)
        result.append(total - 6.0 * here[v])
    return result


def registers(ref, x):
    return [ref[x, v] for v in range(ref.shape[1])]


def strided(ref, x):
    many = ref.shape[1] // LANES
    return [ref[x, pl.ds(v, LANES, stride=many)] for v in range(many)]


def sweep(count, fields, body, unroll):
    many = fields[0].shape[1]
    zero = [jnp.zeros(fields[0].shape[2:], jnp.float32)] * many
    first = [(zero, registers(field, 0)) for field in fields]

    def step(x, carry):
        rows = [
            (before, here, registers(field, x + 1))
            for (before, here), field in zip(carry, fields)
        ]
        body(x, rows)
        return [(here, after) for _, here, after in rows]

    lax.fori_loop(0, count, step, first, unroll=unroll)


def start_kernel(prev_ref, now_ref, wave_ref, grad_ref, next_ref, flat, flat_prev, field):
    span_x, span_y, depth = now_ref.shape
    many = span_y // LANES
    masks = ends((LANES, depth))

    def load(x, carry):
        flat[x] = now_ref[x].astype(jnp.float32)
        flat_prev[x] = prev_ref[x].astype(jnp.float32)
        return carry

    lax.fori_loop(0, span_x, load, 0, unroll=2)

    def order(x, carry):
        rows = strided(flat, x)
        older = strided(flat_prev, x)
        for v in range(many):
            field[x, v] = rows[v]
            wave_ref[x, v] = rows[v]
            next_ref[x, v] = 2.0 * rows[v] - older[v]
        return carry

    lax.fori_loop(0, span_x, order, 0, unroll=2)
    for v in range(many):
        field[span_x, v] = jnp.zeros((LANES, depth), jnp.float32)

    def body(x, rows):
        grads = laplace(*rows[0], masks)
        for v in range(many):
            grad_ref[x, v] = grads[v]

    sweep(span_x, [field], body, 16)


def start(before, current):
    span_x, span_y, depth = before.shape
    many = span_y // LANES
    out = jax.ShapeDtypeStruct((span_x, many, LANES, depth), jnp.float32)
    flat = pltpu.VMEM((span_x, span_y, depth), jnp.float32)
    return pl.pallas_call(
        start_kernel,
        out_shape=(out, out, out),
        in_specs=[vmem()] * 2,
        out_specs=(vmem(),) * 3,
        scratch_shapes=[flat, flat, pltpu.VMEM((span_x + 1, many, LANES, depth), jnp.float32)],
        compiler_params=limit(8),
        cost_estimate=pl.CostEstimate(
            flops=20 * before.size, bytes_accessed=16 * before.size, transcendentals=0
        ),
        name="start",
    )(before, current)


def wave_kernel(near, *refs):
    chips = near // 2
    model_refs = refs[:chips][::-1]
    u_0, g_0, next_ref = refs[chips:chips + 3]
    refs = refs[chips + 3:]
    out_refs = refs[:chips][::-1]
    kap, con, u_1, u_2, u_3, d_0, d_1, d_2, kb_3, kb_2, kb_1 = refs[chips:chips + 11]
    g_1, g_2, d_3, b_2, b_1, image, result = refs[chips + 11:]
    span_x, many = u_0.shape[:2]
    depth = u_0.shape[3]
    block_y = model_refs[0].shape[1]
    block_x = span_x // APX
    place = lax.axis_index("shot") % near
    masks = ends((LANES, depth))
    each = range(many)
    for field in (u_1, u_2, u_3, d_0, d_1, d_2, kb_3, kb_2, kb_1):
        for v in each:
            field[span_x, v] = jnp.zeros((LANES, depth), jnp.float32)

    for k, model_ref in enumerate(model_refs):
        for x in range(APX):
            for y in range(APY):
                rows = pl.ds(y * block_y, block_y)
                for r in range(2):
                    at = x * block_x + 2 * (place // 2 ^ k) + r
                    tile = 4 * (x * APY + y) + 2 * r
                    kap[at, rows] = model_ref[tile].astype(jnp.float32)
                    con[at, rows] = speed_factor * model_ref[tile + 1].astype(jnp.float32)

    def forward_0(x, carry):
        kaps, cons, grads = strided(kap, x), strided(con, x), registers(g_0, x)
        older = registers(next_ref, x)
        for v in each:
            d_0[x, v] = cons[v] * grads[v]
            u_1[x, v] = older[v] + kaps[v] * grads[v]
        return carry

    lax.fori_loop(0, span_x, forward_0, 0, unroll=16)

    def forward(u_now, u_prev, d_now, d_prev, u_next, d_next, g_now):
        def body(x, rows):
            waves, deltas = rows
            grads = laplace(*waves, masks)
            spread = laplace(*deltas, masks)
            kaps, cons = strided(kap, x), strided(con, x)
            for v in each:
                value = 2.0 * deltas[1][v] + kaps[v] * spread[v] + cons[v] * grads[v]
                if d_prev is not None:
                    value = value - d_prev[x, v]
                d_next[x, v] = value
                if u_next is None:
                    image[x, v] = grads[v] * value
                    kb_3[x, v] = kaps[v] * value
                else:
                    g_now[x, v] = grads[v]
                    u_next[x, v] = 2.0 * waves[1][v] - u_prev[x, v] + kaps[v] * grads[v]

        sweep(span_x, [u_now, d_now], body, 16)

    forward(u_1, u_0, d_0, None, u_2, d_1, g_1)
    forward(u_2, u_1, d_1, d_0, u_3, d_2, g_2)
    forward(u_3, u_2, d_2, d_1, None, d_3, None)

    def adjoint(kb, b_now, b_after, data, grad, kb_next, b_next):
        def body(x, rows):
            spread = laplace(*rows[0], masks)
            kaps = None if kb_next is None else strided(kap, x)
            for v in each:
                back = 2.0 * b_now[x, v] + spread[v] + data[x, v]
                if b_after is not None:
                    back = back - b_after[x, v]
                total = image[x, v] + grad[x, v] * back
                if kb_next is None:
                    total = (image_scale * total).astype(result.dtype)
                    result[x % block_x, x // block_x * many + v] = total
                else:
                    image[x, v] = total
                    b_next[x, v] = back
                    kb_next[x, v] = kaps[v] * back

        sweep(span_x, [kb], body, 16)

    adjoint(kb_3, d_3, None, d_2, g_2, kb_2, b_2)
    adjoint(kb_2, b_2, d_3, d_1, g_1, kb_1, b_1)
    adjoint(kb_1, b_1, b_2, d_0, g_0, None, None)
    length = result.shape[1]
    for t in range(near):
        out_refs[t // 2][pl.ds(t % 2 * length, length)] = result[place ^ t]


def wave(models, started):
    span_x, many, _, depth = started[0].shape
    near = 2 * len(models)
    flat = pltpu.VMEM((span_x, many * LANES, depth), jnp.float32)
    field = pltpu.VMEM((span_x + 1, many, LANES, depth), jnp.float32)
    plain = pltpu.VMEM((span_x, many, LANES, depth), jnp.float32)
    tiles = APX * many
    out = jax.ShapeDtypeStruct((2 * tiles, LANES, depth), jnp.bfloat16)
    terms = pl.pallas_call(
        functools.partial(wave_kernel, near),
        out_shape=(out,) * (near // 2),
        in_specs=[vmem()] * (near // 2 + 3),
        out_specs=(vmem(),) * (near // 2),
        scratch_shapes=[flat] * 2 + [field] * 9 + [plain] * 6
        + [pltpu.VMEM((near, tiles, LANES, depth), jnp.bfloat16)],
        compiler_params=limit(20),
        name="wave",
    )(*models, *started)
    return terms[::-1]


def wave_split_depth(models, before, current):
    chips = len(models)
    near = 2 * chips
    order = (lax.axis_index("shot") % near) ^ jnp.arange(near)
    model = jnp.stack(models[::-1])[chip_place(chips) ^ jnp.arange(chips)]
    span_x, span_y, depth = before.shape
    block_x, block_y = 2 * chips, model.shape[2]
    grids = model.reshape(chips, APX, APY, 2, 2, block_y, depth).transpose(4, 1, 0, 3, 2, 5, 6)
    grids = grids.reshape(2, span_x, span_y, depth).astype(jnp.float32)
    image = image_scale * propagate(
        grids[0],
        speed_factor * grids[1],
        before.astype(jnp.float32),
        current.astype(jnp.float32),
        laplace_many,
    )
    many = span_y // LANES
    image = image.reshape(APX, block_x, LANES, many, depth).transpose(1, 0, 3, 2, 4)
    image = image.reshape(near, APX * many, LANES, depth).astype(jnp.bfloat16)[order]
    return [jnp.concatenate([image[2 * k], image[2 * k + 1]]) for k in range(chips)]


def stack_kernel(slots, near, facts_ref, *refs):
    terms_refs = parts(refs[:near])
    out_ref, facts, total, lined, sem = refs[near:]
    tiles = terms_refs[0].shape[0]
    wide = tiles // APX
    width = LANES // APY
    grid_rows = total.shape[0] // wide
    copy = pltpu.make_async_copy(facts_ref, facts, sem)
    copy.start()
    me = lax.axis_index("shot")

    def clear(index, carry):
        total[index] = jnp.zeros(total.shape[1:], total.dtype)
        return carry

    lax.fori_loop(0, total.shape[0], clear, 0, unroll=8)
    copy.wait()

    for k, terms_ref in enumerate(terms_refs):
        first = facts[k, slots] * wide
        rows = pl.ds(facts[k, slots + 1] * width, LANES)
        sums = [
            total[first + tile, rows] + terms_ref[tile].astype(jnp.float32)
            for tile in range(tiles)
        ]
        for tile in range(tiles):
            total[first + tile, rows] = sums[tile]

    for row in range(grid_rows):
        for part in range(wide):
            for tile in range(total.shape[1] // LANES):
                at = pl.ds(tile * LANES * wide + part, LANES, stride=wide)
                lined[row, at] = total[row * wide + part, tile * LANES:(tile + 1) * LANES]

    def give(owner, carry):
        found = []
        for slot in range(slots):
            block = facts[me ^ owner, slot]
            rows = pl.ds(pl.multiple_of(block % GRID_COLS * LANES, LANES), LANES)
            found.append(lined[block // GRID_COLS, rows])
        for slot in range(slots):
            out_ref[owner, slot] = found[slot].astype(out_ref.dtype)
        return carry

    lax.fori_loop(0, out_ref.shape[0], give, 0, unroll=4)


def finish_kernel(sums_ref, out_ref):
    slots, block_x = out_ref.shape[:2]
    for x in range(block_x):
        for slot in range(slots):
            result = sums_ref[x, slot].astype(jnp.float32)
            for piece in range(x + block_x, sums_ref.shape[0], block_x):
                result = result + sums_ref[piece, slot].astype(jnp.float32)
            out_ref[slot, x] = result


def per_device(
    velocity_p,
    velocity_s,
    density,
    perturbation,
    seafloor,
    owner_ids,
    corner_x,
    corner_y,
    wave_prev,
    wave_now,
):
    slots, block_x, block_y, depth = velocity_p.shape
    count = lax.axis_size("shot")
    assert count == 2 * block_x and block_y == LANES
    patch = APX * APY
    split = lax.axis_size("depth") > 1
    if split:
        seafloor = seafloor - lax.axis_index("depth") * depth

    chips = count // 2
    near = block_x // 2
    assert chips % near == 0 and chips & (chips - 1) == 0

    def swap(values):
        return [
            lax.ppermute(values[k], "shot", [(i, i ^ 2 * k) for i in range(count)])
            if k else values[0]
            for k in range(len(values) - 1, -1, -1)
        ]

    def shared(values):
        return values + [
            lax.ppermute(value, "shot", [(i, i ^ 1) for i in range(count)]) for value in values
        ]

    out = jax.ShapeDtypeStruct((4 * slots + 1, block_y, depth), jnp.bfloat16)
    sent = pl.pallas_call(
        functools.partial(prepare_kernel, near),
        out_shape=(out,) * near,
        in_specs=[smem()] * 2 + [pl.BlockSpec(memory_space=pltpu.HBM)] * 6,
        out_specs=(vmem(),) * near,
        scratch_shapes=[
            pltpu.SMEM(owner_ids.shape, jnp.int32),
            pltpu.VMEM(seafloor.shape, jnp.int32),
            *[pltpu.VMEM(velocity_p.shape, jnp.bfloat16) for _ in range(5)],
            pltpu.SemaphoreType.DMA((6,)),
        ],
        name="prepare",
    )(
        corner_x, corner_y, owner_ids, seafloor,
        velocity_p, velocity_s, density, perturbation,
    )
    pieces = shared(swap([sent[k % near] for k in range(chips)]))
    *picked, facts = pl.pallas_call(
        functools.partial(pick_kernel, slots, near, count),
        out_shape=(
            *[jax.ShapeDtypeStruct((patch * 4, block_y, depth), jnp.bfloat16)] * near,
            jax.ShapeDtypeStruct((count, depth), jnp.int32),
        ),
        in_specs=[vmem()] * count,
        out_specs=(vmem(),) * (near + 1),
        scratch_shapes=[
            pltpu.SMEM((count, depth), jnp.int32),
            pltpu.SMEM((count * slots,), jnp.int32),
            pltpu.VMEM((count * (4 * slots + 1), block_y, depth), jnp.bfloat16),
            pltpu.SemaphoreType.DMA,
        ],
        compiler_params=limit(3),
        name="pick",
    )(*pieces)
    models = swap(picked[::-1])

    if split:
        terms = wave_split_depth(models, wave_prev[0], wave_now[0])
    else:
        terms = wave(models, start(wave_prev[0], wave_now[0]))
    terms = shared(swap(terms))

    grid_rows = count * slots // GRID_COLS
    wide = terms[0].shape[0] // 2 // APX
    sums = pl.pallas_call(
        functools.partial(stack_kernel, slots, 2 * near),
        out_shape=jax.ShapeDtypeStruct((count, slots, block_y, depth), jnp.bfloat16),
        in_specs=[vmem()] * (2 * near + 1),
        out_specs=vmem(),
        scratch_shapes=[
            pltpu.SMEM(facts.shape, jnp.int32),
            pltpu.VMEM((grid_rows * wide, GRID_COLS * LANES // APY, depth), jnp.float32),
            pltpu.VMEM((grid_rows, GRID_COLS * block_y, depth), jnp.float32),
            pltpu.SemaphoreType.DMA,
        ],
        compiler_params=limit(3),
        name="stack",
    )(facts, *terms)
    sums = lax.all_to_all(sums, "shot", 0, 0, tiled=True)
    return pl.pallas_call(
        finish_kernel,
        out_shape=jax.ShapeDtypeStruct(velocity_p.shape, jnp.float32),
        in_specs=[vmem()],
        out_specs=vmem(),
        compiler_params=limit(2),
        name="finish",
    )(sums)


def solution(mesh):
    in_specs = (
        P(("grp", "shot"), None, None, "depth"),
        P(("grp", "shot"), None, None, "depth"),
        P(("grp", "shot"), None, None, "depth"),
        P(("grp", "shot"), None, None, "depth"),
        P(("grp", "shot"), None, None),
        P(("grp", "shot")),
        P(("grp", "shot")),
        P(("grp", "shot")),
        P(("grp", "shot"), None, None, "depth"),
        P(("grp", "shot"), None, None, "depth"),
    )
    out_specs = P(("grp", "shot"), None, None, "depth")
    return jax.shard_map(
        per_device, mesh=mesh, in_specs=in_specs, out_specs=out_specs, check_vma=False
    )
```

```python
import functools

import jax
import jax.numpy as jnp
from jax import lax
from jax.experimental import pallas as pl
from jax.experimental.pallas import tpu as pltpu
from jax.sharding import PartitionSpec as P

APX = 4
APY = 4
STEPS = 4
GRID_COLS = 8
LANES = 8

speed_factor = 0.28
image_scale = 0.01


def with_halo(block, sides, width):
    for axis, dim in sides:
        count = lax.axis_size(axis)
        forward = [(i, i + 1) for i in range(count - 1)]
        backward = [(target, source) for source, target in forward]
        low = lax.ppermute(
            lax.slice_in_dim(block, block.shape[dim] - width, None, axis=dim), axis, forward
        )
        high = lax.ppermute(lax.slice_in_dim(block, 0, width, axis=dim), axis, backward)
        block = jnp.concatenate([low, block, high], axis=dim)
    return block


def laplace_many(fields):
    stacked = jnp.stack(fields)
    padded = with_halo(stacked.astype(jnp.bfloat16), (("depth", 3),), 1).astype(stacked.dtype)
    padded = jnp.pad(padded, ((0, 0), (1, 1), (1, 1), (0, 0)))
    beside = padded[:, 2:, 1:-1, 1:-1] + padded[:, :-2, 1:-1, 1:-1]
    beside = beside + padded[:, 1:-1, 2:, 1:-1] + padded[:, 1:-1, :-2, 1:-1]
    beside = beside + padded[:, 1:-1, 1:-1, 2:] + padded[:, 1:-1, 1:-1, :-2]
    result = beside - 6.0 * stacked
    return [result[index] for index in range(len(fields))]


def propagate(kappa, contrast, before, current, apply):
    grads = []
    datas = []
    grad_now = apply([current])[0]
    delta_prev = jnp.zeros_like(current)
    delta_now = contrast * grad_now
    grads.append(grad_now)
    datas.append(delta_now)
    before, current = (current, 2.0 * current - before + kappa * grad_now)
    for step in range(1, STEPS):
        grad_now, spread = apply([current, delta_now])
        delta_next = 2.0 * delta_now - delta_prev + kappa * spread + contrast * grad_now
        grads.append(grad_now)
        datas.append(delta_next)
        delta_prev, delta_now = (delta_now, delta_next)
        if step + 1 < STEPS:
            before, current = (current, 2.0 * current - before + kappa * grad_now)
    back = datas[STEPS - 1]
    back_after = jnp.zeros_like(back)
    image = grads[STEPS - 1] * back
    for step in range(STEPS - 2, -1, -1):
        spread = apply([kappa * back])
        back_new = 2.0 * back - back_after + spread[0] + datas[step]
        image = image + grads[step] * back_new
        back_after, back = (back, back_new)
    return image


def limit(mebibytes):
    return pltpu.CompilerParams(vmem_limit_bytes=mebibytes * 2**20)


def chip_place(near):
    return lax.axis_index("shot") // 2 % near


def parts(refs):
    chips = len(refs) // 2
    own, other = refs[:chips][::-1], refs[chips:][::-1]
    length = refs[0].shape[0] // 2
    return [
        ref.at[pl.ds(side * length, length)]
        for pair in zip(own, other)
        for side, ref in enumerate(pair)
    ]


def vmem():
    return pl.BlockSpec(memory_space=pltpu.VMEM)


def smem():
    return pl.BlockSpec(memory_space=pltpu.SMEM)


def prepare_kernel(
    row_ref, col_ref, ids_hbm, floor_hbm, p_hbm, s_hbm, rho_hbm, pert_hbm, out_ref,
    ids, floors, p, s, rho, pert, sems,
):
    slots, block_x, block_y, depth = p.shape
    near = block_x
    copies = [
        pltpu.make_async_copy(source, target, sems.at[index])
        for index, (source, target) in enumerate(
            [(p_hbm, p), (s_hbm, s), (rho_hbm, rho), (floor_hbm, floors), (pert_hbm, pert),
             (ids_hbm, ids)]
        )
    ]
    for copy in copies:
        copy.start()
    shape = (block_y, depth)
    deep = lax.broadcasted_iota(jnp.int32, shape, 1).astype(jnp.float32)
    lane = lax.broadcasted_iota(jnp.int32, shape, 1)
    same = lax.broadcasted_iota(jnp.int32, (block_y, block_y), 0) == (
        lax.broadcasted_iota(jnp.int32, (block_y, block_y), 1)
    )
    for copy in copies:
        copy.wait()
    for slot in range(slots):
        lines = floors[slot].astype(jnp.float32)
        for x in range(block_x):
            line = jnp.broadcast_to(lines[x:x + 1], (block_y, block_y))
            floor = jnp.sum(jnp.where(same, line, 0.0), axis=1, keepdims=True)
            primary = p[slot, x].astype(jnp.float32)
            shear = s[slot, x].astype(jnp.float32)
            square = primary * primary
            stiffness = jnp.where(deep >= floor, square + shear * shear, square)
            coef = speed_factor * stiffness / rho[slot, x].astype(jnp.float32)
            coef = coef.astype(out_ref.dtype)
            for piece in range(x, out_ref.shape[0], near):
                out_ref[piece, 2 * slot] = coef
                out_ref[piece, 2 * slot + 1] = pert[slot, x]
    facts = jnp.where(lane == slots, row_ref[0], 0)
    facts = jnp.where(lane == slots + 1, col_ref[0], facts)
    for slot in range(slots):
        facts = jnp.where(lane == slot, ids[slot], facts)
    facts = facts.astype(jnp.float32).astype(out_ref.dtype)
    for piece in range(out_ref.shape[0]):
        out_ref[piece, 2 * slots] = facts


def pick_kernel(slots, near, pieces_ref, *refs):
    chips = near // 2
    out_refs = refs[:chips][::-1]
    facts_ref, facts, spots, sem = refs[chips:]
    count = facts_ref.shape[0]
    tiles = 2 * slots + 1
    for piece in range(count):
        tile = pieces_ref[piece * tiles + 2 * slots].astype(jnp.float32)
        facts_ref[piece:piece + 1] = tile.astype(jnp.int32)[0:1]
    copy = pltpu.make_async_copy(facts_ref, facts, sem)
    copy.start()
    me = lax.axis_index("shot")
    copy.wait()
    for piece in range(count):
        for slot in range(slots):
            spots[facts[piece, slot]] = piece * tiles + 2 * slot
    for t in range(near):
        shot = me ^ t
        out_ref, start_tile = out_refs[t // 2], t % 2 * APX * APY * 2
        first = facts[shot, slots] * GRID_COLS + facts[shot, slots + 1]
        for x in range(APX):
            found = []
            for y in range(APY):
                spot = spots[first + x * GRID_COLS + y]
                found += [pieces_ref[spot], pieces_ref[spot + 1]]
            for index, tile in enumerate(found):
                out_ref[start_tile + x * APY * 2 + index] = tile


def ends(shape):
    lane = lax.broadcasted_iota(jnp.int32, shape, 1)
    row = lax.broadcasted_iota(jnp.int32, shape, 0)
    return lane == 0, lane == shape[1] - 1, row == 0, row == shape[0] - 1


def laplace(before, here, after, masks):
    lane_0, lane_n, row_0, row_n = masks
    many = len(here)
    depth = here[0].shape[1]
    low = [jnp.where(row_0, 0.0, pltpu.roll(here[-1], 1, 0))] + here[:-1]
    high = here[1:] + [jnp.where(row_n, 0.0, pltpu.roll(here[0], LANES - 1, 0))]
    result = []
    for v in range(many):
        up = jnp.where(lane_0, 0.0, pltpu.roll(here[v], 1, 1))
        down = jnp.where(lane_n, 0.0, pltpu.roll(here[v], depth - 1, 1))
        total = (before[v] + after[v]) + (low[v] + high[v]) + (up + down)
        result.append(total - 6.0 * here[v])
    return result


def registers(ref, x):
    return [ref[x, v] for v in range(ref.shape[1])]


def strided(ref, x):
    many = ref.shape[1] // LANES
    return [ref[x, pl.ds(v, LANES, stride=many)] for v in range(many)]


def sweep(count, fields, body, unroll):
    many = fields[0].shape[1]
    zero = [jnp.zeros(fields[0].shape[2:], jnp.float32)] * many
    first = [(zero, registers(field, 0)) for field in fields]

    def step(x, carry):
        rows = [
            (before, here, registers(field, x + 1))
            for (before, here), field in zip(carry, fields)
        ]
        body(x, rows)
        return [(here, after) for _, here, after in rows]

    lax.fori_loop(0, count, step, first, unroll=unroll)


def start_kernel(prev_ref, now_ref, wave_ref, grad_ref, next_ref, flat, flat_prev, field):
    span_x, span_y, depth = now_ref.shape
    many = span_y // LANES
    masks = ends((LANES, depth))

    def load(x, carry):
        flat[x] = now_ref[x].astype(jnp.float32)
        flat_prev[x] = prev_ref[x].astype(jnp.float32)
        return carry

    lax.fori_loop(0, span_x, load, 0, unroll=2)

    def order(x, carry):
        rows = strided(flat, x)
        older = strided(flat_prev, x)
        for v in range(many):
            field[x, v] = rows[v]
            wave_ref[x, v] = rows[v]
            next_ref[x, v] = 2.0 * rows[v] - older[v]
        return carry

    lax.fori_loop(0, span_x, order, 0, unroll=2)
    for v in range(many):
        field[span_x, v] = jnp.zeros((LANES, depth), jnp.float32)

    def body(x, rows):
        grads = laplace(*rows[0], masks)
        for v in range(many):
            grad_ref[x, v] = grads[v]

    sweep(span_x, [field], body, 32)


def start(before, current):
    span_x, span_y, depth = before.shape
    many = span_y // LANES
    out = jax.ShapeDtypeStruct((span_x, many, LANES, depth), jnp.float32)
    flat = pltpu.VMEM((span_x, span_y, depth), jnp.float32)
    return pl.pallas_call(
        start_kernel,
        out_shape=(out, out, out),
        in_specs=[vmem()] * 2,
        out_specs=(vmem(),) * 3,
        scratch_shapes=[flat, flat, pltpu.VMEM((span_x + 1, many, LANES, depth), jnp.float32)],
        compiler_params=limit(8),
        cost_estimate=pl.CostEstimate(
            flops=20 * before.size, bytes_accessed=16 * before.size, transcendentals=0
        ),
        name="start",
    )(before, current)


def wave_kernel(near, *refs):
    chips = near // 2
    model_refs = parts(refs[:near])
    u_0, g_0, next_ref = refs[near:near + 3]
    refs = refs[near + 3:]
    out_refs = refs[:chips][::-1]
    kap, con, u_1, u_2, u_3, d_0, d_1, d_2, kb_3, kb_2, kb_1 = refs[chips:chips + 11]
    g_1, g_2, d_3, b_2, b_1, image, result = refs[chips + 11:]
    span_x, many = u_0.shape[:2]
    depth = u_0.shape[3]
    block_y = model_refs[0].shape[1]
    block_x = span_x // APX
    place = lax.axis_index("shot") % near
    masks = ends((LANES, depth))
    each = range(many)
    for field in (u_1, u_2, u_3, d_0, d_1, d_2, kb_3, kb_2, kb_1):
        for v in each:
            field[span_x, v] = jnp.zeros((LANES, depth), jnp.float32)

    for k, model_ref in enumerate(model_refs):
        for x in range(APX):
            at = x * block_x + (place ^ k)
            for y in range(APY):
                rows = pl.ds(y * block_y, block_y)
                tile = 2 * (x * APY + y)
                kap[at, rows] = model_ref[tile].astype(jnp.float32)
                con[at, rows] = speed_factor * model_ref[tile + 1].astype(jnp.float32)

    def forward_0(x, carry):
        kaps, cons, grads = strided(kap, x), strided(con, x), registers(g_0, x)
        older = registers(next_ref, x)
        for v in each:
            d_0[x, v] = cons[v] * grads[v]
            u_1[x, v] = older[v] + kaps[v] * grads[v]
        return carry

    lax.fori_loop(0, span_x, forward_0, 0, unroll=32)

    def forward(u_now, u_prev, d_now, d_prev, u_next, d_next, g_now):
        def body(x, rows):
            waves, deltas = rows
            grads = laplace(*waves, masks)
            spread = laplace(*deltas, masks)
            kaps, cons = strided(kap, x), strided(con, x)
            for v in each:
                value = 2.0 * deltas[1][v] + kaps[v] * spread[v] + cons[v] * grads[v]
                if d_prev is not None:
                    value = value - d_prev[x, v]
                d_next[x, v] = value
                if u_next is None:
                    image[x, v] = grads[v] * value
                    kb_3[x, v] = kaps[v] * value
                else:
                    g_now[x, v] = grads[v]
                    u_next[x, v] = 2.0 * waves[1][v] - u_prev[x, v] + kaps[v] * grads[v]

        sweep(span_x, [u_now, d_now], body, 32)

    forward(u_1, u_0, d_0, None, u_2, d_1, g_1)
    forward(u_2, u_1, d_1, d_0, u_3, d_2, g_2)
    forward(u_3, u_2, d_2, d_1, None, d_3, None)

    def adjoint(kb, b_now, b_after, data, grad, kb_next, b_next):
        def body(x, rows):
            spread = laplace(*rows[0], masks)
            kaps = None if kb_next is None else strided(kap, x)
            for v in each:
                back = 2.0 * b_now[x, v] + spread[v] + data[x, v]
                if b_after is not None:
                    back = back - b_after[x, v]
                total = image[x, v] + grad[x, v] * back
                if kb_next is None:
                    total = (image_scale * total).astype(result.dtype)
                    result[x % block_x // 2, (x % 2 * APX + x // block_x) * many + v] = total
                else:
                    image[x, v] = total
                    b_next[x, v] = back
                    kb_next[x, v] = kaps[v] * back

        sweep(span_x, [kb], body, 32)

    adjoint(kb_3, d_3, None, d_2, g_2, kb_2, b_2)
    adjoint(kb_2, b_2, d_3, d_1, g_1, kb_1, b_1)
    adjoint(kb_1, b_1, b_2, d_0, g_0, None, None)
    for k, out_ref in enumerate(out_refs):
        out_ref[...] = result[place // 2 ^ k]


def wave(models, started):
    span_x, many, _, depth = started[0].shape
    near = len(models)
    flat = pltpu.VMEM((span_x, many * LANES, depth), jnp.float32)
    field = pltpu.VMEM((span_x + 1, many, LANES, depth), jnp.float32)
    plain = pltpu.VMEM((span_x, many, LANES, depth), jnp.float32)
    tiles = APX * many
    out = jax.ShapeDtypeStruct((2 * tiles, LANES, depth), jnp.bfloat16)
    terms = pl.pallas_call(
        functools.partial(wave_kernel, near),
        out_shape=(out,) * (near // 2),
        in_specs=[vmem()] * (near + 3),
        out_specs=(vmem(),) * (near // 2),
        scratch_shapes=[flat] * 2 + [field] * 9 + [plain] * 6
        + [pltpu.VMEM((near // 2, 2 * tiles, LANES, depth), jnp.bfloat16)],
        compiler_params=limit(20),
        name="wave",
    )(*models, *started)
    return terms[::-1]


def wave_split_depth(models, before, current):
    near = len(models)
    order = (lax.axis_index("shot") % near) ^ jnp.arange(near)
    chips = near // 2
    length = models[0].shape[0] // 2
    pairs = zip(models[:chips][::-1], models[chips:][::-1])
    model = jnp.stack([part for own, other in pairs for part in (own[:length], other[length:])])
    model = model[order]
    span_x, span_y, depth = before.shape
    block_x, tiles, block_y, _ = model.shape
    grids = model.reshape(block_x, APX, APY, 2, block_y, depth).transpose(3, 1, 0, 2, 4, 5)
    grids = grids.reshape(2, span_x, span_y, depth).astype(jnp.float32)
    image = image_scale * propagate(
        grids[0],
        speed_factor * grids[1],
        before.astype(jnp.float32),
        current.astype(jnp.float32),
        laplace_many,
    )
    many = span_y // LANES
    image = image.reshape(APX, chips, 2, LANES, many, depth).transpose(1, 2, 0, 4, 3, 5)
    image = image.reshape(chips, 2 * APX * many, LANES, depth).astype(jnp.bfloat16)
    image = image[chip_place(chips) ^ jnp.arange(chips)]
    return [image[k] for k in range(chips)]


def stack_kernel(slots, near, facts_ref, *refs):
    terms_refs = refs[:near][::-1]
    mine_ref, other_ref, facts, total, lined, sem = refs[near:]
    count = facts_ref.shape[0]
    half = terms_refs[0].shape[0] // 2
    wide = half // APX
    width = LANES // APY
    grid_rows = total.shape[1] // wide
    copy = pltpu.make_async_copy(facts_ref, facts, sem)
    copy.start()
    me = lax.axis_index("shot")

    def clear(index, carry):
        for r in range(2):
            total[r, index] = jnp.zeros(total.shape[2:], total.dtype)
        return carry

    lax.fori_loop(0, total.shape[1], clear, 0, unroll=8)
    copy.wait()
    for k, terms_ref in enumerate(terms_refs):
        first = facts[me ^ 2 * k, slots] * wide
        rows = pl.ds(facts[me ^ 2 * k, slots + 1] * width, LANES)
        for r in range(2):
            sums = [
                total[r, first + tile, rows] + terms_ref[r * half + tile].astype(jnp.float32)
                for tile in range(half)
            ]
            for tile in range(half):
                total[r, first + tile, rows] = sums[tile]

    def line(row, carry):
        for r in range(2):
            for part in range(wide):
                for tile in range(total.shape[2] // LANES):
                    at = pl.ds(tile * LANES * wide + part, LANES, stride=wide)
                    lined[r, row, at] = total[
                        r, row * wide + part, tile * LANES:(tile + 1) * LANES
                    ]
        return carry

    lax.fori_loop(0, grid_rows, line, 0, unroll=4)

    def give(chip, carry):
        for own, out_ref in enumerate((mine_ref, other_ref)):
            found = []
            for slot in range(slots):
                block = facts[2 * chip + (me + own) % 2, slot]
                rows = pl.ds(pl.multiple_of(block % GRID_COLS * LANES, LANES), LANES)
                found += [lined[r, block // GRID_COLS, rows] for r in range(2)]
            for index, tile in enumerate(found):
                out_ref[chip, index] = tile.astype(out_ref.dtype)
        return carry

    lax.fori_loop(0, count // 2, give, 0, unroll=2)


def join_kernel(mine_ref, other_ref, out_ref):
    for chip in range(out_ref.shape[0]):
        total = mine_ref[chip] + other_ref[chip].astype(jnp.float32)
        out_ref[chip] = total.astype(out_ref.dtype)


def finish_kernel(near, sums_ref, out_ref):
    for place in range(near):
        for slot in range(out_ref.shape[0]):
            for r in range(2):
                result = sums_ref[place, 2 * slot + r].astype(jnp.float32)
                for chip in range(place + near, sums_ref.shape[0], near):
                    result = result + sums_ref[chip, 2 * slot + r].astype(jnp.float32)
                out_ref[slot, 2 * place + r] = result


def per_device(
    velocity_p,
    velocity_s,
    density,
    perturbation,
    seafloor,
    owner_ids,
    corner_x,
    corner_y,
    wave_prev,
    wave_now,
):
    slots, block_x, block_y, depth = velocity_p.shape
    count = lax.axis_size("shot")
    assert count == 2 * block_x and block_y == LANES
    patch = APX * APY
    split = lax.axis_size("depth") > 1
    if split:
        seafloor = seafloor - lax.axis_index("depth") * depth

    near = block_x
    assert count % near == 0 and near & (near - 1) == 0

    def swap(values):
        return [
            lax.ppermute(values[k], "shot", [(i, i ^ 2 * k) for i in range(count)])
            if k else values[0]
            for k in range(len(values) - 1, -1, -1)
        ]

    def across(value):
        return lax.ppermute(value, "shot", [(i, i ^ 1) for i in range(count)])

    sent = pl.pallas_call(
        prepare_kernel,
        out_shape=jax.ShapeDtypeStruct((count, 2 * slots + 1, block_y, depth), jnp.bfloat16),
        in_specs=[smem()] * 2 + [pl.BlockSpec(memory_space=pltpu.HBM)] * 6,
        out_specs=vmem(),
        scratch_shapes=[
            pltpu.SMEM(owner_ids.shape, jnp.int32),
            pltpu.VMEM(seafloor.shape, jnp.int32),
            *[pltpu.VMEM(velocity_p.shape, jnp.bfloat16) for _ in range(4)],
            pltpu.SemaphoreType.DMA((6,)),
        ],
        name="prepare",
    )(
        corner_x, corner_y, owner_ids, seafloor,
        velocity_p, velocity_s, density, perturbation,
    )
    pieces = lax.all_to_all(sent, "shot", 0, 0, tiled=True)

    if not split:
        started = start(wave_prev[0], wave_now[0])
        pieces, started = lax.optimization_barrier((pieces, started))
    *picked, facts = pl.pallas_call(
        functools.partial(pick_kernel, slots, near),
        out_shape=(
            *[jax.ShapeDtypeStruct((patch * 4, block_y, depth), jnp.bfloat16)] * (near // 2),
            jax.ShapeDtypeStruct((count, depth), jnp.int32),
        ),
        in_specs=[vmem()],
        out_specs=(vmem(),) * (near // 2 + 1),
        scratch_shapes=[
            pltpu.SMEM((count, depth), jnp.int32),
            pltpu.SMEM((count * slots,), jnp.int32),
            pltpu.SemaphoreType.DMA,
        ],
        compiler_params=limit(3),
        name="pick",
    )(pieces.reshape(count * (2 * slots + 1), block_y, depth))
    models = swap(picked[::-1])
    models = models + [across(value) for value in models]

    if split:
        terms = wave_split_depth(models, wave_prev[0], wave_now[0])
    else:
        terms = wave(models, started)
    terms = swap(terms)

    chips = count // 2
    grid_rows = count * slots // GRID_COLS
    wide = terms[0].shape[0] // 2 // APX
    shape = (chips, 2 * slots, block_y, depth)
    mine, other = pl.pallas_call(
        functools.partial(stack_kernel, slots, near // 2),
        out_shape=(
            jax.ShapeDtypeStruct(shape, jnp.float32), jax.ShapeDtypeStruct(shape, jnp.bfloat16)
        ),
        in_specs=[vmem()] * (near // 2 + 1),
        out_specs=(vmem(), vmem()),
        scratch_shapes=[
            pltpu.SMEM(facts.shape, jnp.int32),
            pltpu.VMEM((2, grid_rows * wide, GRID_COLS * LANES // APY, depth), jnp.float32),
            pltpu.VMEM((2, grid_rows, GRID_COLS * block_y, depth), jnp.float32),
            pltpu.SemaphoreType.DMA,
        ],
        compiler_params=limit(4),
        name="stack",
    )(facts, *terms)
    joined = pl.pallas_call(
        join_kernel,
        out_shape=jax.ShapeDtypeStruct(shape, jnp.bfloat16),
        in_specs=[vmem()] * 2,
        out_specs=vmem(),
        compiler_params=limit(2),
        name="join",
    )(mine, across(other))
    sums = lax.all_to_all(
        joined, "shot", 0, 0, tiled=True,
        axis_index_groups=[list(range(core, count, 2)) for core in range(2)],
    )
    return pl.pallas_call(
        functools.partial(finish_kernel, near // 2),
        out_shape=jax.ShapeDtypeStruct(velocity_p.shape, jnp.float32),
        in_specs=[vmem()],
        out_specs=vmem(),
        compiler_params=limit(2),
        name="finish",
    )(sums)


def solution(mesh):
    in_specs = (
        P(("grp", "shot"), None, None, "depth"),
        P(("grp", "shot"), None, None, "depth"),
        P(("grp", "shot"), None, None, "depth"),
        P(("grp", "shot"), None, None, "depth"),
        P(("grp", "shot"), None, None),
        P(("grp", "shot")),
        P(("grp", "shot")),
        P(("grp", "shot")),
        P(("grp", "shot"), None, None, "depth"),
        P(("grp", "shot"), None, None, "depth"),
    )
    out_specs = P(("grp", "shot"), None, None, "depth")
    return jax.shard_map(
        per_device, mesh=mesh, in_specs=in_specs, out_specs=out_specs, check_vma=False
    )
```

```python
import functools

import jax
import jax.numpy as jnp
from jax import lax
from jax.experimental import pallas as pl
from jax.experimental.pallas import tpu as pltpu
from jax.sharding import PartitionSpec as P

APX = 4
APY = 4
STEPS = 4
GRID_COLS = 8
LANES = 8

speed_factor = 0.28
image_scale = 0.01


def with_halo(block, sides, width):
    for axis, dim in sides:
        count = lax.axis_size(axis)
        forward = [(i, i + 1) for i in range(count - 1)]
        backward = [(target, source) for source, target in forward]
        low = lax.ppermute(
            lax.slice_in_dim(block, block.shape[dim] - width, None, axis=dim), axis, forward
        )
        high = lax.ppermute(lax.slice_in_dim(block, 0, width, axis=dim), axis, backward)
        block = jnp.concatenate([low, block, high], axis=dim)
    return block


def laplace_many(fields):
    stacked = jnp.stack(fields)
    padded = with_halo(stacked.astype(jnp.bfloat16), (("depth", 3),), 1).astype(stacked.dtype)
    padded = jnp.pad(padded, ((0, 0), (1, 1), (1, 1), (0, 0)))
    beside = padded[:, 2:, 1:-1, 1:-1] + padded[:, :-2, 1:-1, 1:-1]
    beside = beside + padded[:, 1:-1, 2:, 1:-1] + padded[:, 1:-1, :-2, 1:-1]
    beside = beside + padded[:, 1:-1, 1:-1, 2:] + padded[:, 1:-1, 1:-1, :-2]
    result = beside - 6.0 * stacked
    return [result[index] for index in range(len(fields))]


def propagate(kappa, contrast, before, current, apply):
    grads = []
    datas = []
    grad_now = apply([current])[0]
    delta_prev = jnp.zeros_like(current)
    delta_now = contrast * grad_now
    grads.append(grad_now)
    datas.append(delta_now)
    before, current = (current, 2.0 * current - before + kappa * grad_now)
    for step in range(1, STEPS):
        grad_now, spread = apply([current, delta_now])
        delta_next = 2.0 * delta_now - delta_prev + kappa * spread + contrast * grad_now
        grads.append(grad_now)
        datas.append(delta_next)
        delta_prev, delta_now = (delta_now, delta_next)
        if step + 1 < STEPS:
            before, current = (current, 2.0 * current - before + kappa * grad_now)
    back = datas[STEPS - 1]
    back_after = jnp.zeros_like(back)
    image = grads[STEPS - 1] * back
    for step in range(STEPS - 2, -1, -1):
        spread = apply([kappa * back])
        back_new = 2.0 * back - back_after + spread[0] + datas[step]
        image = image + grads[step] * back_new
        back_after, back = (back, back_new)
    return image


def limit(mebibytes):
    return pltpu.CompilerParams(vmem_limit_bytes=mebibytes * 2**20)


def chip_place(near):
    return lax.axis_index("shot") // 2 % near


def parts(refs, length):
    chips = len(refs) // 2
    own, other = refs[:chips][::-1], refs[chips:][::-1]
    return [
        part for first, second in zip(own, other) for part in (first.at[pl.ds(0, length)], second)
    ]


def vmem():
    return pl.BlockSpec(memory_space=pltpu.VMEM)


def smem():
    return pl.BlockSpec(memory_space=pltpu.SMEM)


def prepare_kernel(
    row_ref, col_ref, ids_hbm, floor_hbm, p_hbm, s_hbm, rho_hbm, pert_hbm, out_ref,
    ids, floors, p, s, rho, pert, sems,
):
    slots, block_x, block_y, depth = p.shape
    near = block_x
    copies = [
        pltpu.make_async_copy(source, target, sems.at[index])
        for index, (source, target) in enumerate(
            [(p_hbm, p), (s_hbm, s), (rho_hbm, rho), (floor_hbm, floors), (pert_hbm, pert),
             (ids_hbm, ids)]
        )
    ]
    for copy in copies:
        copy.start()
    shape = (block_y, depth)
    deep = lax.broadcasted_iota(jnp.int32, shape, 1).astype(jnp.float32)
    lane = lax.broadcasted_iota(jnp.int32, shape, 1)
    same = lax.broadcasted_iota(jnp.int32, (block_y, block_y), 0) == (
        lax.broadcasted_iota(jnp.int32, (block_y, block_y), 1)
    )
    for copy in copies:
        copy.wait()
    for slot in range(slots):
        lines = floors[slot].astype(jnp.float32)
        for x in range(block_x):
            line = jnp.broadcast_to(lines[x:x + 1], (block_y, block_y))
            floor = jnp.sum(jnp.where(same, line, 0.0), axis=1, keepdims=True)
            primary = p[slot, x].astype(jnp.float32)
            shear = s[slot, x].astype(jnp.float32)
            square = primary * primary
            stiffness = jnp.where(deep >= floor, square + shear * shear, square)
            coef = speed_factor * stiffness / rho[slot, x].astype(jnp.float32)
            coef = coef.astype(out_ref.dtype)
            for piece in range(x, out_ref.shape[0], near):
                out_ref[piece, 2 * slot] = coef
                out_ref[piece, 2 * slot + 1] = pert[slot, x]
    facts = jnp.where(lane == slots, row_ref[0], 0)
    facts = jnp.where(lane == slots + 1, col_ref[0], facts)
    for slot in range(slots):
        facts = jnp.where(lane == slot, ids[slot], facts)
    facts = facts.astype(jnp.float32).astype(out_ref.dtype)
    for piece in range(out_ref.shape[0]):
        out_ref[piece, 2 * slots] = facts


def pick_kernel(slots, near, pieces_ref, *refs):
    chips = near // 2
    out_refs = refs[:chips][::-1]
    beside_ref, facts_ref, facts, spots, sem = refs[chips:]
    count = facts_ref.shape[0]
    tiles = 2 * slots + 1
    for piece in range(count):
        tile = pieces_ref[piece * tiles + 2 * slots].astype(jnp.float32)
        facts_ref[piece:piece + 1] = tile.astype(jnp.int32)[0:1]
    copy = pltpu.make_async_copy(facts_ref, facts, sem)
    copy.start()
    me = lax.axis_index("shot")
    copy.wait()
    for piece in range(count):
        for slot in range(slots):
            spots[facts[piece, slot]] = piece * tiles + 2 * slot
    for t in range(near):
        shot = me ^ t
        out_ref, start_tile = out_refs[t // 2], t % 2 * APX * APY * 2
        if t == 1:
            out_ref, start_tile = beside_ref, 0
        first = facts[shot, slots] * GRID_COLS + facts[shot, slots + 1]
        for x in range(APX):
            found = []
            for y in range(APY):
                spot = spots[first + x * GRID_COLS + y]
                found += [pieces_ref[spot], pieces_ref[spot + 1]]
            for index, tile in enumerate(found):
                out_ref[start_tile + x * APY * 2 + index] = tile


def ends(shape):
    lane = lax.broadcasted_iota(jnp.int32, shape, 1)
    row = lax.broadcasted_iota(jnp.int32, shape, 0)
    return lane == 0, lane == shape[1] - 1, row == 0, row == shape[0] - 1


def laplace(before, here, after, masks):
    lane_0, lane_n, row_0, row_n = masks
    many = len(here)
    depth = here[0].shape[1]
    low = [jnp.where(row_0, 0.0, pltpu.roll(here[-1], 1, 0))] + here[:-1]
    high = here[1:] + [jnp.where(row_n, 0.0, pltpu.roll(here[0], LANES - 1, 0))]
    result = []
    for v in range(many):
        up = jnp.where(lane_0, 0.0, pltpu.roll(here[v], 1, 1))
        down = jnp.where(lane_n, 0.0, pltpu.roll(here[v], depth - 1, 1))
        total = (before[v] + after[v]) + (low[v] + high[v]) + (up + down)
        result.append(total - 6.0 * here[v])
    return result


def registers(ref, x):
    return [ref[x, v] for v in range(ref.shape[1])]


def strided(ref, x):
    many = ref.shape[1] // LANES
    return [ref[x, pl.ds(v, LANES, stride=many)] for v in range(many)]


def sweep(count, fields, body, unroll):
    many = fields[0].shape[1]
    zero = [jnp.zeros(fields[0].shape[2:], jnp.float32)] * many
    first = [(zero, registers(field, 0)) for field in fields]

    def step(x, carry):
        rows = [
            (before, here, registers(field, x + 1))
            for (before, here), field in zip(carry, fields)
        ]
        body(x, rows)
        return [(here, after) for _, here, after in rows]

    lax.fori_loop(0, count, step, first, unroll=unroll)


def start_kernel(prev_ref, now_ref, wave_ref, grad_ref, next_ref, flat, flat_prev, field):
    span_x, span_y, depth = now_ref.shape
    many = span_y // LANES
    masks = ends((LANES, depth))

    def load(x, carry):
        flat[x] = now_ref[x].astype(jnp.float32)
        flat_prev[x] = prev_ref[x].astype(jnp.float32)
        return carry

    lax.fori_loop(0, span_x, load, 0, unroll=2)

    def order(x, carry):
        rows = strided(flat, x)
        older = strided(flat_prev, x)
        for v in range(many):
            field[x, v] = rows[v]
            wave_ref[x, v] = rows[v]
            next_ref[x, v] = 2.0 * rows[v] - older[v]
        return carry

    lax.fori_loop(0, span_x, order, 0, unroll=2)
    for v in range(many):
        field[span_x, v] = jnp.zeros((LANES, depth), jnp.float32)

    def body(x, rows):
        grads = laplace(*rows[0], masks)
        for v in range(many):
            grad_ref[x, v] = grads[v]

    sweep(span_x, [field], body, 32)


def start(before, current):
    span_x, span_y, depth = before.shape
    many = span_y // LANES
    out = jax.ShapeDtypeStruct((span_x, many, LANES, depth), jnp.float32)
    flat = pltpu.VMEM((span_x, span_y, depth), jnp.float32)
    return pl.pallas_call(
        start_kernel,
        out_shape=(out, out, out),
        in_specs=[vmem()] * 2,
        out_specs=(vmem(),) * 3,
        scratch_shapes=[flat, flat, pltpu.VMEM((span_x + 1, many, LANES, depth), jnp.float32)],
        compiler_params=limit(8),
        cost_estimate=pl.CostEstimate(
            flops=20 * before.size, bytes_accessed=16 * before.size, transcendentals=0
        ),
        name="start",
    )(before, current)


def wave_kernel(near, *refs):
    chips = near // 2
    model_refs = parts(refs[:near], 2 * APX * APY)
    u_0, g_0, next_ref = refs[near:near + 3]
    refs = refs[near + 3:]
    out_refs = refs[:chips][::-1]
    kap, con, u_1, u_2, u_3, d_0, d_1, d_2, kb_3, kb_2, kb_1 = refs[chips:chips + 11]
    g_1, g_2, d_3, b_2, b_1, image, result = refs[chips + 11:]
    span_x, many = u_0.shape[:2]
    depth = u_0.shape[3]
    block_y = model_refs[0].shape[1]
    block_x = span_x // APX
    place = lax.axis_index("shot") % near
    masks = ends((LANES, depth))
    each = range(many)
    for field in (u_1, u_2, u_3, d_0, d_1, d_2, kb_3, kb_2, kb_1):
        for v in each:
            field[span_x, v] = jnp.zeros((LANES, depth), jnp.float32)

    for k, model_ref in enumerate(model_refs):
        for x in range(APX):
            at = x * block_x + (place ^ k)
            for y in range(APY):
                rows = pl.ds(y * block_y, block_y)
                tile = 2 * (x * APY + y)
                kap[at, rows] = model_ref[tile].astype(jnp.float32)
                con[at, rows] = speed_factor * model_ref[tile + 1].astype(jnp.float32)

    def forward_0(x, carry):
        kaps, cons, grads = strided(kap, x), strided(con, x), registers(g_0, x)
        older = registers(next_ref, x)
        for v in each:
            d_0[x, v] = cons[v] * grads[v]
            u_1[x, v] = older[v] + kaps[v] * grads[v]
        return carry

    lax.fori_loop(0, span_x, forward_0, 0, unroll=32)

    def forward(u_now, u_prev, d_now, d_prev, u_next, d_next, g_now):
        def body(x, rows):
            waves, deltas = rows
            grads = laplace(*waves, masks)
            spread = laplace(*deltas, masks)
            kaps, cons = strided(kap, x), strided(con, x)
            for v in each:
                value = 2.0 * deltas[1][v] + kaps[v] * spread[v] + cons[v] * grads[v]
                if d_prev is not None:
                    value = value - d_prev[x, v]
                d_next[x, v] = value
                if u_next is None:
                    image[x, v] = grads[v] * value
                    kb_3[x, v] = kaps[v] * value
                else:
                    g_now[x, v] = grads[v]
                    u_next[x, v] = 2.0 * waves[1][v] - u_prev[x, v] + kaps[v] * grads[v]

        sweep(span_x, [u_now, d_now], body, 32)

    forward(u_1, u_0, d_0, None, u_2, d_1, g_1)
    forward(u_2, u_1, d_1, d_0, u_3, d_2, g_2)
    forward(u_3, u_2, d_2, d_1, None, d_3, None)

    def adjoint(kb, b_now, b_after, data, grad, kb_next, b_next):
        def body(x, rows):
            spread = laplace(*rows[0], masks)
            kaps = None if kb_next is None else strided(kap, x)
            for v in each:
                back = 2.0 * b_now[x, v] + spread[v] + data[x, v]
                if b_after is not None:
                    back = back - b_after[x, v]
                total = image[x, v] + grad[x, v] * back
                if kb_next is None:
                    total = (image_scale * total).astype(result.dtype)
                    result[x % block_x // 2, (x % 2 * APX + x // block_x) * many + v] = total
                else:
                    image[x, v] = total
                    b_next[x, v] = back
                    kb_next[x, v] = kaps[v] * back

        sweep(span_x, [kb], body, 32)

    adjoint(kb_3, d_3, None, d_2, g_2, kb_2, b_2)
    adjoint(kb_2, b_2, d_3, d_1, g_1, kb_1, b_1)
    adjoint(kb_1, b_1, b_2, d_0, g_0, None, None)
    for k, out_ref in enumerate(out_refs):
        out_ref[...] = result[place // 2 ^ k]


def wave(models, started):
    span_x, many, _, depth = started[0].shape
    near = len(models)
    flat = pltpu.VMEM((span_x, many * LANES, depth), jnp.float32)
    field = pltpu.VMEM((span_x + 1, many, LANES, depth), jnp.float32)
    plain = pltpu.VMEM((span_x, many, LANES, depth), jnp.float32)
    tiles = APX * many
    out = jax.ShapeDtypeStruct((2 * tiles, LANES, depth), jnp.bfloat16)
    terms = pl.pallas_call(
        functools.partial(wave_kernel, near),
        out_shape=(out,) * (near // 2),
        in_specs=[vmem()] * (near + 3),
        out_specs=(vmem(),) * (near // 2),
        scratch_shapes=[flat] * 2 + [field] * 9 + [plain] * 6
        + [pltpu.VMEM((near // 2, 2 * tiles, LANES, depth), jnp.bfloat16)],
        compiler_params=limit(20),
        name="wave",
    )(*models, *started)
    return terms[::-1]


def wave_split_depth(models, before, current):
    near = len(models)
    order = (lax.axis_index("shot") % near) ^ jnp.arange(near)
    chips = near // 2
    length = models[-1].shape[0]
    pairs = zip(models[:chips][::-1], models[chips:][::-1])
    model = jnp.stack([part for own, other in pairs for part in (own[:length], other)])
    model = model[order]
    span_x, span_y, depth = before.shape
    block_x, tiles, block_y, _ = model.shape
    grids = model.reshape(block_x, APX, APY, 2, block_y, depth).transpose(3, 1, 0, 2, 4, 5)
    grids = grids.reshape(2, span_x, span_y, depth).astype(jnp.float32)
    image = image_scale * propagate(
        grids[0],
        speed_factor * grids[1],
        before.astype(jnp.float32),
        current.astype(jnp.float32),
        laplace_many,
    )
    many = span_y // LANES
    image = image.reshape(APX, chips, 2, LANES, many, depth).transpose(1, 2, 0, 4, 3, 5)
    image = image.reshape(chips, 2 * APX * many, LANES, depth).astype(jnp.bfloat16)
    image = image[chip_place(chips) ^ jnp.arange(chips)]
    return [image[k] for k in range(chips)]


def stack_kernel(slots, near, facts_ref, *refs):
    terms_refs = refs[:near][::-1]
    mine_ref, other_ref, facts, total, lined, sem = refs[near:]
    count = facts_ref.shape[0]
    half = terms_refs[0].shape[0] // 2
    wide = half // APX
    width = LANES // APY
    grid_rows = total.shape[1] // wide
    copy = pltpu.make_async_copy(facts_ref, facts, sem)
    copy.start()
    me = lax.axis_index("shot")

    def clear(index, carry):
        for r in range(2):
            total[r, index] = jnp.zeros(total.shape[2:], total.dtype)
        return carry

    lax.fori_loop(0, total.shape[1], clear, 0, unroll=8)
    copy.wait()
    for k, terms_ref in enumerate(terms_refs):
        first = facts[me ^ 2 * k, slots] * wide
        rows = pl.ds(facts[me ^ 2 * k, slots + 1] * width, LANES)
        for r in range(2):
            sums = [
                total[r, first + tile, rows] + terms_ref[r * half + tile].astype(jnp.float32)
                for tile in range(half)
            ]
            for tile in range(half):
                total[r, first + tile, rows] = sums[tile]

    def line(row, carry):
        for r in range(2):
            for part in range(wide):
                for tile in range(total.shape[2] // LANES):
                    at = pl.ds(tile * LANES * wide + part, LANES, stride=wide)
                    lined[r, row, at] = total[
                        r, row * wide + part, tile * LANES:(tile + 1) * LANES
                    ]
        return carry

    lax.fori_loop(0, grid_rows, line, 0, unroll=8)

    def give(chip, carry):
        for own, out_ref in enumerate((mine_ref, other_ref)):
            found = []
            for slot in range(slots):
                block = facts[2 * chip + (me + own) % 2, slot]
                rows = pl.ds(pl.multiple_of(block % GRID_COLS * LANES, LANES), LANES)
                found += [lined[r, block // GRID_COLS, rows] for r in range(2)]
            for index, tile in enumerate(found):
                out_ref[chip, index] = tile.astype(out_ref.dtype)
        return carry

    lax.fori_loop(0, count // 2, give, 0, unroll=8)


def join_kernel(mine_ref, other_ref, out_ref):
    for chip in range(out_ref.shape[0]):
        total = mine_ref[chip] + other_ref[chip].astype(jnp.float32)
        out_ref[chip] = total.astype(out_ref.dtype)


def finish_kernel(near, sums_ref, out_ref):
    for place in range(near):
        for slot in range(out_ref.shape[0]):
            for r in range(2):
                result = sums_ref[place, 2 * slot + r].astype(jnp.float32)
                for chip in range(place + near, sums_ref.shape[0], near):
                    result = result + sums_ref[chip, 2 * slot + r].astype(jnp.float32)
                out_ref[slot, 2 * place + r] = result


def per_device(
    velocity_p,
    velocity_s,
    density,
    perturbation,
    seafloor,
    owner_ids,
    corner_x,
    corner_y,
    wave_prev,
    wave_now,
):
    slots, block_x, block_y, depth = velocity_p.shape
    count = lax.axis_size("shot")
    assert count == 2 * block_x and block_y == LANES
    patch = APX * APY
    split = lax.axis_size("depth") > 1
    if split:
        seafloor = seafloor - lax.axis_index("depth") * depth

    near = block_x
    assert count % near == 0 and near & (near - 1) == 0

    def swap(values):
        return [
            lax.ppermute(values[k], "shot", [(i, i ^ 2 * k) for i in range(count)])
            if k else values[0]
            for k in range(len(values) - 1, -1, -1)
        ]

    def across(value):
        return lax.ppermute(value, "shot", [(i, i ^ 1) for i in range(count)])

    sent = pl.pallas_call(
        prepare_kernel,
        out_shape=jax.ShapeDtypeStruct((count, 2 * slots + 1, block_y, depth), jnp.bfloat16),
        in_specs=[smem()] * 2 + [pl.BlockSpec(memory_space=pltpu.HBM)] * 6,
        out_specs=vmem(),
        scratch_shapes=[
            pltpu.SMEM(owner_ids.shape, jnp.int32),
            pltpu.VMEM(seafloor.shape, jnp.int32),
            *[pltpu.VMEM(velocity_p.shape, jnp.bfloat16) for _ in range(4)],
            pltpu.SemaphoreType.DMA((6,)),
        ],
        name="prepare",
    )(
        corner_x, corner_y, owner_ids, seafloor,
        velocity_p, velocity_s, density, perturbation,
    )
    pieces = lax.all_to_all(sent, "shot", 0, 0, tiled=True)

    if not split:
        started = start(wave_prev[0], wave_now[0])
        pieces, started = lax.optimization_barrier((pieces, started))
    *picked, facts = pl.pallas_call(
        functools.partial(pick_kernel, slots, near),
        out_shape=(
            *[
                jax.ShapeDtypeStruct((patch * tiles, block_y, depth), jnp.bfloat16)
                for tiles in [4] * (near // 2 - 1) + [2, 2]
            ],
            jax.ShapeDtypeStruct((count, depth), jnp.int32),
        ),
        in_specs=[vmem()],
        out_specs=(vmem(),) * (near // 2 + 2),
        scratch_shapes=[
            pltpu.SMEM((count, depth), jnp.int32),
            pltpu.SMEM((count * slots,), jnp.int32),
            pltpu.SemaphoreType.DMA,
        ],
        compiler_params=limit(3),
        name="pick",
    )(pieces.reshape(count * (2 * slots + 1), block_y, depth))
    *picked, beside = picked
    models = swap(picked[::-1])
    handed = [value[patch * 2:] for value in models[:-1]] + [beside]
    models = models + [across(value) for value in handed]

    if split:
        terms = wave_split_depth(models, wave_prev[0], wave_now[0])
    else:
        terms = wave(models, started)
    terms = swap(terms)

    chips = count // 2
    grid_rows = count * slots // GRID_COLS
    wide = terms[0].shape[0] // 2 // APX
    shape = (chips, 2 * slots, block_y, depth)
    mine, other = pl.pallas_call(
        functools.partial(stack_kernel, slots, near // 2),
        out_shape=(
            jax.ShapeDtypeStruct(shape, jnp.float32), jax.ShapeDtypeStruct(shape, jnp.bfloat16)
        ),
        in_specs=[vmem()] * (near // 2 + 1),
        out_specs=(vmem(), vmem()),
        scratch_shapes=[
            pltpu.SMEM(facts.shape, jnp.int32),
            pltpu.VMEM((2, grid_rows * wide, GRID_COLS * LANES // APY, depth), jnp.float32),
            pltpu.VMEM((2, grid_rows, GRID_COLS * block_y, depth), jnp.float32),
            pltpu.SemaphoreType.DMA,
        ],
        compiler_params=limit(4),
        name="stack",
    )(facts, *terms)
    joined = pl.pallas_call(
        join_kernel,
        out_shape=jax.ShapeDtypeStruct(shape, jnp.bfloat16),
        in_specs=[vmem()] * 2,
        out_specs=vmem(),
        compiler_params=limit(2),
        name="join",
    )(mine, across(other))
    sums = lax.all_to_all(
        joined, "shot", 0, 0, tiled=True,
        axis_index_groups=[list(range(core, count, 2)) for core in range(2)],
    )
    return pl.pallas_call(
        functools.partial(finish_kernel, near // 2),
        out_shape=jax.ShapeDtypeStruct(velocity_p.shape, jnp.float32),
        in_specs=[vmem()],
        out_specs=vmem(),
        compiler_params=limit(2),
        name="finish",
    )(sums)


def solution(mesh):
    in_specs = (
        P(("grp", "shot"), None, None, "depth"),
        P(("grp", "shot"), None, None, "depth"),
        P(("grp", "shot"), None, None, "depth"),
        P(("grp", "shot"), None, None, "depth"),
        P(("grp", "shot"), None, None),
        P(("grp", "shot")),
        P(("grp", "shot")),
        P(("grp", "shot")),
        P(("grp", "shot"), None, None, "depth"),
        P(("grp", "shot"), None, None, "depth"),
    )
    out_specs = P(("grp", "shot"), None, None, "depth")
    return jax.shard_map(
        per_device, mesh=mesh, in_specs=in_specs, out_specs=out_specs, check_vma=False
    )
```

```python
import functools

import jax
import jax.numpy as jnp
from jax import lax
from jax.experimental import pallas as pl
from jax.experimental.pallas import tpu as pltpu
from jax.sharding import PartitionSpec as P

APX = 4
APY = 4
STEPS = 4
GRID_COLS = 8
LANES = 8

speed_factor = 0.28
image_scale = 0.01


def with_halo(block, sides, width):
    for axis, dim in sides:
        count = lax.axis_size(axis)
        forward = [(i, i + 1) for i in range(count - 1)]
        backward = [(target, source) for source, target in forward]
        low = lax.ppermute(
            lax.slice_in_dim(block, block.shape[dim] - width, None, axis=dim), axis, forward
        )
        high = lax.ppermute(lax.slice_in_dim(block, 0, width, axis=dim), axis, backward)
        block = jnp.concatenate([low, block, high], axis=dim)
    return block


def laplace_many(fields):
    stacked = jnp.stack(fields)
    padded = with_halo(stacked.astype(jnp.bfloat16), (("depth", 3),), 1).astype(stacked.dtype)
    padded = jnp.pad(padded, ((0, 0), (1, 1), (1, 1), (0, 0)))
    beside = padded[:, 2:, 1:-1, 1:-1] + padded[:, :-2, 1:-1, 1:-1]
    beside = beside + padded[:, 1:-1, 2:, 1:-1] + padded[:, 1:-1, :-2, 1:-1]
    beside = beside + padded[:, 1:-1, 1:-1, 2:] + padded[:, 1:-1, 1:-1, :-2]
    result = beside - 6.0 * stacked
    return [result[index] for index in range(len(fields))]


def propagate(kappa, contrast, before, current, apply):
    grads = []
    datas = []
    grad_now = apply([current])[0]
    delta_prev = jnp.zeros_like(current)
    delta_now = contrast * grad_now
    grads.append(grad_now)
    datas.append(delta_now)
    before, current = (current, 2.0 * current - before + kappa * grad_now)
    for step in range(1, STEPS):
        grad_now, spread = apply([current, delta_now])
        delta_next = 2.0 * delta_now - delta_prev + kappa * spread + contrast * grad_now
        grads.append(grad_now)
        datas.append(delta_next)
        delta_prev, delta_now = (delta_now, delta_next)
        if step + 1 < STEPS:
            before, current = (current, 2.0 * current - before + kappa * grad_now)
    back = datas[STEPS - 1]
    back_after = jnp.zeros_like(back)
    image = grads[STEPS - 1] * back
    for step in range(STEPS - 2, -1, -1):
        spread = apply([kappa * back])
        back_new = 2.0 * back - back_after + spread[0] + datas[step]
        image = image + grads[step] * back_new
        back_after, back = (back, back_new)
    return image


def limit(mebibytes):
    return pltpu.CompilerParams(vmem_limit_bytes=mebibytes * 2**20)


def chip_place(near):
    return lax.axis_index("shot") // 2 % near


def parts(refs, length):
    chips = len(refs) // 2
    own, other = refs[:chips][::-1], refs[chips:][::-1]
    return [
        part for first, second in zip(own, other) for part in (first.at[pl.ds(0, length)], second)
    ]


def vmem():
    return pl.BlockSpec(memory_space=pltpu.VMEM)


def smem():
    return pl.BlockSpec(memory_space=pltpu.SMEM)


def prepare_kernel(
    row_ref, col_ref, ids_hbm, floor_hbm, p_hbm, s_hbm, rho_hbm, pert_hbm, out_ref,
    ids, floors, p, s, rho, pert, sems,
):
    slots, block_x, block_y, depth = p.shape
    near = block_x
    copies = [
        pltpu.make_async_copy(source, target, sems.at[index])
        for index, (source, target) in enumerate(
            [(p_hbm, p), (s_hbm, s), (rho_hbm, rho), (floor_hbm, floors), (pert_hbm, pert),
             (ids_hbm, ids)]
        )
    ]
    for copy in copies:
        copy.start()
    shape = (block_y, depth)
    deep = lax.broadcasted_iota(jnp.int32, shape, 1).astype(jnp.float32)
    lane = lax.broadcasted_iota(jnp.int32, shape, 1)
    same = lax.broadcasted_iota(jnp.int32, (block_y, block_y), 0) == (
        lax.broadcasted_iota(jnp.int32, (block_y, block_y), 1)
    )
    for copy in copies:
        copy.wait()
    for slot in range(slots):
        lines = floors[slot].astype(jnp.float32)
        for x in range(block_x):
            line = jnp.broadcast_to(lines[x:x + 1], (block_y, block_y))
            floor = jnp.sum(jnp.where(same, line, 0.0), axis=1, keepdims=True)
            primary = p[slot, x].astype(jnp.float32)
            shear = s[slot, x].astype(jnp.float32)
            square = primary * primary
            stiffness = jnp.where(deep >= floor, square + shear * shear, square)
            coef = speed_factor * stiffness / rho[slot, x].astype(jnp.float32)
            coef = coef.astype(out_ref.dtype)
            for piece in range(x, out_ref.shape[0], near):
                out_ref[piece, 2 * slot] = coef
                out_ref[piece, 2 * slot + 1] = pert[slot, x]
    facts = jnp.where(lane == slots, row_ref[0], 0)
    facts = jnp.where(lane == slots + 1, col_ref[0], facts)
    for slot in range(slots):
        facts = jnp.where(lane == slot, ids[slot], facts)
    facts = facts.astype(jnp.float32).astype(out_ref.dtype)
    for piece in range(out_ref.shape[0]):
        out_ref[piece, 2 * slots] = facts


def pick_kernel(slots, near, pieces_ref, *refs):
    chips = near // 2
    out_refs = refs[:chips][::-1]
    beside_ref, facts_ref, facts, spots, sem = refs[chips:]
    count = facts_ref.shape[0]
    tiles = 2 * slots + 1
    for piece in range(count):
        tile = pieces_ref[piece * tiles + 2 * slots].astype(jnp.float32)
        facts_ref[piece:piece + 1] = tile.astype(jnp.int32)[0:1]
    copy = pltpu.make_async_copy(facts_ref, facts, sem)
    copy.start()
    me = lax.axis_index("shot")
    copy.wait()
    for piece in range(count):
        for slot in range(slots):
            spots[facts[piece, slot]] = piece * tiles + 2 * slot
    for t in range(near):
        shot = me ^ t
        out_ref, start_tile = out_refs[t // 2], t % 2 * APX * APY * 2
        if t == 1:
            out_ref, start_tile = beside_ref, 0
        first = facts[shot, slots] * GRID_COLS + facts[shot, slots + 1]
        for x in range(APX):
            found = []
            for y in range(APY):
                spot = spots[first + x * GRID_COLS + y]
                found += [pieces_ref[spot], pieces_ref[spot + 1]]
            for index, tile in enumerate(found):
                out_ref[start_tile + x * APY * 2 + index] = tile


def ends(shape):
    lane = lax.broadcasted_iota(jnp.int32, shape, 1)
    row = lax.broadcasted_iota(jnp.int32, shape, 0)
    return lane == 0, lane == shape[1] - 1, row == 0, row == shape[0] - 1


def laplace(before, here, after, masks):
    lane_0, lane_n, row_0, row_n = masks
    many = len(here)
    depth = here[0].shape[1]
    low = [jnp.where(row_0, 0.0, pltpu.roll(here[-1], 1, 0))] + here[:-1]
    high = here[1:] + [jnp.where(row_n, 0.0, pltpu.roll(here[0], LANES - 1, 0))]
    result = []
    for v in range(many):
        up = jnp.where(lane_0, 0.0, pltpu.roll(here[v], 1, 1))
        down = jnp.where(lane_n, 0.0, pltpu.roll(here[v], depth - 1, 1))
        total = (before[v] + after[v]) + (low[v] + high[v]) + (up + down)
        result.append(total - 6.0 * here[v])
    return result


def registers(ref, x):
    return [ref[x, v] for v in range(ref.shape[1])]


def strided(ref, x):
    many = ref.shape[1] // LANES
    return [ref[x, pl.ds(v, LANES, stride=many)] for v in range(many)]


def sweep(count, fields, body, unroll):
    many = fields[0].shape[1]
    zero = [jnp.zeros(fields[0].shape[2:], jnp.float32)] * many
    first = [(zero, registers(field, 0)) for field in fields]

    def step(x, carry):
        rows = [
            (before, here, registers(field, x + 1))
            for (before, here), field in zip(carry, fields)
        ]
        body(x, rows)
        return [(here, after) for _, here, after in rows]

    lax.fori_loop(0, count, step, first, unroll=unroll)


def start_kernel(prev_ref, now_ref, wave_ref, grad_ref, next_ref, flat, flat_prev, field):
    span_x, span_y, depth = now_ref.shape
    many = span_y // LANES
    masks = ends((LANES, depth))

    def load(x, carry):
        flat[x] = now_ref[x].astype(jnp.float32)
        flat_prev[x] = prev_ref[x].astype(jnp.float32)
        return carry

    lax.fori_loop(0, span_x, load, 0, unroll=2)

    def order(x, carry):
        rows = strided(flat, x)
        older = strided(flat_prev, x)
        for v in range(many):
            field[x, v] = rows[v]
            wave_ref[x, v] = rows[v]
            next_ref[x, v] = 2.0 * rows[v] - older[v]
        return carry

    lax.fori_loop(0, span_x, order, 0, unroll=2)
    for v in range(many):
        field[span_x, v] = jnp.zeros((LANES, depth), jnp.float32)

    def body(x, rows):
        grads = laplace(*rows[0], masks)
        for v in range(many):
            grad_ref[x, v] = grads[v]

    sweep(span_x, [field], body, 32)


def start(before, current):
    span_x, span_y, depth = before.shape
    many = span_y // LANES
    out = jax.ShapeDtypeStruct((span_x, many, LANES, depth), jnp.float32)
    flat = pltpu.VMEM((span_x, span_y, depth), jnp.float32)
    return pl.pallas_call(
        start_kernel,
        out_shape=(out, out, out),
        in_specs=[vmem()] * 2,
        out_specs=(vmem(),) * 3,
        scratch_shapes=[flat, flat, pltpu.VMEM((span_x + 1, many, LANES, depth), jnp.float32)],
        compiler_params=limit(8),
        cost_estimate=pl.CostEstimate(
            flops=20 * before.size, bytes_accessed=16 * before.size, transcendentals=0
        ),
        name="start",
    )(before, current)


def wave_kernel(near, *refs):
    chips = near // 2
    model_refs = parts(refs[:near], 2 * APX * APY)
    u_0, g_0, next_ref = refs[near:near + 3]
    refs = refs[near + 3:]
    out_refs = refs[:chips][::-1]
    kap, con, u_1, u_2, u_3, d_0, d_1, d_2, kb_3, kb_2, kb_1 = refs[chips:chips + 11]
    g_1, g_2, d_3, b_2, b_1, image, result = refs[chips + 11:]
    span_x, many = u_0.shape[:2]
    depth = u_0.shape[3]
    block_y = model_refs[0].shape[1]
    block_x = span_x // APX
    place = lax.axis_index("shot") % near
    masks = ends((LANES, depth))
    each = range(many)
    for field in (u_1, u_2, u_3, d_0, d_1, d_2, kb_3, kb_2, kb_1):
        for v in each:
            field[span_x, v] = jnp.zeros((LANES, depth), jnp.float32)

    for k, model_ref in enumerate(model_refs):
        for x in range(APX):
            at = x * block_x + (place ^ k)
            for y in range(APY):
                rows = pl.ds(y * block_y, block_y)
                tile = 2 * (x * APY + y)
                kap[at, rows] = model_ref[tile].astype(jnp.float32)
                con[at, rows] = speed_factor * model_ref[tile + 1].astype(jnp.float32)

    def forward_0(x, carry):
        kaps, cons, grads = strided(kap, x), strided(con, x), registers(g_0, x)
        older = registers(next_ref, x)
        for v in each:
            d_0[x, v] = cons[v] * grads[v]
            u_1[x, v] = older[v] + kaps[v] * grads[v]
        return carry

    lax.fori_loop(0, span_x, forward_0, 0, unroll=32)

    def forward(u_now, u_prev, d_now, d_prev, u_next, d_next, g_now):
        def body(x, rows):
            waves, deltas = rows
            grads = laplace(*waves, masks)
            spread = laplace(*deltas, masks)
            kaps, cons = strided(kap, x), strided(con, x)
            for v in each:
                value = 2.0 * deltas[1][v] + kaps[v] * spread[v] + cons[v] * grads[v]
                if d_prev is not None:
                    value = value - d_prev[x, v]
                d_next[x, v] = value
                if u_next is None:
                    image[x, v] = grads[v] * value
                    kb_3[x, v] = kaps[v] * value
                else:
                    g_now[x, v] = grads[v]
                    u_next[x, v] = 2.0 * waves[1][v] - u_prev[x, v] + kaps[v] * grads[v]

        sweep(span_x, [u_now, d_now], body, 32)

    forward(u_1, u_0, d_0, None, u_2, d_1, g_1)
    forward(u_2, u_1, d_1, d_0, u_3, d_2, g_2)
    forward(u_3, u_2, d_2, d_1, None, d_3, None)

    def adjoint(kb, b_now, b_after, data, grad, kb_next, b_next):
        def body(x, rows):
            spread = laplace(*rows[0], masks)
            kaps = None if kb_next is None else strided(kap, x)
            for v in each:
                back = 2.0 * b_now[x, v] + spread[v] + data[x, v]
                if b_after is not None:
                    back = back - b_after[x, v]
                total = image[x, v] + grad[x, v] * back
                if kb_next is None:
                    total = (image_scale * total).astype(result.dtype)
                    result[x % block_x // 2, (x % 2 * APX + x // block_x) * many + v] = total
                else:
                    image[x, v] = total
                    b_next[x, v] = back
                    kb_next[x, v] = kaps[v] * back

        sweep(span_x, [kb], body, 32)

    adjoint(kb_3, d_3, None, d_2, g_2, kb_2, b_2)
    adjoint(kb_2, b_2, d_3, d_1, g_1, kb_1, b_1)
    adjoint(kb_1, b_1, b_2, d_0, g_0, None, None)
    for k, out_ref in enumerate(out_refs):
        out_ref[...] = result[place // 2 ^ k]


def wave(models, started):
    span_x, many, _, depth = started[0].shape
    near = len(models)
    flat = pltpu.VMEM((span_x, many * LANES, depth), jnp.float32)
    field = pltpu.VMEM((span_x + 1, many, LANES, depth), jnp.float32)
    plain = pltpu.VMEM((span_x, many, LANES, depth), jnp.float32)
    tiles = APX * many
    out = jax.ShapeDtypeStruct((2 * tiles, LANES, depth), jnp.bfloat16)
    terms = pl.pallas_call(
        functools.partial(wave_kernel, near),
        out_shape=(out,) * (near // 2),
        in_specs=[vmem()] * (near + 3),
        out_specs=(vmem(),) * (near // 2),
        scratch_shapes=[flat] * 2 + [field] * 9 + [plain] * 6
        + [pltpu.VMEM((near // 2, 2 * tiles, LANES, depth), jnp.bfloat16)],
        compiler_params=limit(20),
        name="wave",
    )(*models, *started)
    return terms[::-1]


def wave_split_depth(models, before, current):
    near = len(models)
    order = (lax.axis_index("shot") % near) ^ jnp.arange(near)
    chips = near // 2
    length = models[-1].shape[0]
    pairs = zip(models[:chips][::-1], models[chips:][::-1])
    model = jnp.stack([part for own, other in pairs for part in (own[:length], other)])
    model = model[order]
    span_x, span_y, depth = before.shape
    block_x, tiles, block_y, _ = model.shape
    grids = model.reshape(block_x, APX, APY, 2, block_y, depth).transpose(3, 1, 0, 2, 4, 5)
    grids = grids.reshape(2, span_x, span_y, depth).astype(jnp.float32)
    image = image_scale * propagate(
        grids[0],
        speed_factor * grids[1],
        before.astype(jnp.float32),
        current.astype(jnp.float32),
        laplace_many,
    )
    many = span_y // LANES
    image = image.reshape(APX, chips, 2, LANES, many, depth).transpose(1, 2, 0, 4, 3, 5)
    image = image.reshape(chips, 2 * APX * many, LANES, depth).astype(jnp.bfloat16)
    image = image[chip_place(chips) ^ jnp.arange(chips)]
    return [image[k] for k in range(chips)]


def stack_kernel(slots, near, r, facts_ref, *refs):
    terms_refs = refs[:near][::-1]
    mine_ref, other_ref, facts, total, lined, sem = refs[near:]
    count = facts_ref.shape[0]
    half = terms_refs[0].shape[0] // 2
    wide = half // APX
    width = LANES // APY
    grid_rows = total.shape[0] // wide
    copy = pltpu.make_async_copy(facts_ref, facts, sem)
    copy.start()
    me = lax.axis_index("shot")

    def clear(index, carry):
        total[index] = jnp.zeros(total.shape[1:], total.dtype)
        return carry

    lax.fori_loop(0, total.shape[0], clear, 0, unroll=16)
    copy.wait()
    for k, terms_ref in enumerate(terms_refs):
        first = facts[me ^ 2 * k, slots] * wide
        rows = pl.ds(facts[me ^ 2 * k, slots + 1] * width, LANES)
        sums = [
            total[first + tile, rows] + terms_ref[r * half + tile].astype(jnp.float32)
            for tile in range(half)
        ]
        for tile in range(half):
            total[first + tile, rows] = sums[tile]

    def line(row, carry):
        for part in range(wide):
            for tile in range(total.shape[1] // LANES):
                at = pl.ds(tile * LANES * wide + part, LANES, stride=wide)
                lined[row, at] = total[row * wide + part, tile * LANES:(tile + 1) * LANES]
        return carry

    lax.fori_loop(0, grid_rows, line, 0, unroll=8)

    def give(chip, carry):
        for own, out_ref in enumerate((mine_ref, other_ref)):
            found = []
            for slot in range(slots):
                block = facts[2 * chip + (me + own) % 2, slot]
                rows = pl.ds(pl.multiple_of(block % GRID_COLS * LANES, LANES), LANES)
                found.append(lined[block // GRID_COLS, rows])
            for index, tile in enumerate(found):
                out_ref[chip, index] = tile.astype(out_ref.dtype)
        return carry

    lax.fori_loop(0, count // 2, give, 0, unroll=8)


def join_kernel(*refs):
    mine_refs, other_refs, out_ref = refs[:2], refs[2:4], refs[4]
    for chip in range(out_ref.shape[0]):
        for r in range(2):
            total = mine_refs[r][chip] + other_refs[r][chip].astype(jnp.float32)
            out_ref[chip, r] = total.astype(out_ref.dtype)


def finish_kernel(near, sums_ref, out_ref):
    for place in range(near):
        for slot in range(out_ref.shape[0]):
            for r in range(2):
                result = sums_ref[place, r, slot].astype(jnp.float32)
                for chip in range(place + near, sums_ref.shape[0], near):
                    result = result + sums_ref[chip, r, slot].astype(jnp.float32)
                out_ref[slot, 2 * place + r] = result


def per_device(
    velocity_p,
    velocity_s,
    density,
    perturbation,
    seafloor,
    owner_ids,
    corner_x,
    corner_y,
    wave_prev,
    wave_now,
):
    slots, block_x, block_y, depth = velocity_p.shape
    count = lax.axis_size("shot")
    assert count == 2 * block_x and block_y == LANES
    patch = APX * APY
    split = lax.axis_size("depth") > 1
    if split:
        seafloor = seafloor - lax.axis_index("depth") * depth

    near = block_x
    assert count % near == 0 and near & (near - 1) == 0

    def swap(values):
        return [
            lax.ppermute(values[k], "shot", [(i, i ^ 2 * k) for i in range(count)])
            if k else values[0]
            for k in range(len(values) - 1, -1, -1)
        ]

    def across(value):
        return lax.ppermute(value, "shot", [(i, i ^ 1) for i in range(count)])

    sent = pl.pallas_call(
        prepare_kernel,
        out_shape=jax.ShapeDtypeStruct((count, 2 * slots + 1, block_y, depth), jnp.bfloat16),
        in_specs=[smem()] * 2 + [pl.BlockSpec(memory_space=pltpu.HBM)] * 6,
        out_specs=vmem(),
        scratch_shapes=[
            pltpu.SMEM(owner_ids.shape, jnp.int32),
            pltpu.VMEM(seafloor.shape, jnp.int32),
            *[pltpu.VMEM(velocity_p.shape, jnp.bfloat16) for _ in range(4)],
            pltpu.SemaphoreType.DMA((6,)),
        ],
        name="prepare",
    )(
        corner_x, corner_y, owner_ids, seafloor,
        velocity_p, velocity_s, density, perturbation,
    )
    pieces = lax.all_to_all(sent, "shot", 0, 0, tiled=True)

    if not split:
        started = start(wave_prev[0], wave_now[0])
        pieces, started = lax.optimization_barrier((pieces, started))
    *picked, facts = pl.pallas_call(
        functools.partial(pick_kernel, slots, near),
        out_shape=(
            *[
                jax.ShapeDtypeStruct((patch * tiles, block_y, depth), jnp.bfloat16)
                for tiles in [4] * (near // 2 - 1) + [2, 2]
            ],
            jax.ShapeDtypeStruct((count, depth), jnp.int32),
        ),
        in_specs=[vmem()],
        out_specs=(vmem(),) * (near // 2 + 2),
        scratch_shapes=[
            pltpu.SMEM((count, depth), jnp.int32),
            pltpu.SMEM((count * slots,), jnp.int32),
            pltpu.SemaphoreType.DMA,
        ],
        compiler_params=limit(3),
        name="pick",
    )(pieces.reshape(count * (2 * slots + 1), block_y, depth))
    *picked, beside = picked
    models = swap(picked[::-1])
    handed = [value[patch * 2:] for value in models[:-1]] + [beside]
    models = models + [across(value) for value in handed]

    if split:
        terms = wave_split_depth(models, wave_prev[0], wave_now[0])
    else:
        terms = wave(models, started)
    terms = swap(terms)

    chips = count // 2
    grid_rows = count * slots // GRID_COLS
    wide = terms[0].shape[0] // 2 // APX
    shape = (chips, slots, block_y, depth)
    mine, other = [], []
    for r in range(2):
        own, theirs = pl.pallas_call(
            functools.partial(stack_kernel, slots, near // 2, r),
            out_shape=(
                jax.ShapeDtypeStruct(shape, jnp.float32), jax.ShapeDtypeStruct(shape, jnp.bfloat16)
            ),
            in_specs=[vmem()] * (near // 2 + 1),
            out_specs=(vmem(), vmem()),
            scratch_shapes=[
                pltpu.SMEM(facts.shape, jnp.int32),
                pltpu.VMEM((grid_rows * wide, GRID_COLS * LANES // APY, depth), jnp.float32),
                pltpu.VMEM((grid_rows, GRID_COLS * block_y, depth), jnp.float32),
                pltpu.SemaphoreType.DMA,
            ],
            compiler_params=limit(4),
            cost_estimate=pl.CostEstimate(
                flops=8 * terms[0].size, bytes_accessed=8 * terms[0].size, transcendentals=0
            ),
            name="stack",
        )(facts, *terms)
        mine.append(own)
        other.append(across(theirs))
    joined = pl.pallas_call(
        join_kernel,
        out_shape=jax.ShapeDtypeStruct((chips, 2) + shape[1:], jnp.bfloat16),
        in_specs=[vmem()] * 4,
        out_specs=vmem(),
        compiler_params=limit(2),
        name="join",
    )(*mine, *other)
    sums = lax.all_to_all(
        joined, "shot", 0, 0, tiled=True,
        axis_index_groups=[list(range(core, count, 2)) for core in range(2)],
    )
    return pl.pallas_call(
        functools.partial(finish_kernel, near // 2),
        out_shape=jax.ShapeDtypeStruct(velocity_p.shape, jnp.float32),
        in_specs=[vmem()],
        out_specs=vmem(),
        compiler_params=limit(2),
        name="finish",
    )(sums)


def solution(mesh):
    in_specs = (
        P(("grp", "shot"), None, None, "depth"),
        P(("grp", "shot"), None, None, "depth"),
        P(("grp", "shot"), None, None, "depth"),
        P(("grp", "shot"), None, None, "depth"),
        P(("grp", "shot"), None, None),
        P(("grp", "shot")),
        P(("grp", "shot")),
        P(("grp", "shot")),
        P(("grp", "shot"), None, None, "depth"),
        P(("grp", "shot"), None, None, "depth"),
    )
    out_specs = P(("grp", "shot"), None, None, "depth")
    return jax.shard_map(
        per_device, mesh=mesh, in_specs=in_specs, out_specs=out_specs, check_vma=False
    )
```

```python
import functools

import jax
import jax.numpy as jnp
from jax import lax
from jax.experimental import pallas as pl
from jax.experimental.pallas import tpu as pltpu
from jax.sharding import PartitionSpec as P

APX = 4
APY = 4
STEPS = 4
GRID_COLS = 8
FACTS = 8
LANES = 8

speed_factor = 0.28
image_scale = 0.01


def with_halo(block, sides, width):
    for axis, dim in sides:
        count = lax.axis_size(axis)
        forward = [(i, i + 1) for i in range(count - 1)]
        backward = [(target, source) for source, target in forward]
        low = lax.ppermute(
            lax.slice_in_dim(block, block.shape[dim] - width, None, axis=dim), axis, forward
        )
        high = lax.ppermute(lax.slice_in_dim(block, 0, width, axis=dim), axis, backward)
        block = jnp.concatenate([low, block, high], axis=dim)
    return block


def laplace_many(fields):
    stacked = jnp.stack(fields)
    padded = with_halo(stacked.astype(jnp.bfloat16), (("depth", 3),), 1).astype(stacked.dtype)
    padded = jnp.pad(padded, ((0, 0), (1, 1), (1, 1), (0, 0)))
    beside = padded[:, 2:, 1:-1, 1:-1] + padded[:, :-2, 1:-1, 1:-1]
    beside = beside + padded[:, 1:-1, 2:, 1:-1] + padded[:, 1:-1, :-2, 1:-1]
    beside = beside + padded[:, 1:-1, 1:-1, 2:] + padded[:, 1:-1, 1:-1, :-2]
    result = beside - 6.0 * stacked
    return [result[index] for index in range(len(fields))]


def propagate(kappa, contrast, before, current, apply):
    grads = []
    datas = []
    grad_now = apply([current])[0]
    delta_prev = jnp.zeros_like(current)
    delta_now = contrast * grad_now
    grads.append(grad_now)
    datas.append(delta_now)
    before, current = (current, 2.0 * current - before + kappa * grad_now)
    for step in range(1, STEPS):
        grad_now, spread = apply([current, delta_now])
        delta_next = 2.0 * delta_now - delta_prev + kappa * spread + contrast * grad_now
        grads.append(grad_now)
        datas.append(delta_next)
        delta_prev, delta_now = (delta_now, delta_next)
        if step + 1 < STEPS:
            before, current = (current, 2.0 * current - before + kappa * grad_now)
    back = datas[STEPS - 1]
    back_after = jnp.zeros_like(back)
    image = grads[STEPS - 1] * back
    for step in range(STEPS - 2, -1, -1):
        spread = apply([kappa * back])
        back_new = 2.0 * back - back_after + spread[0] + datas[step]
        image = image + grads[step] * back_new
        back_after, back = (back, back_new)
    return image


def limit(mebibytes):
    return pltpu.CompilerParams(vmem_limit_bytes=mebibytes * 2**20)


def chip_place(near):
    return lax.axis_index("shot") // 2 % near


def parts(refs, length):
    chips = len(refs) // 2
    own, other = refs[:chips][::-1], refs[chips:][::-1]
    return [
        part for first, second in zip(own, other) for part in (first.at[pl.ds(0, length)], second)
    ]


def vmem():
    return pl.BlockSpec(memory_space=pltpu.VMEM)


def smem():
    return pl.BlockSpec(memory_space=pltpu.SMEM)


def prepare_kernel(
    row_ref, col_ref, ids_hbm, floor_hbm, p_hbm, s_hbm, rho_hbm, pert_hbm, out_ref,
    ids, floors, p, s, rho, pert, sems,
):
    slots, block_x, block_y, depth = p.shape
    near = block_x
    copies = [
        pltpu.make_async_copy(source, target, sems.at[index])
        for index, (source, target) in enumerate(
            [(p_hbm, p), (s_hbm, s), (rho_hbm, rho), (floor_hbm, floors), (pert_hbm, pert),
             (ids_hbm, ids)]
        )
    ]
    for copy in copies:
        copy.start()
    shape = (block_y, depth)
    deep = lax.broadcasted_iota(jnp.int32, shape, 1).astype(jnp.float32)
    lane = lax.broadcasted_iota(jnp.int32, shape, 1)
    same = lax.broadcasted_iota(jnp.int32, (block_y, block_y), 0) == (
        lax.broadcasted_iota(jnp.int32, (block_y, block_y), 1)
    )
    for copy in copies:
        copy.wait()
    for slot in range(slots):
        lines = floors[slot].astype(jnp.float32)
        for x in range(block_x):
            line = jnp.broadcast_to(lines[x:x + 1], (block_y, block_y))
            floor = jnp.sum(jnp.where(same, line, 0.0), axis=1, keepdims=True)
            primary = p[slot, x].astype(jnp.float32)
            shear = s[slot, x].astype(jnp.float32)
            square = primary * primary
            stiffness = jnp.where(deep >= floor, square + shear * shear, square)
            coef = speed_factor * stiffness / rho[slot, x].astype(jnp.float32)
            coef = coef.astype(out_ref.dtype)
            for piece in range(x, out_ref.shape[0], near):
                out_ref[piece, 2 * slot] = coef
                out_ref[piece, 2 * slot + 1] = pert[slot, x]
    lane = lane - FACTS * lax.axis_index("shot")
    facts = jnp.where(lane == slots, row_ref[0], 0)
    facts = jnp.where(lane == slots + 1, col_ref[0], facts)
    for slot in range(slots):
        facts = jnp.where(lane == slot, ids[slot], facts)
    facts = facts.astype(jnp.float32).astype(out_ref.dtype)
    for piece in range(out_ref.shape[0]):
        out_ref[piece, 2 * slots] = facts


def pick_kernel(slots, near, pieces_ref, *refs):
    chips = near // 2
    out_refs = refs[:chips][::-1]
    beside_ref, facts_ref, facts, spots, sem = refs[chips:]
    count = spots.shape[0] // slots
    tiles = 2 * slots + 1
    line = pieces_ref[2 * slots].astype(jnp.float32)
    for piece in range(1, count):
        line = line + pieces_ref[piece * tiles + 2 * slots].astype(jnp.float32)
    facts_ref[...] = line.astype(jnp.int32)[0:1]
    copy = pltpu.make_async_copy(facts_ref, facts, sem)
    copy.start()
    me = lax.axis_index("shot")
    copy.wait()
    for piece in range(count):
        for slot in range(slots):
            spots[facts[0, FACTS * piece + slot]] = piece * tiles + 2 * slot
    for t in range(near):
        shot = me ^ t
        out_ref, start_tile = out_refs[t // 2], t % 2 * APX * APY * 2
        if t == 1:
            out_ref, start_tile = beside_ref, 0
        first = facts[0, FACTS * shot + slots] * GRID_COLS + facts[0, FACTS * shot + slots + 1]
        for x in range(APX):
            found = []
            for y in range(APY):
                spot = spots[first + x * GRID_COLS + y]
                found += [pieces_ref[spot], pieces_ref[spot + 1]]
            for index, tile in enumerate(found):
                out_ref[start_tile + x * APY * 2 + index] = tile


def ends(shape):
    lane = lax.broadcasted_iota(jnp.int32, shape, 1)
    row = lax.broadcasted_iota(jnp.int32, shape, 0)
    return lane == 0, lane == shape[1] - 1, row == 0, row == shape[0] - 1


def laplace(before, here, after, masks):
    lane_0, lane_n, row_0, row_n = masks
    many = len(here)
    depth = here[0].shape[1]
    low = [jnp.where(row_0, 0.0, pltpu.roll(here[-1], 1, 0))] + here[:-1]
    high = here[1:] + [jnp.where(row_n, 0.0, pltpu.roll(here[0], LANES - 1, 0))]
    result = []
    for v in range(many):
        up = jnp.where(lane_0, 0.0, pltpu.roll(here[v], 1, 1))
        down = jnp.where(lane_n, 0.0, pltpu.roll(here[v], depth - 1, 1))
        total = (before[v] + after[v]) + (low[v] + high[v]) + (up + down)
        result.append(total - 6.0 * here[v])
    return result


def registers(ref, x):
    return [ref[x, v] for v in range(ref.shape[1])]


def strided(ref, x):
    many = ref.shape[1] // LANES
    return [ref[x, pl.ds(v, LANES, stride=many)] for v in range(many)]


def sweep(count, fields, body, unroll):
    many = fields[0].shape[1]
    zero = [jnp.zeros(fields[0].shape[2:], jnp.float32)] * many
    first = [(zero, registers(field, 0)) for field in fields]

    def step(x, carry):
        rows = [
            (before, here, registers(field, x + 1))
            for (before, here), field in zip(carry, fields)
        ]
        body(x, rows)
        return [(here, after) for _, here, after in rows]

    lax.fori_loop(0, count, step, first, unroll=unroll)


def start_kernel(prev_ref, now_ref, wave_ref, grad_ref, next_ref, flat, flat_prev, field):
    span_x, span_y, depth = now_ref.shape
    many = span_y // LANES
    masks = ends((LANES, depth))

    def load(x, carry):
        flat[x] = now_ref[x].astype(jnp.float32)
        flat_prev[x] = prev_ref[x].astype(jnp.float32)
        return carry

    lax.fori_loop(0, span_x, load, 0, unroll=2)

    def order(x, carry):
        rows = strided(flat, x)
        older = strided(flat_prev, x)
        for v in range(many):
            field[x, v] = rows[v]
            wave_ref[x, v] = rows[v]
            next_ref[x, v] = 2.0 * rows[v] - older[v]
        return carry

    lax.fori_loop(0, span_x, order, 0, unroll=2)
    for v in range(many):
        field[span_x, v] = jnp.zeros((LANES, depth), jnp.float32)

    def body(x, rows):
        grads = laplace(*rows[0], masks)
        for v in range(many):
            grad_ref[x, v] = grads[v]

    sweep(span_x, [field], body, 32)


def start(before, current):
    span_x, span_y, depth = before.shape
    many = span_y // LANES
    out = jax.ShapeDtypeStruct((span_x, many, LANES, depth), jnp.float32)
    flat = pltpu.VMEM((span_x, span_y, depth), jnp.float32)
    return pl.pallas_call(
        start_kernel,
        out_shape=(out, out, out),
        in_specs=[vmem()] * 2,
        out_specs=(vmem(),) * 3,
        scratch_shapes=[flat, flat, pltpu.VMEM((span_x + 1, many, LANES, depth), jnp.float32)],
        compiler_params=limit(8),
        cost_estimate=pl.CostEstimate(
            flops=20 * before.size, bytes_accessed=16 * before.size, transcendentals=0
        ),
        name="start",
    )(before, current)


def wave_kernel(near, *refs):
    chips = near // 2
    model_refs = parts(refs[:near], 2 * APX * APY)
    u_0, g_0, next_ref = refs[near:near + 3]
    refs = refs[near + 3:]
    out_refs = refs[:chips][::-1]
    kap, con, u_1, u_2, u_3, d_0, d_1, d_2, kb_3, kb_2, kb_1 = refs[chips:chips + 11]
    g_1, g_2, d_3, b_2, b_1, image, result = refs[chips + 11:]
    span_x, many = u_0.shape[:2]
    depth = u_0.shape[3]
    block_y = model_refs[0].shape[1]
    block_x = span_x // APX
    place = lax.axis_index("shot") % near
    masks = ends((LANES, depth))
    each = range(many)
    for field in (u_1, u_2, u_3, d_0, d_1, d_2, kb_3, kb_2, kb_1):
        for v in each:
            field[span_x, v] = jnp.zeros((LANES, depth), jnp.float32)

    for k, model_ref in enumerate(model_refs):
        for x in range(APX):
            at = x * block_x + (place ^ k)
            for y in range(APY):
                rows = pl.ds(y * block_y, block_y)
                tile = 2 * (x * APY + y)
                kap[at, rows] = model_ref[tile].astype(jnp.float32)
                con[at, rows] = speed_factor * model_ref[tile + 1].astype(jnp.float32)

    def forward_0(x, carry):
        kaps, cons, grads = strided(kap, x), strided(con, x), registers(g_0, x)
        older = registers(next_ref, x)
        for v in each:
            d_0[x, v] = cons[v] * grads[v]
            u_1[x, v] = older[v] + kaps[v] * grads[v]
        return carry

    lax.fori_loop(0, span_x, forward_0, 0, unroll=32)

    def forward(u_now, u_prev, d_now, d_prev, u_next, d_next, g_now):
        def body(x, rows):
            waves, deltas = rows
            grads = laplace(*waves, masks)
            spread = laplace(*deltas, masks)
            kaps, cons = strided(kap, x), strided(con, x)
            for v in each:
                value = 2.0 * deltas[1][v] + kaps[v] * spread[v] + cons[v] * grads[v]
                if d_prev is not None:
                    value = value - d_prev[x, v]
                d_next[x, v] = value
                if u_next is None:
                    image[x, v] = grads[v] * value
                    kb_3[x, v] = kaps[v] * value
                else:
                    g_now[x, v] = grads[v]
                    u_next[x, v] = 2.0 * waves[1][v] - u_prev[x, v] + kaps[v] * grads[v]

        sweep(span_x, [u_now, d_now], body, 32)

    forward(u_1, u_0, d_0, None, u_2, d_1, g_1)
    forward(u_2, u_1, d_1, d_0, u_3, d_2, g_2)
    forward(u_3, u_2, d_2, d_1, None, d_3, None)

    def adjoint(kb, b_now, b_after, data, grad, kb_next, b_next):
        def body(x, rows):
            spread = laplace(*rows[0], masks)
            kaps = None if kb_next is None else strided(kap, x)
            for v in each:
                back = 2.0 * b_now[x, v] + spread[v] + data[x, v]
                if b_after is not None:
                    back = back - b_after[x, v]
                total = image[x, v] + grad[x, v] * back
                if kb_next is None:
                    total = (image_scale * total).astype(result.dtype)
                    result[x % block_x // 2, (x % 2 * APX + x // block_x) * many + v] = total
                else:
                    image[x, v] = total
                    b_next[x, v] = back
                    kb_next[x, v] = kaps[v] * back

        sweep(span_x, [kb], body, 32)

    adjoint(kb_3, d_3, None, d_2, g_2, kb_2, b_2)
    adjoint(kb_2, b_2, d_3, d_1, g_1, kb_1, b_1)
    adjoint(kb_1, b_1, b_2, d_0, g_0, None, None)
    for k, out_ref in enumerate(out_refs):
        out_ref[...] = result[place // 2 ^ k]


def wave(models, started):
    span_x, many, _, depth = started[0].shape
    near = len(models)
    flat = pltpu.VMEM((span_x, many * LANES, depth), jnp.float32)
    field = pltpu.VMEM((span_x + 1, many, LANES, depth), jnp.float32)
    plain = pltpu.VMEM((span_x, many, LANES, depth), jnp.float32)
    tiles = APX * many
    out = jax.ShapeDtypeStruct((2 * tiles, LANES, depth), jnp.bfloat16)
    terms = pl.pallas_call(
        functools.partial(wave_kernel, near),
        out_shape=(out,) * (near // 2),
        in_specs=[vmem()] * (near + 3),
        out_specs=(vmem(),) * (near // 2),
        scratch_shapes=[flat] * 2 + [field] * 9 + [plain] * 6
        + [pltpu.VMEM((near // 2, 2 * tiles, LANES, depth), jnp.bfloat16)],
        compiler_params=limit(20),
        name="wave",
    )(*models, *started)
    return terms[::-1]


def wave_split_depth(models, before, current):
    near = len(models)
    order = (lax.axis_index("shot") % near) ^ jnp.arange(near)
    chips = near // 2
    length = models[-1].shape[0]
    pairs = zip(models[:chips][::-1], models[chips:][::-1])
    model = jnp.stack([part for own, other in pairs for part in (own[:length], other)])
    model = model[order]
    span_x, span_y, depth = before.shape
    block_x, tiles, block_y, _ = model.shape
    grids = model.reshape(block_x, APX, APY, 2, block_y, depth).transpose(3, 1, 0, 2, 4, 5)
    grids = grids.reshape(2, span_x, span_y, depth).astype(jnp.float32)
    image = image_scale * propagate(
        grids[0],
        speed_factor * grids[1],
        before.astype(jnp.float32),
        current.astype(jnp.float32),
        laplace_many,
    )
    many = span_y // LANES
    image = image.reshape(APX, chips, 2, LANES, many, depth).transpose(1, 2, 0, 4, 3, 5)
    image = image.reshape(chips, 2 * APX * many, LANES, depth).astype(jnp.bfloat16)
    image = image[chip_place(chips) ^ jnp.arange(chips)]
    return [image[k] for k in range(chips)]


def stack_kernel(slots, near, facts_ref, *refs):
    terms_refs = refs[:near][::-1]
    mine_ref, other_ref, facts, total, lined, sem = refs[near:]
    count = 2 * mine_ref.shape[0]
    half = terms_refs[0].shape[0] // 2
    wide = half // APX
    width = LANES // APY
    grid_rows = total.shape[1] // wide
    copy = pltpu.make_async_copy(facts_ref, facts, sem)
    copy.start()
    me = lax.axis_index("shot")

    def clear(index, carry):
        for r in range(2):
            total[r, index] = jnp.zeros(total.shape[2:], total.dtype)
        return carry

    lax.fori_loop(0, total.shape[1], clear, 0, unroll=8)
    copy.wait()
    for k, terms_ref in enumerate(terms_refs):
        shot = FACTS * (me ^ 2 * k)
        first = facts[0, shot + slots] * wide
        rows = pl.ds(facts[0, shot + slots + 1] * width, LANES)
        for r in range(2):
            sums = [
                total[r, first + tile, rows] + terms_ref[r * half + tile].astype(jnp.float32)
                for tile in range(half)
            ]
            for tile in range(half):
                total[r, first + tile, rows] = sums[tile]

    def line(row, carry):
        for r in range(2):
            for part in range(wide):
                for tile in range(total.shape[2] // LANES):
                    at = pl.ds(tile * LANES * wide + part, LANES, stride=wide)
                    lined[r, row, at] = total[
                        r, row * wide + part, tile * LANES:(tile + 1) * LANES
                    ]
        return carry

    lax.fori_loop(0, grid_rows, line, 0, unroll=8)

    def give(chip, carry):
        for own, out_ref in enumerate((mine_ref, other_ref)):
            found = []
            for slot in range(slots):
                block = facts[0, FACTS * (2 * chip + (me + own) % 2) + slot]
                rows = pl.ds(pl.multiple_of(block % GRID_COLS * LANES, LANES), LANES)
                found += [lined[r, block // GRID_COLS, rows] for r in range(2)]
            for index, tile in enumerate(found):
                out_ref[chip, index] = tile.astype(out_ref.dtype)
        return carry

    lax.fori_loop(0, count // 2, give, 0, unroll=8)


def join_kernel(mine_ref, other_ref, out_ref):
    for chip in range(out_ref.shape[0]):
        total = mine_ref[chip] + other_ref[chip].astype(jnp.float32)
        out_ref[chip] = total.astype(out_ref.dtype)


def finish_kernel(near, sums_ref, out_ref):
    for place in range(near):
        for slot in range(out_ref.shape[0]):
            for r in range(2):
                result = sums_ref[place, 2 * slot + r].astype(jnp.float32)
                for chip in range(place + near, sums_ref.shape[0], near):
                    result = result + sums_ref[chip, 2 * slot + r].astype(jnp.float32)
                out_ref[slot, 2 * place + r] = result


def per_device(
    velocity_p,
    velocity_s,
    density,
    perturbation,
    seafloor,
    owner_ids,
    corner_x,
    corner_y,
    wave_prev,
    wave_now,
):
    slots, block_x, block_y, depth = velocity_p.shape
    count = lax.axis_size("shot")
    assert count == 2 * block_x and block_y == LANES
    assert slots + 2 <= FACTS and FACTS * count <= depth
    patch = APX * APY
    split = lax.axis_size("depth") > 1
    if split:
        seafloor = seafloor - lax.axis_index("depth") * depth

    near = block_x
    assert count % near == 0 and near & (near - 1) == 0

    def swap(values):
        return [
            lax.ppermute(values[k], "shot", [(i, i ^ 2 * k) for i in range(count)])
            if k else values[0]
            for k in range(len(values) - 1, -1, -1)
        ]

    def across(value):
        return lax.ppermute(value, "shot", [(i, i ^ 1) for i in range(count)])

    sent = pl.pallas_call(
        prepare_kernel,
        out_shape=jax.ShapeDtypeStruct((count, 2 * slots + 1, block_y, depth), jnp.bfloat16),
        in_specs=[smem()] * 2 + [pl.BlockSpec(memory_space=pltpu.HBM)] * 6,
        out_specs=vmem(),
        scratch_shapes=[
            pltpu.SMEM(owner_ids.shape, jnp.int32),
            pltpu.VMEM(seafloor.shape, jnp.int32),
            *[pltpu.VMEM(velocity_p.shape, jnp.bfloat16) for _ in range(4)],
            pltpu.SemaphoreType.DMA((6,)),
        ],
        name="prepare",
    )(
        corner_x, corner_y, owner_ids, seafloor,
        velocity_p, velocity_s, density, perturbation,
    )
    pieces = lax.all_to_all(sent, "shot", 0, 0, tiled=True)

    if not split:
        started = start(wave_prev[0], wave_now[0])
        pieces, started = lax.optimization_barrier((pieces, started))
    *picked, facts = pl.pallas_call(
        functools.partial(pick_kernel, slots, near),
        out_shape=(
            *[
                jax.ShapeDtypeStruct((patch * tiles, block_y, depth), jnp.bfloat16)
                for tiles in [4] * (near // 2 - 1) + [2, 2]
            ],
            jax.ShapeDtypeStruct((1, depth), jnp.int32),
        ),
        in_specs=[vmem()],
        out_specs=(vmem(),) * (near // 2 + 2),
        scratch_shapes=[
            pltpu.SMEM((1, depth), jnp.int32),
            pltpu.SMEM((count * slots,), jnp.int32),
            pltpu.SemaphoreType.DMA,
        ],
        compiler_params=limit(3),
        name="pick",
    )(pieces.reshape(count * (2 * slots + 1), block_y, depth))
    *picked, beside = picked
    models = swap(picked[::-1])
    handed = [value[patch * 2:] for value in models[:-1]] + [beside]
    models = models + [across(value) for value in handed]

    if split:
        terms = wave_split_depth(models, wave_prev[0], wave_now[0])
    else:
        terms = wave(models, started)
    terms = swap(terms)

    chips = count // 2
    grid_rows = count * slots // GRID_COLS
    wide = terms[0].shape[0] // 2 // APX
    shape = (chips, 2 * slots, block_y, depth)
    mine, other = pl.pallas_call(
        functools.partial(stack_kernel, slots, near // 2),
        out_shape=(
            jax.ShapeDtypeStruct(shape, jnp.float32), jax.ShapeDtypeStruct(shape, jnp.bfloat16)
        ),
        in_specs=[vmem()] * (near // 2 + 1),
        out_specs=(vmem(), vmem()),
        scratch_shapes=[
            pltpu.SMEM(facts.shape, jnp.int32),
            pltpu.VMEM((2, grid_rows * wide, GRID_COLS * LANES // APY, depth), jnp.float32),
            pltpu.VMEM((2, grid_rows, GRID_COLS * block_y, depth), jnp.float32),
            pltpu.SemaphoreType.DMA,
        ],
        compiler_params=limit(4),
        name="stack",
    )(facts, *terms)
    joined = pl.pallas_call(
        join_kernel,
        out_shape=jax.ShapeDtypeStruct(shape, jnp.bfloat16),
        in_specs=[vmem()] * 2,
        out_specs=vmem(),
        compiler_params=limit(2),
        name="join",
    )(mine, across(other))
    sums = lax.all_to_all(
        joined, "shot", 0, 0, tiled=True,
        axis_index_groups=[list(range(core, count, 2)) for core in range(2)],
    )
    return pl.pallas_call(
        functools.partial(finish_kernel, near // 2),
        out_shape=jax.ShapeDtypeStruct(velocity_p.shape, jnp.float32),
        in_specs=[vmem()],
        out_specs=vmem(),
        compiler_params=limit(2),
        name="finish",
    )(sums)


def solution(mesh):
    in_specs = (
        P(("grp", "shot"), None, None, "depth"),
        P(("grp", "shot"), None, None, "depth"),
        P(("grp", "shot"), None, None, "depth"),
        P(("grp", "shot"), None, None, "depth"),
        P(("grp", "shot"), None, None),
        P(("grp", "shot")),
        P(("grp", "shot")),
        P(("grp", "shot")),
        P(("grp", "shot"), None, None, "depth"),
        P(("grp", "shot"), None, None, "depth"),
    )
    out_specs = P(("grp", "shot"), None, None, "depth")
    return jax.shard_map(
        per_device, mesh=mesh, in_specs=in_specs, out_specs=out_specs, check_vma=False
    )
```

```python
import functools

import jax
import jax.numpy as jnp
from jax import lax
from jax.experimental import pallas as pl
from jax.experimental.pallas import tpu as pltpu
from jax.sharding import PartitionSpec as P

APX = 4
APY = 4
STEPS = 4
GRID_COLS = 8
FACTS = 8
LANES = 8

speed_factor = 0.28
image_scale = 0.01


def with_halo(block, sides, width):
    for axis, dim in sides:
        count = lax.axis_size(axis)
        forward = [(i, i + 1) for i in range(count - 1)]
        backward = [(target, source) for source, target in forward]
        low = lax.ppermute(
            lax.slice_in_dim(block, block.shape[dim] - width, None, axis=dim), axis, forward
        )
        high = lax.ppermute(lax.slice_in_dim(block, 0, width, axis=dim), axis, backward)
        block = jnp.concatenate([low, block, high], axis=dim)
    return block


def laplace_many(fields):
    stacked = jnp.stack(fields)
    padded = with_halo(stacked.astype(jnp.bfloat16), (("depth", 3),), 1).astype(stacked.dtype)
    padded = jnp.pad(padded, ((0, 0), (1, 1), (1, 1), (0, 0)))
    beside = padded[:, 2:, 1:-1, 1:-1] + padded[:, :-2, 1:-1, 1:-1]
    beside = beside + padded[:, 1:-1, 2:, 1:-1] + padded[:, 1:-1, :-2, 1:-1]
    beside = beside + padded[:, 1:-1, 1:-1, 2:] + padded[:, 1:-1, 1:-1, :-2]
    result = beside - 6.0 * stacked
    return [result[index] for index in range(len(fields))]


def propagate(kappa, contrast, before, current, apply):
    grads = []
    datas = []
    grad_now = apply([current])[0]
    delta_prev = jnp.zeros_like(current)
    delta_now = contrast * grad_now
    grads.append(grad_now)
    datas.append(delta_now)
    before, current = (current, 2.0 * current - before + kappa * grad_now)
    for step in range(1, STEPS):
        grad_now, spread = apply([current, delta_now])
        delta_next = 2.0 * delta_now - delta_prev + kappa * spread + contrast * grad_now
        grads.append(grad_now)
        datas.append(delta_next)
        delta_prev, delta_now = (delta_now, delta_next)
        if step + 1 < STEPS:
            before, current = (current, 2.0 * current - before + kappa * grad_now)
    back = datas[STEPS - 1]
    back_after = jnp.zeros_like(back)
    image = grads[STEPS - 1] * back
    for step in range(STEPS - 2, -1, -1):
        spread = apply([kappa * back])
        back_new = 2.0 * back - back_after + spread[0] + datas[step]
        image = image + grads[step] * back_new
        back_after, back = (back, back_new)
    return image


def limit(mebibytes):
    return pltpu.CompilerParams(vmem_limit_bytes=mebibytes * 2**20)


def chip_place(near):
    return lax.axis_index("shot") // 2 % near


def parts(refs, length):
    chips = len(refs) // 2
    own, other = refs[:chips][::-1], refs[chips:][::-1]
    return [
        part for first, second in zip(own, other) for part in (first.at[pl.ds(0, length)], second)
    ]


def vmem():
    return pl.BlockSpec(memory_space=pltpu.VMEM)


def smem():
    return pl.BlockSpec(memory_space=pltpu.SMEM)


def prepare_kernel(
    row_ref, col_ref, ids_hbm, floor_hbm, p_hbm, s_hbm, rho_hbm, pert_hbm, out_ref,
    ids, floors, p, s, rho, pert, sems,
):
    slots, block_x, block_y, depth = p.shape
    near = block_x
    copies = [
        pltpu.make_async_copy(source, target, sems.at[index])
        for index, (source, target) in enumerate(
            [(p_hbm, p), (s_hbm, s), (rho_hbm, rho), (floor_hbm, floors), (pert_hbm, pert),
             (ids_hbm, ids)]
        )
    ]
    for copy in copies:
        copy.start()
    shape = (block_y, depth)
    deep = lax.broadcasted_iota(jnp.int32, shape, 1).astype(jnp.float32)
    lane = lax.broadcasted_iota(jnp.int32, shape, 1)
    same = lax.broadcasted_iota(jnp.int32, (block_y, block_y), 0) == (
        lax.broadcasted_iota(jnp.int32, (block_y, block_y), 1)
    )
    for copy in copies:
        copy.wait()
    for slot in range(slots):
        lines = floors[slot].astype(jnp.float32)
        for x in range(block_x):
            line = jnp.broadcast_to(lines[x:x + 1], (block_y, block_y))
            floor = jnp.sum(jnp.where(same, line, 0.0), axis=1, keepdims=True)
            primary = p[slot, x].astype(jnp.float32)
            shear = s[slot, x].astype(jnp.float32)
            square = primary * primary
            stiffness = jnp.where(deep >= floor, square + shear * shear, square)
            coef = speed_factor * stiffness / rho[slot, x].astype(jnp.float32)
            coef = coef.astype(out_ref.dtype)
            for piece in range(x, out_ref.shape[0], near):
                out_ref[piece, 2 * slot] = coef
                out_ref[piece, 2 * slot + 1] = pert[slot, x]
    lane = lane - FACTS * lax.axis_index("shot")
    facts = jnp.where(lane == slots, row_ref[0], 0)
    facts = jnp.where(lane == slots + 1, col_ref[0], facts)
    for slot in range(slots):
        facts = jnp.where(lane == slot, ids[slot], facts)
    facts = facts.astype(jnp.float32).astype(out_ref.dtype)
    for piece in range(out_ref.shape[0]):
        out_ref[piece, 2 * slots] = facts


def pick_kernel(slots, near, pieces_ref, *refs):
    chips = near // 2
    out_refs = refs[:chips][::-1]
    beside_ref, facts_ref, facts, spots, sem = refs[chips:]
    count = spots.shape[0] // slots
    tiles = 2 * slots + 1
    line = pieces_ref[2 * slots].astype(jnp.float32)
    for piece in range(1, count):
        line = line + pieces_ref[piece * tiles + 2 * slots].astype(jnp.float32)
    facts_ref[...] = line.astype(jnp.int32)[0:1]
    copy = pltpu.make_async_copy(facts_ref, facts, sem)
    copy.start()
    me = lax.axis_index("shot")
    copy.wait()
    for piece in range(count):
        for slot in range(slots):
            spots[facts[0, FACTS * piece + slot]] = piece * tiles + 2 * slot
    for t in range(near):
        shot = me ^ t
        out_ref, start_tile = out_refs[t // 2], t % 2 * APX * APY * 2
        if t == 1:
            out_ref, start_tile = beside_ref, 0
        first = facts[0, FACTS * shot + slots] * GRID_COLS + facts[0, FACTS * shot + slots + 1]
        for x in range(APX):
            found = []
            for y in range(APY):
                spot = spots[first + x * GRID_COLS + y]
                found += [pieces_ref[spot], pieces_ref[spot + 1]]
            for index, tile in enumerate(found):
                out_ref[start_tile + x * APY * 2 + index] = tile


def ends(shape):
    lane = lax.broadcasted_iota(jnp.int32, shape, 1)
    row = lax.broadcasted_iota(jnp.int32, shape, 0)
    return lane == 0, lane == shape[1] - 1, row == 0, row == shape[0] - 1


def laplace(before, here, after, masks):
    lane_0, lane_n, row_0, row_n = masks
    many = len(here)
    depth = here[0].shape[1]
    low = [jnp.where(row_0, 0.0, pltpu.roll(here[-1], 1, 0))] + here[:-1]
    high = here[1:] + [jnp.where(row_n, 0.0, pltpu.roll(here[0], LANES - 1, 0))]
    result = []
    for v in range(many):
        up = jnp.where(lane_0, 0.0, pltpu.roll(here[v], 1, 1))
        down = jnp.where(lane_n, 0.0, pltpu.roll(here[v], depth - 1, 1))
        total = (before[v] + after[v]) + (low[v] + high[v]) + (up + down)
        result.append(total - 6.0 * here[v])
    return result


def registers(ref, x):
    return [ref[x, v] for v in range(ref.shape[1])]


def strided(ref, x):
    many = ref.shape[1] // LANES
    return [ref[x, pl.ds(v, LANES, stride=many)] for v in range(many)]


def sweep(count, fields, body, unroll):
    many = fields[0].shape[1]
    zero = [jnp.zeros(fields[0].shape[2:], jnp.float32)] * many
    first = [(zero, registers(field, 0)) for field in fields]

    def step(x, carry):
        rows = [
            (before, here, registers(field, x + 1))
            for (before, here), field in zip(carry, fields)
        ]
        body(x, rows)
        return [(here, after) for _, here, after in rows]

    lax.fori_loop(0, count, step, first, unroll=unroll)


def start_kernel(prev_ref, now_ref, wave_ref, grad_ref, next_ref, flat, flat_prev, field):
    span_x, span_y, depth = now_ref.shape
    many = span_y // LANES
    masks = ends((LANES, depth))

    def load(x, carry):
        flat[x] = now_ref[x].astype(jnp.float32)
        flat_prev[x] = prev_ref[x].astype(jnp.float32)
        return carry

    lax.fori_loop(0, span_x, load, 0, unroll=2)

    def order(x, carry):
        rows = strided(flat, x)
        older = strided(flat_prev, x)
        for v in range(many):
            field[x, v] = rows[v]
            wave_ref[x, v] = rows[v]
            next_ref[x, v] = 2.0 * rows[v] - older[v]
        return carry

    lax.fori_loop(0, span_x, order, 0, unroll=2)
    for v in range(many):
        field[span_x, v] = jnp.zeros((LANES, depth), jnp.float32)

    def body(x, rows):
        grads = laplace(*rows[0], masks)
        for v in range(many):
            grad_ref[x, v] = grads[v]

    sweep(span_x, [field], body, 32)


def start(before, current):
    span_x, span_y, depth = before.shape
    many = span_y // LANES
    out = jax.ShapeDtypeStruct((span_x, many, LANES, depth), jnp.float32)
    flat = pltpu.VMEM((span_x, span_y, depth), jnp.float32)
    return pl.pallas_call(
        start_kernel,
        out_shape=(out, out, out),
        in_specs=[vmem()] * 2,
        out_specs=(vmem(),) * 3,
        scratch_shapes=[flat, flat, pltpu.VMEM((span_x + 1, many, LANES, depth), jnp.float32)],
        compiler_params=limit(8),
        cost_estimate=pl.CostEstimate(
            flops=20 * before.size, bytes_accessed=16 * before.size, transcendentals=0
        ),
        name="start",
    )(before, current)


def wave_kernel(near, *refs):
    chips = near // 2
    model_refs = parts(refs[:near], 2 * APX * APY)
    u_0, g_0, next_ref = refs[near:near + 3]
    refs = refs[near + 3:]
    out_refs = refs[:chips][::-1]
    kap, con, u_1, u_2, u_3, d_0, d_1, d_2, kb_3, kb_2, kb_1 = refs[chips:chips + 11]
    g_1, g_2, d_3, b_2, b_1, image, result = refs[chips + 11:]
    span_x, many = u_0.shape[:2]
    depth = u_0.shape[3]
    block_y = model_refs[0].shape[1]
    block_x = span_x // APX
    place = lax.axis_index("shot") % near
    masks = ends((LANES, depth))
    each = range(many)
    for field in (u_1, u_2, u_3, d_0, d_1, d_2, kb_3, kb_2, kb_1):
        for v in each:
            field[span_x, v] = jnp.zeros((LANES, depth), jnp.float32)

    for k, model_ref in enumerate(model_refs):
        for x in range(APX):
            at = x * block_x + (place ^ k)
            for y in range(APY):
                rows = pl.ds(y * block_y, block_y)
                tile = 2 * (x * APY + y)
                kap[at, rows] = model_ref[tile].astype(jnp.float32)
                con[at, rows] = speed_factor * model_ref[tile + 1].astype(jnp.float32)

    def forward_0(x, carry):
        kaps, cons, grads = strided(kap, x), strided(con, x), registers(g_0, x)
        older = registers(next_ref, x)
        for v in each:
            d_0[x, v] = cons[v] * grads[v]
            u_1[x, v] = older[v] + kaps[v] * grads[v]
        return carry

    lax.fori_loop(0, span_x, forward_0, 0, unroll=32)

    def forward(u_now, u_prev, d_now, d_prev, u_next, d_next, g_now):
        def body(x, rows):
            waves, deltas = rows
            grads = laplace(*waves, masks)
            spread = laplace(*deltas, masks)
            kaps, cons = strided(kap, x), strided(con, x)
            for v in each:
                value = 2.0 * deltas[1][v] + kaps[v] * spread[v] + cons[v] * grads[v]
                if d_prev is not None:
                    value = value - d_prev[x, v]
                d_next[x, v] = value
                if u_next is None:
                    image[x, v] = grads[v] * value
                    kb_3[x, v] = kaps[v] * value
                else:
                    g_now[x, v] = grads[v]
                    u_next[x, v] = 2.0 * waves[1][v] - u_prev[x, v] + kaps[v] * grads[v]

        sweep(span_x, [u_now, d_now], body, 32)

    forward(u_1, u_0, d_0, None, u_2, d_1, g_1)
    forward(u_2, u_1, d_1, d_0, u_3, d_2, g_2)
    forward(u_3, u_2, d_2, d_1, None, d_3, None)

    def adjoint(kb, b_now, b_after, data, grad, kb_next, b_next):
        def body(x, rows):
            spread = laplace(*rows[0], masks)
            kaps = None if kb_next is None else strided(kap, x)
            for v in each:
                back = 2.0 * b_now[x, v] + spread[v] + data[x, v]
                if b_after is not None:
                    back = back - b_after[x, v]
                total = image[x, v] + grad[x, v] * back
                if kb_next is None:
                    total = (image_scale * total).astype(result.dtype)
                    result[x % block_x // 2, (x % 2 * APX + x // block_x) * many + v] = total
                else:
                    image[x, v] = total
                    b_next[x, v] = back
                    kb_next[x, v] = kaps[v] * back

        sweep(span_x, [kb], body, 32)

    adjoint(kb_3, d_3, None, d_2, g_2, kb_2, b_2)
    adjoint(kb_2, b_2, d_3, d_1, g_1, kb_1, b_1)
    adjoint(kb_1, b_1, b_2, d_0, g_0, None, None)
    for k, out_ref in enumerate(out_refs):
        out_ref[...] = result[place // 2 ^ k]


def wave(models, started):
    span_x, many, _, depth = started[0].shape
    near = len(models)
    flat = pltpu.VMEM((span_x, many * LANES, depth), jnp.float32)
    field = pltpu.VMEM((span_x + 1, many, LANES, depth), jnp.float32)
    plain = pltpu.VMEM((span_x, many, LANES, depth), jnp.float32)
    tiles = APX * many
    out = jax.ShapeDtypeStruct((2 * tiles, LANES, depth), jnp.bfloat16)
    terms = pl.pallas_call(
        functools.partial(wave_kernel, near),
        out_shape=(out,) * (near // 2),
        in_specs=[vmem()] * (near + 3),
        out_specs=(vmem(),) * (near // 2),
        scratch_shapes=[flat] * 2 + [field] * 9 + [plain] * 6
        + [pltpu.VMEM((near // 2, 2 * tiles, LANES, depth), jnp.bfloat16)],
        compiler_params=limit(20),
        name="wave",
    )(*models, *started)
    return terms[::-1]


def wave_split_depth(models, before, current):
    near = len(models)
    order = (lax.axis_index("shot") % near) ^ jnp.arange(near)
    chips = near // 2
    length = models[-1].shape[0]
    pairs = zip(models[:chips][::-1], models[chips:][::-1])
    model = jnp.stack([part for own, other in pairs for part in (own[:length], other)])
    model = model[order]
    span_x, span_y, depth = before.shape
    block_x, tiles, block_y, _ = model.shape
    grids = model.reshape(block_x, APX, APY, 2, block_y, depth).transpose(3, 1, 0, 2, 4, 5)
    grids = grids.reshape(2, span_x, span_y, depth).astype(jnp.float32)
    image = image_scale * propagate(
        grids[0],
        speed_factor * grids[1],
        before.astype(jnp.float32),
        current.astype(jnp.float32),
        laplace_many,
    )
    many = span_y // LANES
    image = image.reshape(APX, chips, 2, LANES, many, depth).transpose(1, 2, 0, 4, 3, 5)
    image = image.reshape(chips, 2 * APX * many, LANES, depth).astype(jnp.bfloat16)
    image = image[chip_place(chips) ^ jnp.arange(chips)]
    return [image[k] for k in range(chips)]


def stack_kernel(slots, near, facts_ref, *refs):
    terms_refs = refs[:near][::-1]
    mine_ref, other_ref, facts, total, lined, sem = refs[near:]
    count = 2 * mine_ref.shape[0]
    half = terms_refs[0].shape[0] // 2
    wide = half // APX
    width = LANES // APY
    grid_rows = total.shape[1] // wide
    copy = pltpu.make_async_copy(facts_ref, facts, sem)
    copy.start()
    me = lax.axis_index("shot")

    def clear(index, carry):
        for r in range(2):
            total[r, index] = jnp.zeros(total.shape[2:], total.dtype)
        return carry

    lax.fori_loop(0, total.shape[1], clear, 0, unroll=8)
    copy.wait()
    for k, terms_ref in enumerate(terms_refs):
        shot = FACTS * (me ^ 2 * k)
        first = facts[0, shot + slots] * wide
        rows = pl.ds(facts[0, shot + slots + 1] * width, LANES)
        for r in range(2):
            sums = [
                total[r, first + tile, rows] + terms_ref[r * half + tile].astype(jnp.float32)
                for tile in range(half)
            ]
            for tile in range(half):
                total[r, first + tile, rows] = sums[tile]

    def line(row, carry):
        for r in range(2):
            for part in range(wide):
                for tile in range(total.shape[2] // LANES):
                    at = pl.ds(tile * LANES * wide + part, LANES, stride=wide)
                    lined[r, row, at] = total[
                        r, row * wide + part, tile * LANES:(tile + 1) * LANES
                    ]
        return carry

    lax.fori_loop(0, grid_rows, line, 0, unroll=8)

    def give(chip, carry):
        for own, out_ref in enumerate((mine_ref, other_ref)):
            found = []
            for slot in range(slots):
                block = facts[0, FACTS * (2 * chip + (me + own) % 2) + slot]
                rows = pl.ds(pl.multiple_of(block % GRID_COLS * LANES, LANES), LANES)
                found += [lined[r, block // GRID_COLS, rows] for r in range(2)]
            for index, tile in enumerate(found):
                out_ref[chip, index] = tile.astype(out_ref.dtype)
        return carry

    lax.fori_loop(0, count // 2, give, 0, unroll=8)


def join_kernel(mine_ref, other_ref, out_ref):
    for chip in range(out_ref.shape[0]):
        total = mine_ref[chip] + other_ref[chip].astype(jnp.float32)
        out_ref[chip] = total.astype(out_ref.dtype)


def finish_kernel(near, sums_ref, out_ref):
    for place in range(near):
        for slot in range(out_ref.shape[0]):
            for r in range(2):
                result = sums_ref[place, 2 * slot + r].astype(jnp.float32)
                for chip in range(place + near, sums_ref.shape[0], near):
                    result = result + sums_ref[chip, 2 * slot + r].astype(jnp.float32)
                out_ref[slot, 2 * place + r] = result


def per_device(
    velocity_p,
    velocity_s,
    density,
    perturbation,
    seafloor,
    owner_ids,
    corner_x,
    corner_y,
    wave_prev,
    wave_now,
):
    slots, block_x, block_y, depth = velocity_p.shape
    count = lax.axis_size("shot")
    assert count == 2 * block_x and block_y == LANES
    assert slots + 2 <= FACTS and FACTS * count <= depth
    patch = APX * APY
    split = lax.axis_size("depth") > 1
    if split:
        seafloor = seafloor - lax.axis_index("depth") * depth

    near = block_x
    assert count % near == 0 and near & (near - 1) == 0

    def swap(values):
        return [
            lax.ppermute(values[k], "shot", [(i, i ^ 2 * k) for i in range(count)])
            if k else values[0]
            for k in range(len(values) - 1, -1, -1)
        ]

    def across(value):
        return lax.ppermute(value, "shot", [(i, i ^ 1) for i in range(count)])

    sent = pl.pallas_call(
        prepare_kernel,
        out_shape=jax.ShapeDtypeStruct((count, 2 * slots + 1, block_y, depth), jnp.bfloat16),
        in_specs=[smem()] * 2 + [pl.BlockSpec(memory_space=pltpu.HBM)] * 6,
        out_specs=vmem(),
        scratch_shapes=[
            pltpu.SMEM(owner_ids.shape, jnp.int32),
            pltpu.VMEM(seafloor.shape, jnp.int32),
            *[pltpu.VMEM(velocity_p.shape, jnp.bfloat16) for _ in range(4)],
            pltpu.SemaphoreType.DMA((6,)),
        ],
        name="prepare",
    )(
        corner_x, corner_y, owner_ids, seafloor,
        velocity_p, velocity_s, density, perturbation,
    )
    pieces = lax.all_to_all(sent, "shot", 0, 0, tiled=True)

    if not split:
        started = start(wave_prev[0], wave_now[0])
    *picked, facts = pl.pallas_call(
        functools.partial(pick_kernel, slots, near),
        out_shape=(
            *[
                jax.ShapeDtypeStruct((patch * tiles, block_y, depth), jnp.bfloat16)
                for tiles in [4] * (near // 2 - 1) + [2, 2]
            ],
            jax.ShapeDtypeStruct((1, depth), jnp.int32),
        ),
        in_specs=[vmem()],
        out_specs=(vmem(),) * (near // 2 + 2),
        scratch_shapes=[
            pltpu.SMEM((1, depth), jnp.int32),
            pltpu.SMEM((count * slots,), jnp.int32),
            pltpu.SemaphoreType.DMA,
        ],
        compiler_params=limit(3),
        name="pick",
    )(pieces.reshape(count * (2 * slots + 1), block_y, depth))
    *picked, beside = picked
    models = swap(picked[::-1])
    handed = [value[patch * 2:] for value in models[:-1]] + [beside]
    models = models + [across(value) for value in handed]

    if split:
        terms = wave_split_depth(models, wave_prev[0], wave_now[0])
    else:
        terms = wave(models, started)
    terms = swap(terms)

    chips = count // 2
    grid_rows = count * slots // GRID_COLS
    wide = terms[0].shape[0] // 2 // APX
    shape = (chips, 2 * slots, block_y, depth)
    mine, other = pl.pallas_call(
        functools.partial(stack_kernel, slots, near // 2),
        out_shape=(
            jax.ShapeDtypeStruct(shape, jnp.float32), jax.ShapeDtypeStruct(shape, jnp.bfloat16)
        ),
        in_specs=[vmem()] * (near // 2 + 1),
        out_specs=(vmem(), vmem()),
        scratch_shapes=[
            pltpu.SMEM(facts.shape, jnp.int32),
            pltpu.VMEM((2, grid_rows * wide, GRID_COLS * LANES // APY, depth), jnp.float32),
            pltpu.VMEM((2, grid_rows, GRID_COLS * block_y, depth), jnp.float32),
            pltpu.SemaphoreType.DMA,
        ],
        compiler_params=limit(4),
        name="stack",
    )(facts, *terms)
    joined = pl.pallas_call(
        join_kernel,
        out_shape=jax.ShapeDtypeStruct(shape, jnp.bfloat16),
        in_specs=[vmem()] * 2,
        out_specs=vmem(),
        compiler_params=limit(2),
        name="join",
    )(mine, across(other))
    sums = lax.all_to_all(
        joined, "shot", 0, 0, tiled=True,
        axis_index_groups=[list(range(core, count, 2)) for core in range(2)],
    )
    return pl.pallas_call(
        functools.partial(finish_kernel, near // 2),
        out_shape=jax.ShapeDtypeStruct(velocity_p.shape, jnp.float32),
        in_specs=[vmem()],
        out_specs=vmem(),
        compiler_params=limit(2),
        name="finish",
    )(sums)


def solution(mesh):
    in_specs = (
        P(("grp", "shot"), None, None, "depth"),
        P(("grp", "shot"), None, None, "depth"),
        P(("grp", "shot"), None, None, "depth"),
        P(("grp", "shot"), None, None, "depth"),
        P(("grp", "shot"), None, None),
        P(("grp", "shot")),
        P(("grp", "shot")),
        P(("grp", "shot")),
        P(("grp", "shot"), None, None, "depth"),
        P(("grp", "shot"), None, None, "depth"),
    )
    out_specs = P(("grp", "shot"), None, None, "depth")
    return jax.shard_map(
        per_device, mesh=mesh, in_specs=in_specs, out_specs=out_specs, check_vma=False
    )
```

```python
import functools

import jax
import jax.numpy as jnp
from jax import lax
from jax.experimental import pallas as pl
from jax.experimental.pallas import tpu as pltpu
from jax.sharding import PartitionSpec as P

APX = 4
APY = 4
STEPS = 4
GRID_COLS = 8
FACTS = 8
LANES = 8

speed_factor = 0.28
image_scale = 0.01


def with_halo(block, sides, width):
    for axis, dim in sides:
        count = lax.axis_size(axis)
        forward = [(i, i + 1) for i in range(count - 1)]
        backward = [(target, source) for source, target in forward]
        low = lax.ppermute(
            lax.slice_in_dim(block, block.shape[dim] - width, None, axis=dim), axis, forward
        )
        high = lax.ppermute(lax.slice_in_dim(block, 0, width, axis=dim), axis, backward)
        block = jnp.concatenate([low, block, high], axis=dim)
    return block


def laplace_many(fields):
    stacked = jnp.stack(fields)
    padded = with_halo(stacked.astype(jnp.bfloat16), (("depth", 3),), 1).astype(stacked.dtype)
    padded = jnp.pad(padded, ((0, 0), (1, 1), (1, 1), (0, 0)))
    beside = padded[:, 2:, 1:-1, 1:-1] + padded[:, :-2, 1:-1, 1:-1]
    beside = beside + padded[:, 1:-1, 2:, 1:-1] + padded[:, 1:-1, :-2, 1:-1]
    beside = beside + padded[:, 1:-1, 1:-1, 2:] + padded[:, 1:-1, 1:-1, :-2]
    result = beside - 6.0 * stacked
    return [result[index] for index in range(len(fields))]


def propagate(kappa, contrast, before, current, apply):
    grads = []
    datas = []
    grad_now = apply([current])[0]
    delta_prev = jnp.zeros_like(current)
    delta_now = contrast * grad_now
    grads.append(grad_now)
    datas.append(delta_now)
    before, current = (current, 2.0 * current - before + kappa * grad_now)
    for step in range(1, STEPS):
        grad_now, spread = apply([current, delta_now])
        delta_next = 2.0 * delta_now - delta_prev + kappa * spread + contrast * grad_now
        grads.append(grad_now)
        datas.append(delta_next)
        delta_prev, delta_now = (delta_now, delta_next)
        if step + 1 < STEPS:
            before, current = (current, 2.0 * current - before + kappa * grad_now)
    back = datas[STEPS - 1]
    back_after = jnp.zeros_like(back)
    image = grads[STEPS - 1] * back
    for step in range(STEPS - 2, -1, -1):
        spread = apply([kappa * back])
        back_new = 2.0 * back - back_after + spread[0] + datas[step]
        image = image + grads[step] * back_new
        back_after, back = (back, back_new)
    return image


def limit(mebibytes):
    return pltpu.CompilerParams(vmem_limit_bytes=mebibytes * 2**20)


def chip_place(near):
    return lax.axis_index("shot") // 2 % near


def parts(refs, length):
    chips = len(refs) // 2
    own, other = refs[:chips][::-1], refs[chips:][::-1]
    return [
        part for first, second in zip(own, other) for part in (first.at[pl.ds(0, length)], second)
    ]


def vmem():
    return pl.BlockSpec(memory_space=pltpu.VMEM)


def smem():
    return pl.BlockSpec(memory_space=pltpu.SMEM)


def prepare_kernel(
    row_ref, col_ref, ids_hbm, floor_hbm, p_hbm, s_hbm, rho_hbm, pert_hbm, out_ref,
    ids, floors, p, s, rho, pert, sems,
):
    slots, block_x, block_y, depth = p.shape
    near = block_x
    copies = [
        pltpu.make_async_copy(source, target, sems.at[index])
        for index, (source, target) in enumerate(
            [(p_hbm, p), (s_hbm, s), (rho_hbm, rho), (floor_hbm, floors), (pert_hbm, pert),
             (ids_hbm, ids)]
        )
    ]
    for copy in copies:
        copy.start()
    shape = (block_y, depth)
    deep = lax.broadcasted_iota(jnp.int32, shape, 1).astype(jnp.float32)
    lane = lax.broadcasted_iota(jnp.int32, shape, 1)
    same = lax.broadcasted_iota(jnp.int32, (block_y, block_y), 0) == (
        lax.broadcasted_iota(jnp.int32, (block_y, block_y), 1)
    )
    for copy in copies:
        copy.wait()
    for slot in range(slots):
        lines = floors[slot].astype(jnp.float32)
        for x in range(block_x):
            line = jnp.broadcast_to(lines[x:x + 1], (block_y, block_y))
            floor = jnp.sum(jnp.where(same, line, 0.0), axis=1, keepdims=True)
            primary = p[slot, x].astype(jnp.float32)
            shear = s[slot, x].astype(jnp.float32)
            square = primary * primary
            stiffness = jnp.where(deep >= floor, square + shear * shear, square)
            coef = speed_factor * stiffness / rho[slot, x].astype(jnp.float32)
            coef = coef.astype(out_ref.dtype)
            for piece in range(x, out_ref.shape[0], near):
                out_ref[piece, 2 * slot] = coef
                out_ref[piece, 2 * slot + 1] = pert[slot, x]
    lane = lane - FACTS * lax.axis_index("shot")
    facts = jnp.where(lane == slots, row_ref[0], 0)
    facts = jnp.where(lane == slots + 1, col_ref[0], facts)
    for slot in range(slots):
        facts = jnp.where(lane == slot, ids[slot], facts)
    facts = facts.astype(jnp.float32).astype(out_ref.dtype)
    for piece in range(out_ref.shape[0]):
        out_ref[piece, 2 * slots] = facts


def pick_kernel(slots, near, pieces_ref, *refs):
    chips = near // 2
    out_refs = refs[:chips][::-1]
    beside_ref, facts_ref, facts, spots, sem = refs[chips:]
    count = spots.shape[0] // slots
    tiles = 2 * slots + 1
    line = pieces_ref[2 * slots].astype(jnp.float32)
    for piece in range(1, count):
        line = line + pieces_ref[piece * tiles + 2 * slots].astype(jnp.float32)
    facts_ref[...] = line.astype(jnp.int32)[0:1]
    copy = pltpu.make_async_copy(facts_ref, facts, sem)
    copy.start()
    me = lax.axis_index("shot")
    copy.wait()
    for piece in range(count):
        for slot in range(slots):
            spots[facts[0, FACTS * piece + slot]] = piece * tiles + 2 * slot
    for t in range(near):
        shot = me ^ t
        out_ref, start_tile = out_refs[t // 2], t % 2 * APX * APY * 2
        if t == 1:
            out_ref, start_tile = beside_ref, 0
        first = facts[0, FACTS * shot + slots] * GRID_COLS + facts[0, FACTS * shot + slots + 1]
        for x in range(APX):
            found = []
            for y in range(APY):
                spot = spots[first + x * GRID_COLS + y]
                found += [pieces_ref[spot], pieces_ref[spot + 1]]
            for index, tile in enumerate(found):
                out_ref[start_tile + x * APY * 2 + index] = tile


def ends(shape):
    lane = lax.broadcasted_iota(jnp.int32, shape, 1)
    row = lax.broadcasted_iota(jnp.int32, shape, 0)
    return lane == 0, lane == shape[1] - 1, row == 0, row == shape[0] - 1


def laplace(before, here, after, masks):
    lane_0, lane_n, row_0, row_n = masks
    many = len(here)
    depth = here[0].shape[1]
    low = [jnp.where(row_0, 0.0, pltpu.roll(here[-1], 1, 0))] + here[:-1]
    high = here[1:] + [jnp.where(row_n, 0.0, pltpu.roll(here[0], LANES - 1, 0))]
    result = []
    for v in range(many):
        up = jnp.where(lane_0, 0.0, pltpu.roll(here[v], 1, 1))
        down = jnp.where(lane_n, 0.0, pltpu.roll(here[v], depth - 1, 1))
        total = (before[v] + after[v]) + (low[v] + high[v]) + (up + down)
        result.append(total - 6.0 * here[v])
    return result


def registers(ref, x):
    return [ref[x, v] for v in range(ref.shape[1])]


def strided(ref, x):
    many = ref.shape[1] // LANES
    return [ref[x, pl.ds(v, LANES, stride=many)] for v in range(many)]


def sweep(count, fields, body, unroll):
    many = fields[0].shape[1]
    zero = [jnp.zeros(fields[0].shape[2:], jnp.float32)] * many
    first = [(zero, registers(field, 0)) for field in fields]

    def step(x, carry):
        rows = [
            (before, here, registers(field, x + 1))
            for (before, here), field in zip(carry, fields)
        ]
        body(x, rows)
        return [(here, after) for _, here, after in rows]

    lax.fori_loop(0, count, step, first, unroll=unroll)


def start_kernel(prev_ref, now_ref, wave_ref, grad_ref, next_ref, flat, flat_prev, field):
    span_x, span_y, depth = now_ref.shape
    many = span_y // LANES
    masks = ends((LANES, depth))

    def load(x, carry):
        flat[x] = now_ref[x].astype(jnp.float32)
        flat_prev[x] = prev_ref[x].astype(jnp.float32)
        return carry

    lax.fori_loop(0, span_x, load, 0, unroll=2)

    def order(x, carry):
        rows = strided(flat, x)
        older = strided(flat_prev, x)
        for v in range(many):
            field[x, v] = rows[v]
            wave_ref[x, v] = rows[v]
            next_ref[x, v] = 2.0 * rows[v] - older[v]
        return carry

    lax.fori_loop(0, span_x, order, 0, unroll=2)
    for v in range(many):
        field[span_x, v] = jnp.zeros((LANES, depth), jnp.float32)

    def body(x, rows):
        grads = laplace(*rows[0], masks)
        for v in range(many):
            grad_ref[x, v] = grads[v]

    sweep(span_x, [field], body, 32)


def start(before, current):
    span_x, span_y, depth = before.shape
    many = span_y // LANES
    out = jax.ShapeDtypeStruct((span_x, many, LANES, depth), jnp.float32)
    flat = pltpu.VMEM((span_x, span_y, depth), jnp.float32)
    return pl.pallas_call(
        start_kernel,
        out_shape=(out, out, out),
        in_specs=[vmem()] * 2,
        out_specs=(vmem(),) * 3,
        scratch_shapes=[flat, flat, pltpu.VMEM((span_x + 1, many, LANES, depth), jnp.float32)],
        compiler_params=limit(8),
        cost_estimate=pl.CostEstimate(
            flops=20 * before.size, bytes_accessed=16 * before.size, transcendentals=0
        ),
        name="start",
    )(before, current)


def wave_kernel(near, *refs):
    chips = near // 2
    model_refs = parts(refs[:near], 2 * APX * APY)
    u_0, g_0, next_ref = refs[near:near + 3]
    refs = refs[near + 3:]
    out_refs = refs[:chips][::-1]
    kap, con, u_1, u_2, u_3, d_0, d_1, d_2, kb_3, kb_2, kb_1 = refs[chips:chips + 11]
    g_1, g_2, d_3, b_2, b_1, image, result = refs[chips + 11:]
    span_x, many = u_0.shape[:2]
    depth = u_0.shape[3]
    block_y = model_refs[0].shape[1]
    block_x = span_x // APX
    place = lax.axis_index("shot") % near
    masks = ends((LANES, depth))
    each = range(many)
    for field in (u_1, u_2, u_3, d_0, d_1, d_2, kb_3, kb_2, kb_1):
        for v in each:
            field[span_x, v] = jnp.zeros((LANES, depth), jnp.float32)

    for k, model_ref in enumerate(model_refs):
        for x in range(APX):
            at = x * block_x + (place ^ k)
            for y in range(APY):
                rows = pl.ds(y * block_y, block_y)
                tile = 2 * (x * APY + y)
                kap[at, rows] = model_ref[tile].astype(jnp.float32)
                con[at, rows] = speed_factor * model_ref[tile + 1].astype(jnp.float32)

    def forward_0(x, carry):
        kaps, cons, grads = strided(kap, x), strided(con, x), registers(g_0, x)
        older = registers(next_ref, x)
        for v in each:
            d_0[x, v] = cons[v] * grads[v]
            u_1[x, v] = older[v] + kaps[v] * grads[v]
        return carry

    lax.fori_loop(0, span_x, forward_0, 0, unroll=32)

    def forward(u_now, u_prev, d_now, d_prev, u_next, d_next, g_now):
        def body(x, rows):
            waves, deltas = rows
            grads = laplace(*waves, masks)
            spread = laplace(*deltas, masks)
            kaps, cons = strided(kap, x), strided(con, x)
            for v in each:
                value = 2.0 * deltas[1][v] + kaps[v] * spread[v] + cons[v] * grads[v]
                if d_prev is not None:
                    value = value - d_prev[x, v]
                d_next[x, v] = value
                if u_next is None:
                    image[x, v] = grads[v] * value
                    kb_3[x, v] = kaps[v] * value
                else:
                    g_now[x, v] = grads[v]
                    u_next[x, v] = 2.0 * waves[1][v] - u_prev[x, v] + kaps[v] * grads[v]

        sweep(span_x, [u_now, d_now], body, 32)

    forward(u_1, u_0, d_0, None, u_2, d_1, g_1)
    forward(u_2, u_1, d_1, d_0, u_3, d_2, g_2)
    forward(u_3, u_2, d_2, d_1, None, d_3, None)

    def adjoint(kb, b_now, b_after, data, grad, kb_next, b_next):
        def body(x, rows):
            spread = laplace(*rows[0], masks)
            kaps = None if kb_next is None else strided(kap, x)
            for v in each:
                back = 2.0 * b_now[x, v] + spread[v] + data[x, v]
                if b_after is not None:
                    back = back - b_after[x, v]
                total = image[x, v] + grad[x, v] * back
                if kb_next is None:
                    total = (image_scale * total).astype(result.dtype)
                    result[x % block_x // 2, (x % 2 * APX + x // block_x) * many + v] = total
                else:
                    image[x, v] = total
                    b_next[x, v] = back
                    kb_next[x, v] = kaps[v] * back

        sweep(span_x, [kb], body, 32)

    adjoint(kb_3, d_3, None, d_2, g_2, kb_2, b_2)
    adjoint(kb_2, b_2, d_3, d_1, g_1, kb_1, b_1)
    adjoint(kb_1, b_1, b_2, d_0, g_0, None, None)
    for k, out_ref in enumerate(out_refs):
        out_ref[...] = result[place // 2 ^ k]


def wave(models, started):
    span_x, many, _, depth = started[0].shape
    near = len(models)
    flat = pltpu.VMEM((span_x, many * LANES, depth), jnp.float32)
    field = pltpu.VMEM((span_x + 1, many, LANES, depth), jnp.float32)
    plain = pltpu.VMEM((span_x, many, LANES, depth), jnp.float32)
    tiles = APX * many
    out = jax.ShapeDtypeStruct((2 * tiles, LANES, depth), jnp.bfloat16)
    terms = pl.pallas_call(
        functools.partial(wave_kernel, near),
        out_shape=(out,) * (near // 2),
        in_specs=[vmem()] * (near + 3),
        out_specs=(vmem(),) * (near // 2),
        scratch_shapes=[flat] * 2 + [field] * 9 + [plain] * 6
        + [pltpu.VMEM((near // 2, 2 * tiles, LANES, depth), jnp.bfloat16)],
        compiler_params=limit(20),
        name="wave",
    )(*models, *started)
    return terms[::-1]


def wave_split_depth(models, before, current):
    near = len(models)
    order = (lax.axis_index("shot") % near) ^ jnp.arange(near)
    chips = near // 2
    length = models[-1].shape[0]
    pairs = zip(models[:chips][::-1], models[chips:][::-1])
    model = jnp.stack([part for own, other in pairs for part in (own[:length], other)])
    model = model[order]
    span_x, span_y, depth = before.shape
    block_x, tiles, block_y, _ = model.shape
    grids = model.reshape(block_x, APX, APY, 2, block_y, depth).transpose(3, 1, 0, 2, 4, 5)
    grids = grids.reshape(2, span_x, span_y, depth).astype(jnp.float32)
    image = image_scale * propagate(
        grids[0],
        speed_factor * grids[1],
        before.astype(jnp.float32),
        current.astype(jnp.float32),
        laplace_many,
    )
    many = span_y // LANES
    image = image.reshape(APX, chips, 2, LANES, many, depth).transpose(1, 2, 0, 4, 3, 5)
    image = image.reshape(chips, 2 * APX * many, LANES, depth).astype(jnp.bfloat16)
    image = image[chip_place(chips) ^ jnp.arange(chips)]
    return [image[k] for k in range(chips)]


def stack_kernel(slots, near, facts_ref, *refs):
    terms_refs = refs[:near][::-1]
    mine_ref, other_ref, facts, total, lined, sem = refs[near:]
    count = 2 * mine_ref.shape[0]
    half = terms_refs[0].shape[0] // 2
    wide = half // APX
    width = LANES // APY
    grid_rows = total.shape[1] // wide
    copy = pltpu.make_async_copy(facts_ref, facts, sem)
    copy.start()
    me = lax.axis_index("shot")

    def clear(index, carry):
        for r in range(2):
            total[r, index] = jnp.zeros(total.shape[2:], total.dtype)
        return carry

    lax.fori_loop(0, total.shape[1], clear, 0, unroll=32)
    copy.wait()
    for k, terms_ref in enumerate(terms_refs):
        shot = FACTS * (me ^ 2 * k)
        first = facts[0, shot + slots] * wide
        rows = pl.ds(facts[0, shot + slots + 1] * width, LANES)
        for r in range(2):
            sums = [
                total[r, first + tile, rows] + terms_ref[r * half + tile].astype(jnp.float32)
                for tile in range(half)
            ]
            for tile in range(half):
                total[r, first + tile, rows] = sums[tile]

    def line(row, carry):
        for r in range(2):
            for part in range(wide):
                for tile in range(total.shape[2] // LANES):
                    at = pl.ds(tile * LANES * wide + part, LANES, stride=wide)
                    lined[r, row, at] = total[
                        r, row * wide + part, tile * LANES:(tile + 1) * LANES
                    ]
        return carry

    lax.fori_loop(0, grid_rows, line, 0, unroll=8)

    def give(chip, carry):
        for own, out_ref in enumerate((mine_ref, other_ref)):
            found = []
            for slot in range(slots):
                block = facts[0, FACTS * (2 * chip + (me + own) % 2) + slot]
                rows = pl.ds(pl.multiple_of(block % GRID_COLS * LANES, LANES), LANES)
                found += [lined[r, block // GRID_COLS, rows] for r in range(2)]
            for index, tile in enumerate(found):
                out_ref[chip, index] = tile.astype(out_ref.dtype)
        return carry

    lax.fori_loop(0, count // 2, give, 0, unroll=8)


def join_kernel(mine_ref, other_ref, out_ref):
    for chip in range(out_ref.shape[0]):
        total = mine_ref[chip] + other_ref[chip].astype(jnp.float32)
        out_ref[chip] = total.astype(out_ref.dtype)


def finish_kernel(near, sums_ref, out_ref):
    for place in range(near):
        for slot in range(out_ref.shape[0]):
            for r in range(2):
                result = sums_ref[place, 2 * slot + r].astype(jnp.float32)
                for chip in range(place + near, sums_ref.shape[0], near):
                    result = result + sums_ref[chip, 2 * slot + r].astype(jnp.float32)
                out_ref[slot, 2 * place + r] = result


def per_device(
    velocity_p,
    velocity_s,
    density,
    perturbation,
    seafloor,
    owner_ids,
    corner_x,
    corner_y,
    wave_prev,
    wave_now,
):
    slots, block_x, block_y, depth = velocity_p.shape
    count = lax.axis_size("shot")
    assert count == 2 * block_x and block_y == LANES
    assert slots + 2 <= FACTS and FACTS * count <= depth
    patch = APX * APY
    split = lax.axis_size("depth") > 1
    if split:
        seafloor = seafloor - lax.axis_index("depth") * depth

    near = block_x
    assert count % near == 0 and near & (near - 1) == 0

    def swap(values):
        return [
            lax.ppermute(values[k], "shot", [(i, i ^ 2 * k) for i in range(count)])
            if k else values[0]
            for k in range(len(values) - 1, -1, -1)
        ]

    def across(value):
        return lax.ppermute(value, "shot", [(i, i ^ 1) for i in range(count)])

    sent = pl.pallas_call(
        prepare_kernel,
        out_shape=jax.ShapeDtypeStruct((count, 2 * slots + 1, block_y, depth), jnp.bfloat16),
        in_specs=[smem()] * 2 + [pl.BlockSpec(memory_space=pltpu.HBM)] * 6,
        out_specs=vmem(),
        scratch_shapes=[
            pltpu.SMEM(owner_ids.shape, jnp.int32),
            pltpu.VMEM(seafloor.shape, jnp.int32),
            *[pltpu.VMEM(velocity_p.shape, jnp.bfloat16) for _ in range(4)],
            pltpu.SemaphoreType.DMA((6,)),
        ],
        name="prepare",
    )(
        corner_x, corner_y, owner_ids, seafloor,
        velocity_p, velocity_s, density, perturbation,
    )
    pieces = lax.all_to_all(sent, "shot", 0, 0, tiled=True)

    if not split:
        started = start(wave_prev[0], wave_now[0])
        pieces, started = lax.optimization_barrier((pieces, started))
    *picked, facts = pl.pallas_call(
        functools.partial(pick_kernel, slots, near),
        out_shape=(
            *[
                jax.ShapeDtypeStruct((patch * tiles, block_y, depth), jnp.bfloat16)
                for tiles in [4] * (near // 2 - 1) + [2, 2]
            ],
            jax.ShapeDtypeStruct((1, depth), jnp.int32),
        ),
        in_specs=[vmem()],
        out_specs=(vmem(),) * (near // 2 + 2),
        scratch_shapes=[
            pltpu.SMEM((1, depth), jnp.int32),
            pltpu.SMEM((count * slots,), jnp.int32),
            pltpu.SemaphoreType.DMA,
        ],
        compiler_params=limit(3),
        name="pick",
    )(pieces.reshape(count * (2 * slots + 1), block_y, depth))
    *picked, beside = picked
    models = swap(picked[::-1])
    handed = [value[patch * 2:] for value in models[:-1]] + [beside]
    models = models + [across(value) for value in handed]

    if split:
        terms = wave_split_depth(models, wave_prev[0], wave_now[0])
    else:
        terms = wave(models, started)
    terms = swap(terms)

    chips = count // 2
    grid_rows = count * slots // GRID_COLS
    wide = terms[0].shape[0] // 2 // APX
    shape = (chips, 2 * slots, block_y, depth)
    mine, other = pl.pallas_call(
        functools.partial(stack_kernel, slots, near // 2),
        out_shape=(
            jax.ShapeDtypeStruct(shape, jnp.float32), jax.ShapeDtypeStruct(shape, jnp.bfloat16)
        ),
        in_specs=[vmem()] * (near // 2 + 1),
        out_specs=(vmem(), vmem()),
        scratch_shapes=[
            pltpu.SMEM(facts.shape, jnp.int32),
            pltpu.VMEM((2, grid_rows * wide, GRID_COLS * LANES // APY, depth), jnp.float32),
            pltpu.VMEM((2, grid_rows, GRID_COLS * block_y, depth), jnp.float32),
            pltpu.SemaphoreType.DMA,
        ],
        compiler_params=limit(4),
        name="stack",
    )(facts, *terms)
    joined = pl.pallas_call(
        join_kernel,
        out_shape=jax.ShapeDtypeStruct(shape, jnp.bfloat16),
        in_specs=[vmem()] * 2,
        out_specs=vmem(),
        compiler_params=limit(2),
        name="join",
    )(mine, across(other))
    sums = lax.all_to_all(
        joined, "shot", 0, 0, tiled=True,
        axis_index_groups=[list(range(core, count, 2)) for core in range(2)],
    )
    return pl.pallas_call(
        functools.partial(finish_kernel, near // 2),
        out_shape=jax.ShapeDtypeStruct(velocity_p.shape, jnp.float32),
        in_specs=[vmem()],
        out_specs=vmem(),
        compiler_params=limit(2),
        name="finish",
    )(sums)


def solution(mesh):
    in_specs = (
        P(("grp", "shot"), None, None, "depth"),
        P(("grp", "shot"), None, None, "depth"),
        P(("grp", "shot"), None, None, "depth"),
        P(("grp", "shot"), None, None, "depth"),
        P(("grp", "shot"), None, None),
        P(("grp", "shot")),
        P(("grp", "shot")),
        P(("grp", "shot")),
        P(("grp", "shot"), None, None, "depth"),
        P(("grp", "shot"), None, None, "depth"),
    )
    out_specs = P(("grp", "shot"), None, None, "depth")
    return jax.shard_map(
        per_device, mesh=mesh, in_specs=in_specs, out_specs=out_specs, check_vma=False
    )
```
